32 devices in a mesh: sp: 2 (over core), dp: 16 (over z, y, x).
Axes of the slice: x: 2, y: 2, z: 4, core: 2. Of those that a mesh axis runs over, the one named last changes fastest.
Arguments:
- hidden: bfloat16 [16, 256, 2048], P('dp', 'sp'), may hold values from -6 to 6
- cotangent: bfloat16 [16, 256, 2048], P('dp', 'sp'), may hold values from -6 to 6
- exit_layers: int32 [16, 2], P('dp'), may hold values from 4 to 24, as said below
- qkv_weight: bfloat16 [2048, 6144], P('sp'), may hold values from -0.125 to 0.125
- out_weight: bfloat16 [2048, 2048], P('sp'), may hold values from -3 to 3
- up_weight: bfloat16 [2048, 8192], P('sp'), may hold values from -0.125 to 0.125
- down_weight: bfloat16 [8192, 2048], P('sp'), may hold values from -0.0625 to 0.0625
- query_bias: float32 [2048], replicated, may hold values from -2 to 2
- value_bias: float32 [2048], replicated, may hold values from -2 to 2
- out_bias: float32 [2048], replicated, may hold values from -2 to 2
- up_bias: float32 [8192], replicated, may hold values from -2 to 2
- down_bias: float32 [2048], replicated, may hold values from -2 to 2
- attn_gain: float32 [2048], replicated, may hold values from 0.5 to 1.5
- attn_shift: float32 [2048], replicated, may hold values from -2 to 2
- ffn_gain: float32 [2048], replicated, may hold values from 0.5 to 1.5
- ffn_shift: float32 [2048], replicated, may hold values from -2 to 2
Outputs:
- mixed: bfloat16 [16, 256, 2048], P('dp', 'sp')
- input_grad: bfloat16 [16, 256, 2048], P('dp', 'sp')
- qkv_grad: float32 [2048, 6144], P('sp')
- out_grad: float32 [2048, 2048], P('sp')
- up_grad: float32 [2048, 8192], P('sp')
- down_grad: float32 [8192, 2048], P('sp')
- query_bias_grad: float32 [2048], replicated
- value_bias_grad: float32 [2048], replicated
- out_bias_grad: float32 [2048], replicated
- up_bias_grad: float32 [8192], replicated
- down_bias_grad: float32 [2048], replicated
- attn_gain_grad: float32 [2048], replicated
- attn_shift_grad: float32 [2048], replicated
- ffn_gain_grad: float32 [2048], replicated
- ffn_shift_grad: float32 [2048], replicated
The draws below stay inside these ranges and needn't reach their ends.
Inputs may be any that keep to these rules, and one draw needn't show every extreme that they name: `exit_layers`: row s holds sequence s's smallest exit layer, then its largest; the smallest is at most 11 and the largest at least 13, and some row holds 4, some row 24.
All inputs are finite; a program needn't handle non-finite values.
Results may differ from the reference program's by a relative error of at most 0.02.
Values may be sent and summed in bfloat16 or wider, within the bound.
No kernel may reach another device: no remote copies, remote signals or barrier semaphores. Data moves between devices by JAX's collectives and lax.ppermute only.
A program may use at most 704 MiB of HBM per device.

```python
import jax
import jax.numpy as jnp
from jax import lax

D = 2048
HEADS = 32
HEAD_DIM = 64
FF = 8192
TILE = 128
LAYER = 12
LEN = 256
SEQS = 16


def draw_exit_layers(key, part):
    key = jax.random.fold_in(key, 7)
    first_key, second_key, third_key = jax.random.split(key, 3)
    lowest = jax.random.randint(first_key, (SEQS,), 4, 12)
    highest = jax.random.randint(second_key, (SEQS,), 13, 25)
    chosen = jax.random.randint(third_key, (2,), 0, SEQS)
    lowest = lowest.at[chosen[0]].set(4)
    highest = highest.at[chosen[1]].set(24)
    return jnp.stack([lowest, highest], axis=1).astype(jnp.int32)


def shard_levels(stream_key, shape, pieces, low, top_value):
    level = 1.0
    for dim, parts in pieces:
        draws = jax.random.uniform(jax.random.fold_in(jax.random.fold_in(stream_key, 6), dim), (parts,), jnp.float32, low / len(pieces), top_value / len(pieces))
        level = level * jnp.repeat(jnp.exp(draws), shape[dim] // parts).reshape((-1,) + (1,) * (len(shape) - 1 - dim))
    return level


def normal_values(rng, extent, width, bound, cuts=(), held_as=jnp.bfloat16):
    level = shard_levels(rng, extent, cuts, -0.22, 0.18) if cuts else 1.0
    values = jax.random.normal(rng, extent, jnp.float32) * width * level
    return jnp.minimum(jnp.maximum(values, -bound), bound).astype(held_as)


def setup_inputs(seed: int = 0) -> dict:
    seeds = jax.random.split(jax.random.key(seed), 17)
    return {
        "hidden": normal_values(seeds[0], (SEQS, LEN, D), 1.0, 6.0, ((0, 16), (1, 2))),
        "cotangent": normal_values(seeds[1], (SEQS, LEN, D), 1.0, 6.0, ((0, 16), (1, 2))),
        "exit_layers": draw_exit_layers(jax.random.fold_in(seeds[16], 71), 0),
        "qkv_weight": normal_values(seeds[3], (D, 3 * D), D ** -0.5, 0.125, ((0, 2),)),
        "out_weight": normal_values(seeds[4], (D, D), (max(D // 512, 1)) ** -0.5, 3.0, ((0, 2),)),
        "up_weight": normal_values(seeds[5], (D, FF), D ** -0.5, 0.125, ((0, 2),)),
        "down_weight": normal_values(seeds[6], (FF, D), FF ** -0.5, 0.0625, ((0, 2),)),
        "query_bias": normal_values(seeds[7], (D,), 0.3, 2.0, (), jnp.float32),
        "value_bias": normal_values(seeds[8], (D,), 0.3, 2.0, (), jnp.float32),
        "out_bias": normal_values(seeds[9], (D,), 0.3, 2.0, (), jnp.float32),
        "up_bias": normal_values(seeds[10], (FF,), 0.3, 2.0, (), jnp.float32),
        "down_bias": normal_values(seeds[11], (D,), 0.3, 2.0, (), jnp.float32),
        "attn_gain": jnp.clip(1.0 + 0.1 * jax.random.normal(seeds[12], (D,), jnp.float32), 0.5, 1.5),
        "attn_shift": normal_values(seeds[13], (D,), 0.3, 2.0, (), jnp.float32),
        "ffn_gain": jnp.clip(1.0 + 0.1 * jax.random.normal(seeds[14], (D,), jnp.float32), 0.5, 1.5),
        "ffn_shift": normal_values(seeds[15], (D,), 0.3, 2.0, (), jnp.float32),
    }


@jax.custom_vjp
def low(v):
    return lax.optimization_barrier(v.astype(jnp.bfloat16)).astype(jnp.float32)

@jax.custom_vjp
def low_back(v):
    return v

def low_keep(v):
    return (low(v), None)

def low_pass(kept, grad):
    return (grad,)

def back_keep(v):
    return (v, None)

def back_low(kept, grad):
    return (low(grad),)
low.defvjp(low_keep, low_pass)
low_back.defvjp(back_keep, back_low)
precise = lax.Precision.HIGHEST

def layer_norm(values, gain, shift):
    center = lax.optimization_barrier(jnp.mean(values, axis=-1, keepdims=True))
    centered = values - center
    variance = lax.optimization_barrier(jnp.mean(centered * centered, axis=-1, keepdims=True))
    return centered * lax.rsqrt(variance + 1e-05) * gain + shift

def active_rows(bounds, first_row, row_count, sequence_length):
    position = first_row + jnp.arange(row_count, dtype=jnp.int32)
    tile_start = position // TILE * TILE
    exit_layer = bounds[1] - (bounds[1] - bounds[0]) * tile_start // sequence_length
    return (exit_layer > LAYER).astype(jnp.float32)[:, None]

def attention(queries, key_rows, value_rows):
    sequence_length = queries.shape[0]
    block_rows = min(512, sequence_length)
    key_place = jnp.arange(sequence_length, dtype=jnp.int32)

    def query_block(block_index):
        first_row = block_index * block_rows
        query_part = lax.dynamic_slice_in_dim(queries, first_row, block_rows, 0)
        scores = low_back(jnp.einsum('qhd,khd->hqk', query_part, key_rows, precision=precise) * HEAD_DIM ** (-0.5))
        query_place = first_row + jnp.arange(block_rows, dtype=jnp.int32)
        allowed = key_place[None, :] <= query_place[:, None]
        scores = jnp.where(allowed[None], scores, -1e+30)
        row_peak = lax.optimization_barrier(jnp.max(scores, axis=-1, keepdims=True))
        raised = jnp.exp(scores - row_peak)
        chances = low(raised / lax.optimization_barrier(jnp.sum(raised, axis=-1, keepdims=True)))
        return jnp.einsum('hqk,khd->qhd', chances, value_rows, precision=precise)
    blocks = lax.map(jax.checkpoint(query_block), jnp.arange(sequence_length // block_rows, dtype=jnp.int32))
    return blocks.reshape(sequence_length, -1)

def layer_forward(inputs, params, active):
    qkv_w, out_w, up_w, down_w, query_b, value_b, out_b, up_b, down_b, gain_one, shift_one, gain_two, shift_two = params
    sequence_length = inputs.shape[0]
    normed_one = low(layer_norm(inputs, gain_one, shift_one))
    bias_cat = jnp.concatenate([query_b, jnp.zeros_like(query_b), value_b])
    qkv = low(low_back(jnp.dot(normed_one, qkv_w, precision=precise) + bias_cat))
    split_heads = qkv.reshape(sequence_length, 3, HEADS, HEAD_DIM)
    attended = attention(split_heads[:, 0], split_heads[:, 1], split_heads[:, 2])
    attended = low(low_back(attended))
    attn_out = low_back(jnp.dot(attended, out_w, precision=precise) + out_b)
    middle = inputs + active * attn_out
    normed_two = low(layer_norm(middle, gain_two, shift_two))
    up_rows = low_back(jnp.dot(normed_two, up_w, precision=precise) + up_b)
    inner_act = low(jax.nn.gelu(up_rows))
    down_rows = low_back(jnp.dot(inner_act, down_w, precision=precise) + down_b)
    return middle + active * down_rows

def reference(hidden, cotangent, exit_layers, qkv_weight, out_weight, up_weight, down_weight, query_bias, value_bias, out_bias, up_bias, down_bias, attn_gain, attn_shift, ffn_gain, ffn_shift):
    params = tuple((item.astype(jnp.float32) for item in (qkv_weight, out_weight, up_weight, down_weight, query_bias, value_bias, out_bias, up_bias, down_bias, attn_gain, attn_shift, ffn_gain, ffn_shift)))
    sequence_length = hidden.shape[1]
    initial = jax.tree.map(jnp.zeros_like, params)

    def sequence_step(running, sequence):
        seq_input, seq_cot, bounds = sequence
        active = active_rows(bounds, 0, sequence_length, sequence_length)
        result, pullback = jax.vjp(lambda inputs, weights: layer_forward(inputs, weights, active), seq_input, params)
        in_grad, param_grads = pullback(seq_cot)
        return (jax.tree.map(jnp.add, running, param_grads), (result, in_grad))
    totals, (results, in_grads) = lax.scan(sequence_step, initial, (hidden.astype(jnp.float32), cotangent.astype(jnp.float32), exit_layers))
    return (results.astype(jnp.bfloat16), in_grads.astype(jnp.bfloat16), totals[0], totals[1], totals[2], totals[3], totals[4], totals[5], totals[6], totals[7], totals[8], totals[9], totals[10], totals[11], totals[12])
```

```python
import functools

import jax
import jax.numpy as jnp
from jax import lax
from jax.experimental import pallas as pl
from jax.experimental.pallas import tpu as pltpu
from jax.sharding import PartitionSpec as P

HEAD_DIM = 64
TILE = 128
LAYER = 12
LINE = 4
GROUP = 4
F32 = jnp.float32
LOW = jnp.bfloat16


def layer_norm(values, gain, shift):
    center = jnp.mean(values, axis=-1, keepdims=True)
    centered = values - center
    variance = jnp.mean(centered * centered, axis=-1, keepdims=True)
    return centered * lax.rsqrt(variance + 1e-05) * gain + shift


def active_rows(bounds, first_row, row_count, sequence_length):
    position = first_row + jnp.arange(row_count, dtype=jnp.int32)
    tile_start = position // TILE * TILE
    exit_layer = bounds[1] - (bounds[1] - bounds[0]) * tile_start // sequence_length
    return (exit_layer > LAYER).astype(F32)[:, None]


def gelu_and_slope(values):
    scale = (2.0 / jnp.pi) ** 0.5
    square = values * values
    bend = jnp.tanh(scale * values * (1.0 + 0.044715 * square))
    rise = 0.5 * (1.0 + bend)
    slope = rise + 0.5 * values * (1.0 - bend * bend) * scale * (1.0 + 0.134145 * square)
    return values * rise, slope


def dot(left, right, left_dim, right_dim):
    return lax.dot_general(
        left, right, (((left_dim,), (right_dim,)), ((), ())), preferred_element_type=F32
    )


def roll_rows(value):
    rows = value.shape[0] // 2
    return jnp.concatenate([value[rows:], value[:rows]])


def estimate(flops, *arrays):
    return pl.CostEstimate(
        flops=flops,
        bytes_accessed=sum(a.size * a.dtype.itemsize for a in arrays),
        transcendentals=0,
    )


def far(value):
    return pltpu.with_memory_space_constraint(value, pltpu.HBM)


def limit(mebibytes):
    return pltpu.CompilerParams(vmem_limit_bytes=mebibytes << 20)


def halves(core_ref, values, mine_ref, theirs_ref):
    width = mine_ref.shape[1]
    first = core_ref[0] == 0
    low, high = values[:, :width], values[:, width:]
    mine_ref[...] = jnp.where(first, low, high).astype(LOW)
    theirs_ref[...] = jnp.where(first, high, low).astype(LOW)


def norm_one_kernel(core_ref, x_ref, gain_ref, shift_ref, mine_ref, theirs_ref):
    normed = layer_norm(x_ref[...].astype(F32), gain_ref[...], shift_ref[...])
    halves(core_ref, normed, mine_ref, theirs_ref)


def norm_two_kernel(
    core_ref, x_ref, active_ref, part_ref, theirs_part_ref, bias_ref, gain_ref, shift_ref,
    middle_ref, mine_ref, theirs_ref,
):
    rows = x_ref.shape[0]
    attn = part_ref[:rows] + theirs_part_ref[...] + bias_ref[...]
    middle = x_ref[...].astype(F32) + active_ref[...] * attn
    middle_ref[...] = middle
    halves(core_ref, layer_norm(middle, gain_ref[...], shift_ref[...]), mine_ref, theirs_ref)


def norm(kernel, core, rows, width, whole, *operands):
    half = jax.ShapeDtypeStruct((rows, width // 2), LOW)
    outs = [jax.ShapeDtypeStruct((rows, width), F32)] * whole + [half, half]
    vmem = pl.BlockSpec(memory_space=pltpu.VMEM)
    return pl.pallas_call(
        kernel,
        in_specs=[pl.BlockSpec(memory_space=pltpu.SMEM)] + [vmem] * len(operands),
        out_specs=[vmem] * len(outs),
        out_shape=outs,
        compiler_params=limit(24),
        cost_estimate=estimate(20 * rows * width, *operands),
    )(core, *operands)


def columns_kernel(table_ref, left_ref, weight_ref, out_ref):
    out_ref[...] = dot(left_ref[...], weight_ref[...], 1, 0)


def times_columns(left, weight, table, block):
    rows, depth = left.shape
    steps = table.shape[0]
    return pl.pallas_call(
        columns_kernel,
        grid_spec=pltpu.PrefetchScalarGridSpec(
            num_scalar_prefetch=1,
            grid=(steps,),
            in_specs=[
                pl.BlockSpec((rows, depth), lambda i, t: (0, 0)),
                pl.BlockSpec((depth, block), lambda i, t: (0, t[i])),
            ],
            out_specs=pl.BlockSpec((rows, block), lambda i, t: (0, i)),
        ),
        out_shape=jax.ShapeDtypeStruct((rows, steps * block), F32),
        compiler_params=limit(24),
        cost_estimate=pl.CostEstimate(
            flops=2 * rows * depth * steps * block,
            bytes_accessed=2 * depth * (rows + steps * block) + 4 * rows * steps * block,
            transcendentals=0,
        ),
    )(table, left, far(weight))


def back_kernel(turned, table_ref, left_ref, weight_ref, *rest):
    out_ref = rest[-1]
    left = left_ref[...]
    if turned:
        left = roll_rows(left)
    part = dot(left, weight_ref[...], 1, 1)

    @pl.when(pl.program_id(1) == 0)
    def _():
        out_ref[...] = part + rest[0][...] if len(rest) > 1 else part

    @pl.when(pl.program_id(1) > 0)
    def _():
        out_ref[...] += part


def times_back(left, weight, table, block, deep, start=None, turned=False):
    rows = left.shape[0]
    depth = weight.shape[0]
    steps = table.shape[0]
    out_spec = pl.BlockSpec((rows, deep), lambda k, i, t: (0, k))
    in_specs = [
        pl.BlockSpec((rows, block), lambda k, i, t: (0, i)),
        pl.BlockSpec((deep, block), lambda k, i, t: (k, t[i])),
    ]
    operands = [table, left, far(weight)]
    if start is not None:
        in_specs.append(out_spec)
        operands.append(start)
    return pl.pallas_call(
        functools.partial(back_kernel, turned),
        grid_spec=pltpu.PrefetchScalarGridSpec(
            num_scalar_prefetch=1,
            grid=(depth // deep, steps),
            in_specs=in_specs,
            out_specs=out_spec,
        ),
        out_shape=jax.ShapeDtypeStruct((rows, depth), F32),
        compiler_params=limit(32),
        cost_estimate=pl.CostEstimate(
            flops=2 * rows * depth * steps * block,
            bytes_accessed=2 * steps * block * (rows + depth) + 8 * rows * depth,
            transcendentals=0,
        ),
    )(*operands)


def inner_kernel(grad_ref, weight_ref, mine_ref, theirs_ref, bias_ref, act_ref, out_ref, sum_ref):
    act, slope = gelu_and_slope(mine_ref[...] + roll_rows(theirs_ref[...]) + bias_ref[...])
    act_ref[...] = act.astype(LOW)
    grad = (dot(grad_ref[...], weight_ref[...], 1, 1) * slope).astype(LOW)
    out_ref[...] = grad
    sum_ref[...] = jnp.sum(grad.astype(F32), axis=0, keepdims=True)


def inner_layer(grads, weight, mine, theirs, bias, block):
    rows, width = grads.shape
    hidden = weight.shape[0]
    part = pl.BlockSpec((rows, block), lambda i: (0, i))
    line = pl.BlockSpec((1, block), lambda i: (0, i))
    return pl.pallas_call(
        inner_kernel,
        grid=(hidden // block,),
        in_specs=[
            pl.BlockSpec((rows, width), lambda i: (0, 0)),
            pl.BlockSpec((block, width), lambda i: (i, 0)),
            part,
            part,
            line,
        ],
        out_specs=[part, part, line],
        out_shape=[
            jax.ShapeDtypeStruct((rows, hidden), LOW),
            jax.ShapeDtypeStruct((rows, hidden), LOW),
            jax.ShapeDtypeStruct((1, hidden), F32),
        ],
        compiler_params=limit(32),
        cost_estimate=pl.CostEstimate(
            flops=2 * rows * width * hidden,
            bytes_accessed=2 * width * (rows + hidden) + 12 * rows * hidden,
            transcendentals=rows * hidden,
        ),
    )(grads, far(weight), mine, theirs, bias)


def head_chances(queries, keys, lanes_of_head, allowed):
    keys_of_head = jnp.where(lanes_of_head, keys, jnp.zeros_like(keys))
    scores = dot(queries, keys_of_head, 1, 1) * (HEAD_DIM**-0.5)
    scores = jnp.where(allowed, scores, -1e30)
    raised = jnp.exp(scores - jnp.max(scores, axis=-1, keepdims=True))
    return raised / jnp.sum(raised, axis=-1, keepdims=True)


def attend_masks(first, length, lanes):
    lane = lax.broadcasted_iota(jnp.int32, (length, lanes), 1)
    row = lax.broadcasted_iota(jnp.int32, (length, length), 0) + first
    column = lax.broadcasted_iota(jnp.int32, (length, length), 1) + first
    row = jnp.where(row >= length, row - length, row)
    column = jnp.where(column >= length, column - length, column)
    return lane, column <= row


def attend_forward_kernel(first_ref, *refs):
    mine, theirs, biases, lows, o_ref = refs[:3], refs[3:6], refs[6:9], refs[9:12], refs[12]
    sums = [
        (m[...] + roll_rows(t[...]) + b[...]).astype(LOW)
        for m, t, b in zip(mine, theirs, biases)
    ]
    for low, value in zip(lows, sums):
        low[...] = value
    queries, keys, values = sums
    lane, allowed = attend_masks(first_ref[0], *queries.shape)
    total = jnp.zeros(queries.shape, F32)
    for head in range(queries.shape[1] // HEAD_DIM):
        own = lane // HEAD_DIM == head
        chances = head_chances(queries, keys, own, allowed).astype(LOW)
        total += dot(chances, jnp.where(own, values, jnp.zeros_like(values)), 1, 0)
    o_ref[...] = total.astype(LOW)


def attend_forward(first, mine, theirs, bias):
    length, width = mine.shape
    width //= 3
    steps = width // 128
    parts = [
        pl.BlockSpec((length, 128), functools.partial(lambda p, i, t: (0, p * steps + i), p))
        for p in range(3)
    ]
    lines = [
        pl.BlockSpec((1, 128), functools.partial(lambda p, i, t: (0, p * steps + i), p))
        for p in range(3)
    ]
    return pl.pallas_call(
        attend_forward_kernel,
        grid_spec=pltpu.PrefetchScalarGridSpec(
            num_scalar_prefetch=1,
            grid=(steps,),
            in_specs=parts + parts + lines,
            out_specs=[parts[0]] * 4,
        ),
        out_shape=[jax.ShapeDtypeStruct((length, width), LOW)] * 4,
        compiler_params=limit(16),
        cost_estimate=pl.CostEstimate(
            flops=4 * length * length * width,
            bytes_accessed=32 * length * width,
            transcendentals=length * length * width // HEAD_DIM,
        ),
    )(first, mine, mine, mine, theirs, theirs, theirs, bias, bias, bias)


def attend_backward_kernel(first_ref, q_ref, k_ref, v_ref, g_ref, out_ref):
    queries, keys, values, grads = q_ref[...], k_ref[...], v_ref[...], g_ref[...]
    lane, allowed = attend_masks(first_ref[0], *queries.shape)
    dq = jnp.zeros(queries.shape, F32)
    dk = jnp.zeros(queries.shape, F32)
    dv = jnp.zeros(queries.shape, F32)
    for head in range(queries.shape[1] // HEAD_DIM):
        own = lane // HEAD_DIM == head
        chances = head_chances(queries, keys, own, allowed)
        head_grads = jnp.where(own, grads, jnp.zeros_like(grads))
        dv += dot(chances.astype(LOW), head_grads, 0, 0)
        chance_grads = dot(head_grads, values, 1, 1)
        inner = jnp.sum(chances * chance_grads, axis=-1, keepdims=True)
        score_grads = (chances * (chance_grads - inner)).astype(LOW)
        dq += dot(score_grads, jnp.where(own, keys, jnp.zeros_like(keys)), 1, 0)
        dk += dot(score_grads, jnp.where(own, queries, jnp.zeros_like(queries)), 0, 0)
    scale = HEAD_DIM**-0.5
    out_ref[0] = (dq * scale).astype(LOW)
    out_ref[1] = (dk * scale).astype(LOW)
    out_ref[2] = dv.astype(LOW)


def attend_backward(first, *operands):
    length, width = operands[0].shape
    block = pl.BlockSpec((length, 128), lambda i, t: (0, i))
    return pl.pallas_call(
        attend_backward_kernel,
        grid_spec=pltpu.PrefetchScalarGridSpec(
            num_scalar_prefetch=1,
            grid=(width // 128,),
            in_specs=[block] * 4,
            out_specs=pl.BlockSpec((3, length, 128), lambda i, t: (0, 0, i)),
        ),
        out_shape=jax.ShapeDtypeStruct((3, length, width), LOW),
        compiler_params=limit(16),
        cost_estimate=pl.CostEstimate(
            flops=10 * length * length * width,
            bytes_accessed=14 * length * width,
            transcendentals=length * length * width // HEAD_DIM,
        ),
    )(first, *operands)


def place_kernel(high, table_ref, *refs):
    count = len(refs) - 4
    pieces, out_ref, held, sems = refs[:count], refs[-3], refs[-2], refs[-1]
    slots, broad = held.shape[0], held.shape[2]

    def copy(step):
        row = pl.multiple_of(table_ref[2 * step] * high, high)
        column = pl.multiple_of(table_ref[2 * step + 1] * broad, broad)
        return pltpu.make_async_copy(
            held.at[step % slots],
            out_ref.at[pl.ds(row, high), pl.ds(column, broad)],
            sems.at[step % slots],
        )

    step = 0
    for piece in pieces:
        for i in range(piece.shape[0] // high):
            for j in range(piece.shape[1] // broad):
                if step >= slots:
                    copy(step - slots).wait()
                part = piece[i * high : (i + 1) * high, j * broad : (j + 1) * broad]
                held[step % slots] = part.astype(F32)
                copy(step).start()
                step += 1
    for waited in range(max(step - slots, 0), step):
        copy(waited).wait()


def place(pieces, whole, places, high, broad):
    slots = 4
    vmem = pl.BlockSpec(memory_space=pltpu.VMEM)
    return pl.pallas_call(
        functools.partial(place_kernel, high),
        in_specs=[pl.BlockSpec(memory_space=pltpu.SMEM)]
        + [vmem] * len(pieces)
        + [pl.BlockSpec(memory_space=pl.ANY)],
        out_specs=pl.BlockSpec(memory_space=pl.ANY),
        out_shape=jax.ShapeDtypeStruct(whole.shape, F32),
        scratch_shapes=[
            pltpu.VMEM((slots, high, broad), F32),
            pltpu.SemaphoreType.DMA((slots,)),
        ],
        input_output_aliases={len(pieces) + 1: 0},
        compiler_params=limit(32),
        cost_estimate=pl.CostEstimate(
            flops=0, bytes_accessed=sum(6 * p.size for p in pieces), transcendentals=0
        ),
    )(jnp.stack(places).astype(jnp.int32), *pieces, whole)


def blank_kernel(out_ref):
    pass


def blank(shape):
    return pl.pallas_call(
        blank_kernel,
        out_specs=pl.BlockSpec(memory_space=pl.ANY),
        out_shape=jax.ShapeDtypeStruct(shape, F32),
    )()


class Lane:
    def __init__(self):
        self.last = None

    def send(self, sends, after=()):
        if self.last is not None:
            held = lax.optimization_barrier(([v for v, _ in sends], self.last, after))
            sends = [(v, m) for v, (_, m) in zip(held[0], sends)]
        results = [lax.ppermute(v, "dp", m) for v, m in sends]
        self.last = results
        return results


def per_device(
    hidden,
    cotangent,
    exit_layers,
    qkv_weight,
    out_weight,
    up_weight,
    down_weight,
    query_bias,
    value_bias,
    out_bias,
    up_bias,
    down_bias,
    attn_gain,
    attn_shift,
    ffn_gain,
    ffn_shift,
):
    core = lax.axis_index("sp")
    other = 1 - core
    chips = lax.axis_size("dp")
    plane = chips // LINE
    chip = lax.axis_index("dp")
    spot = chip % GROUP
    level = chip // plane
    rows = hidden.shape[1]
    width = hidden.shape[2]
    length = 2 * rows
    half = width // 2
    inner = up_weight.shape[1]
    inner_half = inner // 2
    across, first_hop, middle_hop, last_hop = Lane(), Lane(), Lane(), Lane()

    def swap(value):
        return lax.ppermute(value, "sp", [(0, 1), (1, 0)])

    def in_plane(distance):
        return [(i, i // plane * plane + ((i % plane) ^ distance)) for i in range(chips)]

    def along(*moves):
        return [(a * plane + i, b * plane + i) for a, b in moves for i in range(plane)]

    inward, middle_moves, outward = (
        along((0, 1), (3, 2)),
        along((1, 2), (2, 1)),
        along((1, 0), (2, 3)),
    )

    def split(value, axis, size):
        return (
            lax.dynamic_slice_in_dim(value, core * size, size, axis),
            lax.dynamic_slice_in_dim(value, other * size, size, axis),
        )

    def in_order(mine, theirs, axis):
        return jnp.where(
            core == 0,
            jnp.concatenate([mine, theirs], axis),
            jnp.concatenate([theirs, mine], axis),
        )

    def gather_group(value):
        return [value] + across.send([(value, in_plane(d)) for d in range(1, GROUP)])

    def scatter_group(value, axis, size):
        blocks = [
            lax.dynamic_slice_in_dim(value, (spot ^ d) * size, size, axis) for d in range(GROUP)
        ]
        return blocks[:1] + across.send([(blocks[d], in_plane(d)) for d in range(1, GROUP)])

    def both(mine):
        mine = jnp.concatenate(mine)
        theirs = swap(mine)
        pair = [v.reshape(GROUP, 1, rows, -1) for v in (mine, theirs)]
        return jnp.concatenate(pair, 1).reshape(GROUP * length, -1)

    def turn(value):
        return value.reshape(-1, 2, rows, value.shape[-1])[:, ::-1].reshape(value.shape)

    end = (level == 0) | (level == LINE - 1)

    def line_sum(value):
        value = value + first_hop.send([(value, inward)])[0]
        value = value + middle_hop.send([(value, middle_moves)])[0]
        value = jnp.where(end, last_hop.send([(value, outward)])[0], value)
        distance = GROUP
        while distance < plane:
            value = value + lax.ppermute(value, "dp", in_plane(distance))
            distance *= 2
        return value

    def spread(value, after):
        size = value.shape[0] // 2
        first, second = across.send([(value, in_plane(1)), (value, in_plane(2))], after)
        upper, lower = across.send([(first[:size], in_plane(2)), (second[size:], in_plane(1))])
        return [value, first, second, upper, lower]

    def table(size, start, count=None):
        return jnp.arange(size if count is None else count, dtype=jnp.int32) + start

    inputs = hidden[0].astype(F32)
    active = active_rows(exit_layers[0], core * rows, rows, length)
    first_row = (core * rows).astype(jnp.int32)[None]
    grad_output = cotangent[0].astype(F32)
    down_grad = (active * grad_output).astype(LOW)
    down_grad_all = jnp.concatenate([down_grad, swap(down_grad)])

    core_number = core.astype(jnp.int32)[None]
    mine, theirs = norm(
        norm_one_kernel, core_number, rows, width, 0,
        hidden[0], attn_gain[None], attn_shift[None],
    )
    normed_one_half = jnp.concatenate([mine, swap(theirs)])
    down_mine = gather_group(down_grad)
    qkv_left = gather_group(normed_one_half)
    block = min(512, half)
    count = half // block

    def qkv_table(c):
        return jnp.concatenate([table(count, (2 * p + c) * count) for p in range(3)])

    theirs = times_columns(normed_one_half, qkv_weight, qkv_table(other), block)
    theirs = swap(theirs)
    mine = times_columns(normed_one_half, qkv_weight, qkv_table(core), block)
    bias = jnp.stack([query_bias, jnp.zeros_like(query_bias), value_bias])
    bias = lax.dynamic_slice_in_dim(bias, core * half, half, 1).reshape(1, -1)
    queries, keys, values, attended = attend_forward(first_row, mine, theirs, bias)
    attended, down_mine = lax.optimization_barrier((attended, down_mine))
    out_part = dot(attended, out_weight, 1, 0)
    middle, mine, theirs = norm(
        norm_two_kernel, core_number, rows, width, 1,
        hidden[0], active, out_part, swap(out_part[rows:]),
        out_bias[None], ffn_gain[None], ffn_shift[None],
    )
    normed_two_half = jnp.concatenate([mine, swap(theirs)])
    count = inner_half // block
    theirs = times_columns(normed_two_half, up_weight, table(count, other * count), block)
    theirs = swap(theirs)
    mine = times_columns(normed_two_half, up_weight, table(count, core * count), block)
    bias = lax.dynamic_slice_in_dim(up_bias, core * inner_half, inner_half).reshape(1, -1)
    mine, qkv_left = lax.optimization_barrier((mine, qkv_left))
    inner_low, up_grad, up_sums = inner_layer(
        down_grad_all, down_weight, mine, theirs, bias, block
    )
    down_left = scatter_group(inner_low, 1, inner_half // GROUP)
    up_right = scatter_group(up_grad, 1, inner_half // GROUP)
    up_left = gather_group(normed_two_half)
    out_left = gather_group(attended)
    block = min(1024, inner_half)
    count = inner_half // block
    up_grad_theirs = swap(up_grad)
    part = times_back(up_grad, up_weight, table(count, core * count), block, 512)
    part = times_back(
        up_grad_theirs, up_weight, table(count, other * count), block, 512, part, True
    )
    normed_two_grad = in_order(part[:rows], swap(part[rows:]), 1)
    _, norm_two_back = jax.vjp(layer_norm, middle, ffn_gain, ffn_shift)
    middle_part, gain_two_grad, shift_two_grad = norm_two_back(normed_two_grad)
    middle_grad = grad_output + middle_part
    attn_grad = (active * middle_grad).astype(LOW)
    attn_grad_all = jnp.concatenate([attn_grad, swap(attn_grad)])
    out_right = scatter_group(attn_grad, 1, width // GROUP)
    head_grads = dot(attn_grad_all, out_weight, 1, 1).astype(LOW)
    qkv_grad = attend_backward(first_row, queries, keys, values, head_grads)
    qkv_right = scatter_group(qkv_grad, 2, half // GROUP)
    flat = jnp.concatenate([qkv_grad[0], qkv_grad[1], qkv_grad[2]], 1)
    flat_theirs = swap(flat)
    block = min(1024, half)
    count = half // block

    def qkv_table(c):
        return jnp.concatenate([table(count, (2 * p + c) * count) for p in range(3)])

    inner_low, flat_theirs = lax.optimization_barrier((inner_low, flat_theirs))
    down_part = dot(inner_low, down_weight, 1, 0)
    output = middle + active * (down_part[:rows] + swap(down_part[rows:]) + down_bias)
    part = times_back(flat, qkv_weight, qkv_table(core), block, 512)
    part = times_back(flat_theirs, qkv_weight, qkv_table(other), block, 512, part, True)
    normed_one_grad = in_order(part[:rows], swap(part[rows:]), 1)
    _, norm_one_back = jax.vjp(layer_norm, inputs, attn_gain, attn_shift)
    input_part, gain_one_grad, shift_one_grad = norm_one_back(normed_one_grad)
    input_grad = (middle_grad + input_part).astype(LOW)

    chunks = []
    down_right = both(down_mine)
    down_left = jnp.concatenate(down_left)
    size = inner_half // GROUP
    first = 0
    for cut in (width // 4, width // 4, width // 2):
        chunks.append(("down", down_left, down_right[:, first : first + cut], first // cut))
        first += cut
    up_left = jnp.concatenate(up_left)
    up_right = jnp.concatenate(up_right)
    chunks.append(("up", up_left, up_right, core))
    chunks.append(("up", up_left, turn(swap(up_right)), other))
    chunks.append(("out", jnp.concatenate(out_left), both(out_right), 0))
    qkv_left = jnp.concatenate(qkv_left)
    qkv_right = jnp.concatenate(
        [jnp.concatenate([r[0], r[1], r[2]], 1) for r in qkv_right]
    )
    chunks.append(("qkv", qkv_left, qkv_right, core))
    chunks.append(("qkv", qkv_left, turn(swap(qkv_right)), other))

    shapes = {
        "down": (inner_half, width),
        "up": (half, inner),
        "out": (half, width),
        "qkv": (half, 3 * width),
    }
    wholes = {name: blank(shape) for name, shape in shapes.items()}
    sums = [line_sum(dot(left, right, 0, 0).astype(LOW)) for _, left, right, _ in chunks]
    done = [()] * 2
    for (name, _, _, where), total in zip(chunks, sums):
        pieces = spread(total, done[-2])
        tall, wide = total.shape
        high = min(256, tall)
        broad = wide // 3 if name == "qkv" else wide
        places = []
        for d in range(GROUP):
            owner = spot ^ d
            for i in range(tall // high):
                row = jnp.int32(i)
                if name == "down":
                    row, columns = owner * (tall // high) + i, [jnp.int32(where)]
                elif name == "up":
                    columns = [where * GROUP + owner]
                elif name == "out":
                    columns = [owner]
                else:
                    columns = [(2 * p + where) * GROUP + owner for p in range(3)]
                for column in columns:
                    places += [row, column]
        wholes[name] = place(pieces, wholes[name], places, high, broad)
        done.append(wholes[name])

    def widen(value):
        return in_order(value, jnp.zeros_like(value), 0)

    qkv_sums = jnp.sum(qkv_grad.astype(F32), axis=1)
    small = jnp.concatenate(
        [
            widen(qkv_sums[0]),
            widen(qkv_sums[2]),
            jnp.sum(attn_grad.astype(F32), axis=0),
            widen(up_sums[0]),
            jnp.sum(down_grad.astype(F32), axis=0),
            gain_one_grad,
            shift_one_grad,
            gain_two_grad,
            shift_two_grad,
        ]
    ).reshape(-1, 128)
    small = small + swap(small)
    distance = 1
    while distance < plane:
        small = small + lax.ppermute(small, "dp", in_plane(distance))
        distance *= 2
    small = small + lax.ppermute(small, "dp", inward)
    small = small + lax.ppermute(small, "dp", middle_moves)
    small = jnp.where(end, lax.ppermute(small, "dp", outward), small).reshape(-1)
    small_grads = []
    first = 0
    for size in (width, width, width, inner, width, width, width, width, width):
        small_grads.append(small[first : first + size])
        first += size

    return (
        output.astype(LOW)[None],
        input_grad[None],
        wholes["qkv"],
        wholes["out"],
        wholes["up"],
        wholes["down"],
        *small_grads,
    )


def solution(mesh):
    return jax.shard_map(
        per_device,
        mesh=mesh,
        in_specs=(
            P("dp", "sp", None),
            P("dp", "sp", None),
            P("dp", None),
            P("sp", None),
            P("sp", None),
            P("sp", None),
            P("sp", None),
            P(),
            P(),
            P(),
            P(),
            P(),
            P(),
            P(),
            P(),
            P(),
        ),
        out_specs=(
            P("dp", "sp", None),
            P("dp", "sp", None),
            P("sp", None),
            P("sp", None),
            P("sp", None),
            P("sp", None),
            P(),
            P(),
            P(),
            P(),
            P(),
            P(),
            P(),
            P(),
            P(),
        ),
        check_vma=False,
    )
```

```python
import functools

import jax
import jax.numpy as jnp
from jax import lax
from jax.experimental import pallas as pl
from jax.experimental.pallas import tpu as pltpu
from jax.sharding import PartitionSpec as P

HEAD_DIM = 64
TILE = 128
LAYER = 12
LINE = 4
STREAMS = 4
LATE = 2
GROUP = 4
F32 = jnp.float32
LOW = jnp.bfloat16


def layer_norm(values, gain, shift):
    center = jnp.mean(values, axis=-1, keepdims=True)
    centered = values - center
    variance = jnp.mean(centered * centered, axis=-1, keepdims=True)
    return centered * lax.rsqrt(variance + 1e-05) * gain + shift


def active_rows(bounds, first_row, row_count, sequence_length):
    position = first_row + jnp.arange(row_count, dtype=jnp.int32)
    tile_start = position // TILE * TILE
    exit_layer = bounds[1] - (bounds[1] - bounds[0]) * tile_start // sequence_length
    return (exit_layer > LAYER).astype(F32)[:, None]


def gelu_and_slope(values):
    scale = (2.0 / jnp.pi) ** 0.5
    square = values * values
    bend = jnp.tanh(scale * values * (1.0 + 0.044715 * square))
    rise = 0.5 * (1.0 + bend)
    slope = rise + 0.5 * values * (1.0 - bend * bend) * scale * (1.0 + 0.134145 * square)
    return values * rise, slope


def dot(left, right, left_dim, right_dim):
    return lax.dot_general(
        left, right, (((left_dim,), (right_dim,)), ((), ())), preferred_element_type=F32
    )


def roll_rows(value):
    rows = value.shape[0] // 2
    return jnp.concatenate([value[rows:], value[:rows]])


def estimate(flops, size):
    return pl.CostEstimate(flops=flops // 4, bytes_accessed=size // 4, transcendentals=0)


def far(value):
    return pltpu.with_memory_space_constraint(value, pltpu.HBM)


def limit(mebibytes):
    return pltpu.CompilerParams(vmem_limit_bytes=mebibytes << 20)


def halves(core_ref, values, mine_ref, theirs_ref):
    width = mine_ref.shape[1]
    first = core_ref[0] == 0
    low, high = values[:, :width], values[:, width:]
    mine_ref[...] = jnp.where(first, low, high).astype(LOW)
    theirs_ref[...] = jnp.where(first, high, low).astype(LOW)


def norm_one_kernel(
    core_ref, x_ref, gain_ref, shift_ref, grad_ref, active_ref,
    mine_ref, theirs_ref, masked_ref, sum_ref,
):
    normed = layer_norm(x_ref[...].astype(F32), gain_ref[...], shift_ref[...])
    halves(core_ref, normed, mine_ref, theirs_ref)
    masked = active_ref[...] * grad_ref[...].astype(F32)
    masked_ref[...] = masked.astype(LOW)
    sum_ref[...] = jnp.sum(masked, axis=0, keepdims=True)


def norm_two_kernel(
    core_ref, x_ref, active_ref, part_ref, theirs_part_ref, bias_ref, gain_ref, shift_ref,
    middle_ref, mine_ref, theirs_ref,
):
    rows = x_ref.shape[0]
    attn = part_ref[:rows] + theirs_part_ref[...] + bias_ref[...]
    middle = x_ref[...].astype(F32) + active_ref[...] * attn
    middle_ref[...] = middle
    halves(core_ref, layer_norm(middle, gain_ref[...], shift_ref[...]), mine_ref, theirs_ref)


def norm_back(core_ref, value_ref, gain_ref, mine_ref, theirs_ref, gain_out_ref, shift_out_ref):
    values = value_ref[...].astype(F32)
    mine, theirs = mine_ref[: values.shape[0]], theirs_ref[...]
    grads = jnp.where(
        core_ref[0] == 0,
        jnp.concatenate([mine, theirs], 1),
        jnp.concatenate([theirs, mine], 1),
    )
    centered = values - jnp.mean(values, axis=-1, keepdims=True)
    scale = lax.rsqrt(jnp.mean(centered * centered, axis=-1, keepdims=True) + 1e-05)
    unit = centered * scale
    gain_out_ref[...] = jnp.sum(grads * unit, axis=0, keepdims=True)
    shift_out_ref[...] = jnp.sum(grads, axis=0, keepdims=True)
    grads = grads * gain_ref[...]
    inner = jnp.mean(grads * unit, axis=-1, keepdims=True)
    return scale * (grads - jnp.mean(grads, axis=-1, keepdims=True) - unit * inner)


def norm_two_back_kernel(
    core_ref, value_ref, gain_ref, mine_ref, theirs_ref, grad_ref, active_ref,
    total_ref, masked_ref, sum_ref, gain_out_ref, shift_out_ref,
):
    part = norm_back(
        core_ref, value_ref, gain_ref, mine_ref, theirs_ref, gain_out_ref, shift_out_ref
    )
    total = grad_ref[...].astype(F32) + part
    total_ref[...] = total
    masked = (active_ref[...] * total).astype(LOW)
    masked_ref[...] = masked
    sum_ref[...] = jnp.sum(masked.astype(F32), axis=0, keepdims=True)


def norm_one_back_kernel(
    core_ref, value_ref, gain_ref, mine_ref, theirs_ref, grad_ref,
    total_ref, gain_out_ref, shift_out_ref,
):
    part = norm_back(
        core_ref, value_ref, gain_ref, mine_ref, theirs_ref, gain_out_ref, shift_out_ref
    )
    total_ref[...] = (grad_ref[...].astype(F32) + part).astype(LOW)


def by_rows(kernel, core, outs, *operands):
    vmem = pl.BlockSpec(memory_space=pltpu.VMEM)
    return pl.pallas_call(
        kernel,
        in_specs=[pl.BlockSpec(memory_space=pltpu.SMEM)] + [vmem] * len(operands),
        out_specs=[vmem] * len(outs),
        out_shape=[jax.ShapeDtypeStruct(shape, dtype) for shape, dtype in outs],
        compiler_params=limit(24),
        cost_estimate=estimate(
            20 * operands[0].size, sum(o.size * o.dtype.itemsize for o in operands)
        ),
    )(core, *operands)


def product_kernel(count, turned, *refs):
    lefts, out_ref, left_turned, right = refs[:count], refs[-3], refs[-2], refs[-1]
    rights = refs[count:-3]
    length = lefts[0].shape[0]

    @pl.when(pl.program_id(0) == 0)
    def _():
        for d, left in enumerate(lefts):
            left_turned[:, d * length : (d + 1) * length] = left[...].T

    row = 0
    for piece in rights:
        value = piece[0] if len(piece.shape) == 3 else piece[...]
        if turned:
            value = roll_rows(value)
        right[row : row + value.shape[0]] = value
        row += value.shape[0]
    out_ref[...] = dot(left_turned[...], right[...], 1, 0).astype(LOW)


def rows_product(lefts, rights, block, first, steps, turned=False):
    length, tall = lefts[0].shape

    def spec(right):
        if right.ndim == 3:
            return pl.BlockSpec((1, right.shape[1], block), lambda j: (first + j, 0, 0))
        return pl.BlockSpec((right.shape[0], block), lambda j: (0, first + j))

    total = length * len(lefts)
    return pl.pallas_call(
        functools.partial(product_kernel, len(lefts), turned),
        grid=(steps,),
        in_specs=[pl.BlockSpec((length, tall), lambda j: (0, 0))] * len(lefts)
        + [spec(right) for right in rights],
        out_specs=pl.BlockSpec((tall, block), lambda j: (0, j)),
        out_shape=jax.ShapeDtypeStruct((tall, steps * block), LOW),
        scratch_shapes=[pltpu.VMEM((tall, total), LOW), pltpu.VMEM((total, block), LOW)],
        compiler_params=limit(32),
        cost_estimate=estimate(
            2 * tall * total * steps * block, 2 * total * (tall + steps * block)
        ),
    )(*lefts, *rights)


def hold(values, after):
    return lax.optimization_barrier((values, after))[0]


def columns_kernel(table_ref, left_ref, *refs):
    total, first = 0.0, 0
    for weight_ref in refs[:-1]:
        depth = weight_ref.shape[0]
        total += dot(left_ref[:, first : first + depth], weight_ref[...], 1, 0)
        first += depth
    refs[-1][...] = total.astype(refs[-1].dtype)


def times_columns(left, weight, table, block, dtype):
    rows, depth = left.shape
    steps = table.shape[0]
    return pl.pallas_call(
        columns_kernel,
        grid_spec=pltpu.PrefetchScalarGridSpec(
            num_scalar_prefetch=1,
            grid=(steps,),
            in_specs=[
                pl.BlockSpec((rows, depth), lambda i, t: (0, 0)),
                *[
                    pl.BlockSpec(
                        (depth // STREAMS, block),
                        functools.partial(lambda r, i, t: (r, t[i]), r),
                    )
                    for r in range(STREAMS)
                ],
            ],
            out_specs=pl.BlockSpec((rows, block), lambda i, t: (0, i)),
        ),
        out_shape=jax.ShapeDtypeStruct((rows, steps * block), dtype),
        compiler_params=limit(24),
        cost_estimate=estimate(2 * rows * depth * steps * block, 2 * depth * (rows + steps * block) + 4 * rows * steps * block),
    )(table, left, *[far(weight)] * STREAMS)


def back_kernel(turned, table_ref, left_ref, *refs):
    weights, out_ref = refs[:STREAMS], refs[-1]
    starts = refs[STREAMS:-1]
    left = left_ref[...]
    if turned:
        left = roll_rows(left)
    first = 0
    for weight_ref in weights:
        deep = weight_ref.shape[0]
        part = dot(left, weight_ref[...], 1, 1)
        columns = slice(first, first + deep)
        first += deep

        @pl.when(pl.program_id(1) == 0)
        def _(part=part, columns=columns):
            out_ref[:, columns] = part + starts[0][:, columns] if starts else part

        @pl.when(pl.program_id(1) > 0)
        def _(part=part, columns=columns):
            out_ref[:, columns] += part


def times_back(left, weight, table, block, deep, start=None, turned=False):
    rows = left.shape[0]
    depth = weight.shape[0]
    steps = table.shape[0]
    out_spec = pl.BlockSpec((rows, deep), lambda k, i, t: (0, k))
    in_specs = [
        pl.BlockSpec((rows, block), lambda k, i, t: (0, i)),
        *[
            pl.BlockSpec(
                (deep // STREAMS, block),
                functools.partial(lambda r, k, i, t: (k * STREAMS + r, t[i]), r),
            )
            for r in range(STREAMS)
        ],
    ]
    operands = [table, left, *[far(weight)] * STREAMS]
    if start is not None:
        in_specs.append(out_spec)
        operands.append(start)
    return pl.pallas_call(
        functools.partial(back_kernel, turned),
        grid_spec=pltpu.PrefetchScalarGridSpec(
            num_scalar_prefetch=1,
            grid=(depth // deep, steps),
            in_specs=in_specs,
            out_specs=out_spec,
        ),
        out_shape=jax.ShapeDtypeStruct((rows, depth), F32),
        compiler_params=limit(32),
        cost_estimate=estimate(2 * rows * depth * steps * block, 2 * steps * block * (rows + depth) + 8 * rows * depth),
    )(*operands)


def inner_kernel(grad_ref, *refs):
    weights = refs[:STREAMS]
    mine_ref, theirs_ref, bias_ref, act_ref, out_ref, sum_ref = refs[STREAMS:]
    first = 0
    for weight_ref in weights:
        columns = slice(first, first + weight_ref.shape[0])
        first += weight_ref.shape[0]
        theirs = roll_rows(theirs_ref[:, columns])
        act, slope = gelu_and_slope(mine_ref[:, columns] + theirs + bias_ref[:, columns])
        act_ref[:, columns] = act.astype(LOW)
        grad = (dot(grad_ref[...], weight_ref[...], 1, 1) * slope).astype(LOW)
        out_ref[:, columns] = grad
        sum_ref[:, columns] = jnp.sum(grad.astype(F32), axis=0, keepdims=True)


def inner_layer(grads, weight, mine, theirs, bias, block):
    rows, width = grads.shape
    hidden = weight.shape[0]
    part = pl.BlockSpec((rows, block), lambda i: (0, i))
    line = pl.BlockSpec((1, block), lambda i: (0, i))
    return pl.pallas_call(
        inner_kernel,
        grid=(hidden // block,),
        in_specs=[
            pl.BlockSpec((rows, width), lambda i: (0, 0)),
            *[
                pl.BlockSpec(
                    (block // STREAMS, width),
                    functools.partial(lambda r, i: (i * STREAMS + r, 0), r),
                )
                for r in range(STREAMS)
            ],
            part,
            part,
            line,
        ],
        out_specs=[part, part, line],
        out_shape=[
            jax.ShapeDtypeStruct((rows, hidden), LOW),
            jax.ShapeDtypeStruct((rows, hidden), LOW),
            jax.ShapeDtypeStruct((1, hidden), F32),
        ],
        compiler_params=limit(32),
        cost_estimate=estimate(2 * rows * width * hidden, 2 * width * (rows + hidden) + 12 * rows * hidden),
    )(grads, *[far(weight)] * STREAMS, mine, theirs, bias)


def head_chances(queries, keys, lanes_of_head, allowed):
    keys_of_head = jnp.where(lanes_of_head, keys, jnp.zeros_like(keys))
    scores = dot(queries, keys_of_head, 1, 1) * (HEAD_DIM**-0.5)
    scores = jnp.where(allowed, scores, -1e30)
    raised = jnp.exp(scores - jnp.max(scores, axis=-1, keepdims=True))
    return raised / jnp.sum(raised, axis=-1, keepdims=True)


def attend_masks(first, length, lanes):
    lane = lax.broadcasted_iota(jnp.int32, (length, lanes), 1)
    row = lax.broadcasted_iota(jnp.int32, (length, length), 0) + first
    column = lax.broadcasted_iota(jnp.int32, (length, length), 1) + first
    row = jnp.where(row >= length, row - length, row)
    column = jnp.where(column >= length, column - length, column)
    return lane, column <= row


def attend_forward_kernel(first_ref, *refs):
    mine, theirs, biases, lows, o_ref = refs[:3], refs[3:6], refs[6:9], refs[9:12], refs[12]
    sums = [
        (m[...] + roll_rows(t[...]) + b[...]).astype(LOW)
        for m, t, b in zip(mine, theirs, biases)
    ]
    for low, value in zip(lows, sums):
        low[...] = value
    queries, keys, values = sums
    lane, allowed = attend_masks(first_ref[0], *queries.shape)
    total = jnp.zeros(queries.shape, F32)
    for head in range(queries.shape[1] // HEAD_DIM):
        own = lane // HEAD_DIM == head
        chances = head_chances(queries, keys, own, allowed).astype(LOW)
        total += dot(chances, jnp.where(own, values, jnp.zeros_like(values)), 1, 0)
    o_ref[...] = total.astype(LOW)


def attend_forward(first, mine, theirs, bias):
    length, width = mine.shape
    width //= 3
    steps = width // 128
    parts = [
        pl.BlockSpec((length, 128), functools.partial(lambda p, i, t: (0, p * steps + i), p))
        for p in range(3)
    ]
    lines = [
        pl.BlockSpec((1, 128), functools.partial(lambda p, i, t: (0, p * steps + i), p))
        for p in range(3)
    ]
    return pl.pallas_call(
        attend_forward_kernel,
        grid_spec=pltpu.PrefetchScalarGridSpec(
            num_scalar_prefetch=1,
            grid=(steps,),
            in_specs=parts + parts + lines,
            out_specs=[parts[0]] * 4,
        ),
        out_shape=[jax.ShapeDtypeStruct((length, width), LOW)] * 4,
        compiler_params=limit(16),
        cost_estimate=estimate(4 * length * length * width, 32 * length * width),
    )(first, mine, mine, mine, theirs, theirs, theirs, bias, bias, bias)


def attend_backward_kernel(first_ref, q_ref, k_ref, v_ref, g_ref, out_ref):
    queries, keys, values, grads = q_ref[...], k_ref[...], v_ref[...], g_ref[...]
    lane, allowed = attend_masks(first_ref[0], *queries.shape)
    dq = jnp.zeros(queries.shape, F32)
    dk = jnp.zeros(queries.shape, F32)
    dv = jnp.zeros(queries.shape, F32)
    for head in range(queries.shape[1] // HEAD_DIM):
        own = lane // HEAD_DIM == head
        chances = head_chances(queries, keys, own, allowed)
        head_grads = jnp.where(own, grads, jnp.zeros_like(grads))
        dv += dot(chances.astype(LOW), head_grads, 0, 0)
        chance_grads = dot(head_grads, values, 1, 1)
        inner = jnp.sum(chances * chance_grads, axis=-1, keepdims=True)
        score_grads = (chances * (chance_grads - inner)).astype(LOW)
        dq += dot(score_grads, jnp.where(own, keys, jnp.zeros_like(keys)), 1, 0)
        dk += dot(score_grads, jnp.where(own, queries, jnp.zeros_like(queries)), 0, 0)
    scale = HEAD_DIM**-0.5
    out_ref[0] = (dq * scale).astype(LOW)
    out_ref[1] = (dk * scale).astype(LOW)
    out_ref[2] = dv.astype(LOW)


def attend_backward(first, *operands):
    length, width = operands[0].shape
    block = pl.BlockSpec((length, 128), lambda i, t: (0, i))
    return pl.pallas_call(
        attend_backward_kernel,
        grid_spec=pltpu.PrefetchScalarGridSpec(
            num_scalar_prefetch=1,
            grid=(width // 128,),
            in_specs=[block] * 4,
            out_specs=pl.BlockSpec((3, length, 128), lambda i, t: (0, 0, i)),
        ),
        out_shape=jax.ShapeDtypeStruct((3, length, width), LOW),
        compiler_params=limit(16),
        cost_estimate=estimate(10 * length * length * width, 14 * length * width),
    )(first, *operands)


def place_kernel(high, table_ref, *refs):
    count = len(refs) - 4
    pieces, out_ref, held, sems = refs[:count], refs[-3], refs[-2], refs[-1]
    slots, broad = held.shape[0], held.shape[2]

    def copy(step):
        row = pl.multiple_of(table_ref[2 * step] * high, high)
        column = pl.multiple_of(table_ref[2 * step + 1] * broad, broad)
        return pltpu.make_async_copy(
            held.at[step % slots],
            out_ref.at[pl.ds(row, high), pl.ds(column, broad)],
            sems.at[step % slots],
        )

    step = 0
    for piece in pieces:
        for i in range(piece.shape[0] // high):
            for j in range(piece.shape[1] // broad):
                if step >= slots:
                    copy(step - slots).wait()
                part = piece[i * high : (i + 1) * high, j * broad : (j + 1) * broad]
                held[step % slots] = part.astype(F32)
                copy(step).start()
                step += 1
    for waited in range(max(step - slots, 0), step):
        copy(waited).wait()


def place(pieces, whole, places, high, broad):
    slots = 4
    vmem = pl.BlockSpec(memory_space=pltpu.VMEM)
    return pl.pallas_call(
        functools.partial(place_kernel, high),
        in_specs=[pl.BlockSpec(memory_space=pltpu.SMEM)]
        + [vmem] * len(pieces)
        + [pl.BlockSpec(memory_space=pl.ANY)],
        out_specs=pl.BlockSpec(memory_space=pl.ANY),
        out_shape=jax.ShapeDtypeStruct(whole.shape, F32),
        scratch_shapes=[
            pltpu.VMEM((slots, high, broad), F32),
            pltpu.SemaphoreType.DMA((slots,)),
        ],
        input_output_aliases={len(pieces) + 1: 0},
        compiler_params=limit(32),
        cost_estimate=estimate(0, sum(6 * p.size for p in pieces)),
    )(jnp.stack(places).astype(jnp.int32), *pieces, whole)


def blank_kernel(out_ref):
    pass


def blank(shape):
    return pl.pallas_call(
        blank_kernel,
        out_specs=pl.BlockSpec(memory_space=pl.ANY),
        out_shape=jax.ShapeDtypeStruct(shape, F32),
    )()


class Lane:
    def __init__(self):
        self.last = ()

    def send(self, sends, after=()):
        values = hold([v for v, _ in sends], (self.last, after))
        self.last = [lax.ppermute(v, "dp", m) for v, (_, m) in zip(values, sends)]
        return self.last


def per_device(
    hidden,
    cotangent,
    exit_layers,
    qkv_weight,
    out_weight,
    up_weight,
    down_weight,
    query_bias,
    value_bias,
    out_bias,
    up_bias,
    down_bias,
    attn_gain,
    attn_shift,
    ffn_gain,
    ffn_shift,
):
    core = lax.axis_index("sp")
    other = 1 - core
    chips = lax.axis_size("dp")
    plane = chips // LINE
    chip = lax.axis_index("dp")
    spot = chip % GROUP
    level = chip // plane
    rows = hidden.shape[1]
    width = hidden.shape[2]
    length = 2 * rows
    half = width // 2
    inner = up_weight.shape[1]
    inner_half = inner // 2
    across, middle_across, first_hop, middle_hop, last_hop = (Lane() for _ in range(5))

    def swap(value):
        return lax.ppermute(value, "sp", [(0, 1), (1, 0)])

    def in_plane(distance):
        return [(i, i // plane * plane + ((i % plane) ^ distance)) for i in range(chips)]

    def along(*moves):
        return [(a * plane + i, b * plane + i) for a, b in moves for i in range(plane)]

    inward, middle_moves, outward = (
        along((0, 1), (3, 2)),
        along((1, 2), (2, 1)),
        along((1, 0), (2, 3)),
    )

    def split(value, axis, size):
        return (
            lax.dynamic_slice_in_dim(value, core * size, size, axis),
            lax.dynamic_slice_in_dim(value, other * size, size, axis),
        )

    def exchange(blocks):
        (far_one,) = across.send([(blocks[3], in_plane(3))])
        near = across.send([(blocks[1], in_plane(1)), (blocks[2], in_plane(2))])
        return [blocks[0], *near, far_one]

    def gather_group(value):
        return exchange([value] * GROUP)

    def scatter_group(value, axis, size):
        blocks = [
            lax.dynamic_slice_in_dim(value, (spot ^ d) * size, size, axis) for d in range(GROUP)
        ]
        return exchange(blocks)

    def pairs(mine, theirs):
        return [piece for pair in zip(mine, theirs) for piece in pair]

    end = (level == 0) | (level == LINE - 1)

    def line_start(value, after=()):
        return value + hold(first_hop.send([(value, inward)])[0], after)

    def line_middle(value):
        return value + middle_hop.send([(value, middle_moves)])[0]

    def line_end(value):
        return jnp.where(end, last_hop.send([(value, outward)])[0], value)

    def blocks_sum(value):
        distance = GROUP
        while distance < plane:
            value = value + lax.ppermute(value, "dp", in_plane(distance))
            distance *= 2
        return value

    def spread(value, after):
        size = value.shape[0] // 2
        first, second = across.send([(value, in_plane(1)), (value, in_plane(2))], after[0])
        upper, lower = across.send(
            [(first[:size], in_plane(2)), (second[size:], in_plane(1))], after[1]
        )
        return [value, first, second, upper, lower]

    def spread_late(value, after):
        size = value.shape[0] // 2

        def middle_only(distance):
            return [(a, b) for a, b in in_plane(distance) if 0 < a // plane < LINE - 1]

        near = middle_across.send(
            [(value[:size], middle_only(1)), (value[size:], middle_only(2))]
        )
        own = line_end(value)
        first = across.send([(own[:size], in_plane(2)), (own[size:], in_plane(1))], after[0])
        near_ends = last_hop.send([(v, outward) for v in near])
        near = [jnp.where(end, e, v) for e, v in zip(near_ends, near)]
        second = across.send([(near[0], in_plane(2)), (near[1], in_plane(1))], after[1])
        return [own, near[0], first[1], first[0], near[1], *second]

    def table(size, start, count=None):
        return jnp.arange(size if count is None else count, dtype=jnp.int32) + start

    active = active_rows(exit_layers[0], core * rows, rows, length)
    core_number = core.astype(jnp.int32)[None]
    first_row = (core * rows).astype(jnp.int32)[None]
    full, part, line = (rows, width), (rows, half), (1, width)

    mine, theirs, down_grad, down_sums = by_rows(
        norm_one_kernel,
        core_number,
        [(part, LOW), (part, LOW), (full, LOW), (line, F32)],
        hidden[0],
        attn_gain[None],
        attn_shift[None],
        cotangent[0],
        active,
    )
    normed_one_half = jnp.concatenate([mine, swap(theirs)])
    down_grad_all = jnp.concatenate([down_grad, swap(down_grad)])
    down_mine = gather_group(down_grad)
    block = min(512, half)
    count = half // block

    def qkv_table(c):
        return jnp.concatenate([table(count, (2 * p + c) * count) for p in range(3)])

    theirs = times_columns(normed_one_half, qkv_weight, qkv_table(other), block, LOW)
    theirs = hold(swap(theirs), down_mine[3])
    mine = times_columns(normed_one_half, qkv_weight, qkv_table(core), block, F32)
    bias = jnp.stack([query_bias, jnp.zeros_like(query_bias), value_bias])
    bias = lax.dynamic_slice_in_dim(bias, core * half, half, 1).reshape(1, -1)
    queries, keys, values, attended = attend_forward(first_row, mine, theirs, bias)
    out_part = dot(attended, out_weight, 1, 0)
    middle, mine, theirs = by_rows(
        norm_two_kernel,
        core_number,
        [(full, F32), (part, LOW), (part, LOW)],
        hidden[0],
        active,
        out_part,
        swap(out_part[rows:]),
        out_bias[None],
        ffn_gain[None],
        ffn_shift[None],
    )
    theirs = hold(theirs, down_mine[1:3])
    qkv_left = gather_group(normed_one_half)
    down_theirs = [swap(g) for g in down_mine]
    normed_two_half = jnp.concatenate([mine, swap(theirs)])
    count = inner_half // block
    theirs = times_columns(
        normed_two_half, up_weight, table(count, other * count), block, LOW
    )
    theirs = hold(swap(theirs), qkv_left[3])
    mine = times_columns(normed_two_half, up_weight, table(count, core * count), block, F32)
    bias = lax.dynamic_slice_in_dim(up_bias, core * inner_half, inner_half).reshape(1, -1)
    inner_low, up_grad, up_sums = inner_layer(
        down_grad_all, down_weight, mine, theirs, bias, block
    )

    down_left = scatter_group(inner_low, 1, inner_half // GROUP)
    up_right = scatter_group(up_grad, 1, inner_half // GROUP)
    block = min(1024, inner_half)
    count = inner_half // block
    up_grad_theirs = swap(up_grad)
    grads = times_back(up_grad, up_weight, table(count, core * count), block, 512)
    grads = times_back(
        up_grad_theirs, up_weight, table(count, other * count), block, 512, grads, True
    )
    middle_grad, attn_grad, attn_sums, gain_two_grad, shift_two_grad = by_rows(
        norm_two_back_kernel,
        core_number,
        [(full, F32), (full, LOW), (line, F32), (line, F32), (line, F32)],
        middle,
        ffn_gain[None],
        grads,
        swap(grads[rows:]),
        cotangent[0],
        active,
    )
    attn_grad_all = jnp.concatenate([attn_grad, swap(attn_grad)])
    head_grads = dot(attn_grad_all, out_weight, 1, 1).astype(LOW)
    down_right = pairs(down_mine, down_theirs)
    down_left = hold(down_left, attn_grad)
    quarter = width // 4
    down_parts = [rows_product(down_left, down_right, quarter, 0, 1)]
    head_grads = hold(head_grads, down_parts)
    qkv_grad = attend_backward(first_row, queries, keys, values, head_grads)
    down_parts[0] = line_start(down_parts[0], qkv_grad)
    qkv_grad = hold(qkv_grad, up_right[3])
    up_left = gather_group(normed_two_half)
    out_right = scatter_group(attn_grad, 1, width // GROUP)
    out_left = gather_group(attended)
    qkv_right = scatter_group(qkv_grad, 2, half // GROUP)
    flat = jnp.concatenate([qkv_grad[0], qkv_grad[1], qkv_grad[2]], 1)
    flat_theirs = swap(flat)
    block = min(1024, half)
    count = half // block

    def qkv_table(c):
        return jnp.concatenate([table(count, (2 * p + c) * count) for p in range(3)])

    grads = times_back(flat, qkv_weight, qkv_table(core), block, 512)
    grads = times_back(flat_theirs, qkv_weight, qkv_table(other), block, 512, grads, True)
    input_grad, gain_one_grad, shift_one_grad = by_rows(
        norm_one_back_kernel,
        core_number,
        [(full, LOW), (line, F32), (line, F32)],
        hidden[0],
        attn_gain[None],
        grads,
        hold(swap(grads[rows:]), up_right[1:3]),
        middle_grad,
    )
    down_part = dot(hold(inner_low, (input_grad, up_left[3])), down_weight, 1, 0)
    output = middle + active * (down_part[:rows] + swap(down_part[rows:]) + down_bias)

    def widen(value):
        none = jnp.zeros_like(value)
        return jnp.where(
            core == 0, jnp.concatenate([value, none]), jnp.concatenate([none, value])
        )

    qkv_sums = jnp.sum(qkv_grad.astype(F32), axis=1)
    small = jnp.concatenate(
        [
            widen(qkv_sums[0]),
            widen(qkv_sums[2]),
            attn_sums[0],
            widen(up_sums[0]),
            down_sums[0],
            gain_one_grad[0],
            shift_one_grad[0],
            gain_two_grad[0],
            shift_two_grad[0],
        ]
    ).reshape(-1, 128)
    small = small + swap(small)
    distance = 1
    while distance < plane:
        small = small + lax.ppermute(small, "dp", in_plane(distance))
        distance *= 2
    small = small + lax.ppermute(small, "dp", inward)
    small = small + lax.ppermute(small, "dp", middle_moves)
    small = jnp.where(end, lax.ppermute(small, "dp", outward), small).reshape(-1)
    small_grads = []
    first = 0
    for size in (width, width, width, inner, width, width, width, width, width):
        small_grads.append(small[first : first + size])
        first += size

    chunks = [("down", down_parts[0], 0)]
    value = rows_product(down_left, down_right, quarter, 1, 1)
    chunks.append(("down", line_start(value), 1))
    value = rows_product(down_left, down_right, quarter, 2, 2)
    chunks.append(("down", line_start(value), 1))
    size = inner_half // GROUP
    block = min(512, size)
    value = rows_product(up_left, up_right, block, 0, size // block)
    chunks.append(("up", line_start(value), core))
    theirs = [swap(r) for r in up_right]
    value = rows_product(up_left, theirs, block, 0, size // block, True)
    chunks.append(("up", line_start(value), other))
    right = pairs(out_right, [swap(r) for r in out_right])
    value = rows_product(out_left, right, width // GROUP, 0, 1)
    chunks.append(("out", line_start(value), 0))
    size = half // GROUP
    value = rows_product(qkv_left, qkv_right, size, 0, 3)
    chunks.append(("qkv", line_start(value), core))
    theirs = [swap(r) for r in qkv_right]
    value = rows_product(qkv_left, theirs, size, 0, 3, True)
    chunks.append(("qkv", line_start(value), other))

    wholes = {
        "down": blank((inner_half, width)),
        "up": blank((half, inner)),
        "out": blank((half, width)),
        "qkv": blank((half, 3 * width)),
    }
    done = [(), ()]
    for index, (name, value, where) in enumerate(chunks):
        value = line_middle(value)
        after = done[-2], (done[-1], small if index == 3 else ())
        if plane == GROUP and index >= len(chunks) - LATE:
            pieces = spread_late(value, after)
        else:
            pieces = spread(blocks_sum(line_end(value)), after)
        tall, wide = value.shape
        high = min(256, tall)
        broad = wide // 3 if name == "qkv" else wide
        places = []
        for d in range(GROUP):
            owner = spot ^ d
            for i in range(tall // high):
                row = jnp.int32(i)
                if name == "down":
                    row, columns = owner * (tall // high) + i, [jnp.int32(where)]
                elif name == "up":
                    columns = [where * GROUP + owner]
                elif name == "out":
                    columns = [owner]
                else:
                    columns = [(2 * p + where) * GROUP + owner for p in range(3)]
                for column in columns:
                    places += [row, column]
        wholes[name] = place(pieces, wholes[name], places, high, broad)
        done.append(wholes[name])

    return (
        output.astype(LOW)[None],
        input_grad[None],
        wholes["qkv"],
        wholes["out"],
        wholes["up"],
        wholes["down"],
        *small_grads,
    )


def solution(mesh):
    return jax.shard_map(
        per_device,
        mesh=mesh,
        in_specs=(
            P("dp", "sp", None),
            P("dp", "sp", None),
            P("dp", None),
            P("sp", None),
            P("sp", None),
            P("sp", None),
            P("sp", None),
            P(),
            P(),
            P(),
            P(),
            P(),
            P(),
            P(),
            P(),
            P(),
        ),
        out_specs=(
            P("dp", "sp", None),
            P("dp", "sp", None),
            P("sp", None),
            P("sp", None),
            P("sp", None),
            P("sp", None),
            P(),
            P(),
            P(),
            P(),
            P(),
            P(),
            P(),
            P(),
            P(),
        ),
        check_vma=False,
    )
```

```python
import functools

import jax
import jax.numpy as jnp
from jax import lax
from jax.experimental import pallas as pl
from jax.experimental.pallas import tpu as pltpu
from jax.sharding import PartitionSpec as P

HEAD_DIM = 64
TILE = 128
LAYER = 12
LINE = 4
STREAMS = 1
LATE = ("up",)
GROUP = 4
F32 = jnp.float32
LOW = jnp.bfloat16


def layer_norm(values, gain, shift):
    center = jnp.mean(values, axis=-1, keepdims=True)
    centered = values - center
    variance = jnp.mean(centered * centered, axis=-1, keepdims=True)
    return centered * lax.rsqrt(variance + 1e-05) * gain + shift


def active_rows(bounds, first_row, row_count, sequence_length):
    position = first_row + jnp.arange(row_count, dtype=jnp.int32)
    tile_start = position // TILE * TILE
    exit_layer = bounds[1] - (bounds[1] - bounds[0]) * tile_start // sequence_length
    return (exit_layer > LAYER).astype(F32)[:, None]


def gelu_and_slope(values):
    scale = (2.0 / jnp.pi) ** 0.5
    square = values * values
    bend = jnp.tanh(scale * values * (1.0 + 0.044715 * square))
    rise = 0.5 * (1.0 + bend)
    slope = rise + 0.5 * values * (1.0 - bend * bend) * scale * (1.0 + 0.134145 * square)
    return values * rise, slope


def dot(left, right, left_dim, right_dim):
    return lax.dot_general(
        left, right, (((left_dim,), (right_dim,)), ((), ())), preferred_element_type=F32
    )


def roll_rows(value):
    rows = value.shape[0] // 2
    return jnp.concatenate([value[rows:], value[:rows]])


def estimate(flops, size):
    return pl.CostEstimate(flops=flops // 4, bytes_accessed=size // 4, transcendentals=0)


def far(value):
    return pltpu.with_memory_space_constraint(value, pltpu.HBM)


def limit(mebibytes):
    return pltpu.CompilerParams(vmem_limit_bytes=mebibytes << 20)


def halves(core_ref, values, mine_ref, theirs_ref):
    width = mine_ref.shape[1]
    first = core_ref[0] == 0
    low, high = values[:, :width], values[:, width:]
    mine_ref[...] = jnp.where(first, low, high).astype(LOW)
    theirs_ref[...] = jnp.where(first, high, low).astype(LOW)


def norm_one_kernel(
    core_ref, x_ref, gain_ref, shift_ref, grad_ref, active_ref,
    mine_ref, theirs_ref, masked_ref, sum_ref,
):
    normed = layer_norm(x_ref[...].astype(F32), gain_ref[...], shift_ref[...])
    halves(core_ref, normed, mine_ref, theirs_ref)
    masked = active_ref[...] * grad_ref[...].astype(F32)
    masked_ref[...] = masked.astype(LOW)
    sum_ref[...] = jnp.sum(masked, axis=0, keepdims=True)


def norm_two_kernel(
    core_ref, x_ref, active_ref, part_ref, theirs_part_ref, bias_ref, gain_ref, shift_ref,
    middle_ref, mine_ref, theirs_ref,
):
    rows = x_ref.shape[0]
    attn = part_ref[:rows] + theirs_part_ref[...] + bias_ref[...]
    middle = x_ref[...].astype(F32) + active_ref[...] * attn
    middle_ref[...] = middle
    halves(core_ref, layer_norm(middle, gain_ref[...], shift_ref[...]), mine_ref, theirs_ref)


def norm_back(core_ref, value_ref, gain_ref, mine_ref, theirs_ref, gain_out_ref, shift_out_ref):
    values = value_ref[...].astype(F32)
    mine, theirs = mine_ref[: values.shape[0]], theirs_ref[...]
    grads = jnp.where(
        core_ref[0] == 0,
        jnp.concatenate([mine, theirs], 1),
        jnp.concatenate([theirs, mine], 1),
    )
    centered = values - jnp.mean(values, axis=-1, keepdims=True)
    scale = lax.rsqrt(jnp.mean(centered * centered, axis=-1, keepdims=True) + 1e-05)
    unit = centered * scale
    gain_out_ref[...] = jnp.sum(grads * unit, axis=0, keepdims=True)
    shift_out_ref[...] = jnp.sum(grads, axis=0, keepdims=True)
    grads = grads * gain_ref[...]
    inner = jnp.mean(grads * unit, axis=-1, keepdims=True)
    return scale * (grads - jnp.mean(grads, axis=-1, keepdims=True) - unit * inner)


def norm_two_back_kernel(
    core_ref, value_ref, gain_ref, mine_ref, theirs_ref, grad_ref, active_ref,
    total_ref, masked_ref, sum_ref, gain_out_ref, shift_out_ref,
):
    part = norm_back(
        core_ref, value_ref, gain_ref, mine_ref, theirs_ref, gain_out_ref, shift_out_ref
    )
    total = grad_ref[...].astype(F32) + part
    total_ref[...] = total
    masked = (active_ref[...] * total).astype(LOW)
    masked_ref[...] = masked
    sum_ref[...] = jnp.sum(masked.astype(F32), axis=0, keepdims=True)


def norm_one_back_kernel(
    core_ref, value_ref, gain_ref, mine_ref, theirs_ref, grad_ref,
    total_ref, gain_out_ref, shift_out_ref,
):
    part = norm_back(
        core_ref, value_ref, gain_ref, mine_ref, theirs_ref, gain_out_ref, shift_out_ref
    )
    total_ref[...] = (grad_ref[...].astype(F32) + part).astype(LOW)


def by_rows(kernel, core, outs, *operands):
    vmem = pl.BlockSpec(memory_space=pltpu.VMEM)
    return pl.pallas_call(
        kernel,
        in_specs=[pl.BlockSpec(memory_space=pltpu.SMEM)] + [vmem] * len(operands),
        out_specs=[vmem] * len(outs),
        out_shape=[jax.ShapeDtypeStruct(shape, dtype) for shape, dtype in outs],
        compiler_params=limit(24),
        cost_estimate=estimate(
            20 * operands[0].size, sum(o.size * o.dtype.itemsize for o in operands)
        ),
    )(core, *operands)


def product_kernel(count, turned, *refs):
    lefts, out_ref, left_turned, right = refs[:count], refs[-3], refs[-2], refs[-1]
    rights = refs[count:-3]
    length = lefts[0].shape[0]

    @pl.when(pl.program_id(0) == 0)
    def _():
        for d, left in enumerate(lefts):
            left_turned[:, d * length : (d + 1) * length] = left[...].T

    row = 0
    for piece in rights:
        value = piece[0] if len(piece.shape) == 3 else piece[...]
        if turned:
            value = roll_rows(value)
        right[row : row + value.shape[0]] = value
        row += value.shape[0]
    out_ref[...] = dot(left_turned[...], right[...], 1, 0).astype(LOW)


def rows_product(lefts, rights, block, first, steps, turned=False):
    length, tall = lefts[0].shape

    def spec(right):
        if isinstance(right, tuple):
            _, index, count = right
            return pl.BlockSpec((count, block), lambda j: (index, first + j))
        if right.ndim == 3:
            return pl.BlockSpec((1, right.shape[1], block), lambda j: (first + j, 0, 0))
        return pl.BlockSpec((right.shape[0], block), lambda j: (0, first + j))

    total = length * len(lefts)
    return pl.pallas_call(
        functools.partial(product_kernel, len(lefts), turned),
        grid=(steps,),
        in_specs=[pl.BlockSpec((length, tall), lambda j: (0, 0))] * len(lefts)
        + [spec(right) for right in rights],
        out_specs=pl.BlockSpec((tall, block), lambda j: (0, j)),
        out_shape=jax.ShapeDtypeStruct((tall, steps * block), LOW),
        scratch_shapes=[pltpu.VMEM((tall, total), LOW), pltpu.VMEM((total, block), LOW)],
        compiler_params=limit(32),
        cost_estimate=estimate(
            2 * tall * total * steps * block, 2 * total * (tall + steps * block)
        ),
    )(*lefts, *[r[0] if isinstance(r, tuple) else r for r in rights])


def hold(values, after):
    return lax.optimization_barrier((values, after))[0]


def columns_kernel(table_ref, left_ref, *refs):
    total, first = 0.0, 0
    for weight_ref in refs[:-1]:
        depth = weight_ref.shape[0]
        total += dot(left_ref[:, first : first + depth], weight_ref[...], 1, 0)
        first += depth
    refs[-1][...] = total.astype(refs[-1].dtype)


def times_columns(left, weight, table, block, dtype):
    rows, depth = left.shape
    steps = table.shape[0]
    return pl.pallas_call(
        columns_kernel,
        grid_spec=pltpu.PrefetchScalarGridSpec(
            num_scalar_prefetch=1,
            grid=(steps,),
            in_specs=[
                pl.BlockSpec((rows, depth), lambda i, t: (0, 0)),
                *[
                    pl.BlockSpec(
                        (depth // STREAMS, block),
                        functools.partial(lambda r, i, t: (r, t[i]), r),
                    )
                    for r in range(STREAMS)
                ],
            ],
            out_specs=pl.BlockSpec((rows, block), lambda i, t: (0, i)),
        ),
        out_shape=jax.ShapeDtypeStruct((rows, steps * block), dtype),
        compiler_params=limit(24),
        cost_estimate=estimate(2 * rows * depth * steps * block, 2 * depth * (rows + steps * block) + 4 * rows * steps * block),
    )(table, left, *[far(weight)] * STREAMS)


def back_kernel(turned, table_ref, left_ref, *refs):
    weights, out_ref = refs[:STREAMS], refs[-1]
    starts = refs[STREAMS:-1]
    left = left_ref[...]
    if turned:
        left = roll_rows(left)
    first = 0
    for weight_ref in weights:
        deep = weight_ref.shape[0]
        part = dot(left, weight_ref[...], 1, 1)
        columns = slice(first, first + deep)
        first += deep

        @pl.when(pl.program_id(1) == 0)
        def _(part=part, columns=columns):
            out_ref[:, columns] = part + starts[0][:, columns] if starts else part

        @pl.when(pl.program_id(1) > 0)
        def _(part=part, columns=columns):
            out_ref[:, columns] += part


def times_back(left, weight, table, block, deep, start=None, turned=False):
    rows = left.shape[0]
    depth = weight.shape[0]
    steps = table.shape[0]
    out_spec = pl.BlockSpec((rows, deep), lambda k, i, t: (0, k))
    in_specs = [
        pl.BlockSpec((rows, block), lambda k, i, t: (0, i)),
        *[
            pl.BlockSpec(
                (deep // STREAMS, block),
                functools.partial(lambda r, k, i, t: (k * STREAMS + r, t[i]), r),
            )
            for r in range(STREAMS)
        ],
    ]
    operands = [table, left, *[far(weight)] * STREAMS]
    if start is not None:
        in_specs.append(out_spec)
        operands.append(start)
    return pl.pallas_call(
        functools.partial(back_kernel, turned),
        grid_spec=pltpu.PrefetchScalarGridSpec(
            num_scalar_prefetch=1,
            grid=(depth // deep, steps),
            in_specs=in_specs,
            out_specs=out_spec,
        ),
        out_shape=jax.ShapeDtypeStruct((rows, depth), F32),
        compiler_params=limit(32),
        cost_estimate=estimate(2 * rows * depth * steps * block, 2 * steps * block * (rows + depth) + 8 * rows * depth),
    )(*operands)


def inner_kernel(grad_ref, *refs):
    weights = refs[:STREAMS]
    mine_ref, theirs_ref, bias_ref, act_ref, out_ref, sum_ref = refs[STREAMS:]
    first = 0
    for weight_ref in weights:
        columns = slice(first, first + weight_ref.shape[0])
        first += weight_ref.shape[0]
        theirs = roll_rows(theirs_ref[:, columns])
        act, slope = gelu_and_slope(mine_ref[:, columns] + theirs + bias_ref[:, columns])
        act_ref[:, columns] = act.astype(LOW)
        grad = (dot(grad_ref[...], weight_ref[...], 1, 1) * slope).astype(LOW)
        out_ref[:, columns] = grad
        sum_ref[:, columns] = jnp.sum(grad.astype(F32), axis=0, keepdims=True)


def inner_layer(grads, weight, mine, theirs, bias, block):
    rows, width = grads.shape
    hidden = weight.shape[0]
    part = pl.BlockSpec((rows, block), lambda i: (0, i))
    line = pl.BlockSpec((1, block), lambda i: (0, i))
    return pl.pallas_call(
        inner_kernel,
        grid=(hidden // block,),
        in_specs=[
            pl.BlockSpec((rows, width), lambda i: (0, 0)),
            *[
                pl.BlockSpec(
                    (block // STREAMS, width),
                    functools.partial(lambda r, i: (i * STREAMS + r, 0), r),
                )
                for r in range(STREAMS)
            ],
            part,
            part,
            line,
        ],
        out_specs=[part, part, line],
        out_shape=[
            jax.ShapeDtypeStruct((rows, hidden), LOW),
            jax.ShapeDtypeStruct((rows, hidden), LOW),
            jax.ShapeDtypeStruct((1, hidden), F32),
        ],
        compiler_params=limit(32),
        cost_estimate=estimate(2 * rows * width * hidden, 2 * width * (rows + hidden) + 12 * rows * hidden),
    )(grads, *[far(weight)] * STREAMS, mine, theirs, bias)


def head_chances(queries, keys, lanes_of_head, allowed):
    keys_of_head = jnp.where(lanes_of_head, keys, jnp.zeros_like(keys))
    scores = dot(queries, keys_of_head, 1, 1) * (HEAD_DIM**-0.5)
    scores = jnp.where(allowed, scores, -1e30)
    raised = jnp.exp(scores - jnp.max(scores, axis=-1, keepdims=True))
    return raised / jnp.sum(raised, axis=-1, keepdims=True)


def attend_masks(first, length, lanes):
    lane = lax.broadcasted_iota(jnp.int32, (length, lanes), 1)
    row = lax.broadcasted_iota(jnp.int32, (length, length), 0) + first
    column = lax.broadcasted_iota(jnp.int32, (length, length), 1) + first
    row = jnp.where(row >= length, row - length, row)
    column = jnp.where(column >= length, column - length, column)
    return lane, column <= row


def attend_forward_kernel(first_ref, *refs):
    mine, theirs, biases, lows, o_ref = refs[:3], refs[3:6], refs[6:9], refs[9:12], refs[12]
    sums = [
        (m[...] + roll_rows(t[...]) + b[...]).astype(LOW)
        for m, t, b in zip(mine, theirs, biases)
    ]
    for low, value in zip(lows, sums):
        low[...] = value
    queries, keys, values = sums
    lane, allowed = attend_masks(first_ref[0], *queries.shape)
    total = jnp.zeros(queries.shape, F32)
    for head in range(queries.shape[1] // HEAD_DIM):
        own = lane // HEAD_DIM == head
        chances = head_chances(queries, keys, own, allowed).astype(LOW)
        total += dot(chances, jnp.where(own, values, jnp.zeros_like(values)), 1, 0)
    o_ref[...] = total.astype(LOW)


def attend_forward(first, mine, theirs, bias):
    length, width = mine.shape
    width //= 3
    steps = width // 128
    parts = [
        pl.BlockSpec((length, 128), functools.partial(lambda p, i, t: (0, p * steps + i), p))
        for p in range(3)
    ]
    lines = [
        pl.BlockSpec((1, 128), functools.partial(lambda p, i, t: (0, p * steps + i), p))
        for p in range(3)
    ]
    return pl.pallas_call(
        attend_forward_kernel,
        grid_spec=pltpu.PrefetchScalarGridSpec(
            num_scalar_prefetch=1,
            grid=(steps,),
            in_specs=parts + parts + lines,
            out_specs=[parts[0]] * 4,
        ),
        out_shape=[jax.ShapeDtypeStruct((length, width), LOW)] * 4,
        compiler_params=limit(16),
        cost_estimate=estimate(4 * length * length * width, 32 * length * width),
    )(first, mine, mine, mine, theirs, theirs, theirs, bias, bias, bias)


def attend_backward_kernel(first_ref, q_ref, k_ref, v_ref, g_ref, out_ref):
    queries, keys, values, grads = q_ref[...], k_ref[...], v_ref[...], g_ref[...]
    lane, allowed = attend_masks(first_ref[0], *queries.shape)
    dq = jnp.zeros(queries.shape, F32)
    dk = jnp.zeros(queries.shape, F32)
    dv = jnp.zeros(queries.shape, F32)
    for head in range(queries.shape[1] // HEAD_DIM):
        own = lane // HEAD_DIM == head
        chances = head_chances(queries, keys, own, allowed)
        head_grads = jnp.where(own, grads, jnp.zeros_like(grads))
        dv += dot(chances.astype(LOW), head_grads, 0, 0)
        chance_grads = dot(head_grads, values, 1, 1)
        inner = jnp.sum(chances * chance_grads, axis=-1, keepdims=True)
        score_grads = (chances * (chance_grads - inner)).astype(LOW)
        dq += dot(score_grads, jnp.where(own, keys, jnp.zeros_like(keys)), 1, 0)
        dk += dot(score_grads, jnp.where(own, queries, jnp.zeros_like(queries)), 0, 0)
    scale = HEAD_DIM**-0.5
    out_ref[0] = (dq * scale).astype(LOW)
    out_ref[1] = (dk * scale).astype(LOW)
    out_ref[2] = dv.astype(LOW)


def attend_backward(first, *operands):
    length, width = operands[0].shape
    block = pl.BlockSpec((length, 128), lambda i, t: (0, i))
    return pl.pallas_call(
        attend_backward_kernel,
        grid_spec=pltpu.PrefetchScalarGridSpec(
            num_scalar_prefetch=1,
            grid=(width // 128,),
            in_specs=[block] * 4,
            out_specs=pl.BlockSpec((3, length, 128), lambda i, t: (0, 0, i)),
        ),
        out_shape=jax.ShapeDtypeStruct((3, length, width), LOW),
        compiler_params=limit(16),
        cost_estimate=estimate(10 * length * length * width, 14 * length * width),
    )(first, *operands)


def place_kernel(high, table_ref, *refs):
    count = len(refs) - 4
    pieces, out_ref, held, sems = refs[:count], refs[-3], refs[-2], refs[-1]
    slots, broad = held.shape[0], held.shape[2]

    def copy(step):
        row = pl.multiple_of(table_ref[2 * step] * high, high)
        column = pl.multiple_of(table_ref[2 * step + 1] * broad, broad)
        return pltpu.make_async_copy(
            held.at[step % slots],
            out_ref.at[pl.ds(row, high), pl.ds(column, broad)],
            sems.at[step % slots],
        )

    step = 0
    for piece in pieces:
        for i in range(piece.shape[0] // high):
            for j in range(piece.shape[1] // broad):
                if step >= slots:
                    copy(step - slots).wait()
                part = piece[i * high : (i + 1) * high, j * broad : (j + 1) * broad]
                held[step % slots] = part.astype(F32)
                copy(step).start()
                step += 1
    for waited in range(max(step - slots, 0), step):
        copy(waited).wait()


def place(pieces, whole, places, high, broad):
    slots = 4
    vmem = pl.BlockSpec(memory_space=pltpu.VMEM)
    return pl.pallas_call(
        functools.partial(place_kernel, high),
        in_specs=[pl.BlockSpec(memory_space=pltpu.SMEM)]
        + [vmem] * len(pieces)
        + [pl.BlockSpec(memory_space=pl.ANY)],
        out_specs=pl.BlockSpec(memory_space=pl.ANY),
        out_shape=jax.ShapeDtypeStruct(whole.shape, F32),
        scratch_shapes=[
            pltpu.VMEM((slots, high, broad), F32),
            pltpu.SemaphoreType.DMA((slots,)),
        ],
        input_output_aliases={len(pieces) + 1: 0},
        compiler_params=limit(32),
        cost_estimate=estimate(0, sum(6 * p.size for p in pieces)),
    )(jnp.stack(places).astype(jnp.int32), *pieces, whole)


def blank_kernel(out_ref):
    pass


def blank(shape, dtype=F32):
    return pl.pallas_call(
        blank_kernel,
        out_specs=pl.BlockSpec(memory_space=pl.ANY),
        out_shape=jax.ShapeDtypeStruct(shape, dtype),
    )()


class Lane:
    def __init__(self):
        self.last = ()

    def send(self, sends, after=()):
        values = hold([v for v, _ in sends], (self.last, after))
        self.last = [lax.ppermute(v, "dp", m) for v, (_, m) in zip(values, sends)]
        return self.last


def per_device(
    hidden,
    cotangent,
    exit_layers,
    qkv_weight,
    out_weight,
    up_weight,
    down_weight,
    query_bias,
    value_bias,
    out_bias,
    up_bias,
    down_bias,
    attn_gain,
    attn_shift,
    ffn_gain,
    ffn_shift,
):
    core = lax.axis_index("sp")
    other = 1 - core
    chips = lax.axis_size("dp")
    plane = chips // LINE
    chip = lax.axis_index("dp")
    spot = chip % GROUP
    level = chip // plane
    rows = hidden.shape[1]
    width = hidden.shape[2]
    length = 2 * rows
    half = width // 2
    inner = up_weight.shape[1]
    inner_half = inner // 2
    across, middle_across, first_hop, middle_hop, last_hop = (Lane() for _ in range(5))

    def swap(value):
        return lax.ppermute(value, "sp", [(0, 1), (1, 0)])

    def in_plane(distance):
        return [(i, i // plane * plane + ((i % plane) ^ distance)) for i in range(chips)]

    def along(*moves):
        return [(a * plane + i, b * plane + i) for a, b in moves for i in range(plane)]

    inward, middle_moves, outward = (
        along((0, 1), (3, 2)),
        along((1, 2), (2, 1)),
        along((1, 0), (2, 3)),
    )

    def split(value, axis, size):
        return (
            lax.dynamic_slice_in_dim(value, core * size, size, axis),
            lax.dynamic_slice_in_dim(value, other * size, size, axis),
        )

    def exchange(blocks):
        return blocks[:1] + across.send([(blocks[d], in_plane(d)) for d in range(1, GROUP)])

    def gather_group(value):
        return exchange([value] * GROUP)

    def scatter_group(value, axis, size):
        blocks = [
            lax.dynamic_slice_in_dim(value, (spot ^ d) * size, size, axis) for d in range(GROUP)
        ]
        return exchange(blocks)

    def pairs(mine, theirs):
        return [piece for pair in zip(mine, theirs) for piece in pair]

    end = (level == 0) | (level == LINE - 1)

    def line_start(value, after=()):
        return value + hold(first_hop.send([(value, inward)])[0], after)

    def line_middle(value):
        return value + middle_hop.send([(value, middle_moves)])[0]

    def line_end(value):
        return jnp.where(end, last_hop.send([(value, outward)])[0], value)

    def blocks_sum(value):
        distance = GROUP
        while distance < plane:
            value = value + lax.ppermute(value, "dp", in_plane(distance))
            distance *= 2
        return value

    def spread(value, after):
        size = value.shape[0] // 2
        first, second = across.send([(value, in_plane(1)), (value, in_plane(2))], after[0])
        upper, lower = across.send(
            [(first[:size], in_plane(2)), (second[size:], in_plane(1))], after[1]
        )
        return [value, first, second, upper, lower]

    def spread_late(value, after):
        size = value.shape[0] // 2

        def middle_only(distance):
            return [(a, b) for a, b in in_plane(distance) if 0 < a // plane < LINE - 1]

        near = middle_across.send(
            [(value[:size], middle_only(1)), (value[size:], middle_only(2))]
        )
        own = line_end(value)
        first = across.send([(own[:size], in_plane(2)), (own[size:], in_plane(1))], after[0])
        near_ends = last_hop.send([(v, outward) for v in near])
        near = [jnp.where(end, e, v) for e, v in zip(near_ends, near)]
        second = across.send([(near[0], in_plane(2)), (near[1], in_plane(1))], after[1])
        return [own, near[0], first[1], first[0], near[1], *second]

    def table(size, start, count=None):
        return jnp.arange(size if count is None else count, dtype=jnp.int32) + start

    active = active_rows(exit_layers[0], core * rows, rows, length)
    core_number = core.astype(jnp.int32)[None]
    first_row = (core * rows).astype(jnp.int32)[None]
    full, part, line = (rows, width), (rows, half), (1, width)

    always = exit_layers[0, 1] > 0

    def segment(steps, *operands):
        def skip(*_):
            return [blank(shape.shape, shape.dtype) for shape in jax.eval_shape(steps, *operands)]

        return lax.cond(always, lambda *o: list(steps(*o)), skip, *operands)

    mine, theirs, down_grad, down_sums = by_rows(
        norm_one_kernel,
        core_number,
        [(part, LOW), (part, LOW), (full, LOW), (line, F32)],
        hidden[0],
        attn_gain[None],
        attn_shift[None],
        cotangent[0],
        active,
    )
    down_mine = gather_group(down_grad)
    qkv_block = min(1024, half)
    qkv_count = half // qkv_block
    bias = jnp.stack([query_bias, jnp.zeros_like(query_bias), value_bias])
    bias = lax.dynamic_slice_in_dim(bias, core * half, half, 1).reshape(1, -1)

    def qkv_table(c):
        return jnp.concatenate(
            [table(qkv_count, (2 * p + c) * qkv_count) for p in range(3)]
        )

    def to_attended(mine, theirs, down_grad, qkv_weight, bias, my_table, their_table, first_row):
        normed = jnp.concatenate([mine, swap(theirs)])
        theirs = times_columns(normed, qkv_weight, their_table, qkv_block, LOW)
        theirs = swap(theirs)
        mine = times_columns(normed, qkv_weight, my_table, qkv_block, F32)
        results = attend_forward(first_row, mine, theirs, bias)
        return [normed, *results, swap(down_grad)]

    normed_one_half, queries, keys, values, attended, down_grad_theirs = segment(
        to_attended, mine, theirs, down_grad, qkv_weight, bias,
        qkv_table(core), qkv_table(other), first_row,
    )
    attended, down_mine = lax.optimization_barrier((attended, down_mine))
    qkv_left = gather_group(normed_one_half)
    block = min(1024, inner_half)
    count = inner_half // block

    def to_inner(
        hidden, active, attended, out_weight, lines, up_weight, tables, core_number,
        grads, down_weight,
    ):
        out_part = dot(attended, out_weight, 1, 0)
        middle, mine, theirs = by_rows(
            norm_two_kernel,
            core_number,
            [(full, F32), (part, LOW), (part, LOW)],
            hidden,
            active,
            out_part,
            swap(out_part[rows:]),
            *lines[:3],
        )
        normed = jnp.concatenate([mine, swap(theirs)])
        theirs = times_columns(normed, up_weight, tables[1], block, LOW)
        theirs = swap(theirs)
        mine = times_columns(normed, up_weight, tables[0], block, F32)
        results = inner_layer(
            grads, down_weight, mine, theirs, lines[3], min(512, inner_half)
        )
        return [middle, normed, *results]

    bias = lax.dynamic_slice_in_dim(up_bias, core * inner_half, inner_half).reshape(1, -1)
    middle, normed_two_half, inner_low, up_grad, up_sums = segment(
        to_inner, hidden[0], active, attended, out_weight,
        (out_bias[None], ffn_gain[None], ffn_shift[None], bias), up_weight,
        (table(count, core * count), table(count, other * count)), core_number,
        jnp.concatenate([down_grad, down_grad_theirs]), down_weight,
    )
    (inner_low, up_grad), qkv_left = lax.optimization_barrier(((inner_low, up_grad), qkv_left))

    down_left = scatter_group(inner_low, 1, inner_half // GROUP)

    def to_middle(
        up_grad, up_weight, middle, gain, cotangent, active, core_number, down_mine, tables
    ):
        theirs = swap(up_grad)
        grads = times_back(up_grad, up_weight, tables[0], inner_half, 256)
        grads = times_back(theirs, up_weight, tables[1], inner_half, 256, grads, True)
        results = by_rows(
            norm_two_back_kernel,
            core_number,
            [(full, F32), (full, LOW), (line, F32), (line, F32), (line, F32)],
            middle,
            gain,
            grads,
            swap(grads[rows:]),
            cotangent,
            active,
        )
        return [*results, swap(jnp.concatenate(down_mine[1:]))]

    middle_grad, attn_grad, attn_sums, gain_two_grad, shift_two_grad, down_theirs = segment(
        to_middle, up_grad, up_weight, middle, ffn_gain[None], cotangent[0], active,
        core_number, down_mine, (table(1, core), table(1, other)),
    )
    down_theirs = [down_grad_theirs] + [(down_theirs, d, rows) for d in range(GROUP - 1)]
    down_right = pairs(down_mine, down_theirs)
    quarter = width // 4
    down_left, attn_grad = lax.optimization_barrier((down_left, attn_grad))
    up_right = scatter_group(up_grad, 1, inner_half // GROUP)
    sums = [rows_product(down_left, down_right, quarter, 0, 1)]
    (come,) = first_hop.send([(sums[0], inward)])
    attn_grad, sums[0] = lax.optimization_barrier((attn_grad, sums[0]))

    def to_qkv(attn_grad, out_weight, first_row, *operands):
        grads = jnp.concatenate([attn_grad, swap(attn_grad)])
        grads = dot(grads, out_weight, 1, 1).astype(LOW)
        qkv_grad = attend_backward(first_row, *operands, grads)
        flat = jnp.concatenate([qkv_grad[0], qkv_grad[1], qkv_grad[2]], 1)
        return [qkv_grad, flat, swap(flat)]

    qkv_grad, flat, flat_theirs = segment(to_qkv, attn_grad, out_weight, first_row, queries, keys, values)
    qkv_grad, up_right, come, sums = lax.optimization_barrier((qkv_grad, up_right, come, sums))
    sums[0] += come
    (passed,) = middle_hop.send([(sums[0], middle_moves)])
    up_left = gather_group(normed_two_half)

    def to_input(flat, theirs, qkv_weight, tables):
        grads = times_back(flat, qkv_weight, tables[0], qkv_block, 512)
        return [times_back(theirs, qkv_weight, tables[1], qkv_block, 512, grads, True)]

    (grads,) = segment(
        to_input, hold(flat, qkv_grad), flat_theirs, qkv_weight,
        (qkv_table(core), qkv_table(other)),
    )
    grads, up_left, passed = lax.optimization_barrier((grads, up_left, passed))
    sums[0] = line_end(sums[0] + passed)
    for part_index in range(1, 4):
        value = rows_product(down_left, down_right, quarter, part_index, 1)
        sums.append(line_start(hold(value, grads)))
    out_right = scatter_group(attn_grad, 1, width // GROUP)
    out_left = gather_group(attended)
    qkv_right = scatter_group(qkv_grad, 2, half // GROUP)

    def to_ends(grads, hidden, gain, middle_grad, core_number, inner_low, down_weight):
        results = by_rows(
            norm_one_back_kernel,
            core_number,
            [(full, LOW), (line, F32), (line, F32)],
            hidden,
            gain,
            grads,
            swap(grads[rows:]),
            middle_grad,
        )
        down_part = dot(inner_low, down_weight, 1, 0)
        return [*results, down_part[:rows], swap(down_part[rows:])]

    input_grad, gain_one_grad, shift_one_grad, mine, theirs = segment(
        to_ends, hold(grads, sums[0]), hidden[0], attn_gain[None], middle_grad, core_number,
        inner_low, down_weight,
    )
    output = middle + active * (mine + theirs + down_bias)

    def widen(value):
        none = jnp.zeros_like(value)
        return jnp.where(
            core == 0, jnp.concatenate([value, none]), jnp.concatenate([none, value])
        )

    qkv_sums = jnp.sum(qkv_grad.astype(F32), axis=1)
    small = jnp.concatenate(
        [
            widen(qkv_sums[0]),
            widen(qkv_sums[2]),
            attn_sums[0],
            widen(up_sums[0]),
            down_sums[0],
            gain_one_grad[0],
            shift_one_grad[0],
            gain_two_grad[0],
            shift_two_grad[0],
        ]
    ).reshape(-1, 128)
    small = small + swap(small)
    distance = 1
    while distance < plane:
        small = small + lax.ppermute(small, "dp", in_plane(distance))
        distance *= 2
    small = small + lax.ppermute(small, "dp", inward)
    small = small + lax.ppermute(small, "dp", middle_moves)
    small = jnp.where(end, lax.ppermute(small, "dp", outward), small).reshape(-1)
    small_grads = []
    first = 0
    for size in (width, width, width, inner, width, width, width, width, width):
        small_grads.append(small[first : first + size])
        first += size

    chunks = [("down", value, index) for index, value in enumerate(sums)]
    size = inner_half // GROUP
    block = min(512, size)
    value = rows_product(up_left, up_right, block, 0, size // block)
    chunks.append(("up", line_start(value), core))
    theirs = [swap(r) for r in up_right]
    value = rows_product(up_left, theirs, block, 0, size // block, True)
    chunks.append(("up", line_start(value), other))
    size = half // GROUP
    value = rows_product(qkv_left, qkv_right, size, 0, 3)
    chunks.append(("qkv", line_start(value), core))
    theirs = [swap(r) for r in qkv_right]
    value = rows_product(qkv_left, theirs, size, 0, 3, True)
    chunks.append(("qkv", line_start(value), other))
    right = pairs(out_right, [swap(r) for r in out_right])
    value = rows_product(out_left, right, width // GROUP, 0, 1)
    chunks.append(("out", line_start(value), 0))

    wholes = {
        "down": blank((inner_half, width)),
        "up": blank((half, inner)),
        "out": blank((half, width)),
        "qkv": blank((half, 3 * width)),
    }
    done = [(), ()]
    for index, (name, value, where) in enumerate(chunks):
        after = done[-2], small if index == 3 else ()
        if index == 0:
            pieces = spread(blocks_sum(value), after)
        elif plane == GROUP and name in LATE:
            pieces = spread_late(line_middle(value), after)
        else:
            pieces = spread(blocks_sum(line_end(line_middle(value))), after)
        tall, wide = value.shape
        high = min(256, tall)
        broad = wide // 3 if name == "qkv" else wide
        places = []
        for d in range(GROUP):
            owner = spot ^ d
            for i in range(tall // high):
                row = jnp.int32(i)
                if name == "down":
                    row, columns = owner * (tall // high) + i, [jnp.int32(where)]
                elif name == "up":
                    columns = [where * GROUP + owner]
                elif name == "out":
                    columns = [owner]
                else:
                    columns = [(2 * p + where) * GROUP + owner for p in range(3)]
                for column in columns:
                    places += [row, column]
        wholes[name] = place(pieces, wholes[name], places, high, broad)
        done.append(wholes[name])

    return (
        output.astype(LOW)[None],
        input_grad[None],
        wholes["qkv"],
        wholes["out"],
        wholes["up"],
        wholes["down"],
        *small_grads,
    )


def solution(mesh):
    return jax.shard_map(
        per_device,
        mesh=mesh,
        in_specs=(
            P("dp", "sp", None),
            P("dp", "sp", None),
            P("dp", None),
            P("sp", None),
            P("sp", None),
            P("sp", None),
            P("sp", None),
            P(),
            P(),
            P(),
            P(),
            P(),
            P(),
            P(),
            P(),
            P(),
        ),
        out_specs=(
            P("dp", "sp", None),
            P("dp", "sp", None),
            P("sp", None),
            P("sp", None),
            P("sp", None),
            P("sp", None),
            P(),
            P(),
            P(),
            P(),
            P(),
            P(),
            P(),
            P(),
            P(),
        ),
        check_vma=False,
    )
```

```python
import functools

import jax
import jax.numpy as jnp
from jax import lax
from jax.experimental import pallas as pl
from jax.experimental.pallas import tpu as pltpu
from jax.sharding import PartitionSpec as P

HEAD_DIM = 64
TILE = 128
LAYER = 12
LINE = 4
STREAMS = 1
LATE = ()
GROUP = 4
F32 = jnp.float32
LOW = jnp.bfloat16


def layer_norm(values, gain, shift):
    center = jnp.mean(values, axis=-1, keepdims=True)
    centered = values - center
    variance = jnp.mean(centered * centered, axis=-1, keepdims=True)
    return centered * lax.rsqrt(variance + 1e-05) * gain + shift


def active_rows(bounds, first_row, row_count, sequence_length):
    position = first_row + jnp.arange(row_count, dtype=jnp.int32)
    tile_start = position // TILE * TILE
    exit_layer = bounds[1] - (bounds[1] - bounds[0]) * tile_start // sequence_length
    return (exit_layer > LAYER).astype(F32)[:, None]


def gelu_and_slope(values):
    scale = (2.0 / jnp.pi) ** 0.5
    square = values * values
    bend = jnp.tanh(scale * values * (1.0 + 0.044715 * square))
    rise = 0.5 * (1.0 + bend)
    slope = rise + 0.5 * values * (1.0 - bend * bend) * scale * (1.0 + 0.134145 * square)
    return values * rise, slope


def dot(left, right, left_dim, right_dim):
    return lax.dot_general(
        left, right, (((left_dim,), (right_dim,)), ((), ())), preferred_element_type=F32
    )


def roll_rows(value):
    rows = value.shape[0] // 2
    return jnp.concatenate([value[rows:], value[:rows]])


def estimate(flops, size):
    return pl.CostEstimate(flops=flops // 4, bytes_accessed=size // 4, transcendentals=0)


def far(value):
    return pltpu.with_memory_space_constraint(value, pltpu.HBM)


def limit(mebibytes):
    return pltpu.CompilerParams(vmem_limit_bytes=mebibytes << 20)


def halves(core_ref, values, mine_ref, theirs_ref):
    width = mine_ref.shape[1]
    first = core_ref[0] == 0
    low, high = values[:, :width], values[:, width:]
    mine_ref[...] = jnp.where(first, low, high).astype(LOW)
    theirs_ref[...] = jnp.where(first, high, low).astype(LOW)


def norm_one_kernel(
    core_ref, x_ref, gain_ref, shift_ref, grad_ref, active_ref,
    mine_ref, theirs_ref, masked_ref, sum_ref,
):
    normed = layer_norm(x_ref[...].astype(F32), gain_ref[...], shift_ref[...])
    halves(core_ref, normed, mine_ref, theirs_ref)
    masked = active_ref[...] * grad_ref[...].astype(F32)
    masked_ref[...] = masked.astype(LOW)
    sum_ref[...] = jnp.sum(masked, axis=0, keepdims=True)


def norm_two_kernel(
    core_ref, x_ref, active_ref, part_ref, theirs_part_ref, bias_ref, gain_ref, shift_ref,
    middle_ref, mine_ref, theirs_ref,
):
    rows = x_ref.shape[0]
    attn = part_ref[:rows] + theirs_part_ref[...] + bias_ref[...]
    middle = x_ref[...].astype(F32) + active_ref[...] * attn
    middle_ref[...] = middle
    halves(core_ref, layer_norm(middle, gain_ref[...], shift_ref[...]), mine_ref, theirs_ref)


def norm_back(core_ref, value_ref, gain_ref, mine_ref, theirs_ref, gain_out_ref, shift_out_ref):
    values = value_ref[...].astype(F32)
    mine, theirs = mine_ref[: values.shape[0]], theirs_ref[...]
    grads = jnp.where(
        core_ref[0] == 0,
        jnp.concatenate([mine, theirs], 1),
        jnp.concatenate([theirs, mine], 1),
    )
    centered = values - jnp.mean(values, axis=-1, keepdims=True)
    scale = lax.rsqrt(jnp.mean(centered * centered, axis=-1, keepdims=True) + 1e-05)
    unit = centered * scale
    gain_out_ref[...] = jnp.sum(grads * unit, axis=0, keepdims=True)
    shift_out_ref[...] = jnp.sum(grads, axis=0, keepdims=True)
    grads = grads * gain_ref[...]
    inner = jnp.mean(grads * unit, axis=-1, keepdims=True)
    return scale * (grads - jnp.mean(grads, axis=-1, keepdims=True) - unit * inner)


def norm_two_back_kernel(
    core_ref, value_ref, gain_ref, mine_ref, theirs_ref, grad_ref, active_ref,
    total_ref, masked_ref, sum_ref, gain_out_ref, shift_out_ref,
):
    part = norm_back(
        core_ref, value_ref, gain_ref, mine_ref, theirs_ref, gain_out_ref, shift_out_ref
    )
    total = grad_ref[...].astype(F32) + part
    total_ref[...] = total
    masked = (active_ref[...] * total).astype(LOW)
    masked_ref[...] = masked
    sum_ref[...] = jnp.sum(masked.astype(F32), axis=0, keepdims=True)


def norm_one_back_kernel(
    core_ref, value_ref, gain_ref, mine_ref, theirs_ref, grad_ref,
    total_ref, gain_out_ref, shift_out_ref,
):
    part = norm_back(
        core_ref, value_ref, gain_ref, mine_ref, theirs_ref, gain_out_ref, shift_out_ref
    )
    total_ref[...] = (grad_ref[...].astype(F32) + part).astype(LOW)


def by_rows(kernel, core, outs, *operands):
    vmem = pl.BlockSpec(memory_space=pltpu.VMEM)
    return pl.pallas_call(
        kernel,
        in_specs=[pl.BlockSpec(memory_space=pltpu.SMEM)] + [vmem] * len(operands),
        out_specs=[vmem] * len(outs),
        out_shape=[jax.ShapeDtypeStruct(shape, dtype) for shape, dtype in outs],
        compiler_params=limit(24),
        cost_estimate=estimate(
            20 * operands[0].size, sum(o.size * o.dtype.itemsize for o in operands)
        ),
    )(core, *operands)


def product_kernel(count, turned, *refs):
    lefts, out_ref, left_turned, right = refs[:count], refs[-3], refs[-2], refs[-1]
    rights = refs[count:-3]
    length = lefts[0].shape[0]

    @pl.when(pl.program_id(0) == 0)
    def _():
        for d, left in enumerate(lefts):
            left_turned[:, d * length : (d + 1) * length] = left[...].T

    row = 0
    for piece in rights:
        value = piece[0] if len(piece.shape) == 3 else piece[...]
        if turned:
            value = roll_rows(value)
        right[row : row + value.shape[0]] = value
        row += value.shape[0]
    out_ref[...] = dot(left_turned[...], right[...], 1, 0).astype(LOW)


def rows_product(lefts, rights, block, first, steps, turned=False):
    length, tall = lefts[0].shape

    def spec(right):
        if isinstance(right, tuple):
            _, index, count = right
            return pl.BlockSpec((count, block), lambda j: (index, first + j))
        if right.ndim == 3:
            return pl.BlockSpec((1, right.shape[1], block), lambda j: (first + j, 0, 0))
        return pl.BlockSpec((right.shape[0], block), lambda j: (0, first + j))

    total = length * len(lefts)
    return pl.pallas_call(
        functools.partial(product_kernel, len(lefts), turned),
        grid=(steps,),
        in_specs=[pl.BlockSpec((length, tall), lambda j: (0, 0))] * len(lefts)
        + [spec(right) for right in rights],
        out_specs=pl.BlockSpec((tall, block), lambda j: (0, j)),
        out_shape=jax.ShapeDtypeStruct((tall, steps * block), LOW),
        scratch_shapes=[pltpu.VMEM((tall, total), LOW), pltpu.VMEM((total, block), LOW)],
        compiler_params=limit(32),
        cost_estimate=estimate(
            2 * tall * total * steps * block, 2 * total * (tall + steps * block)
        ),
    )(*lefts, *[r[0] if isinstance(r, tuple) else r for r in rights])


def hold(values, after):
    return lax.optimization_barrier((values, after))[0]


def columns_kernel(table_ref, left_ref, *refs):
    total, first = 0.0, 0
    for weight_ref in refs[:-1]:
        depth = weight_ref.shape[0]
        total += dot(left_ref[:, first : first + depth], weight_ref[...], 1, 0)
        first += depth
    refs[-1][...] = total.astype(refs[-1].dtype)


def times_columns(left, weight, table, block, dtype):
    rows, depth = left.shape
    steps = table.shape[0]
    return pl.pallas_call(
        columns_kernel,
        grid_spec=pltpu.PrefetchScalarGridSpec(
            num_scalar_prefetch=1,
            grid=(steps,),
            in_specs=[
                pl.BlockSpec((rows, depth), lambda i, t: (0, 0)),
                *[
                    pl.BlockSpec(
                        (depth // STREAMS, block),
                        functools.partial(lambda r, i, t: (r, t[i]), r),
                    )
                    for r in range(STREAMS)
                ],
            ],
            out_specs=pl.BlockSpec((rows, block), lambda i, t: (0, i)),
        ),
        out_shape=jax.ShapeDtypeStruct((rows, steps * block), dtype),
        compiler_params=limit(24),
        cost_estimate=estimate(2 * rows * depth * steps * block, 2 * depth * (rows + steps * block) + 4 * rows * steps * block),
    )(table, left, *[far(weight)] * STREAMS)


def back_kernel(turned, table_ref, left_ref, *refs):
    weights, out_ref = refs[:STREAMS], refs[-1]
    starts = refs[STREAMS:-1]
    left = left_ref[...]
    if turned:
        left = roll_rows(left)
    first = 0
    for weight_ref in weights:
        deep = weight_ref.shape[0]
        part = dot(left, weight_ref[...], 1, 1)
        columns = slice(first, first + deep)
        first += deep

        @pl.when(pl.program_id(1) == 0)
        def _(part=part, columns=columns):
            out_ref[:, columns] = part + starts[0][:, columns] if starts else part

        @pl.when(pl.program_id(1) > 0)
        def _(part=part, columns=columns):
            out_ref[:, columns] += part


def times_back(left, weight, table, block, deep, start=None, turned=False):
    rows = left.shape[0]
    depth = weight.shape[0]
    steps = table.shape[0]
    out_spec = pl.BlockSpec((rows, deep), lambda k, i, t: (0, k))
    in_specs = [
        pl.BlockSpec((rows, block), lambda k, i, t: (0, i)),
        *[
            pl.BlockSpec(
                (deep // STREAMS, block),
                functools.partial(lambda r, k, i, t: (k * STREAMS + r, t[i]), r),
            )
            for r in range(STREAMS)
        ],
    ]
    operands = [table, left, *[far(weight)] * STREAMS]
    if start is not None:
        in_specs.append(out_spec)
        operands.append(start)
    return pl.pallas_call(
        functools.partial(back_kernel, turned),
        grid_spec=pltpu.PrefetchScalarGridSpec(
            num_scalar_prefetch=1,
            grid=(depth // deep, steps),
            in_specs=in_specs,
            out_specs=out_spec,
        ),
        out_shape=jax.ShapeDtypeStruct((rows, depth), F32),
        compiler_params=limit(32),
        cost_estimate=estimate(2 * rows * depth * steps * block, 2 * steps * block * (rows + depth) + 8 * rows * depth),
    )(*operands)


def inner_kernel(grad_ref, *refs):
    weights = refs[:STREAMS]
    mine_ref, theirs_ref, bias_ref, act_ref, out_ref, sum_ref = refs[STREAMS:]
    first = 0
    for weight_ref in weights:
        columns = slice(first, first + weight_ref.shape[0])
        first += weight_ref.shape[0]
        theirs = roll_rows(theirs_ref[:, columns])
        act, slope = gelu_and_slope(mine_ref[:, columns] + theirs + bias_ref[:, columns])
        act_ref[:, columns] = act.astype(LOW)
        grad = (dot(grad_ref[...], weight_ref[...], 1, 1) * slope).astype(LOW)
        out_ref[:, columns] = grad
        sum_ref[:, columns] = jnp.sum(grad.astype(F32), axis=0, keepdims=True)


def inner_layer(grads, weight, mine, theirs, bias, block):
    rows, width = grads.shape
    hidden = weight.shape[0]
    part = pl.BlockSpec((rows, block), lambda i: (0, i))
    line = pl.BlockSpec((1, block), lambda i: (0, i))
    return pl.pallas_call(
        inner_kernel,
        grid=(hidden // block,),
        in_specs=[
            pl.BlockSpec((rows, width), lambda i: (0, 0)),
            *[
                pl.BlockSpec(
                    (block // STREAMS, width),
                    functools.partial(lambda r, i: (i * STREAMS + r, 0), r),
                )
                for r in range(STREAMS)
            ],
            part,
            part,
            line,
        ],
        out_specs=[part, part, line],
        out_shape=[
            jax.ShapeDtypeStruct((rows, hidden), LOW),
            jax.ShapeDtypeStruct((rows, hidden), LOW),
            jax.ShapeDtypeStruct((1, hidden), F32),
        ],
        compiler_params=limit(32),
        cost_estimate=estimate(2 * rows * width * hidden, 2 * width * (rows + hidden) + 12 * rows * hidden),
    )(grads, *[far(weight)] * STREAMS, mine, theirs, bias)


def head_chances(queries, keys, lanes_of_head, allowed):
    keys_of_head = jnp.where(lanes_of_head, keys, jnp.zeros_like(keys))
    scores = dot(queries, keys_of_head, 1, 1) * (HEAD_DIM**-0.5)
    scores = jnp.where(allowed, scores, -1e30)
    raised = jnp.exp(scores - jnp.max(scores, axis=-1, keepdims=True))
    return raised / jnp.sum(raised, axis=-1, keepdims=True)


def attend_masks(first, length, lanes):
    lane = lax.broadcasted_iota(jnp.int32, (length, lanes), 1)
    row = lax.broadcasted_iota(jnp.int32, (length, length), 0) + first
    column = lax.broadcasted_iota(jnp.int32, (length, length), 1) + first
    row = jnp.where(row >= length, row - length, row)
    column = jnp.where(column >= length, column - length, column)
    return lane, column <= row


def attend_forward_kernel(first_ref, *refs):
    mine, theirs, biases, lows, o_ref = refs[:3], refs[3:6], refs[6:9], refs[9:12], refs[12]
    sums = [
        (m[...] + roll_rows(t[...]) + b[...]).astype(LOW)
        for m, t, b in zip(mine, theirs, biases)
    ]
    for low, value in zip(lows, sums):
        low[...] = value
    queries, keys, values = sums
    lane, allowed = attend_masks(first_ref[0], *queries.shape)
    total = jnp.zeros(queries.shape, F32)
    for head in range(queries.shape[1] // HEAD_DIM):
        own = lane // HEAD_DIM == head
        chances = head_chances(queries, keys, own, allowed).astype(LOW)
        total += dot(chances, jnp.where(own, values, jnp.zeros_like(values)), 1, 0)
    o_ref[...] = total.astype(LOW)


def attend_forward(first, mine, theirs, bias):
    length, width = mine.shape
    width //= 3
    steps = width // 128
    parts = [
        pl.BlockSpec((length, 128), functools.partial(lambda p, i, t: (0, p * steps + i), p))
        for p in range(3)
    ]
    lines = [
        pl.BlockSpec((1, 128), functools.partial(lambda p, i, t: (0, p * steps + i), p))
        for p in range(3)
    ]
    return pl.pallas_call(
        attend_forward_kernel,
        grid_spec=pltpu.PrefetchScalarGridSpec(
            num_scalar_prefetch=1,
            grid=(steps,),
            in_specs=parts + parts + lines,
            out_specs=[parts[0]] * 4,
        ),
        out_shape=[jax.ShapeDtypeStruct((length, width), LOW)] * 4,
        compiler_params=limit(16),
        cost_estimate=estimate(4 * length * length * width, 32 * length * width),
    )(first, mine, mine, mine, theirs, theirs, theirs, bias, bias, bias)


def attend_backward_kernel(first_ref, q_ref, k_ref, v_ref, g_ref, out_ref):
    queries, keys, values, grads = q_ref[...], k_ref[...], v_ref[...], g_ref[...]
    lane, allowed = attend_masks(first_ref[0], *queries.shape)
    dq = jnp.zeros(queries.shape, F32)
    dk = jnp.zeros(queries.shape, F32)
    dv = jnp.zeros(queries.shape, F32)
    for head in range(queries.shape[1] // HEAD_DIM):
        own = lane // HEAD_DIM == head
        chances = head_chances(queries, keys, own, allowed)
        head_grads = jnp.where(own, grads, jnp.zeros_like(grads))
        dv += dot(chances.astype(LOW), head_grads, 0, 0)
        chance_grads = dot(head_grads, values, 1, 1)
        inner = jnp.sum(chances * chance_grads, axis=-1, keepdims=True)
        score_grads = (chances * (chance_grads - inner)).astype(LOW)
        dq += dot(score_grads, jnp.where(own, keys, jnp.zeros_like(keys)), 1, 0)
        dk += dot(score_grads, jnp.where(own, queries, jnp.zeros_like(queries)), 0, 0)
    scale = HEAD_DIM**-0.5
    out_ref[0] = (dq * scale).astype(LOW)
    out_ref[1] = (dk * scale).astype(LOW)
    out_ref[2] = dv.astype(LOW)


def attend_backward(first, *operands):
    length, width = operands[0].shape
    block = pl.BlockSpec((length, 128), lambda i, t: (0, i))
    return pl.pallas_call(
        attend_backward_kernel,
        grid_spec=pltpu.PrefetchScalarGridSpec(
            num_scalar_prefetch=1,
            grid=(width // 128,),
            in_specs=[block] * 4,
            out_specs=pl.BlockSpec((3, length, 128), lambda i, t: (0, 0, i)),
        ),
        out_shape=jax.ShapeDtypeStruct((3, length, width), LOW),
        compiler_params=limit(16),
        cost_estimate=estimate(10 * length * length * width, 14 * length * width),
    )(first, *operands)


def place_kernel(high, table_ref, *refs):
    count = len(refs) - 4
    pieces, out_ref, held, sems = refs[:count], refs[-3], refs[-2], refs[-1]
    slots, broad = held.shape[0], held.shape[2]

    def copy(step):
        row = pl.multiple_of(table_ref[2 * step] * high, high)
        column = pl.multiple_of(table_ref[2 * step + 1] * broad, broad)
        return pltpu.make_async_copy(
            held.at[step % slots],
            out_ref.at[pl.ds(row, high), pl.ds(column, broad)],
            sems.at[step % slots],
        )

    step = 0
    for piece in pieces:
        for i in range(piece.shape[0] // high):
            for j in range(piece.shape[1] // broad):
                if step >= slots:
                    copy(step - slots).wait()
                part = piece[i * high : (i + 1) * high, j * broad : (j + 1) * broad]
                held[step % slots] = part.astype(F32)
                copy(step).start()
                step += 1
    for waited in range(max(step - slots, 0), step):
        copy(waited).wait()


def place(pieces, whole, places, high, broad):
    slots = 4
    vmem = pl.BlockSpec(memory_space=pltpu.VMEM)
    return pl.pallas_call(
        functools.partial(place_kernel, high),
        in_specs=[pl.BlockSpec(memory_space=pltpu.SMEM)]
        + [vmem] * len(pieces)
        + [pl.BlockSpec(memory_space=pl.ANY)],
        out_specs=pl.BlockSpec(memory_space=pl.ANY),
        out_shape=jax.ShapeDtypeStruct(whole.shape, F32),
        scratch_shapes=[
            pltpu.VMEM((slots, high, broad), F32),
            pltpu.SemaphoreType.DMA((slots,)),
        ],
        input_output_aliases={len(pieces) + 1: 0},
        compiler_params=limit(32),
        cost_estimate=estimate(0, sum(6 * p.size for p in pieces)),
    )(jnp.stack(places).astype(jnp.int32), *pieces, whole)


def blank_kernel(out_ref):
    pass


def blank(shape, dtype=F32):
    return pl.pallas_call(
        blank_kernel,
        out_specs=pl.BlockSpec(memory_space=pl.ANY),
        out_shape=jax.ShapeDtypeStruct(shape, dtype),
    )()


class Lane:
    def __init__(self):
        self.last = ()

    def send(self, sends, after=()):
        values = hold([v for v, _ in sends], (self.last, after))
        self.last = [lax.ppermute(v, "dp", m) for v, (_, m) in zip(values, sends)]
        return self.last


def per_device(
    hidden,
    cotangent,
    exit_layers,
    qkv_weight,
    out_weight,
    up_weight,
    down_weight,
    query_bias,
    value_bias,
    out_bias,
    up_bias,
    down_bias,
    attn_gain,
    attn_shift,
    ffn_gain,
    ffn_shift,
):
    core = lax.axis_index("sp")
    other = 1 - core
    chips = lax.axis_size("dp")
    plane = chips // LINE
    chip = lax.axis_index("dp")
    spot = chip % GROUP
    level = chip // plane
    rows = hidden.shape[1]
    width = hidden.shape[2]
    length = 2 * rows
    half = width // 2
    inner = up_weight.shape[1]
    inner_half = inner // 2
    across, middle_across, first_hop, middle_hop, last_hop = (Lane() for _ in range(5))

    def swap(value):
        return lax.ppermute(value, "sp", [(0, 1), (1, 0)])

    def in_plane(distance):
        return [(i, i // plane * plane + ((i % plane) ^ distance)) for i in range(chips)]

    def along(*moves):
        return [(a * plane + i, b * plane + i) for a, b in moves for i in range(plane)]

    inward, middle_moves, outward = (
        along((0, 1), (3, 2)),
        along((1, 2), (2, 1)),
        along((1, 0), (2, 3)),
    )

    def split(value, axis, size):
        return (
            lax.dynamic_slice_in_dim(value, core * size, size, axis),
            lax.dynamic_slice_in_dim(value, other * size, size, axis),
        )

    def exchange(blocks):
        return blocks[:1] + across.send([(blocks[d], in_plane(d)) for d in range(1, GROUP)])

    def gather_group(value):
        return exchange([value] * GROUP)

    def blocks_of(value, axis, size):
        return [
            lax.dynamic_slice_in_dim(value, (spot ^ d) * size, size, axis) for d in range(GROUP)
        ]

    def scatter_group(value, axis, size):
        return exchange(blocks_of(value, axis, size))

    def pairs(mine, theirs):
        return [piece for pair in zip(mine, theirs) for piece in pair]

    end = (level == 0) | (level == LINE - 1)

    def line_start(value, after=()):
        return value + hold(first_hop.send([(value, inward)])[0], after)

    def line_middle(value):
        return value + middle_hop.send([(value, middle_moves)])[0]

    def line_end(value):
        return jnp.where(end, last_hop.send([(value, outward)])[0], value)

    def blocks_sum(value):
        distance = GROUP
        while distance < plane:
            value = value + lax.ppermute(value, "dp", in_plane(distance))
            distance *= 2
        return value

    def spread(value, after):
        size = value.shape[0] // 2
        first, second = across.send([(value, in_plane(1)), (value, in_plane(2))], after[0])
        upper, lower = across.send(
            [(first[:size], in_plane(2)), (second[size:], in_plane(1))], after[1]
        )
        return [value, first, second, upper, lower]

    def spread_late(value, after):
        size = value.shape[0] // 2

        def middle_only(distance):
            return [(a, b) for a, b in in_plane(distance) if 0 < a // plane < LINE - 1]

        near = middle_across.send(
            [(value[:size], middle_only(1)), (value[size:], middle_only(2))]
        )
        own = line_end(value)
        first = across.send([(own[:size], in_plane(2)), (own[size:], in_plane(1))], after[0])
        near_ends = last_hop.send([(v, outward) for v in near])
        near = [jnp.where(end, e, v) for e, v in zip(near_ends, near)]
        second = across.send([(near[0], in_plane(2)), (near[1], in_plane(1))], after[1])
        return [own, near[0], first[1], first[0], near[1], *second]

    def table(size, start, count=None):
        return jnp.arange(size if count is None else count, dtype=jnp.int32) + start

    active = active_rows(exit_layers[0], core * rows, rows, length)
    core_number = core.astype(jnp.int32)[None]
    first_row = (core * rows).astype(jnp.int32)[None]
    full, part, line = (rows, width), (rows, half), (1, width)

    always = exit_layers[0, 1] > 0

    def segment(steps, *operands):
        def skip(*_):
            return [blank(shape.shape, shape.dtype) for shape in jax.eval_shape(steps, *operands)]

        return lax.cond(always, lambda *o: list(steps(*o)), skip, *operands)

    mine, theirs, down_grad, down_sums = by_rows(
        norm_one_kernel,
        core_number,
        [(part, LOW), (part, LOW), (full, LOW), (line, F32)],
        hidden[0],
        attn_gain[None],
        attn_shift[None],
        cotangent[0],
        active,
    )
    down_mine = gather_group(down_grad)
    qkv_block = min(1024, half)
    qkv_count = half // qkv_block
    bias = jnp.stack([query_bias, jnp.zeros_like(query_bias), value_bias])
    bias = lax.dynamic_slice_in_dim(bias, core * half, half, 1).reshape(1, -1)

    def qkv_table(c):
        return jnp.concatenate(
            [table(qkv_count, (2 * p + c) * qkv_count) for p in range(3)]
        )

    def to_attended(mine, theirs, down_grad, qkv_weight, bias, my_table, their_table, first_row):
        normed = jnp.concatenate([mine, swap(theirs)])
        theirs = times_columns(normed, qkv_weight, their_table, qkv_block, LOW)
        theirs = swap(theirs)
        mine = times_columns(normed, qkv_weight, my_table, qkv_block, F32)
        results = attend_forward(first_row, mine, theirs, bias)
        return [normed, *results, swap(down_grad)]

    normed_one_half, queries, keys, values, attended, down_grad_theirs = segment(
        to_attended, mine, theirs, down_grad, qkv_weight, bias,
        qkv_table(core), qkv_table(other), first_row,
    )
    attended, down_mine = lax.optimization_barrier((attended, down_mine))
    qkv_left = gather_group(normed_one_half)
    block = min(1024, inner_half)
    count = inner_half // block

    def to_inner(
        hidden, active, attended, out_weight, lines, up_weight, tables, core_number,
        grads, down_weight,
    ):
        out_part = dot(attended, out_weight, 1, 0)
        middle, mine, theirs = by_rows(
            norm_two_kernel,
            core_number,
            [(full, F32), (part, LOW), (part, LOW)],
            hidden,
            active,
            out_part,
            swap(out_part[rows:]),
            *lines[:3],
        )
        normed = jnp.concatenate([mine, swap(theirs)])
        theirs = times_columns(normed, up_weight, tables[1], block, LOW)
        theirs = swap(theirs)
        mine = times_columns(normed, up_weight, tables[0], block, F32)
        results = inner_layer(
            grads, down_weight, mine, theirs, lines[3], min(512, inner_half)
        )
        return [middle, normed, *results]

    bias = lax.dynamic_slice_in_dim(up_bias, core * inner_half, inner_half).reshape(1, -1)
    middle, normed_two_half, inner_low, up_grad, up_sums = segment(
        to_inner, hidden[0], active, attended, out_weight,
        (out_bias[None], ffn_gain[None], ffn_shift[None], bias), up_weight,
        (table(count, core * count), table(count, other * count)), core_number,
        jnp.concatenate([down_grad, down_grad_theirs]), down_weight,
    )
    (inner_low, up_grad), qkv_left = lax.optimization_barrier(((inner_low, up_grad), qkv_left))

    down_left = scatter_group(inner_low, 1, inner_half // GROUP)

    def to_middle(
        up_grad, up_weight, middle, gain, cotangent, active, core_number, down_mine, tables
    ):
        theirs = swap(up_grad)
        grads = times_back(up_grad, up_weight, tables[0], inner_half, 256)
        grads = times_back(theirs, up_weight, tables[1], inner_half, 256, grads, True)
        results = by_rows(
            norm_two_back_kernel,
            core_number,
            [(full, F32), (full, LOW), (line, F32), (line, F32), (line, F32)],
            middle,
            gain,
            grads,
            swap(grads[rows:]),
            cotangent,
            active,
        )
        down_theirs = swap(jnp.concatenate(down_mine[1:]))
        return [*results, down_theirs, *blocks_of(up_grad, 1, inner_half // GROUP)]

    (
        middle_grad, attn_grad, attn_sums, gain_two_grad, shift_two_grad, down_theirs, *up_right
    ) = segment(
        to_middle, up_grad, up_weight, middle, ffn_gain[None], cotangent[0], active,
        core_number, down_mine, (table(1, core), table(1, other)),
    )
    down_theirs = [down_grad_theirs] + [(down_theirs, d, rows) for d in range(GROUP - 1)]
    down_right = pairs(down_mine, down_theirs)
    quarter = width // 4
    down_left, attn_grad = lax.optimization_barrier((down_left, attn_grad))
    up_right = exchange(up_right)
    sums = [rows_product(down_left, down_right, quarter, 0, 1)]
    (come,) = first_hop.send([(sums[0], inward)])
    attn_grad, sums[0] = lax.optimization_barrier((attn_grad, sums[0]))

    def to_qkv(attn_grad, out_weight, first_row, *operands):
        grads = jnp.concatenate([attn_grad, swap(attn_grad)])
        grads = dot(grads, out_weight, 1, 1).astype(LOW)
        qkv_grad = attend_backward(first_row, *operands, grads)
        flat = jnp.concatenate([qkv_grad[0], qkv_grad[1], qkv_grad[2]], 1)
        blocks = blocks_of(qkv_grad, 2, half // GROUP)
        return [qkv_grad, flat, swap(flat), *blocks]

    qkv_grad, flat, flat_theirs, *qkv_right = segment(to_qkv, attn_grad, out_weight, first_row, queries, keys, values)
    qkv_grad, up_right, come, sums = lax.optimization_barrier((qkv_grad, up_right, come, sums))
    sums[0] += come
    (passed,) = middle_hop.send([(sums[0], middle_moves)])
    up_left = gather_group(normed_two_half)

    def to_input(flat, theirs, qkv_weight, tables):
        grads = times_back(flat, qkv_weight, tables[0], qkv_block, 512)
        return [times_back(theirs, qkv_weight, tables[1], qkv_block, 512, grads, True)]

    (grads,) = segment(
        to_input, hold(flat, qkv_grad), flat_theirs, qkv_weight,
        (qkv_table(core), qkv_table(other)),
    )
    grads, up_left, passed = lax.optimization_barrier((grads, up_left, passed))
    sums[0] += passed
    qkv_right = exchange(qkv_right)
    value = hold(rows_product(down_left, down_right, quarter, 1, 1), grads)
    come = first_hop.send([(value, inward)])
    passed, come, qkv_right = lax.optimization_barrier(
        (last_hop.send([(sums[0], outward)]), come, qkv_right)
    )
    sums[0] = jnp.where(end, passed[0], sums[0])
    sums.append(value + come[0])
    for part_index in range(2, 4):
        sums.append(line_start(rows_product(down_left, down_right, quarter, part_index, 1)))

    def to_ends(grads, hidden, gain, middle_grad, core_number, inner_low, down_weight):
        results = by_rows(
            norm_one_back_kernel,
            core_number,
            [(full, LOW), (line, F32), (line, F32)],
            hidden,
            gain,
            grads,
            swap(grads[rows:]),
            middle_grad,
        )
        down_part = dot(inner_low, down_weight, 1, 0)
        return [*results, down_part[:rows], swap(down_part[rows:])]

    input_grad, gain_one_grad, shift_one_grad, mine, theirs = to_ends(
        hold(grads, sums[0]), hidden[0], attn_gain[None], middle_grad, core_number,
        inner_low, down_weight,
    )
    output = middle + active * (mine + theirs + down_bias)

    def widen(value):
        none = jnp.zeros_like(value)
        return jnp.where(
            core == 0, jnp.concatenate([value, none]), jnp.concatenate([none, value])
        )

    qkv_sums = jnp.sum(qkv_grad.astype(F32), axis=1)
    small = jnp.concatenate(
        [
            widen(qkv_sums[0]),
            widen(qkv_sums[2]),
            attn_sums[0],
            widen(up_sums[0]),
            down_sums[0],
            gain_one_grad[0],
            shift_one_grad[0],
            gain_two_grad[0],
            shift_two_grad[0],
        ]
    ).reshape(-1, 128)
    small = small + swap(small)
    distance = 1
    while distance < plane:
        small = small + lax.ppermute(small, "dp", in_plane(distance))
        distance *= 2
    small = small + lax.ppermute(small, "dp", inward)
    small = small + lax.ppermute(small, "dp", middle_moves)
    small_last = lax.ppermute(small, "dp", outward)
    small = jnp.where(end, small_last, small).reshape(-1)
    small_grads = []
    first = 0
    for size in (width, width, width, inner, width, width, width, width, width):
        small_grads.append(small[first : first + size])
        first += size

    chunks = [("down", value, index) for index, value in enumerate(sums)]
    size = inner_half // GROUP
    block = min(512, size)
    value = rows_product(up_left, up_right, block, 0, size // block)
    chunks.append(("up", line_start(value), core))
    theirs = [swap(r) for r in up_right]
    value = rows_product(up_left, theirs, block, 0, size // block, True)
    chunks.append(("up", line_start(value), other))
    size = half // GROUP
    value = rows_product(qkv_left, qkv_right, size, 0, 3)
    chunks.append(("qkv", line_start(value), core))
    theirs = [swap(r) for r in qkv_right]
    value = rows_product(qkv_left, theirs, size, 0, 3, True)
    chunks.append(("qkv", line_start(value), other))
    chunks.append(("out", None, 0))

    wholes = {
        "down": blank((inner_half, width)),
        "up": blank((half, inner)),
        "out": blank((half, width)),
        "qkv": blank((half, 3 * width)),
    }
    done = [(), ()]
    for index, (name, value, where) in enumerate(chunks):
        if name == "out":
            right = pairs(out_right, [swap(r) for r in out_right])
            value = line_start(rows_product(out_left, right, width // GROUP, 0, 1))
        after = done[-2], small_last if index == 2 else ()
        if index > 0:
            value = line_middle(value)
        if plane == GROUP and name in LATE:
            pieces = spread_late(value, after)
        else:
            value = blocks_sum(line_end(value) if index > 0 else value)
            pieces = spread(value, after)
        if index == 1:
            out_right = scatter_group(attn_grad, 1, width // GROUP)
            out_left = gather_group(attended)
        tall, wide = value.shape
        high = min(256, tall)
        broad = wide // 3 if name == "qkv" else wide
        places = []
        for d in range(GROUP):
            owner = spot ^ d
            for i in range(tall // high):
                row = jnp.int32(i)
                if name == "down":
                    row, columns = owner * (tall // high) + i, [jnp.int32(where)]
                elif name == "up":
                    columns = [where * GROUP + owner]
                elif name == "out":
                    columns = [owner]
                else:
                    columns = [(2 * p + where) * GROUP + owner for p in range(3)]
                for column in columns:
                    places += [row, column]
        wholes[name] = place(pieces, wholes[name], places, high, broad)
        done.append(wholes[name])

    return (
        output.astype(LOW)[None],
        input_grad[None],
        wholes["qkv"],
        wholes["out"],
        wholes["up"],
        wholes["down"],
        *small_grads,
    )


def solution(mesh):
    return jax.shard_map(
        per_device,
        mesh=mesh,
        in_specs=(
            P("dp", "sp", None),
            P("dp", "sp", None),
            P("dp", None),
            P("sp", None),
            P("sp", None),
            P("sp", None),
            P("sp", None),
            P(),
            P(),
            P(),
            P(),
            P(),
            P(),
            P(),
            P(),
            P(),
        ),
        out_specs=(
            P("dp", "sp", None),
            P("dp", "sp", None),
            P("sp", None),
            P("sp", None),
            P("sp", None),
            P("sp", None),
            P(),
            P(),
            P(),
            P(),
            P(),
            P(),
            P(),
            P(),
            P(),
        ),
        check_vma=False,
    )
```

```python
import functools

import jax
import jax.numpy as jnp
from jax import lax
from jax.experimental import pallas as pl
from jax.experimental.pallas import tpu as pltpu
from jax.sharding import PartitionSpec as P

HEAD_DIM = 64
TILE = 128
LAYER = 12
LINE = 4
STREAMS = 1
LATE = ()
GROUP = 4
F32 = jnp.float32
LOW = jnp.bfloat16


def layer_norm(values, gain, shift):
    center = jnp.mean(values, axis=-1, keepdims=True)
    centered = values - center
    variance = jnp.mean(centered * centered, axis=-1, keepdims=True)
    return centered * lax.rsqrt(variance + 1e-05) * gain + shift


def active_rows(bounds, first_row, row_count, sequence_length):
    position = first_row + jnp.arange(row_count, dtype=jnp.int32)
    tile_start = position // TILE * TILE
    exit_layer = bounds[1] - (bounds[1] - bounds[0]) * tile_start // sequence_length
    return (exit_layer > LAYER).astype(F32)[:, None]


def gelu_and_slope(values):
    scale = (2.0 / jnp.pi) ** 0.5
    square = values * values
    bend = jnp.tanh(scale * values * (1.0 + 0.044715 * square))
    rise = 0.5 * (1.0 + bend)
    slope = rise + 0.5 * values * (1.0 - bend * bend) * scale * (1.0 + 0.134145 * square)
    return values * rise, slope


def dot(left, right, left_dim, right_dim):
    return lax.dot_general(
        left, right, (((left_dim,), (right_dim,)), ((), ())), preferred_element_type=F32
    )


def roll_rows(value):
    rows = value.shape[0] // 2
    return jnp.concatenate([value[rows:], value[:rows]])


def estimate(flops, size):
    return pl.CostEstimate(flops=flops // 4, bytes_accessed=size // 4, transcendentals=0)


def far(value):
    return pltpu.with_memory_space_constraint(value, pltpu.HBM)


def limit(mebibytes):
    return pltpu.CompilerParams(vmem_limit_bytes=mebibytes << 20)


def halves(core_ref, values, mine_ref, theirs_ref):
    width = mine_ref.shape[1]
    first = core_ref[0] == 0
    low, high = values[:, :width], values[:, width:]
    mine_ref[...] = jnp.where(first, low, high).astype(LOW)
    theirs_ref[...] = jnp.where(first, high, low).astype(LOW)


def norm_one_kernel(
    core_ref, x_ref, gain_ref, shift_ref, grad_ref, active_ref,
    mine_ref, theirs_ref, masked_ref, sum_ref,
):
    normed = layer_norm(x_ref[...].astype(F32), gain_ref[...], shift_ref[...])
    halves(core_ref, normed, mine_ref, theirs_ref)
    masked = active_ref[...] * grad_ref[...].astype(F32)
    masked_ref[...] = masked.astype(LOW)
    sum_ref[...] = jnp.sum(masked, axis=0, keepdims=True)


def norm_two_kernel(
    core_ref, x_ref, active_ref, part_ref, theirs_part_ref, bias_ref, gain_ref, shift_ref,
    middle_ref, mine_ref, theirs_ref,
):
    rows = x_ref.shape[0]
    attn = part_ref[:rows] + theirs_part_ref[...] + bias_ref[...]
    middle = x_ref[...].astype(F32) + active_ref[...] * attn
    middle_ref[...] = middle
    halves(core_ref, layer_norm(middle, gain_ref[...], shift_ref[...]), mine_ref, theirs_ref)


def norm_back(core_ref, value_ref, gain_ref, mine_ref, theirs_ref, gain_out_ref, shift_out_ref):
    values = value_ref[...].astype(F32)
    mine, theirs = mine_ref[: values.shape[0]], theirs_ref[...]
    grads = jnp.where(
        core_ref[0] == 0,
        jnp.concatenate([mine, theirs], 1),
        jnp.concatenate([theirs, mine], 1),
    )
    centered = values - jnp.mean(values, axis=-1, keepdims=True)
    scale = lax.rsqrt(jnp.mean(centered * centered, axis=-1, keepdims=True) + 1e-05)
    unit = centered * scale
    gain_out_ref[...] = jnp.sum(grads * unit, axis=0, keepdims=True)
    shift_out_ref[...] = jnp.sum(grads, axis=0, keepdims=True)
    grads = grads * gain_ref[...]
    inner = jnp.mean(grads * unit, axis=-1, keepdims=True)
    return scale * (grads - jnp.mean(grads, axis=-1, keepdims=True) - unit * inner)


def norm_two_back_kernel(
    core_ref, value_ref, gain_ref, mine_ref, theirs_ref, grad_ref, active_ref,
    total_ref, masked_ref, sum_ref, gain_out_ref, shift_out_ref,
):
    part = norm_back(
        core_ref, value_ref, gain_ref, mine_ref, theirs_ref, gain_out_ref, shift_out_ref
    )
    total = grad_ref[...].astype(F32) + part
    total_ref[...] = total
    masked = (active_ref[...] * total).astype(LOW)
    masked_ref[...] = masked
    sum_ref[...] = jnp.sum(masked.astype(F32), axis=0, keepdims=True)


def norm_one_back_kernel(
    core_ref, value_ref, gain_ref, mine_ref, theirs_ref, grad_ref,
    total_ref, gain_out_ref, shift_out_ref,
):
    part = norm_back(
        core_ref, value_ref, gain_ref, mine_ref, theirs_ref, gain_out_ref, shift_out_ref
    )
    total_ref[...] = (grad_ref[...].astype(F32) + part).astype(LOW)


def by_rows(kernel, core, outs, *operands):
    vmem = pl.BlockSpec(memory_space=pltpu.VMEM)
    return pl.pallas_call(
        kernel,
        in_specs=[pl.BlockSpec(memory_space=pltpu.SMEM)] + [vmem] * len(operands),
        out_specs=[vmem] * len(outs),
        out_shape=[jax.ShapeDtypeStruct(shape, dtype) for shape, dtype in outs],
        compiler_params=limit(24),
        cost_estimate=estimate(
            20 * operands[0].size, sum(o.size * o.dtype.itemsize for o in operands)
        ),
    )(core, *operands)


def product_kernel(count, turned, *refs):
    lefts, out_ref, left_turned, right = refs[:count], refs[-3], refs[-2], refs[-1]
    rights = refs[count:-3]
    length = lefts[0].shape[0]

    @pl.when(pl.program_id(0) == 0)
    def _():
        for d, left in enumerate(lefts):
            left_turned[:, d * length : (d + 1) * length] = left[...].T

    row = 0
    for piece in rights:
        value = piece[0] if len(piece.shape) == 3 else piece[...]
        if turned:
            value = roll_rows(value)
        right[row : row + value.shape[0]] = value
        row += value.shape[0]
    out_ref[...] = dot(left_turned[...], right[...], 1, 0).astype(LOW)


def rows_product(lefts, rights, tall, block, steps, turned=False):
    length = lefts[0][0].shape[0]
    left_specs = [
        pl.BlockSpec((length, tall), functools.partial(lambda c, j: (0, c), c)) for _, c in lefts
    ]
    right_specs = [pl.BlockSpec(shape, place) for _, shape, place in rights]
    total = length * len(lefts)
    return pl.pallas_call(
        functools.partial(product_kernel, len(lefts), turned),
        grid=(steps,),
        in_specs=left_specs + right_specs,
        out_specs=pl.BlockSpec((tall, block), lambda j: (0, j)),
        out_shape=jax.ShapeDtypeStruct((tall, steps * block), LOW),
        scratch_shapes=[pltpu.VMEM((tall, total), LOW), pltpu.VMEM((total, block), LOW)],
        compiler_params=limit(32),
        cost_estimate=estimate(
            2 * tall * total * steps * block, 2 * total * (tall + steps * block)
        ),
    )(*[left[0] for left in lefts], *[right[0] for right in rights])


def columns_from(value, rows, row, first, block):
    return value, (rows, block), lambda j: (row, first + j)


def hold(values, after):
    return lax.optimization_barrier((values, after))[0]


def columns_kernel(table_ref, left_ref, *refs):
    total, first = 0.0, 0
    for weight_ref in refs[:-1]:
        depth = weight_ref.shape[0]
        total += dot(left_ref[:, first : first + depth], weight_ref[...], 1, 0)
        first += depth
    refs[-1][...] = total.astype(refs[-1].dtype)


def times_columns(left, weight, table, block, dtype):
    rows, depth = left.shape
    steps = table.shape[0]
    return pl.pallas_call(
        columns_kernel,
        grid_spec=pltpu.PrefetchScalarGridSpec(
            num_scalar_prefetch=1,
            grid=(steps,),
            in_specs=[
                pl.BlockSpec((rows, depth), lambda i, t: (0, 0)),
                *[
                    pl.BlockSpec(
                        (depth // STREAMS, block),
                        functools.partial(lambda r, i, t: (r, t[i]), r),
                    )
                    for r in range(STREAMS)
                ],
            ],
            out_specs=pl.BlockSpec((rows, block), lambda i, t: (0, i)),
        ),
        out_shape=jax.ShapeDtypeStruct((rows, steps * block), dtype),
        compiler_params=limit(24),
        cost_estimate=estimate(2 * rows * depth * steps * block, 2 * depth * (rows + steps * block) + 4 * rows * steps * block),
    )(table, left, *[far(weight)] * STREAMS)


def back_kernel(turned, table_ref, left_ref, *refs):
    weights, out_ref = refs[:STREAMS], refs[-1]
    starts = refs[STREAMS:-1]
    left = left_ref[...]
    if turned:
        left = roll_rows(left)
    first = 0
    for weight_ref in weights:
        deep = weight_ref.shape[0]
        part = dot(left, weight_ref[...], 1, 1)
        columns = slice(first, first + deep)
        first += deep

        @pl.when(pl.program_id(1) == 0)
        def _(part=part, columns=columns):
            out_ref[:, columns] = part + starts[0][:, columns] if starts else part

        @pl.when(pl.program_id(1) > 0)
        def _(part=part, columns=columns):
            out_ref[:, columns] += part


def times_back(left, weight, table, block, deep, start=None, turned=False):
    rows = left.shape[0]
    depth = weight.shape[0]
    steps = table.shape[0]
    out_spec = pl.BlockSpec((rows, deep), lambda k, i, t: (0, k))
    in_specs = [
        pl.BlockSpec((rows, block), lambda k, i, t: (0, i)),
        *[
            pl.BlockSpec(
                (deep // STREAMS, block),
                functools.partial(lambda r, k, i, t: (k * STREAMS + r, t[i]), r),
            )
            for r in range(STREAMS)
        ],
    ]
    operands = [table, left, *[far(weight)] * STREAMS]
    if start is not None:
        in_specs.append(out_spec)
        operands.append(start)
    return pl.pallas_call(
        functools.partial(back_kernel, turned),
        grid_spec=pltpu.PrefetchScalarGridSpec(
            num_scalar_prefetch=1,
            grid=(depth // deep, steps),
            in_specs=in_specs,
            out_specs=out_spec,
        ),
        out_shape=jax.ShapeDtypeStruct((rows, depth), F32),
        compiler_params=limit(32),
        cost_estimate=estimate(2 * rows * depth * steps * block, 2 * steps * block * (rows + depth) + 8 * rows * depth),
    )(*operands)


def inner_kernel(grad_ref, *refs):
    weights = refs[:STREAMS]
    mine_ref, theirs_ref, bias_ref, act_ref, out_ref, sum_ref = refs[STREAMS:]
    first = 0
    for weight_ref in weights:
        columns = slice(first, first + weight_ref.shape[0])
        first += weight_ref.shape[0]
        theirs = roll_rows(theirs_ref[:, columns])
        act, slope = gelu_and_slope(mine_ref[:, columns] + theirs + bias_ref[:, columns])
        act_ref[:, columns] = act.astype(LOW)
        grad = (dot(grad_ref[...], weight_ref[...], 1, 1) * slope).astype(LOW)
        out_ref[:, columns] = grad
        sum_ref[:, columns] = jnp.sum(grad.astype(F32), axis=0, keepdims=True)


def inner_layer(grads, weight, mine, theirs, bias, block):
    rows, width = grads.shape
    hidden = weight.shape[0]
    part = pl.BlockSpec((rows, block), lambda i: (0, i))
    line = pl.BlockSpec((1, block), lambda i: (0, i))
    return pl.pallas_call(
        inner_kernel,
        grid=(hidden // block,),
        in_specs=[
            pl.BlockSpec((rows, width), lambda i: (0, 0)),
            *[
                pl.BlockSpec(
                    (block // STREAMS, width),
                    functools.partial(lambda r, i: (i * STREAMS + r, 0), r),
                )
                for r in range(STREAMS)
            ],
            part,
            part,
            line,
        ],
        out_specs=[part, part, line],
        out_shape=[
            jax.ShapeDtypeStruct((rows, hidden), LOW),
            jax.ShapeDtypeStruct((rows, hidden), LOW),
            jax.ShapeDtypeStruct((1, hidden), F32),
        ],
        compiler_params=limit(32),
        cost_estimate=estimate(2 * rows * width * hidden, 2 * width * (rows + hidden) + 12 * rows * hidden),
    )(grads, *[far(weight)] * STREAMS, mine, theirs, bias)


def head_chances(queries, keys, lanes_of_head, allowed):
    keys_of_head = jnp.where(lanes_of_head, keys, jnp.zeros_like(keys))
    scores = dot(queries, keys_of_head, 1, 1) * (HEAD_DIM**-0.5)
    scores = jnp.where(allowed, scores, -1e30)
    raised = jnp.exp(scores - jnp.max(scores, axis=-1, keepdims=True))
    return raised / jnp.sum(raised, axis=-1, keepdims=True)


def attend_masks(first, length, lanes):
    lane = lax.broadcasted_iota(jnp.int32, (length, lanes), 1)
    row = lax.broadcasted_iota(jnp.int32, (length, length), 0) + first
    column = lax.broadcasted_iota(jnp.int32, (length, length), 1) + first
    row = jnp.where(row >= length, row - length, row)
    column = jnp.where(column >= length, column - length, column)
    return lane, column <= row


def attend_forward_kernel(first_ref, *refs):
    mine, theirs, biases, lows, o_ref = refs[:3], refs[3:6], refs[6:9], refs[9:12], refs[12]
    sums = [
        (m[...] + roll_rows(t[...]) + b[...]).astype(LOW)
        for m, t, b in zip(mine, theirs, biases)
    ]
    for low, value in zip(lows, sums):
        low[...] = value
    queries, keys, values = sums
    lane, allowed = attend_masks(first_ref[0], *queries.shape)
    total = jnp.zeros(queries.shape, F32)
    for head in range(queries.shape[1] // HEAD_DIM):
        own = lane // HEAD_DIM == head
        chances = head_chances(queries, keys, own, allowed).astype(LOW)
        total += dot(chances, jnp.where(own, values, jnp.zeros_like(values)), 1, 0)
    o_ref[...] = total.astype(LOW)


def attend_forward(first, mine, theirs, bias):
    length, width = mine.shape
    width //= 3
    steps = width // 128
    parts = [
        pl.BlockSpec((length, 128), functools.partial(lambda p, i, t: (0, p * steps + i), p))
        for p in range(3)
    ]
    lines = [
        pl.BlockSpec((1, 128), functools.partial(lambda p, i, t: (0, p * steps + i), p))
        for p in range(3)
    ]
    return pl.pallas_call(
        attend_forward_kernel,
        grid_spec=pltpu.PrefetchScalarGridSpec(
            num_scalar_prefetch=1,
            grid=(steps,),
            in_specs=parts + parts + lines,
            out_specs=[parts[0]] * 4,
        ),
        out_shape=[jax.ShapeDtypeStruct((length, width), LOW)] * 4,
        compiler_params=limit(16),
        cost_estimate=estimate(4 * length * length * width, 32 * length * width),
    )(first, mine, mine, mine, theirs, theirs, theirs, bias, bias, bias)


def attend_backward_kernel(first_ref, q_ref, k_ref, v_ref, g_ref, out_ref):
    queries, keys, values, grads = q_ref[...], k_ref[...], v_ref[...], g_ref[...]
    lane, allowed = attend_masks(first_ref[0], *queries.shape)
    dq = jnp.zeros(queries.shape, F32)
    dk = jnp.zeros(queries.shape, F32)
    dv = jnp.zeros(queries.shape, F32)
    for head in range(queries.shape[1] // HEAD_DIM):
        own = lane // HEAD_DIM == head
        chances = head_chances(queries, keys, own, allowed)
        head_grads = jnp.where(own, grads, jnp.zeros_like(grads))
        dv += dot(chances.astype(LOW), head_grads, 0, 0)
        chance_grads = dot(head_grads, values, 1, 1)
        inner = jnp.sum(chances * chance_grads, axis=-1, keepdims=True)
        score_grads = (chances * (chance_grads - inner)).astype(LOW)
        dq += dot(score_grads, jnp.where(own, keys, jnp.zeros_like(keys)), 1, 0)
        dk += dot(score_grads, jnp.where(own, queries, jnp.zeros_like(queries)), 0, 0)
    scale = HEAD_DIM**-0.5
    out_ref[0] = (dq * scale).astype(LOW)
    out_ref[1] = (dk * scale).astype(LOW)
    out_ref[2] = dv.astype(LOW)


def attend_backward(first, *operands):
    length, width = operands[0].shape
    block = pl.BlockSpec((length, 128), lambda i, t: (0, i))
    return pl.pallas_call(
        attend_backward_kernel,
        grid_spec=pltpu.PrefetchScalarGridSpec(
            num_scalar_prefetch=1,
            grid=(width // 128,),
            in_specs=[block] * 4,
            out_specs=pl.BlockSpec((3, length, 128), lambda i, t: (0, 0, i)),
        ),
        out_shape=jax.ShapeDtypeStruct((3, length, width), LOW),
        compiler_params=limit(16),
        cost_estimate=estimate(10 * length * length * width, 14 * length * width),
    )(first, *operands)


def place_kernel(high, table_ref, *refs):
    count = len(refs) - 4
    pieces, out_ref, held, sems = refs[:count], refs[-3], refs[-2], refs[-1]
    slots, broad = held.shape[0], held.shape[2]

    def copy(step):
        row = pl.multiple_of(table_ref[2 * step] * high, high)
        column = pl.multiple_of(table_ref[2 * step + 1] * broad, broad)
        return pltpu.make_async_copy(
            held.at[step % slots],
            out_ref.at[pl.ds(row, high), pl.ds(column, broad)],
            sems.at[step % slots],
        )

    step = 0
    for piece in pieces:
        for i in range(piece.shape[0] // high):
            for j in range(piece.shape[1] // broad):
                if step >= slots:
                    copy(step - slots).wait()
                part = piece[i * high : (i + 1) * high, j * broad : (j + 1) * broad]
                held[step % slots] = part.astype(F32)
                copy(step).start()
                step += 1
    for waited in range(max(step - slots, 0), step):
        copy(waited).wait()


def place(pieces, whole, places, high, broad):
    slots = 4
    vmem = pl.BlockSpec(memory_space=pltpu.VMEM)
    return pl.pallas_call(
        functools.partial(place_kernel, high),
        in_specs=[pl.BlockSpec(memory_space=pltpu.SMEM)]
        + [vmem] * len(pieces)
        + [pl.BlockSpec(memory_space=pl.ANY)],
        out_specs=pl.BlockSpec(memory_space=pl.ANY),
        out_shape=jax.ShapeDtypeStruct(whole.shape, F32),
        scratch_shapes=[
            pltpu.VMEM((slots, high, broad), F32),
            pltpu.SemaphoreType.DMA((slots,)),
        ],
        input_output_aliases={len(pieces) + 1: 0},
        compiler_params=limit(32),
        cost_estimate=estimate(0, sum(6 * p.size for p in pieces)),
    )(jnp.stack(places).astype(jnp.int32), *pieces, whole)


def blank_kernel(out_ref):
    pass


def blank(shape, dtype=F32):
    return pl.pallas_call(
        blank_kernel,
        out_specs=pl.BlockSpec(memory_space=pl.ANY),
        out_shape=jax.ShapeDtypeStruct(shape, dtype),
    )()


class Lane:
    def __init__(self):
        self.last = ()

    def send(self, sends, after=()):
        values = hold([v for v, _ in sends], (self.last, after))
        self.last = [lax.ppermute(v, "dp", m) for v, (_, m) in zip(values, sends)]
        return self.last


def per_device(
    hidden,
    cotangent,
    exit_layers,
    qkv_weight,
    out_weight,
    up_weight,
    down_weight,
    query_bias,
    value_bias,
    out_bias,
    up_bias,
    down_bias,
    attn_gain,
    attn_shift,
    ffn_gain,
    ffn_shift,
):
    core = lax.axis_index("sp")
    other = 1 - core
    chips = lax.axis_size("dp")
    plane = chips // LINE
    chip = lax.axis_index("dp")
    spot = chip % GROUP
    level = chip // plane
    rows = hidden.shape[1]
    width = hidden.shape[2]
    length = 2 * rows
    half = width // 2
    inner = up_weight.shape[1]
    inner_half = inner // 2
    across, middle_across, first_hop, middle_hop, last_hop = (Lane() for _ in range(5))

    def swap(value):
        return lax.ppermute(value, "sp", [(0, 1), (1, 0)])

    def in_plane(distance):
        return [(i, i // plane * plane + ((i % plane) ^ distance)) for i in range(chips)]

    def along(*moves):
        return [(a * plane + i, b * plane + i) for a, b in moves for i in range(plane)]

    inward, middle_moves, outward = (
        along((0, 1), (3, 2)),
        along((1, 2), (2, 1)),
        along((1, 0), (2, 3)),
    )

    def split(value, axis, size):
        return (
            lax.dynamic_slice_in_dim(value, core * size, size, axis),
            lax.dynamic_slice_in_dim(value, other * size, size, axis),
        )

    def exchange(blocks):
        return blocks[:1] + across.send([(blocks[d], in_plane(d)) for d in range(1, GROUP)])

    def gather_group(value):
        return exchange([value] * GROUP)

    def blocks_of(value, axis, size):
        return [
            lax.dynamic_slice_in_dim(value, (spot ^ d) * size, size, axis) for d in range(GROUP)
        ]

    def scatter_group(value, axis, size):
        return exchange(blocks_of(value, axis, size))

    end = (level == 0) | (level == LINE - 1)

    def line_start(value, after=()):
        return value + hold(first_hop.send([(value, inward)])[0], after)

    def line_middle(value):
        return value + middle_hop.send([(value, middle_moves)])[0]

    def line_end(value):
        return jnp.where(end, last_hop.send([(value, outward)])[0], value)

    def blocks_sum(value):
        distance = GROUP
        while distance < plane:
            value = value + lax.ppermute(value, "dp", in_plane(distance))
            distance *= 2
        return value

    def spread(value, after):
        size = value.shape[0] // 2
        first, second = across.send([(value, in_plane(1)), (value, in_plane(2))], after[0])
        upper, lower = across.send(
            [(first[:size], in_plane(2)), (second[size:], in_plane(1))], after[1]
        )
        return [value, first, second, upper, lower]

    def spread_late(value, after):
        size = value.shape[0] // 2

        def middle_only(distance):
            return [(a, b) for a, b in in_plane(distance) if 0 < a // plane < LINE - 1]

        near = middle_across.send(
            [(value[:size], middle_only(1)), (value[size:], middle_only(2))]
        )
        own = line_end(value)
        first = across.send([(own[:size], in_plane(2)), (own[size:], in_plane(1))], after[0])
        near_ends = last_hop.send([(v, outward) for v in near])
        near = [jnp.where(end, e, v) for e, v in zip(near_ends, near)]
        second = across.send([(near[0], in_plane(2)), (near[1], in_plane(1))], after[1])
        return [own, near[0], first[1], first[0], near[1], *second]

    def table(size, start, count=None):
        return jnp.arange(size if count is None else count, dtype=jnp.int32) + start

    active = active_rows(exit_layers[0], core * rows, rows, length)
    core_number = core.astype(jnp.int32)[None]
    first_row = (core * rows).astype(jnp.int32)[None]
    full, part, line = (rows, width), (rows, half), (1, width)

    always = exit_layers[0, 1] > 0

    def segment(steps, *operands):
        def skip(*_):
            return [blank(shape.shape, shape.dtype) for shape in jax.eval_shape(steps, *operands)]

        return lax.cond(always, lambda *o: list(steps(*o)), skip, *operands)

    mine, theirs, down_grad, down_sums = by_rows(
        norm_one_kernel,
        core_number,
        [(part, LOW), (part, LOW), (full, LOW), (line, F32)],
        hidden[0],
        attn_gain[None],
        attn_shift[None],
        cotangent[0],
        active,
    )
    down_mine = gather_group(down_grad)
    qkv_block = min(1024, half)
    qkv_count = half // qkv_block
    bias = jnp.stack([query_bias, jnp.zeros_like(query_bias), value_bias])
    bias = lax.dynamic_slice_in_dim(bias, core * half, half, 1).reshape(1, -1)

    def qkv_table(c):
        return jnp.concatenate(
            [table(qkv_count, (2 * p + c) * qkv_count) for p in range(3)]
        )

    def to_attended(mine, theirs, down_grad, qkv_weight, bias, my_table, their_table, first_row):
        normed = jnp.concatenate([mine, swap(theirs)])
        theirs = times_columns(normed, qkv_weight, their_table, qkv_block, LOW)
        theirs = swap(theirs)
        mine = times_columns(normed, qkv_weight, my_table, qkv_block, F32)
        results = attend_forward(first_row, mine, theirs, bias)
        both = jnp.concatenate([normed, results[3]], 1)
        return [*results, swap(down_grad), both]

    queries, keys, values, attended, down_grad_theirs, early = segment(
        to_attended, mine, theirs, down_grad, qkv_weight, bias,
        qkv_table(core), qkv_table(other), first_row,
    )
    attended, down_mine = lax.optimization_barrier((attended, down_mine))
    early = gather_group(early)
    block = min(1024, inner_half)
    count = inner_half // block

    def to_inner(
        hidden, active, attended, out_weight, lines, up_weight, tables, core_number,
        grads, down_weight,
    ):
        out_part = dot(attended, out_weight, 1, 0)
        middle, mine, theirs = by_rows(
            norm_two_kernel,
            core_number,
            [(full, F32), (part, LOW), (part, LOW)],
            hidden,
            active,
            out_part,
            swap(out_part[rows:]),
            *lines[:3],
        )
        normed = jnp.concatenate([mine, swap(theirs)])
        theirs = times_columns(normed, up_weight, tables[1], block, LOW)
        theirs = swap(theirs)
        mine = times_columns(normed, up_weight, tables[0], block, F32)
        results = inner_layer(
            grads, down_weight, mine, theirs, lines[3], min(512, inner_half)
        )
        return [middle, normed, *results]

    bias = lax.dynamic_slice_in_dim(up_bias, core * inner_half, inner_half).reshape(1, -1)
    middle, normed_two_half, inner_low, up_grad, up_sums = segment(
        to_inner, hidden[0], active, attended, out_weight,
        (out_bias[None], ffn_gain[None], ffn_shift[None], bias), up_weight,
        (table(count, core * count), table(count, other * count)), core_number,
        jnp.concatenate([down_grad, down_grad_theirs]), down_weight,
    )
    (inner_low, up_grad), early = lax.optimization_barrier(((inner_low, up_grad), early))

    down_left = scatter_group(inner_low, 1, inner_half // GROUP)

    def to_middle(
        up_grad, up_weight, middle, gain, cotangent, active, core_number, down_mine, tables
    ):
        theirs = swap(up_grad)
        grads = times_back(up_grad, up_weight, tables[0], inner_half, 256)
        grads = times_back(theirs, up_weight, tables[1], inner_half, 256, grads, True)
        results = by_rows(
            norm_two_back_kernel,
            core_number,
            [(full, F32), (full, LOW), (line, F32), (line, F32), (line, F32)],
            middle,
            gain,
            grads,
            swap(grads[rows:]),
            cotangent,
            active,
        )
        down_theirs = swap(jnp.concatenate(down_mine[1:]))
        return [*results, down_theirs, *blocks_of(up_grad, 1, inner_half // GROUP)]

    (
        middle_grad, attn_grad, attn_sums, gain_two_grad, shift_two_grad, down_theirs, *up_right
    ) = segment(
        to_middle, up_grad, up_weight, middle, ffn_gain[None], cotangent[0], active,
        core_number, down_mine, (table(1, core), table(1, other)),
    )
    down_theirs = [(down_grad_theirs, 0)] + [(down_theirs, d) for d in range(GROUP - 1)]

    def down_product(first, steps):
        rights = []
        for own, (value, row) in zip(down_mine, down_theirs):
            rights.append(columns_from(own, rows, 0, first, quarter))
            rights.append(columns_from(value, rows, row, first, quarter))
        lefts = [(left, 0) for left in down_left]
        return rows_product(lefts, rights, inner_half // GROUP, quarter, steps)

    quarter = width // 4
    down_left, attn_grad = lax.optimization_barrier((down_left, attn_grad))
    up_right = exchange(up_right)
    sums = [down_product(0, 1)]
    (come,) = first_hop.send([(sums[0], inward)])
    attn_grad, sums[0] = lax.optimization_barrier((attn_grad, sums[0]))

    def to_qkv(attn_grad, out_weight, first_row, *operands):
        grads = jnp.concatenate([attn_grad, swap(attn_grad)])
        grads = dot(grads, out_weight, 1, 1).astype(LOW)
        qkv_grad = attend_backward(first_row, *operands, grads)
        flat = jnp.concatenate([qkv_grad[0], qkv_grad[1], qkv_grad[2]], 1)
        blocks = []
        for wide, block in zip(
            blocks_of(attn_grad, 1, width // GROUP), blocks_of(qkv_grad, 2, half // GROUP)
        ):
            narrow = wide.shape[1] // 2
            wide = jnp.concatenate([wide[:, :narrow], wide[:, narrow:]])
            blocks.append(jnp.concatenate([block, wide[None]]))
        return [qkv_grad, flat, swap(flat), *blocks]

    qkv_grad, flat, flat_theirs, *late = segment(to_qkv, attn_grad, out_weight, first_row, queries, keys, values)
    sums.append(down_product(1, 1))
    qkv_grad, up_right, come, sums = lax.optimization_barrier((qkv_grad, up_right, come, sums))
    sums[0] += come
    (passed,) = middle_hop.send([(sums[0], middle_moves)])
    (come,) = first_hop.send([(sums[1], inward)])
    up_left = gather_group(normed_two_half)

    def to_input(flat, theirs, qkv_weight, tables):
        grads = times_back(flat, qkv_weight, tables[0], qkv_block, 512)
        return [times_back(theirs, qkv_weight, tables[1], qkv_block, 512, grads, True)]

    (grads,) = segment(
        to_input, hold(flat, qkv_grad), flat_theirs, qkv_weight,
        (qkv_table(core), qkv_table(other)),
    )
    grads, up_left, passed, come = lax.optimization_barrier((grads, up_left, passed, come))
    sums[0] += passed
    sums[1] += come
    late = exchange(late)
    value = hold(down_product(2, 1), grads)
    come = first_hop.send([(value, inward)])
    passed, come, late = lax.optimization_barrier(
        (last_hop.send([(sums[0], outward)]), come, late)
    )
    sums[0] = jnp.where(end, passed[0], sums[0])
    sums.append(value + come[0])
    sums.append(line_start(hold(down_product(3, 1), late)))

    def to_ends(grads, hidden, gain, middle_grad, core_number, inner_low, down_weight):
        results = by_rows(
            norm_one_back_kernel,
            core_number,
            [(full, LOW), (line, F32), (line, F32)],
            hidden,
            gain,
            grads,
            swap(grads[rows:]),
            middle_grad,
        )
        down_part = dot(inner_low, down_weight, 1, 0)
        return [*results, down_part[:rows], swap(down_part[rows:])]

    input_grad, gain_one_grad, shift_one_grad, mine, theirs = to_ends(
        hold(grads, sums[0]), hidden[0], attn_gain[None], middle_grad, core_number,
        inner_low, down_weight,
    )
    output = middle + active * (mine + theirs + down_bias)

    def widen(value):
        none = jnp.zeros_like(value)
        return jnp.where(
            core == 0, jnp.concatenate([value, none]), jnp.concatenate([none, value])
        )

    qkv_sums = jnp.sum(qkv_grad.astype(F32), axis=1)
    small = jnp.concatenate(
        [
            widen(qkv_sums[0]),
            widen(qkv_sums[2]),
            attn_sums[0],
            widen(up_sums[0]),
            down_sums[0],
            gain_one_grad[0],
            shift_one_grad[0],
            gain_two_grad[0],
            shift_two_grad[0],
        ]
    ).reshape(-1, 128)
    small = small + swap(small)

    def exchange_sum(value, step, count):
        def from_chip(distance):
            moves = []
            for i in range(chips):
                place = i // step % count
                moves.append((i, i + ((place ^ distance) - place) * step))
            return lax.ppermute(value, "dp", moves)

        others = [value] + [from_chip(d) for d in range(1, count)]
        while len(others) > 1:
            others = [a + b for a, b in zip(others[::2], others[1::2])]
        return others[0]

    small = exchange_sum(small, 1, GROUP)
    distance = GROUP
    while distance < plane:
        small = small + lax.ppermute(small, "dp", in_plane(distance))
        distance *= 2
    small_sum = exchange_sum(small, plane, LINE)
    small = small_sum.reshape(-1)
    small_grads = []
    first = 0
    for size in (width, width, width, inner, width, width, width, width, width):
        small_grads.append(small[first : first + size])
        first += size

    chunks = [("down", value, index) for index, value in enumerate(sums)]
    chunks += [("up", None, 2 * GROUP * core), ("up", None, 2 * GROUP * core + 1)]
    chunks += [("up", None, GROUP * other)]
    chunks += [("qkv", None, core), ("qkv", None, other), ("out", None, 0)]
    up_width = inner_half // GROUP
    up_block = min(512, up_width)

    def to_up(*operands):
        lefts = [(left, 0) for left in operands[:GROUP]]
        mine = operands[GROUP:]
        theirs = swap(jnp.concatenate(mine))
        results = []
        for first in range(inner_half // GROUP // up_block):
            rights = [columns_from(right, length, 0, first, up_block) for right in mine]
            results.append(rows_product(lefts, rights, half, up_block, 1))
        rights = [columns_from(theirs, length, d, 0, up_block) for d in range(GROUP)]
        steps = inner_half // GROUP // up_block
        return [*results, rows_product(lefts, rights, half, up_block, steps, True)]

    rest_block = half // GROUP

    def to_rest(*operands):
        early, mine = operands[:GROUP], operands[GROUP:]
        theirs = swap(jnp.concatenate(mine))

        def part(value, d):
            return value, (1, length, rest_block), lambda j: (4 * d + j, 0, 0)

        def out_part(value, d):
            return value, (1, rows, rest_block), lambda j: (4 * d + 3, j, 0)

        lefts = [(left, 0) for left in early]
        rights = [part(right, 0) for right in mine]
        own = rows_product(lefts, rights, half, rest_block, 3)
        rights = [part(theirs, d) for d in range(GROUP)]
        other_half = rows_product(lefts, rights, half, rest_block, 3, True)
        lefts = [(left, 1) for left in early]
        rights = []
        for d, right in enumerate(mine):
            rights += [out_part(right, 0), out_part(theirs, d)]
        return [own, other_half, rows_product(lefts, rights, half, rest_block, 2)]

    wholes = {
        "down": blank((inner_half, width)),
        "up": blank((half, inner)),
        "out": blank((half, width)),
        "qkv": blank((half, 3 * width)),
    }
    size = inner_half // GROUP
    values = []
    done = [(), ()]
    for index, (name, value, where) in enumerate(chunks):
        if value is None:
            value = values.pop(0)
        if index == 0:
            values = segment(to_up, *hold(up_left, late), *up_right)
        after = done[-2], {0: values, 4: small_sum}.get(index, ())
        if index > 0:
            value = line_middle(value)
        if plane == GROUP and name in LATE:
            pieces = spread_late(value, after)
        else:
            value = blocks_sum(line_end(value) if index > 0 else value)
            pieces = spread(value, after)
        if index == 0:
            values = [line_start(v) for v in values]
        if index == 3:
            rest = segment(to_rest, *hold(early, pieces[1:3]), *late)
            values += [line_start(v) for v in rest]
        tall, wide = value.shape
        high = min(256, tall)
        broad = wide // 3 if name == "qkv" else wide
        places = []
        for d in range(GROUP):
            owner = spot ^ d
            for i in range(tall // high):
                row = jnp.int32(i)
                if name == "down":
                    row, columns = owner * (tall // high) + i, [jnp.int32(where)]
                elif name == "up":
                    columns = [where + owner * (size // wide)]
                elif name == "out":
                    columns = [owner]
                else:
                    columns = [(2 * p + where) * GROUP + owner for p in range(3)]
                for column in columns:
                    places += [row, column]
        wholes[name] = place(pieces, wholes[name], places, high, broad)
        done.append(wholes[name])

    return (
        output.astype(LOW)[None],
        input_grad[None],
        wholes["qkv"],
        wholes["out"],
        wholes["up"],
        wholes["down"],
        *small_grads,
    )


def solution(mesh):
    return jax.shard_map(
        per_device,
        mesh=mesh,
        in_specs=(
            P("dp", "sp", None),
            P("dp", "sp", None),
            P("dp", None),
            P("sp", None),
            P("sp", None),
            P("sp", None),
            P("sp", None),
            P(),
            P(),
            P(),
            P(),
            P(),
            P(),
            P(),
            P(),
            P(),
        ),
        out_specs=(
            P("dp", "sp", None),
            P("dp", "sp", None),
            P("sp", None),
            P("sp", None),
            P("sp", None),
            P("sp", None),
            P(),
            P(),
            P(),
            P(),
            P(),
            P(),
            P(),
            P(),
            P(),
        ),
        check_vma=False,
    )
```

```python
import functools

import jax
import jax.numpy as jnp
from jax import lax
from jax.experimental import pallas as pl
from jax.experimental.pallas import tpu as pltpu
from jax.sharding import PartitionSpec as P

HEAD_DIM = 64
TILE = 128
LAYER = 12
LINE = 4
STREAMS = 1
LATE = ()
GROUP = 4
F32 = jnp.float32
LOW = jnp.bfloat16


def layer_norm(values, gain, shift):
    center = jnp.mean(values, axis=-1, keepdims=True)
    centered = values - center
    variance = jnp.mean(centered * centered, axis=-1, keepdims=True)
    return centered * lax.rsqrt(variance + 1e-05) * gain + shift


def active_rows(bounds, first_row, row_count, sequence_length):
    position = first_row + jnp.arange(row_count, dtype=jnp.int32)
    tile_start = position // TILE * TILE
    exit_layer = bounds[1] - (bounds[1] - bounds[0]) * tile_start // sequence_length
    return (exit_layer > LAYER).astype(F32)[:, None]


def gelu_and_slope(values):
    scale = (2.0 / jnp.pi) ** 0.5
    square = values * values
    bend = jnp.tanh(scale * values * (1.0 + 0.044715 * square))
    rise = 0.5 * (1.0 + bend)
    slope = rise + 0.5 * values * (1.0 - bend * bend) * scale * (1.0 + 0.134145 * square)
    return values * rise, slope


def dot(left, right, left_dim, right_dim):
    return lax.dot_general(
        left, right, (((left_dim,), (right_dim,)), ((), ())), preferred_element_type=F32
    )


def roll_rows(value):
    rows = value.shape[0] // 2
    return jnp.concatenate([value[rows:], value[:rows]])


def estimate(flops, size):
    return pl.CostEstimate(flops=flops // 4, bytes_accessed=size // 4, transcendentals=0)


def far(value):
    return pltpu.with_memory_space_constraint(value, pltpu.HBM)


def limit(mebibytes):
    return pltpu.CompilerParams(vmem_limit_bytes=mebibytes << 20)


def halves(core_ref, values, mine_ref, theirs_ref):
    width = mine_ref.shape[1]
    first = core_ref[0] == 0
    low, high = values[:, :width], values[:, width:]
    mine_ref[...] = jnp.where(first, low, high).astype(LOW)
    theirs_ref[...] = jnp.where(first, high, low).astype(LOW)


def norm_one_kernel(
    core_ref, x_ref, gain_ref, shift_ref, grad_ref, active_ref,
    mine_ref, theirs_ref, masked_ref, sum_ref,
):
    normed = layer_norm(x_ref[...].astype(F32), gain_ref[...], shift_ref[...])
    halves(core_ref, normed, mine_ref, theirs_ref)
    masked = active_ref[...] * grad_ref[...].astype(F32)
    masked_ref[...] = masked.astype(LOW)
    sum_ref[...] = jnp.sum(masked, axis=0, keepdims=True)


def norm_two_kernel(
    core_ref, x_ref, active_ref, part_ref, theirs_part_ref, bias_ref, gain_ref, shift_ref,
    middle_ref, mine_ref, theirs_ref,
):
    rows = x_ref.shape[0]
    attn = part_ref[:rows] + theirs_part_ref[...] + bias_ref[...]
    middle = x_ref[...].astype(F32) + active_ref[...] * attn
    middle_ref[...] = middle
    halves(core_ref, layer_norm(middle, gain_ref[...], shift_ref[...]), mine_ref, theirs_ref)


def norm_back(core_ref, value_ref, gain_ref, mine_ref, theirs_ref, gain_out_ref, shift_out_ref):
    values = value_ref[...].astype(F32)
    mine, theirs = mine_ref[: values.shape[0]], theirs_ref[...]
    grads = jnp.where(
        core_ref[0] == 0,
        jnp.concatenate([mine, theirs], 1),
        jnp.concatenate([theirs, mine], 1),
    )
    centered = values - jnp.mean(values, axis=-1, keepdims=True)
    scale = lax.rsqrt(jnp.mean(centered * centered, axis=-1, keepdims=True) + 1e-05)
    unit = centered * scale
    gain_out_ref[...] = jnp.sum(grads * unit, axis=0, keepdims=True)
    shift_out_ref[...] = jnp.sum(grads, axis=0, keepdims=True)
    grads = grads * gain_ref[...]
    inner = jnp.mean(grads * unit, axis=-1, keepdims=True)
    return scale * (grads - jnp.mean(grads, axis=-1, keepdims=True) - unit * inner)


def norm_two_back_kernel(
    core_ref, value_ref, gain_ref, mine_ref, theirs_ref, grad_ref, active_ref,
    total_ref, masked_ref, sum_ref, gain_out_ref, shift_out_ref,
):
    part = norm_back(
        core_ref, value_ref, gain_ref, mine_ref, theirs_ref, gain_out_ref, shift_out_ref
    )
    total = grad_ref[...].astype(F32) + part
    total_ref[...] = total
    masked = (active_ref[...] * total).astype(LOW)
    masked_ref[...] = masked
    sum_ref[...] = jnp.sum(masked.astype(F32), axis=0, keepdims=True)


def norm_one_back_kernel(
    core_ref, value_ref, gain_ref, mine_ref, theirs_ref, grad_ref,
    total_ref, gain_out_ref, shift_out_ref,
):
    part = norm_back(
        core_ref, value_ref, gain_ref, mine_ref, theirs_ref, gain_out_ref, shift_out_ref
    )
    total_ref[...] = (grad_ref[...].astype(F32) + part).astype(LOW)


def by_rows(kernel, core, outs, *operands):
    vmem = pl.BlockSpec(memory_space=pltpu.VMEM)
    return pl.pallas_call(
        kernel,
        in_specs=[pl.BlockSpec(memory_space=pltpu.SMEM)] + [vmem] * len(operands),
        out_specs=[vmem] * len(outs),
        out_shape=[jax.ShapeDtypeStruct(shape, dtype) for shape, dtype in outs],
        compiler_params=limit(24),
        cost_estimate=estimate(
            20 * operands[0].size, sum(o.size * o.dtype.itemsize for o in operands)
        ),
    )(core, *operands)


def product_kernel(count, turned, *refs):
    lefts, out_ref, left_turned, right = refs[:count], refs[-3], refs[-2], refs[-1]
    rights = refs[count:-3]
    length = lefts[0].shape[0]

    @pl.when(pl.program_id(0) == 0)
    def _():
        for d, left in enumerate(lefts):
            left_turned[:, d * length : (d + 1) * length] = left[...].T

    row = 0
    for piece in rights:
        value = piece[0] if len(piece.shape) == 3 else piece[...]
        if turned:
            value = roll_rows(value)
        right[row : row + value.shape[0]] = value
        row += value.shape[0]
    out_ref[...] = dot(left_turned[...], right[...], 1, 0).astype(LOW)


def rows_product(lefts, rights, tall, block, steps, turned=False):
    length = lefts[0][0].shape[0]
    left_specs = [
        pl.BlockSpec((length, tall), functools.partial(lambda c, j: (0, c), c)) for _, c in lefts
    ]
    right_specs = [pl.BlockSpec(shape, place) for _, shape, place in rights]
    total = length * len(lefts)
    return pl.pallas_call(
        functools.partial(product_kernel, len(lefts), turned),
        grid=(steps,),
        in_specs=left_specs + right_specs,
        out_specs=pl.BlockSpec((tall, block), lambda j: (0, j)),
        out_shape=jax.ShapeDtypeStruct((tall, steps * block), LOW),
        scratch_shapes=[pltpu.VMEM((tall, total), LOW), pltpu.VMEM((total, block), LOW)],
        compiler_params=limit(32),
        cost_estimate=estimate(
            2 * tall * total * steps * block, 2 * total * (tall + steps * block)
        ),
    )(*[left[0] for left in lefts], *[right[0] for right in rights])


def columns_from(value, rows, row, first, block):
    return value, (rows, block), lambda j: (row, first + j)


def hold(values, after):
    return lax.optimization_barrier((values, after))[0]


def columns_kernel(table_ref, left_ref, *refs):
    total, first = 0.0, 0
    for weight_ref in refs[:-1]:
        depth = weight_ref.shape[0]
        total += dot(left_ref[:, first : first + depth], weight_ref[...], 1, 0)
        first += depth
    refs[-1][...] = total.astype(refs[-1].dtype)


def times_columns(left, weight, table, block, dtype):
    rows, depth = left.shape
    steps = table.shape[0]
    return pl.pallas_call(
        columns_kernel,
        grid_spec=pltpu.PrefetchScalarGridSpec(
            num_scalar_prefetch=1,
            grid=(steps,),
            in_specs=[
                pl.BlockSpec((rows, depth), lambda i, t: (0, 0)),
                *[
                    pl.BlockSpec(
                        (depth // STREAMS, block),
                        functools.partial(lambda r, i, t: (r, t[i]), r),
                    )
                    for r in range(STREAMS)
                ],
            ],
            out_specs=pl.BlockSpec((rows, block), lambda i, t: (0, i)),
        ),
        out_shape=jax.ShapeDtypeStruct((rows, steps * block), dtype),
        compiler_params=limit(24),
        cost_estimate=estimate(2 * rows * depth * steps * block, 2 * depth * (rows + steps * block) + 4 * rows * steps * block),
    )(table, left, *[far(weight)] * STREAMS)


def back_kernel(turned, table_ref, left_ref, *refs):
    weights, out_ref = refs[:STREAMS], refs[-1]
    starts = refs[STREAMS:-1]
    left = left_ref[...]
    if turned:
        left = roll_rows(left)
    first = 0
    for weight_ref in weights:
        deep = weight_ref.shape[0]
        part = dot(left, weight_ref[...], 1, 1)
        columns = slice(first, first + deep)
        first += deep

        @pl.when(pl.program_id(1) == 0)
        def _(part=part, columns=columns):
            out_ref[:, columns] = part + starts[0][:, columns] if starts else part

        @pl.when(pl.program_id(1) > 0)
        def _(part=part, columns=columns):
            out_ref[:, columns] += part


def times_back(left, weight, table, block, deep, start=None, turned=False):
    rows = left.shape[0]
    depth = weight.shape[0]
    steps = table.shape[0]
    out_spec = pl.BlockSpec((rows, deep), lambda k, i, t: (0, k))
    in_specs = [
        pl.BlockSpec((rows, block), lambda k, i, t: (0, i)),
        *[
            pl.BlockSpec(
                (deep // STREAMS, block),
                functools.partial(lambda r, k, i, t: (k * STREAMS + r, t[i]), r),
            )
            for r in range(STREAMS)
        ],
    ]
    operands = [table, left, *[far(weight)] * STREAMS]
    if start is not None:
        in_specs.append(out_spec)
        operands.append(start)
    return pl.pallas_call(
        functools.partial(back_kernel, turned),
        grid_spec=pltpu.PrefetchScalarGridSpec(
            num_scalar_prefetch=1,
            grid=(depth // deep, steps),
            in_specs=in_specs,
            out_specs=out_spec,
        ),
        out_shape=jax.ShapeDtypeStruct((rows, depth), F32),
        compiler_params=limit(32),
        cost_estimate=estimate(2 * rows * depth * steps * block, 2 * steps * block * (rows + depth) + 8 * rows * depth),
    )(*operands)


def inner_kernel(grad_ref, *refs):
    weights = refs[:STREAMS]
    mine_ref, theirs_ref, bias_ref, act_ref, out_ref, sum_ref = refs[STREAMS:]
    first = 0
    for weight_ref in weights:
        columns = slice(first, first + weight_ref.shape[0])
        first += weight_ref.shape[0]
        theirs = roll_rows(theirs_ref[:, columns])
        act, slope = gelu_and_slope(mine_ref[:, columns] + theirs + bias_ref[:, columns])
        act_ref[:, columns] = act.astype(LOW)
        grad = (dot(grad_ref[...], weight_ref[...], 1, 1) * slope).astype(LOW)
        out_ref[:, columns] = grad
        sum_ref[:, columns] = jnp.sum(grad.astype(F32), axis=0, keepdims=True)


def inner_layer(grads, weight, mine, theirs, bias, block):
    rows, width = grads.shape
    hidden = weight.shape[0]
    part = pl.BlockSpec((rows, block), lambda i: (0, i))
    line = pl.BlockSpec((1, block), lambda i: (0, i))
    return pl.pallas_call(
        inner_kernel,
        grid=(hidden // block,),
        in_specs=[
            pl.BlockSpec((rows, width), lambda i: (0, 0)),
            *[
                pl.BlockSpec(
                    (block // STREAMS, width),
                    functools.partial(lambda r, i: (i * STREAMS + r, 0), r),
                )
                for r in range(STREAMS)
            ],
            part,
            part,
            line,
        ],
        out_specs=[part, part, line],
        out_shape=[
            jax.ShapeDtypeStruct((rows, hidden), LOW),
            jax.ShapeDtypeStruct((rows, hidden), LOW),
            jax.ShapeDtypeStruct((1, hidden), F32),
        ],
        compiler_params=limit(32),
        cost_estimate=estimate(2 * rows * width * hidden, 2 * width * (rows + hidden) + 12 * rows * hidden),
    )(grads, *[far(weight)] * STREAMS, mine, theirs, bias)


def head_chances(queries, keys, lanes_of_head, allowed):
    keys_of_head = jnp.where(lanes_of_head, keys, jnp.zeros_like(keys))
    scores = dot(queries, keys_of_head, 1, 1) * (HEAD_DIM**-0.5)
    scores = jnp.where(allowed, scores, -1e30)
    raised = jnp.exp(scores - jnp.max(scores, axis=-1, keepdims=True))
    return raised / jnp.sum(raised, axis=-1, keepdims=True)


def attend_masks(first, length, lanes):
    lane = lax.broadcasted_iota(jnp.int32, (length, lanes), 1)
    row = lax.broadcasted_iota(jnp.int32, (length, length), 0) + first
    column = lax.broadcasted_iota(jnp.int32, (length, length), 1) + first
    row = jnp.where(row >= length, row - length, row)
    column = jnp.where(column >= length, column - length, column)
    return lane, column <= row


def attend_forward_kernel(first_ref, *refs):
    mine, theirs, biases, lows, o_ref = refs[:3], refs[3:6], refs[6:9], refs[9:12], refs[12]
    sums = [
        (m[...] + roll_rows(t[...]) + b[...]).astype(LOW)
        for m, t, b in zip(mine, theirs, biases)
    ]
    for low, value in zip(lows, sums):
        low[...] = value
    queries, keys, values = sums
    lane, allowed = attend_masks(first_ref[0], *queries.shape)
    total = jnp.zeros(queries.shape, F32)
    for head in range(queries.shape[1] // HEAD_DIM):
        own = lane // HEAD_DIM == head
        chances = head_chances(queries, keys, own, allowed).astype(LOW)
        total += dot(chances, jnp.where(own, values, jnp.zeros_like(values)), 1, 0)
    o_ref[...] = total.astype(LOW)


def attend_forward(first, mine, theirs, bias):
    length, width = mine.shape
    width //= 3
    steps = width // 128
    parts = [
        pl.BlockSpec((length, 128), functools.partial(lambda p, i, t: (0, p * steps + i), p))
        for p in range(3)
    ]
    lines = [
        pl.BlockSpec((1, 128), functools.partial(lambda p, i, t: (0, p * steps + i), p))
        for p in range(3)
    ]
    return pl.pallas_call(
        attend_forward_kernel,
        grid_spec=pltpu.PrefetchScalarGridSpec(
            num_scalar_prefetch=1,
            grid=(steps,),
            in_specs=parts + parts + lines,
            out_specs=[parts[0]] * 4,
        ),
        out_shape=[jax.ShapeDtypeStruct((length, width), LOW)] * 4,
        compiler_params=limit(16),
        cost_estimate=estimate(4 * length * length * width, 32 * length * width),
    )(first, mine, mine, mine, theirs, theirs, theirs, bias, bias, bias)


def attend_backward_kernel(first_ref, q_ref, k_ref, v_ref, g_ref, out_ref):
    queries, keys, values, grads = q_ref[...], k_ref[...], v_ref[...], g_ref[...]
    lane, allowed = attend_masks(first_ref[0], *queries.shape)
    dq = jnp.zeros(queries.shape, F32)
    dk = jnp.zeros(queries.shape, F32)
    dv = jnp.zeros(queries.shape, F32)
    for head in range(queries.shape[1] // HEAD_DIM):
        own = lane // HEAD_DIM == head
        chances = head_chances(queries, keys, own, allowed)
        head_grads = jnp.where(own, grads, jnp.zeros_like(grads))
        dv += dot(chances.astype(LOW), head_grads, 0, 0)
        chance_grads = dot(head_grads, values, 1, 1)
        inner = jnp.sum(chances * chance_grads, axis=-1, keepdims=True)
        score_grads = (chances * (chance_grads - inner)).astype(LOW)
        dq += dot(score_grads, jnp.where(own, keys, jnp.zeros_like(keys)), 1, 0)
        dk += dot(score_grads, jnp.where(own, queries, jnp.zeros_like(queries)), 0, 0)
    scale = HEAD_DIM**-0.5
    out_ref[0] = (dq * scale).astype(LOW)
    out_ref[1] = (dk * scale).astype(LOW)
    out_ref[2] = dv.astype(LOW)


def attend_backward(first, *operands):
    length, width = operands[0].shape
    block = pl.BlockSpec((length, 128), lambda i, t: (0, i))
    return pl.pallas_call(
        attend_backward_kernel,
        grid_spec=pltpu.PrefetchScalarGridSpec(
            num_scalar_prefetch=1,
            grid=(width // 128,),
            in_specs=[block] * 4,
            out_specs=pl.BlockSpec((3, length, 128), lambda i, t: (0, 0, i)),
        ),
        out_shape=jax.ShapeDtypeStruct((3, length, width), LOW),
        compiler_params=limit(16),
        cost_estimate=estimate(10 * length * length * width, 14 * length * width),
    )(first, *operands)


def place_kernel(high, table_ref, *refs):
    count = len(refs) - 4
    pieces, out_ref, held, sems = refs[:count], refs[-3], refs[-2], refs[-1]
    slots, broad = held.shape[0], held.shape[2]

    def copy(step):
        row = pl.multiple_of(table_ref[2 * step] * high, high)
        column = pl.multiple_of(table_ref[2 * step + 1] * broad, broad)
        return pltpu.make_async_copy(
            held.at[step % slots],
            out_ref.at[pl.ds(row, high), pl.ds(column, broad)],
            sems.at[step % slots],
        )

    step = 0
    for piece in pieces:
        for i in range(piece.shape[0] // high):
            for j in range(piece.shape[1] // broad):
                if step >= slots:
                    copy(step - slots).wait()
                part = piece[i * high : (i + 1) * high, j * broad : (j + 1) * broad]
                held[step % slots] = part.astype(F32)
                copy(step).start()
                step += 1
    for waited in range(max(step - slots, 0), step):
        copy(waited).wait()


def place(pieces, whole, places, high, broad):
    slots = 4
    vmem = pl.BlockSpec(memory_space=pltpu.VMEM)
    return pl.pallas_call(
        functools.partial(place_kernel, high),
        in_specs=[pl.BlockSpec(memory_space=pltpu.SMEM)]
        + [vmem] * len(pieces)
        + [pl.BlockSpec(memory_space=pl.ANY)],
        out_specs=pl.BlockSpec(memory_space=pl.ANY),
        out_shape=jax.ShapeDtypeStruct(whole.shape, F32),
        scratch_shapes=[
            pltpu.VMEM((slots, high, broad), F32),
            pltpu.SemaphoreType.DMA((slots,)),
        ],
        input_output_aliases={len(pieces) + 1: 0},
        compiler_params=limit(32),
        cost_estimate=estimate(0, sum(6 * p.size for p in pieces)),
    )(jnp.stack(places).astype(jnp.int32), *pieces, whole)


def blank_kernel(out_ref):
    pass


def blank(shape, dtype=F32):
    return pl.pallas_call(
        blank_kernel,
        out_specs=pl.BlockSpec(memory_space=pl.ANY),
        out_shape=jax.ShapeDtypeStruct(shape, dtype),
    )()


class Lane:
    def __init__(self):
        self.last = ()

    def send(self, sends, after=()):
        values = hold([v for v, _ in sends], (self.last, after))
        self.last = [lax.ppermute(v, "dp", m) for v, (_, m) in zip(values, sends)]
        return self.last


def per_device(
    hidden,
    cotangent,
    exit_layers,
    qkv_weight,
    out_weight,
    up_weight,
    down_weight,
    query_bias,
    value_bias,
    out_bias,
    up_bias,
    down_bias,
    attn_gain,
    attn_shift,
    ffn_gain,
    ffn_shift,
):
    core = lax.axis_index("sp")
    other = 1 - core
    chips = lax.axis_size("dp")
    plane = chips // LINE
    chip = lax.axis_index("dp")
    spot = chip % GROUP
    level = chip // plane
    rows = hidden.shape[1]
    width = hidden.shape[2]
    length = 2 * rows
    half = width // 2
    inner = up_weight.shape[1]
    inner_half = inner // 2
    across, middle_across, first_hop, middle_hop, last_hop = (Lane() for _ in range(5))

    def swap(value):
        return lax.ppermute(value, "sp", [(0, 1), (1, 0)])

    def in_plane(distance):
        return [(i, i // plane * plane + ((i % plane) ^ distance)) for i in range(chips)]

    def along(*moves):
        return [(a * plane + i, b * plane + i) for a, b in moves for i in range(plane)]

    inward, middle_moves, outward = (
        along((0, 1), (3, 2)),
        along((1, 2), (2, 1)),
        along((1, 0), (2, 3)),
    )

    def split(value, axis, size):
        return (
            lax.dynamic_slice_in_dim(value, core * size, size, axis),
            lax.dynamic_slice_in_dim(value, other * size, size, axis),
        )

    def exchange(blocks):
        return blocks[:1] + across.send([(blocks[d], in_plane(d)) for d in range(1, GROUP)])

    def gather_group(value):
        return exchange([value] * GROUP)

    def blocks_of(value, axis, size):
        return [
            lax.dynamic_slice_in_dim(value, (spot ^ d) * size, size, axis) for d in range(GROUP)
        ]

    def scatter_group(value, axis, size):
        return exchange(blocks_of(value, axis, size))

    end = (level == 0) | (level == LINE - 1)

    def line_start(value, after=()):
        return value + hold(first_hop.send([(value, inward)])[0], after)

    def line_middle(value):
        return value + middle_hop.send([(value, middle_moves)])[0]

    def line_end(value):
        return jnp.where(end, last_hop.send([(value, outward)])[0], value)

    def blocks_sum(value):
        distance = GROUP
        while distance < plane:
            value = value + lax.ppermute(value, "dp", in_plane(distance))
            distance *= 2
        return value

    def spread(value, after):
        size = value.shape[0] // 2
        first, second = across.send([(value, in_plane(1)), (value, in_plane(2))], after[0])
        upper, lower = across.send(
            [(first[:size], in_plane(2)), (second[size:], in_plane(1))], after[1]
        )
        return [value, first, second, upper, lower]

    def spread_late(value, after):
        size = value.shape[0] // 2

        def middle_only(distance):
            return [(a, b) for a, b in in_plane(distance) if 0 < a // plane < LINE - 1]

        near = middle_across.send(
            [(value[:size], middle_only(1)), (value[size:], middle_only(2))]
        )
        own = line_end(value)
        first = across.send([(own[:size], in_plane(2)), (own[size:], in_plane(1))], after[0])
        near_ends = last_hop.send([(v, outward) for v in near])
        near = [jnp.where(end, e, v) for e, v in zip(near_ends, near)]
        second = across.send([(near[0], in_plane(2)), (near[1], in_plane(1))], after[1])
        return [own, near[0], first[1], first[0], near[1], *second]

    def table(size, start, count=None):
        return jnp.arange(size if count is None else count, dtype=jnp.int32) + start

    active = active_rows(exit_layers[0], core * rows, rows, length)
    core_number = core.astype(jnp.int32)[None]
    first_row = (core * rows).astype(jnp.int32)[None]
    full, part, line = (rows, width), (rows, half), (1, width)

    always = exit_layers[0, 1] > 0

    def segment(steps, *operands):
        def skip(*_):
            return [blank(shape.shape, shape.dtype) for shape in jax.eval_shape(steps, *operands)]

        return lax.cond(always, lambda *o: list(steps(*o)), skip, *operands)

    mine, theirs, down_grad, down_sums = by_rows(
        norm_one_kernel,
        core_number,
        [(part, LOW), (part, LOW), (full, LOW), (line, F32)],
        hidden[0],
        attn_gain[None],
        attn_shift[None],
        cotangent[0],
        active,
    )
    down_mine = gather_group(down_grad)
    qkv_block = min(1024, half)
    qkv_count = half // qkv_block
    bias = jnp.stack([query_bias, jnp.zeros_like(query_bias), value_bias])
    bias = lax.dynamic_slice_in_dim(bias, core * half, half, 1).reshape(1, -1)

    def qkv_table(c):
        return jnp.concatenate(
            [table(qkv_count, (2 * p + c) * qkv_count) for p in range(3)]
        )

    def to_attended(mine, theirs, down_grad, qkv_weight, bias, my_table, their_table, first_row):
        normed = jnp.concatenate([mine, swap(theirs)])
        theirs = times_columns(normed, qkv_weight, their_table, qkv_block, LOW)
        theirs = swap(theirs)
        mine = times_columns(normed, qkv_weight, my_table, qkv_block, F32)
        results = attend_forward(first_row, mine, theirs, bias)
        both = jnp.concatenate([normed, results[3]], 1)
        return [*results, swap(down_grad), both]

    queries, keys, values, attended, down_grad_theirs, early = segment(
        to_attended, mine, theirs, down_grad, qkv_weight, bias,
        qkv_table(core), qkv_table(other), first_row,
    )
    attended, down_mine = lax.optimization_barrier((attended, down_mine))
    early = gather_group(early)
    block = min(1024, inner_half)
    count = inner_half // block

    def to_inner(
        hidden, active, attended, out_weight, lines, up_weight, tables, core_number,
        grads, down_weight,
    ):
        out_part = dot(attended, out_weight, 1, 0)
        middle, mine, theirs = by_rows(
            norm_two_kernel,
            core_number,
            [(full, F32), (part, LOW), (part, LOW)],
            hidden,
            active,
            out_part,
            swap(out_part[rows:]),
            *lines[:3],
        )
        normed = jnp.concatenate([mine, swap(theirs)])
        theirs = times_columns(normed, up_weight, tables[1], block, LOW)
        theirs = swap(theirs)
        mine = times_columns(normed, up_weight, tables[0], block, F32)
        results = inner_layer(
            grads, down_weight, mine, theirs, lines[3], min(512, inner_half)
        )
        return [middle, normed, *results]

    bias = lax.dynamic_slice_in_dim(up_bias, core * inner_half, inner_half).reshape(1, -1)
    middle, normed_two_half, inner_low, up_grad, up_sums = segment(
        to_inner, hidden[0], active, attended, out_weight,
        (out_bias[None], ffn_gain[None], ffn_shift[None], bias), up_weight,
        (table(count, core * count), table(count, other * count)), core_number,
        jnp.concatenate([down_grad, down_grad_theirs]), down_weight,
    )
    (inner_low, up_grad), early = lax.optimization_barrier(((inner_low, up_grad), early))

    down_left = scatter_group(inner_low, 1, inner_half // GROUP)

    def to_middle(
        up_grad, up_weight, middle, gain, cotangent, active, core_number, down_mine, tables
    ):
        theirs = swap(up_grad)
        grads = times_back(up_grad, up_weight, tables[0], inner_half, 256)
        grads = times_back(theirs, up_weight, tables[1], inner_half, 256, grads, True)
        results = by_rows(
            norm_two_back_kernel,
            core_number,
            [(full, F32), (full, LOW), (line, F32), (line, F32), (line, F32)],
            middle,
            gain,
            grads,
            swap(grads[rows:]),
            cotangent,
            active,
        )
        down_theirs = swap(jnp.concatenate(down_mine[1:]))
        return [*results, down_theirs, *blocks_of(up_grad, 1, inner_half // GROUP)]

    (
        middle_grad, attn_grad, attn_sums, gain_two_grad, shift_two_grad, down_theirs, *up_right
    ) = segment(
        to_middle, up_grad, up_weight, middle, ffn_gain[None], cotangent[0], active,
        core_number, down_mine, (table(1, core), table(1, other)),
    )
    down_theirs = [(down_grad_theirs, 0)] + [(down_theirs, d) for d in range(GROUP - 1)]

    def down_product(first, steps):
        rights = []
        for own, (value, row) in zip(down_mine, down_theirs):
            rights.append(columns_from(own, rows, 0, first, quarter))
            rights.append(columns_from(value, rows, row, first, quarter))
        lefts = [(left, 0) for left in down_left]
        return rows_product(lefts, rights, inner_half // GROUP, quarter, steps)

    quarter = width // 4
    down_left, attn_grad = lax.optimization_barrier((down_left, attn_grad))
    up_right = exchange(up_right)
    sums = [down_product(0, 1)]
    (come,) = first_hop.send([(sums[0], inward)])
    attn_grad, sums[0] = lax.optimization_barrier((attn_grad, sums[0]))

    def to_qkv(attn_grad, out_weight, first_row, *operands):
        grads = jnp.concatenate([attn_grad, swap(attn_grad)])
        grads = dot(grads, out_weight, 1, 1).astype(LOW)
        qkv_grad = attend_backward(first_row, *operands, grads)
        flat = jnp.concatenate([qkv_grad[0], qkv_grad[1], qkv_grad[2]], 1)
        blocks = []
        for wide, block in zip(
            blocks_of(attn_grad, 1, width // GROUP), blocks_of(qkv_grad, 2, half // GROUP)
        ):
            narrow = wide.shape[1] // 2
            wide = jnp.concatenate([wide[:, :narrow], wide[:, narrow:]])
            blocks.append(jnp.concatenate([block, wide[None]]))
        return [qkv_grad, flat, swap(flat), *blocks]

    qkv_grad, flat, flat_theirs, *late = segment(to_qkv, attn_grad, out_weight, first_row, queries, keys, values)
    sums.append(down_product(1, 1))
    qkv_grad, up_right, come, sums = lax.optimization_barrier((qkv_grad, up_right, come, sums))
    sums[0] += come
    (passed,) = middle_hop.send([(sums[0], middle_moves)])
    (come,) = first_hop.send([(sums[1], inward)])
    up_left = gather_group(normed_two_half)

    def to_input(flat, theirs, qkv_weight, tables):
        grads = times_back(flat, qkv_weight, tables[0], qkv_block, 512)
        return [times_back(theirs, qkv_weight, tables[1], qkv_block, 512, grads, True)]

    (grads,) = segment(
        to_input, hold(flat, qkv_grad), flat_theirs, qkv_weight,
        (qkv_table(core), qkv_table(other)),
    )
    grads, up_left, passed, come = lax.optimization_barrier((grads, up_left, passed, come))
    sums[0] += passed
    sums[1] += come
    late = exchange(late)
    value = hold(down_product(2, 1), grads)
    come = first_hop.send([(value, inward)])
    passed, come, late = lax.optimization_barrier(
        (last_hop.send([(sums[0], outward)]), come, late)
    )
    sums[0] = jnp.where(end, passed[0], sums[0])
    sums.append(value + come[0])
    sums.append(line_start(hold(down_product(3, 1), late)))

    def to_ends(grads, hidden, gain, middle_grad, core_number, inner_low, down_weight):
        results = by_rows(
            norm_one_back_kernel,
            core_number,
            [(full, LOW), (line, F32), (line, F32)],
            hidden,
            gain,
            grads,
            swap(grads[rows:]),
            middle_grad,
        )
        down_part = dot(inner_low, down_weight, 1, 0)
        return [*results, down_part[:rows], swap(down_part[rows:])]

    input_grad, gain_one_grad, shift_one_grad, mine, theirs = to_ends(
        hold(grads, sums[0]), hidden[0], attn_gain[None], middle_grad, core_number,
        inner_low, down_weight,
    )
    output = middle + active * (mine + theirs + down_bias)

    def widen(value):
        none = jnp.zeros_like(value)
        return jnp.where(
            core == 0, jnp.concatenate([value, none]), jnp.concatenate([none, value])
        )

    qkv_sums = jnp.sum(qkv_grad.astype(F32), axis=1)
    small = jnp.concatenate(
        [
            widen(qkv_sums[0]),
            widen(qkv_sums[2]),
            attn_sums[0],
            widen(up_sums[0]),
            down_sums[0],
            gain_one_grad[0],
            shift_one_grad[0],
            gain_two_grad[0],
            shift_two_grad[0],
        ]
    ).reshape(-1, 128)
    small = small + swap(small)

    def exchange_sum(value, step, count):
        def from_chip(distance):
            moves = []
            for i in range(chips):
                place = i // step % count
                moves.append((i, i + ((place ^ distance) - place) * step))
            return lax.ppermute(value, "dp", moves)

        others = [value] + [from_chip(d) for d in range(1, count)]
        while len(others) > 1:
            others = [a + b for a, b in zip(others[::2], others[1::2])]
        return others[0]

    small = exchange_sum(small, 1, GROUP)
    distance = GROUP
    while distance < plane:
        small = small + lax.ppermute(small, "dp", in_plane(distance))
        distance *= 2
    small_sum = exchange_sum(small, plane, LINE)
    small = small_sum.reshape(-1)
    small_grads = []
    first = 0
    for size in (width, width, width, inner, width, width, width, width, width):
        small_grads.append(small[first : first + size])
        first += size

    chunks = [("down", value, index) for index, value in enumerate(sums)]
    chunks += [("up", None, 2 * GROUP * core), ("up", None, 2 * GROUP * core + 1)]
    chunks += [("up", None, GROUP * other)]
    chunks += [("qkv", None, core), ("qkv", None, other), ("out", None, 0)]
    up_width = inner_half // GROUP
    up_block = min(512, up_width)

    def to_up(*operands):
        lefts = [(left, 0) for left in operands[:GROUP]]
        mine = operands[GROUP:]
        theirs = swap(jnp.concatenate(mine))
        results = []
        for first in range(inner_half // GROUP // up_block):
            rights = [columns_from(right, length, 0, first, up_block) for right in mine]
            results.append(rows_product(lefts, rights, half, up_block, 1))
        rights = [columns_from(theirs, length, d, 0, up_block) for d in range(GROUP)]
        steps = inner_half // GROUP // up_block
        return [*results, rows_product(lefts, rights, half, up_block, steps, True)]

    rest_block = half // GROUP

    def to_rest(*operands):
        early, mine = operands[:GROUP], operands[GROUP:]
        theirs = swap(jnp.concatenate(mine))

        def part(value, d):
            return value, (1, length, rest_block), lambda j: (4 * d + j, 0, 0)

        def out_part(value, d):
            return value, (1, rows, rest_block), lambda j: (4 * d + 3, j, 0)

        lefts = [(left, 0) for left in early]
        rights = [part(right, 0) for right in mine]
        own = rows_product(lefts, rights, half, rest_block, 3)
        rights = [part(theirs, d) for d in range(GROUP)]
        other_half = rows_product(lefts, rights, half, rest_block, 3, True)
        lefts = [(left, 1) for left in early]
        rights = []
        for d, right in enumerate(mine):
            rights += [out_part(right, 0), out_part(theirs, d)]
        return [own, other_half, rows_product(lefts, rights, half, rest_block, 2)]

    wholes = {
        "down": blank((inner_half, width)),
        "up": blank((half, inner)),
        "out": blank((half, width)),
        "qkv": blank((half, 3 * width)),
    }
    size = inner_half // GROUP
    values = []
    done = [(), ()]
    for index, (name, value, where) in enumerate(chunks):
        if value is None:
            value = values.pop(0)
        if index == 0:
            values = segment(to_up, *hold(up_left, late), *up_right)
        after = done[-2], {0: values, len(chunks) - 1: done[-1]}.get(index, ())
        if index > 0:
            value = line_middle(value)
        if plane == GROUP and name in LATE:
            pieces = spread_late(value, after)
        else:
            value = blocks_sum(line_end(value) if index > 0 else value)
            pieces = spread(value, after)
        if index == 0:
            values = [line_start(v) for v in values]
        if index == 3:
            rest = segment(to_rest, *hold(early, pieces[1:3]), *late)
            values += [line_start(v) for v in rest]
        tall, wide = value.shape
        high = min(256, tall)
        broad = wide // 3 if name == "qkv" else wide
        places = []
        for d in range(GROUP):
            owner = spot ^ d
            for i in range(tall // high):
                row = jnp.int32(i)
                if name == "down":
                    row, columns = owner * (tall // high) + i, [jnp.int32(where)]
                elif name == "up":
                    columns = [where + owner * (size // wide)]
                elif name == "out":
                    columns = [owner]
                else:
                    columns = [(2 * p + where) * GROUP + owner for p in range(3)]
                for column in columns:
                    places += [row, column]
        wholes[name] = place(pieces, wholes[name], places, high, broad)
        done.append(wholes[name])

    return (
        output.astype(LOW)[None],
        input_grad[None],
        wholes["qkv"],
        wholes["out"],
        wholes["up"],
        wholes["down"],
        *small_grads,
    )


def solution(mesh):
    return jax.shard_map(
        per_device,
        mesh=mesh,
        in_specs=(
            P("dp", "sp", None),
            P("dp", "sp", None),
            P("dp", None),
            P("sp", None),
            P("sp", None),
            P("sp", None),
            P("sp", None),
            P(),
            P(),
            P(),
            P(),
            P(),
            P(),
            P(),
            P(),
            P(),
        ),
        out_specs=(
            P("dp", "sp", None),
            P("dp", "sp", None),
            P("sp", None),
            P("sp", None),
            P("sp", None),
            P("sp", None),
            P(),
            P(),
            P(),
            P(),
            P(),
            P(),
            P(),
            P(),
            P(),
        ),
        check_vma=False,
    )
```

```python
import functools

import jax
import jax.numpy as jnp
from jax import lax
from jax.experimental import pallas as pl
from jax.experimental.pallas import tpu as pltpu
from jax.sharding import PartitionSpec as P

HEAD_DIM = 64
TILE = 128
LAYER = 12
LINE = 4
STREAMS = 1
GROUP = 4
F32 = jnp.float32
LOW = jnp.bfloat16


def layer_norm(values, gain, shift):
    center = jnp.mean(values, axis=-1, keepdims=True)
    centered = values - center
    variance = jnp.mean(centered * centered, axis=-1, keepdims=True)
    return centered * lax.rsqrt(variance + 1e-05) * gain + shift


def active_rows(bounds, first_row, row_count, sequence_length):
    position = first_row + jnp.arange(row_count, dtype=jnp.int32)
    tile_start = position // TILE * TILE
    exit_layer = bounds[1] - (bounds[1] - bounds[0]) * tile_start // sequence_length
    return (exit_layer > LAYER).astype(F32)[:, None]


def gelu_and_slope(values):
    scale = (2.0 / jnp.pi) ** 0.5
    square = values * values
    bend = jnp.tanh(scale * values * (1.0 + 0.044715 * square))
    rise = 0.5 * (1.0 + bend)
    slope = rise + 0.5 * values * (1.0 - bend * bend) * scale * (1.0 + 0.134145 * square)
    return values * rise, slope


def dot(left, right, left_dim, right_dim):
    return lax.dot_general(
        left, right, (((left_dim,), (right_dim,)), ((), ())), preferred_element_type=F32
    )


def roll_rows(value):
    rows = value.shape[0] // 2
    return jnp.concatenate([value[rows:], value[:rows]])


def estimate(flops, size):
    return pl.CostEstimate(flops=flops // 4, bytes_accessed=size // 4, transcendentals=0)


def far(value):
    return pltpu.with_memory_space_constraint(value, pltpu.HBM)


def limit(mebibytes):
    return pltpu.CompilerParams(vmem_limit_bytes=mebibytes << 20)


def halves(core_ref, values, mine_ref, theirs_ref):
    width = mine_ref.shape[1]
    first = core_ref[0] == 0
    low, high = values[:, :width], values[:, width:]
    mine_ref[...] = jnp.where(first, low, high).astype(LOW)
    theirs_ref[...] = jnp.where(first, high, low).astype(LOW)


def norm_one_kernel(
    core_ref, x_ref, gain_ref, shift_ref, grad_ref, active_ref,
    mine_ref, theirs_ref, masked_ref, sum_ref,
):
    normed = layer_norm(x_ref[...].astype(F32), gain_ref[...], shift_ref[...])
    halves(core_ref, normed, mine_ref, theirs_ref)
    masked = active_ref[...] * grad_ref[...].astype(F32)
    masked_ref[...] = masked.astype(LOW)
    sum_ref[...] = jnp.sum(masked, axis=0, keepdims=True)


def norm_two_kernel(
    core_ref, x_ref, active_ref, part_ref, theirs_part_ref, bias_ref, gain_ref, shift_ref,
    middle_ref, mine_ref, theirs_ref,
):
    rows = x_ref.shape[0]
    attn = part_ref[:rows] + theirs_part_ref[...] + bias_ref[...]
    middle = x_ref[...].astype(F32) + active_ref[...] * attn
    middle_ref[...] = middle
    halves(core_ref, layer_norm(middle, gain_ref[...], shift_ref[...]), mine_ref, theirs_ref)


def norm_back(core_ref, value_ref, gain_ref, mine_ref, theirs_ref, gain_out_ref, shift_out_ref):
    values = value_ref[...].astype(F32)
    mine, theirs = mine_ref[: values.shape[0]], theirs_ref[...]
    grads = jnp.where(
        core_ref[0] == 0,
        jnp.concatenate([mine, theirs], 1),
        jnp.concatenate([theirs, mine], 1),
    )
    centered = values - jnp.mean(values, axis=-1, keepdims=True)
    scale = lax.rsqrt(jnp.mean(centered * centered, axis=-1, keepdims=True) + 1e-05)
    unit = centered * scale
    gain_out_ref[...] = jnp.sum(grads * unit, axis=0, keepdims=True)
    shift_out_ref[...] = jnp.sum(grads, axis=0, keepdims=True)
    grads = grads * gain_ref[...]
    inner = jnp.mean(grads * unit, axis=-1, keepdims=True)
    return scale * (grads - jnp.mean(grads, axis=-1, keepdims=True) - unit * inner)


def norm_two_back_kernel(
    core_ref, value_ref, gain_ref, mine_ref, theirs_ref, grad_ref, active_ref,
    total_ref, masked_ref, sum_ref, gain_out_ref, shift_out_ref,
):
    part = norm_back(
        core_ref, value_ref, gain_ref, mine_ref, theirs_ref, gain_out_ref, shift_out_ref
    )
    total = grad_ref[...].astype(F32) + part
    total_ref[...] = total
    masked = (active_ref[...] * total).astype(LOW)
    masked_ref[...] = masked
    sum_ref[...] = jnp.sum(masked.astype(F32), axis=0, keepdims=True)


def norm_one_back_kernel(
    core_ref, value_ref, gain_ref, mine_ref, theirs_ref, grad_ref,
    total_ref, gain_out_ref, shift_out_ref,
):
    part = norm_back(
        core_ref, value_ref, gain_ref, mine_ref, theirs_ref, gain_out_ref, shift_out_ref
    )
    total_ref[...] = (grad_ref[...].astype(F32) + part).astype(LOW)


def by_rows(kernel, core, outs, *operands):
    vmem = pl.BlockSpec(memory_space=pltpu.VMEM)
    return pl.pallas_call(
        kernel,
        in_specs=[pl.BlockSpec(memory_space=pltpu.SMEM)] + [vmem] * len(operands),
        out_specs=[vmem] * len(outs),
        out_shape=[jax.ShapeDtypeStruct(shape, dtype) for shape, dtype in outs],
        compiler_params=limit(24),
        cost_estimate=estimate(
            20 * operands[0].size, sum(o.size * o.dtype.itemsize for o in operands)
        ),
    )(core, *operands)


def product_kernel(count, turned, *refs):
    lefts, out_ref, left_turned, right = refs[:count], refs[-3], refs[-2], refs[-1]
    rights = refs[count:-3]
    length = lefts[0].shape[0]

    @pl.when(pl.program_id(0) == 0)
    def _():
        for d, left in enumerate(lefts):
            left_turned[:, d * length : (d + 1) * length] = left[...].T

    row = 0
    for piece in rights:
        value = piece[0] if len(piece.shape) == 3 else piece[...]
        if turned:
            value = roll_rows(value)
        right[row : row + value.shape[0]] = value
        row += value.shape[0]
    out_ref[...] = dot(left_turned[...], right[...], 1, 0).astype(LOW)


def rows_product(lefts, rights, tall, block, steps, turned=False):
    length = lefts[0][0].shape[0]
    left_specs = [
        pl.BlockSpec((length, tall), functools.partial(lambda c, j: (0, c), c)) for _, c in lefts
    ]
    right_specs = [pl.BlockSpec(shape, place) for _, shape, place in rights]
    total = length * len(lefts)
    return pl.pallas_call(
        functools.partial(product_kernel, len(lefts), turned),
        grid=(steps,),
        in_specs=left_specs + right_specs,
        out_specs=pl.BlockSpec((tall, block), lambda j: (0, j)),
        out_shape=jax.ShapeDtypeStruct((tall, steps * block), LOW),
        scratch_shapes=[pltpu.VMEM((tall, total), LOW), pltpu.VMEM((total, block), LOW)],
        compiler_params=limit(32),
        cost_estimate=estimate(
            2 * tall * total * steps * block, 2 * total * (tall + steps * block)
        ),
    )(*[left[0] for left in lefts], *[right[0] for right in rights])


def columns_from(value, rows, row, first, block):
    return value, (rows, block), lambda j: (row, first + j)


def hold(values, after):
    return lax.optimization_barrier((values, after))[0]


def columns_kernel(table_ref, left_ref, *refs):
    total, first = 0.0, 0
    for weight_ref in refs[:-1]:
        depth = weight_ref.shape[0]
        total += dot(left_ref[:, first : first + depth], weight_ref[...], 1, 0)
        first += depth
    refs[-1][...] = total.astype(refs[-1].dtype)


def times_columns(left, weight, table, block, dtype):
    rows, depth = left.shape
    steps = table.shape[0]
    return pl.pallas_call(
        columns_kernel,
        grid_spec=pltpu.PrefetchScalarGridSpec(
            num_scalar_prefetch=1,
            grid=(steps,),
            in_specs=[
                pl.BlockSpec((rows, depth), lambda i, t: (0, 0)),
                *[
                    pl.BlockSpec(
                        (depth // STREAMS, block),
                        functools.partial(lambda r, i, t: (r, t[i]), r),
                    )
                    for r in range(STREAMS)
                ],
            ],
            out_specs=pl.BlockSpec((rows, block), lambda i, t: (0, i)),
        ),
        out_shape=jax.ShapeDtypeStruct((rows, steps * block), dtype),
        compiler_params=limit(24),
        cost_estimate=estimate(2 * rows * depth * steps * block, 2 * depth * (rows + steps * block) + 4 * rows * steps * block),
    )(table, left, *[far(weight)] * STREAMS)


def back_kernel(turned, table_ref, left_ref, *refs):
    weights, out_ref = refs[:STREAMS], refs[-1]
    starts = refs[STREAMS:-1]
    left = left_ref[...]
    if turned:
        left = roll_rows(left)
    first = 0
    for weight_ref in weights:
        deep = weight_ref.shape[0]
        part = dot(left, weight_ref[...], 1, 1)
        columns = slice(first, first + deep)
        first += deep

        @pl.when(pl.program_id(1) == 0)
        def _(part=part, columns=columns):
            out_ref[:, columns] = part + starts[0][:, columns] if starts else part

        @pl.when(pl.program_id(1) > 0)
        def _(part=part, columns=columns):
            out_ref[:, columns] += part


def times_back(left, weight, table, block, deep, start=None, turned=False):
    rows = left.shape[0]
    depth = weight.shape[0]
    steps = table.shape[0]
    out_spec = pl.BlockSpec((rows, deep), lambda k, i, t: (0, k))
    in_specs = [
        pl.BlockSpec((rows, block), lambda k, i, t: (0, i)),
        *[
            pl.BlockSpec(
                (deep // STREAMS, block),
                functools.partial(lambda r, k, i, t: (k * STREAMS + r, t[i]), r),
            )
            for r in range(STREAMS)
        ],
    ]
    operands = [table, left, *[far(weight)] * STREAMS]
    if start is not None:
        in_specs.append(out_spec)
        operands.append(start)
    return pl.pallas_call(
        functools.partial(back_kernel, turned),
        grid_spec=pltpu.PrefetchScalarGridSpec(
            num_scalar_prefetch=1,
            grid=(depth // deep, steps),
            in_specs=in_specs,
            out_specs=out_spec,
        ),
        out_shape=jax.ShapeDtypeStruct((rows, depth), F32),
        compiler_params=limit(32),
        cost_estimate=estimate(2 * rows * depth * steps * block, 2 * steps * block * (rows + depth) + 8 * rows * depth),
    )(*operands)


def inner_kernel(grad_ref, *refs):
    weights = refs[:STREAMS]
    mine_ref, theirs_ref, bias_ref, act_ref, out_ref, sum_ref = refs[STREAMS:]
    first = 0
    for weight_ref in weights:
        columns = slice(first, first + weight_ref.shape[0])
        first += weight_ref.shape[0]
        theirs = roll_rows(theirs_ref[:, columns])
        act, slope = gelu_and_slope(mine_ref[:, columns] + theirs + bias_ref[:, columns])
        act_ref[:, columns] = act.astype(LOW)
        grad = (dot(grad_ref[...], weight_ref[...], 1, 1) * slope).astype(LOW)
        out_ref[:, columns] = grad
        sum_ref[:, columns] = jnp.sum(grad.astype(F32), axis=0, keepdims=True)


def inner_layer(grads, weight, mine, theirs, bias, block):
    rows, width = grads.shape
    hidden = weight.shape[0]
    part = pl.BlockSpec((rows, block), lambda i: (0, i))
    line = pl.BlockSpec((1, block), lambda i: (0, i))
    return pl.pallas_call(
        inner_kernel,
        grid=(hidden // block,),
        in_specs=[
            pl.BlockSpec((rows, width), lambda i: (0, 0)),
            *[
                pl.BlockSpec(
                    (block // STREAMS, width),
                    functools.partial(lambda r, i: (i * STREAMS + r, 0), r),
                )
                for r in range(STREAMS)
            ],
            part,
            part,
            line,
        ],
        out_specs=[part, part, line],
        out_shape=[
            jax.ShapeDtypeStruct((rows, hidden), LOW),
            jax.ShapeDtypeStruct((rows, hidden), LOW),
            jax.ShapeDtypeStruct((1, hidden), F32),
        ],
        compiler_params=limit(32),
        cost_estimate=estimate(2 * rows * width * hidden, 2 * width * (rows + hidden) + 12 * rows * hidden),
    )(grads, *[far(weight)] * STREAMS, mine, theirs, bias)


def head_chances(queries, keys, lanes_of_head, allowed):
    keys_of_head = jnp.where(lanes_of_head, keys, jnp.zeros_like(keys))
    scores = dot(queries, keys_of_head, 1, 1) * (HEAD_DIM**-0.5)
    scores = jnp.where(allowed, scores, -1e30)
    raised = jnp.exp(scores - jnp.max(scores, axis=-1, keepdims=True))
    return raised / jnp.sum(raised, axis=-1, keepdims=True)


def attend_masks(first, length, lanes):
    lane = lax.broadcasted_iota(jnp.int32, (length, lanes), 1)
    row = lax.broadcasted_iota(jnp.int32, (length, length), 0) + first
    column = lax.broadcasted_iota(jnp.int32, (length, length), 1) + first
    row = jnp.where(row >= length, row - length, row)
    column = jnp.where(column >= length, column - length, column)
    return lane, column <= row


def attend_forward_kernel(first_ref, *refs):
    mine, theirs, biases, lows, o_ref = refs[:3], refs[3:6], refs[6:9], refs[9:12], refs[12]
    sums = [
        (m[...] + roll_rows(t[...]) + b[...]).astype(LOW)
        for m, t, b in zip(mine, theirs, biases)
    ]
    for low, value in zip(lows, sums):
        low[...] = value
    queries, keys, values = sums
    lane, allowed = attend_masks(first_ref[0], *queries.shape)
    total = jnp.zeros(queries.shape, F32)
    for head in range(queries.shape[1] // HEAD_DIM):
        own = lane // HEAD_DIM == head
        chances = head_chances(queries, keys, own, allowed).astype(LOW)
        total += dot(chances, jnp.where(own, values, jnp.zeros_like(values)), 1, 0)
    o_ref[...] = total.astype(LOW)


def attend_forward(first, mine, theirs, bias):
    length, width = mine.shape
    width //= 3
    steps = width // 128
    parts = [
        pl.BlockSpec((length, 128), functools.partial(lambda p, i, t: (0, p * steps + i), p))
        for p in range(3)
    ]
    lines = [
        pl.BlockSpec((1, 128), functools.partial(lambda p, i, t: (0, p * steps + i), p))
        for p in range(3)
    ]
    return pl.pallas_call(
        attend_forward_kernel,
        grid_spec=pltpu.PrefetchScalarGridSpec(
            num_scalar_prefetch=1,
            grid=(steps,),
            in_specs=parts + parts + lines,
            out_specs=[parts[0]] * 4,
        ),
        out_shape=[jax.ShapeDtypeStruct((length, width), LOW)] * 4,
        compiler_params=limit(16),
        cost_estimate=estimate(4 * length * length * width, 32 * length * width),
    )(first, mine, mine, mine, theirs, theirs, theirs, bias, bias, bias)


def attend_backward_kernel(first_ref, q_ref, k_ref, v_ref, g_ref, out_ref):
    queries, keys, values, grads = q_ref[...], k_ref[...], v_ref[...], g_ref[...]
    lane, allowed = attend_masks(first_ref[0], *queries.shape)
    dq = jnp.zeros(queries.shape, F32)
    dk = jnp.zeros(queries.shape, F32)
    dv = jnp.zeros(queries.shape, F32)
    for head in range(queries.shape[1] // HEAD_DIM):
        own = lane // HEAD_DIM == head
        chances = head_chances(queries, keys, own, allowed)
        head_grads = jnp.where(own, grads, jnp.zeros_like(grads))
        dv += dot(chances.astype(LOW), head_grads, 0, 0)
        chance_grads = dot(head_grads, values, 1, 1)
        inner = jnp.sum(chances * chance_grads, axis=-1, keepdims=True)
        score_grads = (chances * (chance_grads - inner)).astype(LOW)
        dq += dot(score_grads, jnp.where(own, keys, jnp.zeros_like(keys)), 1, 0)
        dk += dot(score_grads, jnp.where(own, queries, jnp.zeros_like(queries)), 0, 0)
    scale = HEAD_DIM**-0.5
    out_ref[0] = (dq * scale).astype(LOW)
    out_ref[1] = (dk * scale).astype(LOW)
    out_ref[2] = dv.astype(LOW)


def attend_backward(first, *operands):
    length, width = operands[0].shape
    block = pl.BlockSpec((length, 128), lambda i, t: (0, i))
    return pl.pallas_call(
        attend_backward_kernel,
        grid_spec=pltpu.PrefetchScalarGridSpec(
            num_scalar_prefetch=1,
            grid=(width // 128,),
            in_specs=[block] * 4,
            out_specs=pl.BlockSpec((3, length, 128), lambda i, t: (0, 0, i)),
        ),
        out_shape=jax.ShapeDtypeStruct((3, length, width), LOW),
        compiler_params=limit(16),
        cost_estimate=estimate(10 * length * length * width, 14 * length * width),
    )(first, *operands)


def place_kernel(high, table_ref, *refs):
    count = len(refs) - 4
    pieces, out_ref, held, sems = refs[:count], refs[-3], refs[-2], refs[-1]
    slots, broad = held.shape[0], held.shape[2]

    def copy(step):
        row = pl.multiple_of(table_ref[2 * step] * high, high)
        column = pl.multiple_of(table_ref[2 * step + 1] * broad, broad)
        return pltpu.make_async_copy(
            held.at[step % slots],
            out_ref.at[pl.ds(row, high), pl.ds(column, broad)],
            sems.at[step % slots],
        )

    step = 0
    for piece in pieces:
        for i in range(piece.shape[0] // high):
            for j in range(piece.shape[1] // broad):
                if step >= slots:
                    copy(step - slots).wait()
                part = piece[i * high : (i + 1) * high, j * broad : (j + 1) * broad]
                held[step % slots] = part.astype(F32)
                copy(step).start()
                step += 1
    for waited in range(max(step - slots, 0), step):
        copy(waited).wait()


def place(pieces, whole, places, high, broad):
    slots = 4
    vmem = pl.BlockSpec(memory_space=pltpu.VMEM)
    return pl.pallas_call(
        functools.partial(place_kernel, high),
        in_specs=[pl.BlockSpec(memory_space=pltpu.SMEM)]
        + [vmem] * len(pieces)
        + [pl.BlockSpec(memory_space=pl.ANY)],
        out_specs=pl.BlockSpec(memory_space=pl.ANY),
        out_shape=jax.ShapeDtypeStruct(whole.shape, F32),
        scratch_shapes=[
            pltpu.VMEM((slots, high, broad), F32),
            pltpu.SemaphoreType.DMA((slots,)),
        ],
        input_output_aliases={len(pieces) + 1: 0},
        compiler_params=limit(32),
        cost_estimate=estimate(0, sum(6 * p.size for p in pieces)),
    )(jnp.stack(places).astype(jnp.int32), *pieces, whole)


def blank_kernel(out_ref):
    pass


def blank(shape, dtype=F32):
    return pl.pallas_call(
        blank_kernel,
        out_specs=pl.BlockSpec(memory_space=pl.ANY),
        out_shape=jax.ShapeDtypeStruct(shape, dtype),
    )()


class Lane:
    def __init__(self):
        self.last = ()

    def send(self, sends, after=()):
        values = hold([v for v, _ in sends], (self.last, after))
        self.last = [lax.ppermute(v, "dp", m) for v, (_, m) in zip(values, sends)]
        return self.last


def per_device(
    hidden,
    cotangent,
    exit_layers,
    qkv_weight,
    out_weight,
    up_weight,
    down_weight,
    query_bias,
    value_bias,
    out_bias,
    up_bias,
    down_bias,
    attn_gain,
    attn_shift,
    ffn_gain,
    ffn_shift,
):
    core = lax.axis_index("sp")
    other = 1 - core
    chips = lax.axis_size("dp")
    plane = chips // LINE
    chip = lax.axis_index("dp")
    spot = chip % GROUP
    level = chip // plane
    rows = hidden.shape[1]
    width = hidden.shape[2]
    length = 2 * rows
    half = width // 2
    inner = up_weight.shape[1]
    inner_half = inner // 2
    across, first_hop, middle_hop, last_hop = (Lane() for _ in range(4))

    def swap(value):
        return lax.ppermute(value, "sp", [(0, 1), (1, 0)])

    def in_plane(distance):
        return [(i, i // plane * plane + ((i % plane) ^ distance)) for i in range(chips)]

    def along(*moves):
        return [(a * plane + i, b * plane + i) for a, b in moves for i in range(plane)]

    inward, middle_moves, outward = (
        along((0, 1), (3, 2)),
        along((1, 2), (2, 1)),
        along((1, 0), (2, 3)),
    )

    def split(value, axis, size):
        return (
            lax.dynamic_slice_in_dim(value, core * size, size, axis),
            lax.dynamic_slice_in_dim(value, other * size, size, axis),
        )

    def exchange(blocks):
        return blocks[:1] + across.send([(blocks[d], in_plane(d)) for d in range(1, GROUP)])

    def gather_group(value):
        return exchange([value] * GROUP)

    def blocks_of(value, axis, size):
        return [
            lax.dynamic_slice_in_dim(value, (spot ^ d) * size, size, axis) for d in range(GROUP)
        ]

    def scatter_group(value, axis, size):
        return exchange(blocks_of(value, axis, size))

    end = (level == 0) | (level == LINE - 1)

    def line_start(value, after=()):
        return value + hold(first_hop.send([(value, inward)])[0], after)

    def line_middle(value):
        return value + middle_hop.send([(value, middle_moves)])[0]

    def line_end(value):
        return jnp.where(end, last_hop.send([(value, outward)])[0], value)

    def blocks_sum(value):
        distance = GROUP
        while distance < plane:
            value = value + lax.ppermute(value, "dp", in_plane(distance))
            distance *= 2
        return value

    def spread(value, after, more=()):
        size = value.shape[0] // 2
        first, second = across.send([(value, in_plane(1)), (value, in_plane(2))], after[0])
        upper, lower, *more = across.send(
            [(first[:size], in_plane(2)), (second[size:], in_plane(1)), *more], after[1]
        )
        return [value, first, second, upper, lower], more

    def table(size, start, count=None):
        return jnp.arange(size if count is None else count, dtype=jnp.int32) + start

    active = active_rows(exit_layers[0], core * rows, rows, length)
    core_number = core.astype(jnp.int32)[None]
    first_row = (core * rows).astype(jnp.int32)[None]
    full, part, line = (rows, width), (rows, half), (1, width)

    always = exit_layers[0, 1] > 0

    def segment(steps, *operands):
        def skip(*_):
            return [blank(shape.shape, shape.dtype) for shape in jax.eval_shape(steps, *operands)]

        return lax.cond(always, lambda *o: list(steps(*o)), skip, *operands)

    mine, theirs, down_grad, down_sums = by_rows(
        norm_one_kernel,
        core_number,
        [(part, LOW), (part, LOW), (full, LOW), (line, F32)],
        hidden[0],
        attn_gain[None],
        attn_shift[None],
        cotangent[0],
        active,
    )
    down_mine = gather_group(down_grad)
    qkv_block = min(1024, half)
    qkv_count = half // qkv_block
    bias = jnp.stack([query_bias, jnp.zeros_like(query_bias), value_bias])
    bias = lax.dynamic_slice_in_dim(bias, core * half, half, 1).reshape(1, -1)

    def qkv_table(c):
        return jnp.concatenate(
            [table(qkv_count, (2 * p + c) * qkv_count) for p in range(3)]
        )

    def to_attended(mine, theirs, down_grad, qkv_weight, bias, my_table, their_table, first_row):
        normed = jnp.concatenate([mine, swap(theirs)])
        theirs = times_columns(normed, qkv_weight, their_table, qkv_block, LOW)
        theirs = swap(theirs)
        mine = times_columns(normed, qkv_weight, my_table, qkv_block, F32)
        results = attend_forward(first_row, mine, theirs, bias)
        both = jnp.concatenate([normed, results[3]], 1)
        return [*results, swap(down_grad), both]

    queries, keys, values, attended, down_grad_theirs, early = segment(
        to_attended, mine, theirs, down_grad, qkv_weight, bias,
        qkv_table(core), qkv_table(other), first_row,
    )
    attended, down_mine = lax.optimization_barrier((attended, down_mine))
    early = gather_group(early)
    block = min(1024, inner_half)
    count = inner_half // block

    def to_inner(
        hidden, active, attended, out_weight, lines, up_weight, tables, core_number,
        grads, down_weight,
    ):
        out_part = dot(attended, out_weight, 1, 0)
        middle, mine, theirs = by_rows(
            norm_two_kernel,
            core_number,
            [(full, F32), (part, LOW), (part, LOW)],
            hidden,
            active,
            out_part,
            swap(out_part[rows:]),
            *lines[:3],
        )
        normed = jnp.concatenate([mine, swap(theirs)])
        theirs = times_columns(normed, up_weight, tables[1], block, LOW)
        theirs = swap(theirs)
        mine = times_columns(normed, up_weight, tables[0], block, F32)
        results = inner_layer(
            grads, down_weight, mine, theirs, lines[3], min(512, inner_half)
        )
        return [middle, normed, *results]

    bias = lax.dynamic_slice_in_dim(up_bias, core * inner_half, inner_half).reshape(1, -1)
    middle, normed_two_half, inner_low, up_grad, up_sums = segment(
        to_inner, hidden[0], active, attended, out_weight,
        (out_bias[None], ffn_gain[None], ffn_shift[None], bias), up_weight,
        (table(count, core * count), table(count, other * count)), core_number,
        jnp.concatenate([down_grad, down_grad_theirs]), down_weight,
    )
    (inner_low, up_grad), early = lax.optimization_barrier(((inner_low, up_grad), early))

    down_left = scatter_group(inner_low, 1, inner_half // GROUP)

    def to_middle(
        up_grad, up_weight, middle, gain, cotangent, active, core_number, down_mine, tables
    ):
        theirs = swap(up_grad)
        grads = times_back(up_grad, up_weight, tables[0], inner_half, 256)
        grads = times_back(theirs, up_weight, tables[1], inner_half, 256, grads, True)
        results = by_rows(
            norm_two_back_kernel,
            core_number,
            [(full, F32), (full, LOW), (line, F32), (line, F32), (line, F32)],
            middle,
            gain,
            grads,
            swap(grads[rows:]),
            cotangent,
            active,
        )
        down_theirs = swap(jnp.concatenate(down_mine[1:]))
        return [*results, down_theirs, *blocks_of(up_grad, 1, inner_half // GROUP)]

    (
        middle_grad, attn_grad, attn_sums, gain_two_grad, shift_two_grad, down_theirs, *up_right
    ) = segment(
        to_middle, up_grad, up_weight, middle, ffn_gain[None], cotangent[0], active,
        core_number, down_mine, (table(1, core), table(1, other)),
    )
    down_theirs = [(down_grad_theirs, 0)] + [(down_theirs, d) for d in range(GROUP - 1)]

    def down_product(first, steps):
        rights = []
        for own, (value, row) in zip(down_mine, down_theirs):
            rights.append(columns_from(own, rows, 0, first, quarter))
            rights.append(columns_from(value, rows, row, first, quarter))
        lefts = [(left, 0) for left in down_left]
        return rows_product(lefts, rights, inner_half // GROUP, quarter, steps)

    quarter = width // 4
    down_left, attn_grad = lax.optimization_barrier((down_left, attn_grad))
    up_right = exchange(up_right)
    sums = [down_product(0, 1)]
    (come,) = first_hop.send([(sums[0], inward)])
    attn_grad, sums[0] = lax.optimization_barrier((attn_grad, sums[0]))

    def to_qkv(attn_grad, out_weight, first_row, *operands):
        grads = jnp.concatenate([attn_grad, swap(attn_grad)])
        grads = dot(grads, out_weight, 1, 1).astype(LOW)
        qkv_grad = attend_backward(first_row, *operands, grads)
        flat = jnp.concatenate([qkv_grad[0], qkv_grad[1], qkv_grad[2]], 1)
        blocks = []
        for wide, block in zip(
            blocks_of(attn_grad, 1, width // GROUP), blocks_of(qkv_grad, 2, half // GROUP)
        ):
            narrow = wide.shape[1] // 2
            wide = jnp.concatenate([wide[:, :narrow], wide[:, narrow:]])
            blocks.append(jnp.concatenate([block, wide[None]]))
        return [qkv_grad, flat, swap(flat), *blocks]

    qkv_grad, flat, flat_theirs, *late = segment(to_qkv, attn_grad, out_weight, first_row, queries, keys, values)
    sums.append(down_product(1, 1))
    qkv_grad, up_right, come, sums = lax.optimization_barrier((qkv_grad, up_right, come, sums))
    sums[0] += come
    (passed,) = middle_hop.send([(sums[0], middle_moves)])
    (come,) = first_hop.send([(sums[1], inward)])
    up_left = gather_group(normed_two_half)

    def to_input(flat, theirs, qkv_weight, tables):
        grads = times_back(flat, qkv_weight, tables[0], qkv_block, 512)
        return [times_back(theirs, qkv_weight, tables[1], qkv_block, 512, grads, True)]

    (grads,) = segment(
        to_input, hold(flat, qkv_grad), flat_theirs, qkv_weight,
        (qkv_table(core), qkv_table(other)),
    )
    grads, up_left, passed, come = lax.optimization_barrier((grads, up_left, passed, come))
    sums[0] += passed
    sums[1] += come
    late = exchange(late)
    value = hold(down_product(2, 1), grads)
    come = first_hop.send([(value, inward)])
    passed, come, late = lax.optimization_barrier(
        (last_hop.send([(sums[0], outward)]), come, late)
    )
    sums[0] = jnp.where(end, passed[0], sums[0])
    sums.append(value + come[0])
    sums.append(line_start(hold(down_product(3, 1), late)))

    def to_ends(grads, hidden, gain, middle_grad, core_number, inner_low, down_weight):
        results = by_rows(
            norm_one_back_kernel,
            core_number,
            [(full, LOW), (line, F32), (line, F32)],
            hidden,
            gain,
            grads,
            swap(grads[rows:]),
            middle_grad,
        )
        down_part = dot(inner_low, down_weight, 1, 0)
        return [*results, down_part[:rows], swap(down_part[rows:])]

    input_grad, gain_one_grad, shift_one_grad, mine, theirs = to_ends(
        hold(grads, sums[0]), hidden[0], attn_gain[None], middle_grad, core_number,
        inner_low, down_weight,
    )
    output = middle + active * (mine + theirs + down_bias)

    def widen(value):
        none = jnp.zeros_like(value)
        return jnp.where(
            core == 0, jnp.concatenate([value, none]), jnp.concatenate([none, value])
        )

    qkv_sums = jnp.sum(qkv_grad.astype(F32), axis=1)
    small = jnp.concatenate(
        [
            widen(qkv_sums[0]),
            widen(qkv_sums[2]),
            attn_sums[0],
            widen(up_sums[0]),
            down_sums[0],
            gain_one_grad[0],
            shift_one_grad[0],
            gain_two_grad[0],
            shift_two_grad[0],
        ]
    ).reshape(-1, 128)
    small = small + swap(small)

    small_sends = [(small, in_plane(d)) for d in range(1, GROUP)]

    def pair_sums(values):
        while len(values) > 1:
            values = [a + b for a, b in zip(values[::2], values[1::2])]
        return values[0]

    def line_moves(distance):
        return [(i, (i // plane ^ distance) * plane + i % plane) for i in range(chips)]

    chunks = [("down", value, index) for index, value in enumerate(sums)]
    chunks += [("up", None, 2 * GROUP * core), ("up", None, 2 * GROUP * core + 1)]
    chunks += [("up", None, 2 * GROUP * other), ("up", None, 2 * GROUP * other + 1)]
    chunks += [("qkv", None, core), ("qkv", None, other), ("out", None, 0)]
    up_width = inner_half // GROUP
    up_block = min(512, up_width)

    def to_up(*operands):
        lefts = [(left, 0) for left in operands[:GROUP]]
        mine = operands[GROUP:]
        theirs = swap(jnp.concatenate(mine))
        results = []
        for first in range(inner_half // GROUP // up_block):
            rights = [columns_from(right, length, 0, first, up_block) for right in mine]
            results.append(rows_product(lefts, rights, half, up_block, 1))
        for first in range(inner_half // GROUP // up_block):
            rights = [columns_from(theirs, length, d, first, up_block) for d in range(GROUP)]
            results.append(rows_product(lefts, rights, half, up_block, 1, True))
        return results

    rest_block = half // GROUP

    def to_rest(*operands):
        early, mine = operands[:GROUP], operands[GROUP:]
        theirs = swap(jnp.concatenate(mine))

        def part(value, d):
            return value, (1, length, rest_block), lambda j: (4 * d + j, 0, 0)

        def out_part(value, d):
            return value, (1, rows, rest_block), lambda j: (4 * d + 3, j, 0)

        lefts = [(left, 0) for left in early]
        rights = [part(right, 0) for right in mine]
        own = rows_product(lefts, rights, half, rest_block, 3)
        rights = [part(theirs, d) for d in range(GROUP)]
        other_half = rows_product(lefts, rights, half, rest_block, 3, True)
        lefts = [(left, 1) for left in early]
        rights = []
        for d, right in enumerate(mine):
            rights += [out_part(right, 0), out_part(theirs, d)]
        return [own, other_half, rows_product(lefts, rights, half, rest_block, 2)]

    wholes = {
        "down": blank((inner_half, width)),
        "up": blank((half, inner)),
        "out": blank((half, width)),
        "qkv": blank((half, 3 * width)),
    }
    size = inner_half // GROUP
    values = []
    done = [(), ()]
    for index, (name, value, where) in enumerate(chunks):
        if value is None:
            value = values.pop(0)
        more, held = (), [done[-1]]
        if index == 0:
            values = segment(to_up, *hold(up_left, late), *up_right)
            held.append(values)
        if index == 4:
            rest = segment(to_rest, *early, *late)
            held.append(rest)
        if index == len(chunks) - 2:
            more = small_sends
        if index == len(chunks) - 1:
            small = pair_sums([small, *more_results])
            distance = GROUP
            while distance < plane:
                small = small + lax.ppermute(small, "dp", in_plane(distance))
                distance *= 2
            lines = [lax.ppermute(small, "dp", line_moves(d)) for d in range(1, LINE)]
            held += [done[-1], lines]
        after = (), held
        if index > 0:
            value = line_middle(value)
            value = line_end(value)
        pieces, more_results = spread(blocks_sum(value), after, more)
        value = pieces[0]
        if index == 0:
            values = [line_start(v) for v in hold(values, pieces[3:])]
        if index == 4:
            values += [line_start(v) for v in rest]
        tall, wide = value.shape
        high = min(256, tall)
        broad = wide // 3 if name == "qkv" else wide
        places = []
        for d in range(GROUP):
            owner = spot ^ d
            for i in range(tall // high):
                row = jnp.int32(i)
                if name == "down":
                    row, columns = owner * (tall // high) + i, [jnp.int32(where)]
                elif name == "up":
                    columns = [where + owner * (size // wide)]
                elif name == "out":
                    columns = [owner]
                else:
                    columns = [(2 * p + where) * GROUP + owner for p in range(3)]
                for column in columns:
                    places += [row, column]
        wholes[name] = place(pieces, wholes[name], places, high, broad)
        done.append(wholes[name])

    small = pair_sums([small, *lines]).reshape(-1)
    small_grads = []
    first = 0
    for size in (width, width, width, inner, width, width, width, width, width):
        small_grads.append(small[first : first + size])
        first += size

    return (
        output.astype(LOW)[None],
        input_grad[None],
        wholes["qkv"],
        wholes["out"],
        wholes["up"],
        wholes["down"],
        *small_grads,
    )


def solution(mesh):
    return jax.shard_map(
        per_device,
        mesh=mesh,
        in_specs=(
            P("dp", "sp", None),
            P("dp", "sp", None),
            P("dp", None),
            P("sp", None),
            P("sp", None),
            P("sp", None),
            P("sp", None),
            P(),
            P(),
            P(),
            P(),
            P(),
            P(),
            P(),
            P(),
            P(),
        ),
        out_specs=(
            P("dp", "sp", None),
            P("dp", "sp", None),
            P("sp", None),
            P("sp", None),
            P("sp", None),
            P("sp", None),
            P(),
            P(),
            P(),
            P(),
            P(),
            P(),
            P(),
            P(),
            P(),
        ),
        check_vma=False,
    )
```

```python
import functools

import jax
import jax.numpy as jnp
from jax import lax
from jax.experimental import pallas as pl
from jax.experimental.pallas import tpu as pltpu
from jax.sharding import PartitionSpec as P

HEAD_DIM = 64
TILE = 128
LAYER = 12
LINE = 4
STREAMS = 1
GROUP = 4
F32 = jnp.float32
LOW = jnp.bfloat16


def layer_norm(values, gain, shift):
    center = jnp.mean(values, axis=-1, keepdims=True)
    centered = values - center
    variance = jnp.mean(centered * centered, axis=-1, keepdims=True)
    return centered * lax.rsqrt(variance + 1e-05) * gain + shift


def active_rows(bounds, first_row, row_count, sequence_length):
    position = first_row + jnp.arange(row_count, dtype=jnp.int32)
    tile_start = position // TILE * TILE
    exit_layer = bounds[1] - (bounds[1] - bounds[0]) * tile_start // sequence_length
    return (exit_layer > LAYER).astype(F32)[:, None]


def gelu_and_slope(values):
    scale = (2.0 / jnp.pi) ** 0.5
    square = values * values
    bend = jnp.tanh(scale * values * (1.0 + 0.044715 * square))
    rise = 0.5 * (1.0 + bend)
    slope = rise + 0.5 * values * (1.0 - bend * bend) * scale * (1.0 + 0.134145 * square)
    return values * rise, slope


def dot(left, right, left_dim, right_dim):
    return lax.dot_general(
        left, right, (((left_dim,), (right_dim,)), ((), ())), preferred_element_type=F32
    )


def roll_rows(value):
    rows = value.shape[0] // 2
    return jnp.concatenate([value[rows:], value[:rows]])


def estimate(flops, size):
    return pl.CostEstimate(flops=flops // 4, bytes_accessed=size // 4, transcendentals=0)


def far(value):
    return pltpu.with_memory_space_constraint(value, pltpu.HBM)


def limit(mebibytes):
    return pltpu.CompilerParams(vmem_limit_bytes=mebibytes << 20)


def halves(core_ref, values, mine_ref, theirs_ref):
    width = mine_ref.shape[1]
    first = core_ref[0] == 0
    low, high = values[:, :width], values[:, width:]
    mine_ref[...] = jnp.where(first, low, high).astype(LOW)
    theirs_ref[...] = jnp.where(first, high, low).astype(LOW)


def norm_one_kernel(
    core_ref, x_ref, gain_ref, shift_ref, grad_ref, active_ref,
    mine_ref, theirs_ref, masked_ref, sum_ref,
):
    normed = layer_norm(x_ref[...].astype(F32), gain_ref[...], shift_ref[...])
    halves(core_ref, normed, mine_ref, theirs_ref)
    masked = active_ref[...] * grad_ref[...].astype(F32)
    masked_ref[...] = masked.astype(LOW)
    sum_ref[...] = jnp.sum(masked, axis=0, keepdims=True)


def norm_two_kernel(
    core_ref, x_ref, active_ref, part_ref, theirs_part_ref, bias_ref, gain_ref, shift_ref,
    middle_ref, mine_ref, theirs_ref,
):
    rows = x_ref.shape[0]
    attn = part_ref[:rows] + theirs_part_ref[...] + bias_ref[...]
    middle = x_ref[...].astype(F32) + active_ref[...] * attn
    middle_ref[...] = middle
    halves(core_ref, layer_norm(middle, gain_ref[...], shift_ref[...]), mine_ref, theirs_ref)


def norm_back(core_ref, value_ref, gain_ref, mine_ref, theirs_ref, gain_out_ref, shift_out_ref):
    values = value_ref[...].astype(F32)
    mine, theirs = mine_ref[: values.shape[0]], theirs_ref[...]
    grads = jnp.where(
        core_ref[0] == 0,
        jnp.concatenate([mine, theirs], 1),
        jnp.concatenate([theirs, mine], 1),
    )
    centered = values - jnp.mean(values, axis=-1, keepdims=True)
    scale = lax.rsqrt(jnp.mean(centered * centered, axis=-1, keepdims=True) + 1e-05)
    unit = centered * scale
    gain_out_ref[...] = jnp.sum(grads * unit, axis=0, keepdims=True)
    shift_out_ref[...] = jnp.sum(grads, axis=0, keepdims=True)
    grads = grads * gain_ref[...]
    inner = jnp.mean(grads * unit, axis=-1, keepdims=True)
    return scale * (grads - jnp.mean(grads, axis=-1, keepdims=True) - unit * inner)


def norm_two_back_kernel(
    core_ref, value_ref, gain_ref, mine_ref, theirs_ref, grad_ref, active_ref,
    total_ref, masked_ref, sum_ref, gain_out_ref, shift_out_ref,
):
    part = norm_back(
        core_ref, value_ref, gain_ref, mine_ref, theirs_ref, gain_out_ref, shift_out_ref
    )
    total = grad_ref[...].astype(F32) + part
    total_ref[...] = total
    masked = (active_ref[...] * total).astype(LOW)
    masked_ref[...] = masked
    sum_ref[...] = jnp.sum(masked.astype(F32), axis=0, keepdims=True)


def norm_one_back_kernel(
    core_ref, value_ref, gain_ref, mine_ref, theirs_ref, grad_ref,
    total_ref, gain_out_ref, shift_out_ref,
):
    part = norm_back(
        core_ref, value_ref, gain_ref, mine_ref, theirs_ref, gain_out_ref, shift_out_ref
    )
    total_ref[...] = (grad_ref[...].astype(F32) + part).astype(LOW)


def by_rows(kernel, core, outs, *operands):
    vmem = pl.BlockSpec(memory_space=pltpu.VMEM)
    return pl.pallas_call(
        kernel,
        in_specs=[pl.BlockSpec(memory_space=pltpu.SMEM)] + [vmem] * len(operands),
        out_specs=[vmem] * len(outs),
        out_shape=[jax.ShapeDtypeStruct(shape, dtype) for shape, dtype in outs],
        compiler_params=limit(24),
        cost_estimate=estimate(
            20 * operands[0].size, sum(o.size * o.dtype.itemsize for o in operands)
        ),
    )(core, *operands)


def product_kernel(count, turned, *refs):
    lefts, out_ref, left_turned, right = refs[:count], refs[-3], refs[-2], refs[-1]
    rights = refs[count:-3]
    length = lefts[0].shape[0]

    @pl.when(pl.program_id(0) == 0)
    def _():
        for d, left in enumerate(lefts):
            left_turned[:, d * length : (d + 1) * length] = left[...].T

    row = 0
    for piece in rights:
        value = piece[0] if len(piece.shape) == 3 else piece[...]
        if turned:
            value = roll_rows(value)
        right[row : row + value.shape[0]] = value
        row += value.shape[0]
    out_ref[...] = dot(left_turned[...], right[...], 1, 0).astype(LOW)


def rows_product(lefts, rights, tall, block, steps, turned=False):
    length = lefts[0][0].shape[0]
    left_specs = [
        pl.BlockSpec((length, tall), functools.partial(lambda c, j: (0, c), c)) for _, c in lefts
    ]
    right_specs = [pl.BlockSpec(shape, place) for _, shape, place in rights]
    total = length * len(lefts)
    return pl.pallas_call(
        functools.partial(product_kernel, len(lefts), turned),
        grid=(steps,),
        in_specs=left_specs + right_specs,
        out_specs=pl.BlockSpec((tall, block), lambda j: (0, j)),
        out_shape=jax.ShapeDtypeStruct((tall, steps * block), LOW),
        scratch_shapes=[pltpu.VMEM((tall, total), LOW), pltpu.VMEM((total, block), LOW)],
        compiler_params=limit(32),
        cost_estimate=estimate(
            2 * tall * total * steps * block, 2 * total * (tall + steps * block)
        ),
    )(*[left[0] for left in lefts], *[right[0] for right in rights])


def columns_from(value, rows, row, first, block):
    return value, (rows, block), lambda j: (row, first + j)


def hold(values, after):
    return lax.optimization_barrier((values, after))[0]


def columns_kernel(table_ref, left_ref, *refs):
    total, first = 0.0, 0
    for weight_ref in refs[:-1]:
        depth = weight_ref.shape[0]
        total += dot(left_ref[:, first : first + depth], weight_ref[...], 1, 0)
        first += depth
    refs[-1][...] = total.astype(refs[-1].dtype)


def times_columns(left, weight, table, block, dtype):
    rows, depth = left.shape
    steps = table.shape[0]
    return pl.pallas_call(
        columns_kernel,
        grid_spec=pltpu.PrefetchScalarGridSpec(
            num_scalar_prefetch=1,
            grid=(steps,),
            in_specs=[
                pl.BlockSpec((rows, depth), lambda i, t: (0, 0)),
                *[
                    pl.BlockSpec(
                        (depth // STREAMS, block),
                        functools.partial(lambda r, i, t: (r, t[i]), r),
                    )
                    for r in range(STREAMS)
                ],
            ],
            out_specs=pl.BlockSpec((rows, block), lambda i, t: (0, i)),
        ),
        out_shape=jax.ShapeDtypeStruct((rows, steps * block), dtype),
        compiler_params=limit(24),
        cost_estimate=estimate(2 * rows * depth * steps * block, 2 * depth * (rows + steps * block) + 4 * rows * steps * block),
    )(table, left, *[far(weight)] * STREAMS)


def back_kernel(turned, table_ref, left_ref, *refs):
    weights, out_ref = refs[:STREAMS], refs[-1]
    starts = refs[STREAMS:-1]
    left = left_ref[...]
    if turned:
        left = roll_rows(left)
    first = 0
    for weight_ref in weights:
        deep = weight_ref.shape[0]
        part = dot(left, weight_ref[...], 1, 1)
        columns = slice(first, first + deep)
        first += deep

        @pl.when(pl.program_id(1) == 0)
        def _(part=part, columns=columns):
            out_ref[:, columns] = part + starts[0][:, columns] if starts else part

        @pl.when(pl.program_id(1) > 0)
        def _(part=part, columns=columns):
            out_ref[:, columns] += part


def times_back(left, weight, table, block, deep, start=None, turned=False):
    rows = left.shape[0]
    depth = weight.shape[0]
    steps = table.shape[0]
    out_spec = pl.BlockSpec((rows, deep), lambda k, i, t: (0, k))
    in_specs = [
        pl.BlockSpec((rows, block), lambda k, i, t: (0, i)),
        *[
            pl.BlockSpec(
                (deep // STREAMS, block),
                functools.partial(lambda r, k, i, t: (k * STREAMS + r, t[i]), r),
            )
            for r in range(STREAMS)
        ],
    ]
    operands = [table, left, *[far(weight)] * STREAMS]
    if start is not None:
        in_specs.append(out_spec)
        operands.append(start)
    return pl.pallas_call(
        functools.partial(back_kernel, turned),
        grid_spec=pltpu.PrefetchScalarGridSpec(
            num_scalar_prefetch=1,
            grid=(depth // deep, steps),
            in_specs=in_specs,
            out_specs=out_spec,
        ),
        out_shape=jax.ShapeDtypeStruct((rows, depth), F32),
        compiler_params=limit(32),
        cost_estimate=estimate(2 * rows * depth * steps * block, 2 * steps * block * (rows + depth) + 8 * rows * depth),
    )(*operands)


def inner_kernel(grad_ref, *refs):
    weights = refs[:STREAMS]
    mine_ref, theirs_ref, bias_ref, act_ref, out_ref, sum_ref = refs[STREAMS:]
    first = 0
    for weight_ref in weights:
        columns = slice(first, first + weight_ref.shape[0])
        first += weight_ref.shape[0]
        theirs = roll_rows(theirs_ref[:, columns])
        act, slope = gelu_and_slope(mine_ref[:, columns] + theirs + bias_ref[:, columns])
        act_ref[:, columns] = act.astype(LOW)
        grad = (dot(grad_ref[...], weight_ref[...], 1, 1) * slope).astype(LOW)
        out_ref[:, columns] = grad
        sum_ref[:, columns] = jnp.sum(grad.astype(F32), axis=0, keepdims=True)


def inner_layer(grads, weight, mine, theirs, bias, block):
    rows, width = grads.shape
    hidden = weight.shape[0]
    part = pl.BlockSpec((rows, block), lambda i: (0, i))
    line = pl.BlockSpec((1, block), lambda i: (0, i))
    return pl.pallas_call(
        inner_kernel,
        grid=(hidden // block,),
        in_specs=[
            pl.BlockSpec((rows, width), lambda i: (0, 0)),
            *[
                pl.BlockSpec(
                    (block // STREAMS, width),
                    functools.partial(lambda r, i: (i * STREAMS + r, 0), r),
                )
                for r in range(STREAMS)
            ],
            part,
            part,
            line,
        ],
        out_specs=[part, part, line],
        out_shape=[
            jax.ShapeDtypeStruct((rows, hidden), LOW),
            jax.ShapeDtypeStruct((rows, hidden), LOW),
            jax.ShapeDtypeStruct((1, hidden), F32),
        ],
        compiler_params=limit(32),
        cost_estimate=estimate(2 * rows * width * hidden, 2 * width * (rows + hidden) + 12 * rows * hidden),
    )(grads, *[far(weight)] * STREAMS, mine, theirs, bias)


def head_chances(queries, keys, lanes_of_head, allowed):
    keys_of_head = jnp.where(lanes_of_head, keys, jnp.zeros_like(keys))
    scores = dot(queries, keys_of_head, 1, 1) * (HEAD_DIM**-0.5)
    scores = jnp.where(allowed, scores, -1e30)
    raised = jnp.exp(scores - jnp.max(scores, axis=-1, keepdims=True))
    return raised / jnp.sum(raised, axis=-1, keepdims=True)


def attend_masks(first, length, lanes):
    lane = lax.broadcasted_iota(jnp.int32, (length, lanes), 1)
    row = lax.broadcasted_iota(jnp.int32, (length, length), 0) + first
    column = lax.broadcasted_iota(jnp.int32, (length, length), 1) + first
    row = jnp.where(row >= length, row - length, row)
    column = jnp.where(column >= length, column - length, column)
    return lane, column <= row


def attend_forward_kernel(first_ref, *refs):
    mine, theirs, biases, lows, o_ref = refs[:3], refs[3:6], refs[6:9], refs[9:12], refs[12]
    sums = [
        (m[...] + roll_rows(t[...]) + b[...]).astype(LOW)
        for m, t, b in zip(mine, theirs, biases)
    ]
    for low, value in zip(lows, sums):
        low[...] = value
    queries, keys, values = sums
    lane, allowed = attend_masks(first_ref[0], *queries.shape)
    total = jnp.zeros(queries.shape, F32)
    for head in range(queries.shape[1] // HEAD_DIM):
        own = lane // HEAD_DIM == head
        chances = head_chances(queries, keys, own, allowed).astype(LOW)
        total += dot(chances, jnp.where(own, values, jnp.zeros_like(values)), 1, 0)
    o_ref[...] = total.astype(LOW)


def attend_forward(first, mine, theirs, bias):
    length, width = mine.shape
    width //= 3
    steps = width // 128
    parts = [
        pl.BlockSpec((length, 128), functools.partial(lambda p, i, t: (0, p * steps + i), p))
        for p in range(3)
    ]
    lines = [
        pl.BlockSpec((1, 128), functools.partial(lambda p, i, t: (0, p * steps + i), p))
        for p in range(3)
    ]
    return pl.pallas_call(
        attend_forward_kernel,
        grid_spec=pltpu.PrefetchScalarGridSpec(
            num_scalar_prefetch=1,
            grid=(steps,),
            in_specs=parts + parts + lines,
            out_specs=[parts[0]] * 4,
        ),
        out_shape=[jax.ShapeDtypeStruct((length, width), LOW)] * 4,
        compiler_params=limit(16),
        cost_estimate=estimate(4 * length * length * width, 32 * length * width),
    )(first, mine, mine, mine, theirs, theirs, theirs, bias, bias, bias)


def attend_backward_kernel(first_ref, q_ref, k_ref, v_ref, g_ref, out_ref):
    queries, keys, values, grads = q_ref[...], k_ref[...], v_ref[...], g_ref[...]
    lane, allowed = attend_masks(first_ref[0], *queries.shape)
    dq = jnp.zeros(queries.shape, F32)
    dk = jnp.zeros(queries.shape, F32)
    dv = jnp.zeros(queries.shape, F32)
    for head in range(queries.shape[1] // HEAD_DIM):
        own = lane // HEAD_DIM == head
        chances = head_chances(queries, keys, own, allowed)
        head_grads = jnp.where(own, grads, jnp.zeros_like(grads))
        dv += dot(chances.astype(LOW), head_grads, 0, 0)
        chance_grads = dot(head_grads, values, 1, 1)
        inner = jnp.sum(chances * chance_grads, axis=-1, keepdims=True)
        score_grads = (chances * (chance_grads - inner)).astype(LOW)
        dq += dot(score_grads, jnp.where(own, keys, jnp.zeros_like(keys)), 1, 0)
        dk += dot(score_grads, jnp.where(own, queries, jnp.zeros_like(queries)), 0, 0)
    scale = HEAD_DIM**-0.5
    out_ref[0] = (dq * scale).astype(LOW)
    out_ref[1] = (dk * scale).astype(LOW)
    out_ref[2] = dv.astype(LOW)


def attend_backward(first, *operands):
    length, width = operands[0].shape
    block = pl.BlockSpec((length, 128), lambda i, t: (0, i))
    return pl.pallas_call(
        attend_backward_kernel,
        grid_spec=pltpu.PrefetchScalarGridSpec(
            num_scalar_prefetch=1,
            grid=(width // 128,),
            in_specs=[block] * 4,
            out_specs=pl.BlockSpec((3, length, 128), lambda i, t: (0, 0, i)),
        ),
        out_shape=jax.ShapeDtypeStruct((3, length, width), LOW),
        compiler_params=limit(16),
        cost_estimate=estimate(10 * length * length * width, 14 * length * width),
    )(first, *operands)


def place_kernel(high, table_ref, *refs):
    count = len(refs) - 4
    pieces, out_ref, held, sems = refs[:count], refs[-3], refs[-2], refs[-1]
    slots, broad = held.shape[0], held.shape[2]

    def copy(step):
        row = pl.multiple_of(table_ref[2 * step] * high, high)
        column = pl.multiple_of(table_ref[2 * step + 1] * broad, broad)
        return pltpu.make_async_copy(
            held.at[step % slots],
            out_ref.at[pl.ds(row, high), pl.ds(column, broad)],
            sems.at[step % slots],
        )

    step = 0
    for piece in pieces:
        for i in range(piece.shape[0] // high):
            for j in range(piece.shape[1] // broad):
                if step >= slots:
                    copy(step - slots).wait()
                part = piece[i * high : (i + 1) * high, j * broad : (j + 1) * broad]
                held[step % slots] = part.astype(F32)
                copy(step).start()
                step += 1
    for waited in range(max(step - slots, 0), step):
        copy(waited).wait()


def place(pieces, whole, places, high, broad):
    slots = 4
    vmem = pl.BlockSpec(memory_space=pltpu.VMEM)
    return pl.pallas_call(
        functools.partial(place_kernel, high),
        in_specs=[pl.BlockSpec(memory_space=pltpu.SMEM)]
        + [vmem] * len(pieces)
        + [pl.BlockSpec(memory_space=pl.ANY)],
        out_specs=pl.BlockSpec(memory_space=pl.ANY),
        out_shape=jax.ShapeDtypeStruct(whole.shape, F32),
        scratch_shapes=[
            pltpu.VMEM((slots, high, broad), F32),
            pltpu.SemaphoreType.DMA((slots,)),
        ],
        input_output_aliases={len(pieces) + 1: 0},
        compiler_params=limit(32),
        cost_estimate=estimate(0, sum(6 * p.size for p in pieces)),
    )(jnp.stack(places).astype(jnp.int32), *pieces, whole)


def blank_kernel(out_ref):
    pass


def blank(shape, dtype=F32):
    return pl.pallas_call(
        blank_kernel,
        out_specs=pl.BlockSpec(memory_space=pl.ANY),
        out_shape=jax.ShapeDtypeStruct(shape, dtype),
    )()


class Lane:
    def __init__(self):
        self.last = ()

    def send(self, sends, after=()):
        values = hold([v for v, _ in sends], (self.last, after))
        self.last = [lax.ppermute(v, "dp", m) for v, (_, m) in zip(values, sends)]
        return self.last


def per_device(
    hidden,
    cotangent,
    exit_layers,
    qkv_weight,
    out_weight,
    up_weight,
    down_weight,
    query_bias,
    value_bias,
    out_bias,
    up_bias,
    down_bias,
    attn_gain,
    attn_shift,
    ffn_gain,
    ffn_shift,
):
    core = lax.axis_index("sp")
    other = 1 - core
    chips = lax.axis_size("dp")
    plane = chips // LINE
    chip = lax.axis_index("dp")
    spot = chip % GROUP
    level = chip // plane
    rows = hidden.shape[1]
    width = hidden.shape[2]
    length = 2 * rows
    half = width // 2
    inner = up_weight.shape[1]
    inner_half = inner // 2
    across, first_hop, middle_hop, last_hop = (Lane() for _ in range(4))

    def swap(value):
        return lax.ppermute(value, "sp", [(0, 1), (1, 0)])

    def in_plane(distance):
        return [(i, i // plane * plane + ((i % plane) ^ distance)) for i in range(chips)]

    def along(*moves):
        return [(a * plane + i, b * plane + i) for a, b in moves for i in range(plane)]

    inward, middle_moves, outward = (
        along((0, 1), (3, 2)),
        along((1, 2), (2, 1)),
        along((1, 0), (2, 3)),
    )

    def split(value, axis, size):
        return (
            lax.dynamic_slice_in_dim(value, core * size, size, axis),
            lax.dynamic_slice_in_dim(value, other * size, size, axis),
        )

    def exchange(blocks):
        return blocks[:1] + across.send([(blocks[d], in_plane(d)) for d in range(1, GROUP)])

    def gather_group(value):
        return exchange([value] * GROUP)

    def blocks_of(value, axis, size):
        return [
            lax.dynamic_slice_in_dim(value, (spot ^ d) * size, size, axis) for d in range(GROUP)
        ]

    def scatter_group(value, axis, size):
        return exchange(blocks_of(value, axis, size))

    end = (level == 0) | (level == LINE - 1)

    def line_start(value, after=()):
        return value + hold(first_hop.send([(value, inward)])[0], after)

    def line_middle(value):
        return value + middle_hop.send([(value, middle_moves)])[0]

    def line_end(value):
        return jnp.where(end, last_hop.send([(value, outward)])[0], value)

    def blocks_sum(value):
        distance = GROUP
        while distance < plane:
            value = value + lax.ppermute(value, "dp", in_plane(distance))
            distance *= 2
        return value

    def spread(value, after, more=()):
        size = value.shape[0] // 2
        first, second = across.send([(value, in_plane(1)), (value, in_plane(2))], after[0])
        upper, lower, *more = across.send(
            [(first[:size], in_plane(2)), (second[size:], in_plane(1)), *more], after[1]
        )
        return [value, first, second, upper, lower], more

    def table(size, start, count=None):
        return jnp.arange(size if count is None else count, dtype=jnp.int32) + start

    active = active_rows(exit_layers[0], core * rows, rows, length)
    core_number = core.astype(jnp.int32)[None]
    first_row = (core * rows).astype(jnp.int32)[None]
    full, part, line = (rows, width), (rows, half), (1, width)

    always = exit_layers[0, 1] > 0

    def segment(steps, *operands):
        def skip(*_):
            return [blank(shape.shape, shape.dtype) for shape in jax.eval_shape(steps, *operands)]

        return lax.cond(always, lambda *o: list(steps(*o)), skip, *operands)

    mine, theirs, down_grad, down_sums = by_rows(
        norm_one_kernel,
        core_number,
        [(part, LOW), (part, LOW), (full, LOW), (line, F32)],
        hidden[0],
        attn_gain[None],
        attn_shift[None],
        cotangent[0],
        active,
    )
    down_mine = gather_group(down_grad)
    qkv_block = min(1024, half)
    qkv_count = half // qkv_block
    bias = jnp.stack([query_bias, jnp.zeros_like(query_bias), value_bias])
    bias = lax.dynamic_slice_in_dim(bias, core * half, half, 1).reshape(1, -1)

    def qkv_table(c):
        return jnp.concatenate(
            [table(qkv_count, (2 * p + c) * qkv_count) for p in range(3)]
        )

    def to_attended(mine, theirs, down_grad, qkv_weight, bias, my_table, their_table, first_row):
        normed = jnp.concatenate([mine, swap(theirs)])
        theirs = times_columns(normed, qkv_weight, their_table, qkv_block, LOW)
        theirs = swap(theirs)
        mine = times_columns(normed, qkv_weight, my_table, qkv_block, F32)
        results = attend_forward(first_row, mine, theirs, bias)
        both = jnp.concatenate([normed, results[3]], 1)
        return [*results, swap(down_grad), both]

    queries, keys, values, attended, down_grad_theirs, early = segment(
        to_attended, mine, theirs, down_grad, qkv_weight, bias,
        qkv_table(core), qkv_table(other), first_row,
    )
    attended, down_mine = lax.optimization_barrier((attended, down_mine))
    early = gather_group(early)
    block = min(1024, inner_half)
    count = inner_half // block

    def to_inner(
        hidden, active, attended, out_weight, lines, up_weight, tables, core_number,
        grads, down_weight,
    ):
        out_part = dot(attended, out_weight, 1, 0)
        middle, mine, theirs = by_rows(
            norm_two_kernel,
            core_number,
            [(full, F32), (part, LOW), (part, LOW)],
            hidden,
            active,
            out_part,
            swap(out_part[rows:]),
            *lines[:3],
        )
        normed = jnp.concatenate([mine, swap(theirs)])
        theirs = times_columns(normed, up_weight, tables[1], block, LOW)
        theirs = swap(theirs)
        mine = times_columns(normed, up_weight, tables[0], block, F32)
        results = inner_layer(
            grads, down_weight, mine, theirs, lines[3], min(512, inner_half)
        )
        return [middle, normed, *results]

    bias = lax.dynamic_slice_in_dim(up_bias, core * inner_half, inner_half).reshape(1, -1)
    middle, normed_two_half, inner_low, up_grad, up_sums = segment(
        to_inner, hidden[0], active, attended, out_weight,
        (out_bias[None], ffn_gain[None], ffn_shift[None], bias), up_weight,
        (table(count, core * count), table(count, other * count)), core_number,
        jnp.concatenate([down_grad, down_grad_theirs]), down_weight,
    )
    (inner_low, up_grad), early = lax.optimization_barrier(((inner_low, up_grad), early))

    down_left = scatter_group(inner_low, 1, inner_half // GROUP)

    def to_middle(
        up_grad, up_weight, middle, gain, cotangent, active, core_number, down_mine, tables
    ):
        theirs = swap(up_grad)
        grads = times_back(up_grad, up_weight, tables[0], inner_half, 256)
        grads = times_back(theirs, up_weight, tables[1], inner_half, 256, grads, True)
        results = by_rows(
            norm_two_back_kernel,
            core_number,
            [(full, F32), (full, LOW), (line, F32), (line, F32), (line, F32)],
            middle,
            gain,
            grads,
            swap(grads[rows:]),
            cotangent,
            active,
        )
        down_theirs = swap(jnp.concatenate(down_mine[1:]))
        return [*results, down_theirs, *blocks_of(up_grad, 1, inner_half // GROUP)]

    (
        middle_grad, attn_grad, attn_sums, gain_two_grad, shift_two_grad, down_theirs, *up_right
    ) = segment(
        to_middle, up_grad, up_weight, middle, ffn_gain[None], cotangent[0], active,
        core_number, down_mine, (table(1, core), table(1, other)),
    )
    down_theirs = [(down_grad_theirs, 0)] + [(down_theirs, d) for d in range(GROUP - 1)]

    def down_product(first, steps):
        rights = []
        for own, (value, row) in zip(down_mine, down_theirs):
            rights.append(columns_from(own, rows, 0, first, quarter))
            rights.append(columns_from(value, rows, row, first, quarter))
        lefts = [(left, 0) for left in down_left]
        return rows_product(lefts, rights, inner_half // GROUP, quarter, steps)

    quarter = width // 4
    down_left, attn_grad = lax.optimization_barrier((down_left, attn_grad))
    up_right = exchange(up_right)
    sums = [down_product(0, 1)]
    (come,) = first_hop.send([(sums[0], inward)])
    attn_grad, sums[0] = lax.optimization_barrier((attn_grad, sums[0]))

    def to_qkv(attn_grad, out_weight, first_row, *operands):
        grads = jnp.concatenate([attn_grad, swap(attn_grad)])
        grads = dot(grads, out_weight, 1, 1).astype(LOW)
        qkv_grad = attend_backward(first_row, *operands, grads)
        flat = jnp.concatenate([qkv_grad[0], qkv_grad[1], qkv_grad[2]], 1)
        blocks = []
        for wide, block in zip(
            blocks_of(attn_grad, 1, width // GROUP), blocks_of(qkv_grad, 2, half // GROUP)
        ):
            narrow = wide.shape[1] // 2
            wide = jnp.concatenate([wide[:, :narrow], wide[:, narrow:]])
            blocks.append(jnp.concatenate([block, wide[None]]))
        return [qkv_grad, flat, swap(flat), *blocks]

    qkv_grad, flat, flat_theirs, *late = segment(to_qkv, attn_grad, out_weight, first_row, queries, keys, values)
    sums.append(down_product(1, 1))
    qkv_grad, up_right, come, sums = lax.optimization_barrier((qkv_grad, up_right, come, sums))
    sums[0] += come
    (passed,) = middle_hop.send([(sums[0], middle_moves)])
    (come,) = first_hop.send([(sums[1], inward)])
    up_left = gather_group(normed_two_half)

    def to_input(flat, theirs, qkv_weight, tables):
        grads = times_back(flat, qkv_weight, tables[0], qkv_block, 512)
        return [times_back(theirs, qkv_weight, tables[1], qkv_block, 512, grads, True)]

    (grads,) = segment(
        to_input, hold(flat, qkv_grad), flat_theirs, qkv_weight,
        (qkv_table(core), qkv_table(other)),
    )
    grads, up_left, passed, come = lax.optimization_barrier((grads, up_left, passed, come))
    sums[0] += passed
    sums[1] += come
    late = exchange(late)
    value = hold(down_product(2, 1), grads)
    come = first_hop.send([(value, inward)])
    passed, come, late = lax.optimization_barrier(
        (last_hop.send([(sums[0], outward)]), come, late)
    )
    sums[0] = jnp.where(end, passed[0], sums[0])
    sums.append(value + come[0])
    sums.append(line_start(hold(down_product(3, 1), late)))

    def to_ends(grads, hidden, gain, middle_grad, core_number, inner_low, down_weight):
        results = by_rows(
            norm_one_back_kernel,
            core_number,
            [(full, LOW), (line, F32), (line, F32)],
            hidden,
            gain,
            grads,
            swap(grads[rows:]),
            middle_grad,
        )
        down_part = dot(inner_low, down_weight, 1, 0)
        return [*results, down_part[:rows], swap(down_part[rows:])]

    input_grad, gain_one_grad, shift_one_grad, mine, theirs = to_ends(
        hold(grads, sums[0]), hidden[0], attn_gain[None], middle_grad, core_number,
        inner_low, down_weight,
    )
    output = middle + active * (mine + theirs + down_bias)

    def widen(value):
        none = jnp.zeros_like(value)
        return jnp.where(
            core == 0, jnp.concatenate([value, none]), jnp.concatenate([none, value])
        )

    qkv_sums = jnp.sum(qkv_grad.astype(F32), axis=1)
    small = jnp.concatenate(
        [
            widen(qkv_sums[0]),
            widen(qkv_sums[2]),
            attn_sums[0],
            widen(up_sums[0]),
            down_sums[0],
            gain_one_grad[0],
            shift_one_grad[0],
            gain_two_grad[0],
            shift_two_grad[0],
        ]
    ).reshape(-1, 128)
    small = small + swap(small)

    small_sends = [(small, in_plane(d)) for d in range(1, GROUP)]

    def pair_sums(values):
        while len(values) > 1:
            values = [a + b for a, b in zip(values[::2], values[1::2])]
        return values[0]

    def line_moves(distance):
        return [(i, (i // plane ^ distance) * plane + i % plane) for i in range(chips)]

    chunks = [("down", value, index) for index, value in enumerate(sums)]
    chunks += [("up", None, 2 * GROUP * core), ("up", None, 2 * GROUP * core + 1)]
    chunks += [("up", None, 2 * GROUP * other), ("up", None, 2 * GROUP * other + 1)]
    chunks += [("qkv", None, core), ("qkv", None, other), ("out", None, 0)]
    up_width = inner_half // GROUP
    up_block = min(512, up_width)

    def to_up(*operands):
        lefts = [(left, 0) for left in operands[:GROUP]]
        mine = operands[GROUP:]
        theirs = swap(jnp.concatenate(mine))
        results = []
        for first in range(inner_half // GROUP // up_block):
            rights = [columns_from(right, length, 0, first, up_block) for right in mine]
            results.append(rows_product(lefts, rights, half, up_block, 1))
        for first in range(inner_half // GROUP // up_block):
            rights = [columns_from(theirs, length, d, first, up_block) for d in range(GROUP)]
            results.append(rows_product(lefts, rights, half, up_block, 1, True))
        return results

    rest_block = half // GROUP

    def to_rest(*operands):
        early, mine = operands[:GROUP], operands[GROUP:]
        theirs = swap(jnp.concatenate(mine))

        def part(value, d):
            return value, (1, length, rest_block), lambda j: (4 * d + j, 0, 0)

        def out_part(value, d):
            return value, (1, rows, rest_block), lambda j: (4 * d + 3, j, 0)

        lefts = [(left, 0) for left in early]
        rights = [part(right, 0) for right in mine]
        own = rows_product(lefts, rights, half, rest_block, 3)
        rights = [part(theirs, d) for d in range(GROUP)]
        other_half = rows_product(lefts, rights, half, rest_block, 3, True)
        lefts = [(left, 1) for left in early]
        rights = []
        for d, right in enumerate(mine):
            rights += [out_part(right, 0), out_part(theirs, d)]
        return [own, other_half, rows_product(lefts, rights, half, rest_block, 2)]

    wholes = {
        "down": blank((inner_half, width)),
        "up": blank((half, inner)),
        "out": blank((half, width)),
        "qkv": blank((half, 3 * width)),
    }
    size = inner_half // GROUP
    begun, raw = sums, []
    done = [(), ()]
    for index, (name, value, where) in enumerate(chunks):
        value = begun[index]
        more, held = (), [done[-1]]
        if index == 0:
            held.append(begun[3])
        if index == 1:
            raw += segment(to_up, *hold(up_left, late), *up_right)
            held.append(raw)
        if index == 4:
            rest = segment(to_rest, *early, *late)
            raw += rest
            held.append(rest)
        if index == len(chunks) - 2:
            more = small_sends
        if index == len(chunks) - 1:
            small = pair_sums([small, *more_results])
            distance = GROUP
            while distance < plane:
                small = small + lax.ppermute(small, "dp", in_plane(distance))
                distance *= 2
            lines = [lax.ppermute(small, "dp", line_moves(d)) for d in range(1, LINE)]
            held += [done[-1], lines]
        after = (), held
        if 0 < index < len(chunks) - 1:
            value = line_end(line_middle(value))
        if index == len(chunks) - 2:
            begun[-1] = line_end(line_middle(begun[-1]))
            held.append(begun[-1])
        pieces, more_results = spread(blocks_sum(value), after, more)
        value = pieces[0]
        tall, wide = value.shape
        high = min(256, tall)
        broad = wide // 3 if name == "qkv" else wide
        places = []
        for d in range(GROUP):
            owner = spot ^ d
            for i in range(tall // high):
                row = jnp.int32(i)
                if name == "down":
                    row, columns = owner * (tall // high) + i, [jnp.int32(where)]
                elif name == "up":
                    columns = [where + owner * (size // wide)]
                elif name == "out":
                    columns = [owner]
                else:
                    columns = [(2 * p + where) * GROUP + owner for p in range(3)]
                for column in columns:
                    places += [row, column]
        wholes[name] = place(pieces, wholes[name], places, high, broad)
        done.append(wholes[name])
        while len(begun) < len(chunks) and raw:
            number = len(begun)
            placed = number - (4 if number < 8 else 5)
            if placed > index:
                break
            begun.append(line_start(hold(raw.pop(0), done[placed + 2])))

    small = pair_sums([small, *lines]).reshape(-1)
    small_grads = []
    first = 0
    for size in (width, width, width, inner, width, width, width, width, width):
        small_grads.append(small[first : first + size])
        first += size

    return (
        output.astype(LOW)[None],
        input_grad[None],
        wholes["qkv"],
        wholes["out"],
        wholes["up"],
        wholes["down"],
        *small_grads,
    )


def solution(mesh):
    return jax.shard_map(
        per_device,
        mesh=mesh,
        in_specs=(
            P("dp", "sp", None),
            P("dp", "sp", None),
            P("dp", None),
            P("sp", None),
            P("sp", None),
            P("sp", None),
            P("sp", None),
            P(),
            P(),
            P(),
            P(),
            P(),
            P(),
            P(),
            P(),
            P(),
        ),
        out_specs=(
            P("dp", "sp", None),
            P("dp", "sp", None),
            P("sp", None),
            P("sp", None),
            P("sp", None),
            P("sp", None),
            P(),
            P(),
            P(),
            P(),
            P(),
            P(),
            P(),
            P(),
            P(),
        ),
        check_vma=False,
    )
```

```python
import functools

import jax
import jax.numpy as jnp
from jax import lax
from jax.experimental import pallas as pl
from jax.experimental.pallas import tpu as pltpu
from jax.sharding import PartitionSpec as P

HEAD_DIM = 64
TILE = 128
LAYER = 12
LINE = 4
STREAMS = 1
GROUP = 4
F32 = jnp.float32
LOW = jnp.bfloat16


def layer_norm(values, gain, shift):
    center = jnp.mean(values, axis=-1, keepdims=True)
    centered = values - center
    variance = jnp.mean(centered * centered, axis=-1, keepdims=True)
    return centered * lax.rsqrt(variance + 1e-05) * gain + shift


def active_rows(bounds, first_row, row_count, sequence_length):
    position = first_row + jnp.arange(row_count, dtype=jnp.int32)
    tile_start = position // TILE * TILE
    exit_layer = bounds[1] - (bounds[1] - bounds[0]) * tile_start // sequence_length
    return (exit_layer > LAYER).astype(F32)[:, None]


def gelu_and_slope(values):
    scale = (2.0 / jnp.pi) ** 0.5
    square = values * values
    bend = jnp.tanh(scale * values * (1.0 + 0.044715 * square))
    rise = 0.5 * (1.0 + bend)
    slope = rise + 0.5 * values * (1.0 - bend * bend) * scale * (1.0 + 0.134145 * square)
    return values * rise, slope


def dot(left, right, left_dim, right_dim):
    return lax.dot_general(
        left, right, (((left_dim,), (right_dim,)), ((), ())), preferred_element_type=F32
    )


def roll_rows(value):
    rows = value.shape[0] // 2
    return jnp.concatenate([value[rows:], value[:rows]])


def estimate(flops, size):
    return pl.CostEstimate(flops=flops // 4, bytes_accessed=size // 4, transcendentals=0)


def far(value):
    return pltpu.with_memory_space_constraint(value, pltpu.HBM)


def limit(mebibytes):
    return pltpu.CompilerParams(vmem_limit_bytes=mebibytes << 20)


def halves(core_ref, values, mine_ref, theirs_ref):
    width = mine_ref.shape[1]
    first = core_ref[0] == 0
    low, high = values[:, :width], values[:, width:]
    mine_ref[...] = jnp.where(first, low, high).astype(LOW)
    theirs_ref[...] = jnp.where(first, high, low).astype(LOW)


def norm_one_kernel(
    core_ref, x_ref, gain_ref, shift_ref, grad_ref, active_ref,
    mine_ref, theirs_ref, masked_ref, sum_ref,
):
    normed = layer_norm(x_ref[...].astype(F32), gain_ref[...], shift_ref[...])
    halves(core_ref, normed, mine_ref, theirs_ref)
    masked = active_ref[...] * grad_ref[...].astype(F32)
    masked_ref[...] = masked.astype(LOW)
    sum_ref[...] = jnp.sum(masked, axis=0, keepdims=True)


def norm_two_kernel(
    core_ref, x_ref, active_ref, part_ref, theirs_part_ref, bias_ref, gain_ref, shift_ref,
    middle_ref, mine_ref, theirs_ref,
):
    rows = x_ref.shape[0]
    attn = part_ref[:rows] + theirs_part_ref[...] + bias_ref[...]
    middle = x_ref[...].astype(F32) + active_ref[...] * attn
    middle_ref[...] = middle
    halves(core_ref, layer_norm(middle, gain_ref[...], shift_ref[...]), mine_ref, theirs_ref)


def norm_back(core_ref, value_ref, gain_ref, mine_ref, theirs_ref, gain_out_ref, shift_out_ref):
    values = value_ref[...].astype(F32)
    mine, theirs = mine_ref[: values.shape[0]], theirs_ref[...]
    grads = jnp.where(
        core_ref[0] == 0,
        jnp.concatenate([mine, theirs], 1),
        jnp.concatenate([theirs, mine], 1),
    )
    centered = values - jnp.mean(values, axis=-1, keepdims=True)
    scale = lax.rsqrt(jnp.mean(centered * centered, axis=-1, keepdims=True) + 1e-05)
    unit = centered * scale
    gain_out_ref[...] = jnp.sum(grads * unit, axis=0, keepdims=True)
    shift_out_ref[...] = jnp.sum(grads, axis=0, keepdims=True)
    grads = grads * gain_ref[...]
    inner = jnp.mean(grads * unit, axis=-1, keepdims=True)
    return scale * (grads - jnp.mean(grads, axis=-1, keepdims=True) - unit * inner)


def norm_two_back_kernel(
    core_ref, value_ref, gain_ref, mine_ref, theirs_ref, grad_ref, active_ref,
    total_ref, masked_ref, sum_ref, gain_out_ref, shift_out_ref,
):
    part = norm_back(
        core_ref, value_ref, gain_ref, mine_ref, theirs_ref, gain_out_ref, shift_out_ref
    )
    total = grad_ref[...].astype(F32) + part
    total_ref[...] = total
    masked = (active_ref[...] * total).astype(LOW)
    masked_ref[...] = masked
    sum_ref[...] = jnp.sum(masked.astype(F32), axis=0, keepdims=True)


def norm_one_back_kernel(
    core_ref, value_ref, gain_ref, mine_ref, theirs_ref, grad_ref,
    total_ref, gain_out_ref, shift_out_ref,
):
    part = norm_back(
        core_ref, value_ref, gain_ref, mine_ref, theirs_ref, gain_out_ref, shift_out_ref
    )
    total_ref[...] = (grad_ref[...].astype(F32) + part).astype(LOW)


def by_rows(kernel, core, outs, *operands):
    vmem = pl.BlockSpec(memory_space=pltpu.VMEM)
    return pl.pallas_call(
        kernel,
        in_specs=[pl.BlockSpec(memory_space=pltpu.SMEM)] + [vmem] * len(operands),
        out_specs=[vmem] * len(outs),
        out_shape=[jax.ShapeDtypeStruct(shape, dtype) for shape, dtype in outs],
        compiler_params=limit(24),
        cost_estimate=estimate(
            20 * operands[0].size, sum(o.size * o.dtype.itemsize for o in operands)
        ),
    )(core, *operands)


def product_kernel(count, turned, *refs):
    lefts, out_ref, left_turned, right = refs[:count], refs[-3], refs[-2], refs[-1]
    rights = refs[count:-3]
    length = lefts[0].shape[0]

    @pl.when(pl.program_id(0) == 0)
    def _():
        for d, left in enumerate(lefts):
            left_turned[:, d * length : (d + 1) * length] = left[...].T

    row = 0
    for piece in rights:
        value = piece[0] if len(piece.shape) == 3 else piece[...]
        if turned:
            value = roll_rows(value)
        right[row : row + value.shape[0]] = value
        row += value.shape[0]
    out_ref[...] = dot(left_turned[...], right[...], 1, 0).astype(LOW)


def rows_product(lefts, rights, tall, block, steps, turned=False):
    length = lefts[0][0].shape[0]
    left_specs = [
        pl.BlockSpec((length, tall), functools.partial(lambda c, j: (0, c), c)) for _, c in lefts
    ]
    right_specs = [pl.BlockSpec(shape, place) for _, shape, place in rights]
    total = length * len(lefts)
    return pl.pallas_call(
        functools.partial(product_kernel, len(lefts), turned),
        grid=(steps,),
        in_specs=left_specs + right_specs,
        out_specs=pl.BlockSpec((tall, block), lambda j: (0, j)),
        out_shape=jax.ShapeDtypeStruct((tall, steps * block), LOW),
        scratch_shapes=[pltpu.VMEM((tall, total), LOW), pltpu.VMEM((total, block), LOW)],
        compiler_params=limit(32),
        cost_estimate=estimate(
            2 * tall * total * steps * block, 2 * total * (tall + steps * block)
        ),
    )(*[left[0] for left in lefts], *[right[0] for right in rights])


def columns_from(value, rows, row, first, block):
    return value, (rows, block), lambda j: (row, first + j)


def hold(values, after):
    return lax.optimization_barrier((values, after))[0]


def columns_kernel(table_ref, left_ref, *refs):
    total, first = 0.0, 0
    for weight_ref in refs[:-1]:
        depth = weight_ref.shape[0]
        total += dot(left_ref[:, first : first + depth], weight_ref[...], 1, 0)
        first += depth
    refs[-1][...] = total.astype(refs[-1].dtype)


def times_columns(left, weight, table, block, dtype):
    rows, depth = left.shape
    steps = table.shape[0]
    return pl.pallas_call(
        columns_kernel,
        grid_spec=pltpu.PrefetchScalarGridSpec(
            num_scalar_prefetch=1,
            grid=(steps,),
            in_specs=[
                pl.BlockSpec((rows, depth), lambda i, t: (0, 0)),
                *[
                    pl.BlockSpec(
                        (depth // STREAMS, block),
                        functools.partial(lambda r, i, t: (r, t[i]), r),
                    )
                    for r in range(STREAMS)
                ],
            ],
            out_specs=pl.BlockSpec((rows, block), lambda i, t: (0, i)),
        ),
        out_shape=jax.ShapeDtypeStruct((rows, steps * block), dtype),
        compiler_params=limit(24),
        cost_estimate=estimate(2 * rows * depth * steps * block, 2 * depth * (rows + steps * block) + 4 * rows * steps * block),
    )(table, left, *[far(weight)] * STREAMS)


def back_kernel(turned, table_ref, left_ref, *refs):
    weights, out_ref = refs[:STREAMS], refs[-1]
    starts = refs[STREAMS:-1]
    left = left_ref[...]
    if turned:
        left = roll_rows(left)
    first = 0
    for weight_ref in weights:
        deep = weight_ref.shape[0]
        part = dot(left, weight_ref[...], 1, 1)
        columns = slice(first, first + deep)
        first += deep

        @pl.when(pl.program_id(1) == 0)
        def _(part=part, columns=columns):
            out_ref[:, columns] = part + starts[0][:, columns] if starts else part

        @pl.when(pl.program_id(1) > 0)
        def _(part=part, columns=columns):
            out_ref[:, columns] += part


def times_back(left, weight, table, block, deep, start=None, turned=False):
    rows = left.shape[0]
    depth = weight.shape[0]
    steps = table.shape[0]
    out_spec = pl.BlockSpec((rows, deep), lambda k, i, t: (0, k))
    in_specs = [
        pl.BlockSpec((rows, block), lambda k, i, t: (0, i)),
        *[
            pl.BlockSpec(
                (deep // STREAMS, block),
                functools.partial(lambda r, k, i, t: (k * STREAMS + r, t[i]), r),
            )
            for r in range(STREAMS)
        ],
    ]
    operands = [table, left, *[far(weight)] * STREAMS]
    if start is not None:
        in_specs.append(out_spec)
        operands.append(start)
    return pl.pallas_call(
        functools.partial(back_kernel, turned),
        grid_spec=pltpu.PrefetchScalarGridSpec(
            num_scalar_prefetch=1,
            grid=(depth // deep, steps),
            in_specs=in_specs,
            out_specs=out_spec,
        ),
        out_shape=jax.ShapeDtypeStruct((rows, depth), F32),
        compiler_params=limit(32),
        cost_estimate=estimate(2 * rows * depth * steps * block, 2 * steps * block * (rows + depth) + 8 * rows * depth),
    )(*operands)


def inner_kernel(grad_ref, *refs):
    weights = refs[:STREAMS]
    mine_ref, theirs_ref, bias_ref, act_ref, out_ref, sum_ref = refs[STREAMS:]
    first = 0
    for weight_ref in weights:
        columns = slice(first, first + weight_ref.shape[0])
        first += weight_ref.shape[0]
        theirs = roll_rows(theirs_ref[:, columns])
        act, slope = gelu_and_slope(mine_ref[:, columns] + theirs + bias_ref[:, columns])
        act_ref[:, columns] = act.astype(LOW)
        grad = (dot(grad_ref[...], weight_ref[...], 1, 1) * slope).astype(LOW)
        out_ref[:, columns] = grad
        sum_ref[:, columns] = jnp.sum(grad.astype(F32), axis=0, keepdims=True)


def inner_layer(grads, weight, mine, theirs, bias, block):
    rows, width = grads.shape
    hidden = weight.shape[0]
    part = pl.BlockSpec((rows, block), lambda i: (0, i))
    line = pl.BlockSpec((1, block), lambda i: (0, i))
    return pl.pallas_call(
        inner_kernel,
        grid=(hidden // block,),
        in_specs=[
            pl.BlockSpec((rows, width), lambda i: (0, 0)),
            *[
                pl.BlockSpec(
                    (block // STREAMS, width),
                    functools.partial(lambda r, i: (i * STREAMS + r, 0), r),
                )
                for r in range(STREAMS)
            ],
            part,
            part,
            line,
        ],
        out_specs=[part, part, line],
        out_shape=[
            jax.ShapeDtypeStruct((rows, hidden), LOW),
            jax.ShapeDtypeStruct((rows, hidden), LOW),
            jax.ShapeDtypeStruct((1, hidden), F32),
        ],
        compiler_params=limit(32),
        cost_estimate=estimate(2 * rows * width * hidden, 2 * width * (rows + hidden) + 12 * rows * hidden),
    )(grads, *[far(weight)] * STREAMS, mine, theirs, bias)


def head_chances(queries, keys, lanes_of_head, allowed):
    keys_of_head = jnp.where(lanes_of_head, keys, jnp.zeros_like(keys))
    scores = dot(queries, keys_of_head, 1, 1) * (HEAD_DIM**-0.5)
    scores = jnp.where(allowed, scores, -1e30)
    raised = jnp.exp(scores - jnp.max(scores, axis=-1, keepdims=True))
    return raised / jnp.sum(raised, axis=-1, keepdims=True)


def attend_masks(first, length, lanes):
    lane = lax.broadcasted_iota(jnp.int32, (length, lanes), 1)
    row = lax.broadcasted_iota(jnp.int32, (length, length), 0) + first
    column = lax.broadcasted_iota(jnp.int32, (length, length), 1) + first
    row = jnp.where(row >= length, row - length, row)
    column = jnp.where(column >= length, column - length, column)
    return lane, column <= row


def attend_forward_kernel(first_ref, *refs):
    mine, theirs, biases, lows, o_ref = refs[:3], refs[3:6], refs[6:9], refs[9:12], refs[12]
    sums = [
        (m[...] + roll_rows(t[...]) + b[...]).astype(LOW)
        for m, t, b in zip(mine, theirs, biases)
    ]
    for low, value in zip(lows, sums):
        low[...] = value
    queries, keys, values = sums
    lane, allowed = attend_masks(first_ref[0], *queries.shape)
    total = jnp.zeros(queries.shape, F32)
    for head in range(queries.shape[1] // HEAD_DIM):
        own = lane // HEAD_DIM == head
        chances = head_chances(queries, keys, own, allowed).astype(LOW)
        total += dot(chances, jnp.where(own, values, jnp.zeros_like(values)), 1, 0)
    o_ref[...] = total.astype(LOW)


def attend_forward(first, mine, theirs, bias):
    length, width = mine.shape
    width //= 3
    steps = width // 128
    parts = [
        pl.BlockSpec((length, 128), functools.partial(lambda p, i, t: (0, p * steps + i), p))
        for p in range(3)
    ]
    lines = [
        pl.BlockSpec((1, 128), functools.partial(lambda p, i, t: (0, p * steps + i), p))
        for p in range(3)
    ]
    return pl.pallas_call(
        attend_forward_kernel,
        grid_spec=pltpu.PrefetchScalarGridSpec(
            num_scalar_prefetch=1,
            grid=(steps,),
            in_specs=parts + parts + lines,
            out_specs=[parts[0]] * 4,
        ),
        out_shape=[jax.ShapeDtypeStruct((length, width), LOW)] * 4,
        compiler_params=limit(16),
        cost_estimate=estimate(4 * length * length * width, 32 * length * width),
    )(first, mine, mine, mine, theirs, theirs, theirs, bias, bias, bias)


def attend_backward_kernel(first_ref, q_ref, k_ref, v_ref, g_ref, out_ref):
    queries, keys, values, grads = q_ref[...], k_ref[...], v_ref[...], g_ref[...]
    lane, allowed = attend_masks(first_ref[0], *queries.shape)
    dq = jnp.zeros(queries.shape, F32)
    dk = jnp.zeros(queries.shape, F32)
    dv = jnp.zeros(queries.shape, F32)
    for head in range(queries.shape[1] // HEAD_DIM):
        own = lane // HEAD_DIM == head
        chances = head_chances(queries, keys, own, allowed)
        head_grads = jnp.where(own, grads, jnp.zeros_like(grads))
        dv += dot(chances.astype(LOW), head_grads, 0, 0)
        chance_grads = dot(head_grads, values, 1, 1)
        inner = jnp.sum(chances * chance_grads, axis=-1, keepdims=True)
        score_grads = (chances * (chance_grads - inner)).astype(LOW)
        dq += dot(score_grads, jnp.where(own, keys, jnp.zeros_like(keys)), 1, 0)
        dk += dot(score_grads, jnp.where(own, queries, jnp.zeros_like(queries)), 0, 0)
    scale = HEAD_DIM**-0.5
    out_ref[0] = (dq * scale).astype(LOW)
    out_ref[1] = (dk * scale).astype(LOW)
    out_ref[2] = dv.astype(LOW)


def attend_backward(first, *operands):
    length, width = operands[0].shape
    block = pl.BlockSpec((length, 128), lambda i, t: (0, i))
    return pl.pallas_call(
        attend_backward_kernel,
        grid_spec=pltpu.PrefetchScalarGridSpec(
            num_scalar_prefetch=1,
            grid=(width // 128,),
            in_specs=[block] * 4,
            out_specs=pl.BlockSpec((3, length, 128), lambda i, t: (0, 0, i)),
        ),
        out_shape=jax.ShapeDtypeStruct((3, length, width), LOW),
        compiler_params=limit(16),
        cost_estimate=estimate(10 * length * length * width, 14 * length * width),
    )(first, *operands)


def place_kernel(high, table_ref, *refs):
    count = len(refs) - 4
    pieces, out_ref, held, sems = refs[:count], refs[-3], refs[-2], refs[-1]
    slots, broad = held.shape[0], held.shape[2]

    def copy(step):
        row = pl.multiple_of(table_ref[2 * step] * high, high)
        column = pl.multiple_of(table_ref[2 * step + 1] * broad, broad)
        return pltpu.make_async_copy(
            held.at[step % slots],
            out_ref.at[pl.ds(row, high), pl.ds(column, broad)],
            sems.at[step % slots],
        )

    step = 0
    for piece in pieces:
        for i in range(piece.shape[0] // high):
            for j in range(piece.shape[1] // broad):
                if step >= slots:
                    copy(step - slots).wait()
                part = piece[i * high : (i + 1) * high, j * broad : (j + 1) * broad]
                held[step % slots] = part.astype(F32)
                copy(step).start()
                step += 1
    for waited in range(max(step - slots, 0), step):
        copy(waited).wait()


def place(pieces, whole, places, high, broad):
    slots = 4
    vmem = pl.BlockSpec(memory_space=pltpu.VMEM)
    return pl.pallas_call(
        functools.partial(place_kernel, high),
        in_specs=[pl.BlockSpec(memory_space=pltpu.SMEM)]
        + [vmem] * len(pieces)
        + [pl.BlockSpec(memory_space=pl.ANY)],
        out_specs=pl.BlockSpec(memory_space=pl.ANY),
        out_shape=jax.ShapeDtypeStruct(whole.shape, F32),
        scratch_shapes=[
            pltpu.VMEM((slots, high, broad), F32),
            pltpu.SemaphoreType.DMA((slots,)),
        ],
        input_output_aliases={len(pieces) + 1: 0},
        compiler_params=limit(32),
        cost_estimate=estimate(0, sum(6 * p.size for p in pieces)),
    )(jnp.stack(places).astype(jnp.int32), *pieces, whole)


def blank_kernel(out_ref):
    pass


def blank(shape, dtype=F32):
    return pl.pallas_call(
        blank_kernel,
        out_specs=pl.BlockSpec(memory_space=pl.ANY),
        out_shape=jax.ShapeDtypeStruct(shape, dtype),
    )()


class Lane:
    def __init__(self):
        self.last = ()

    def send(self, sends, after=()):
        values = hold([v for v, _ in sends], (self.last, after))
        self.last = [lax.ppermute(v, "dp", m) for v, (_, m) in zip(values, sends)]
        return self.last


def per_device(
    hidden,
    cotangent,
    exit_layers,
    qkv_weight,
    out_weight,
    up_weight,
    down_weight,
    query_bias,
    value_bias,
    out_bias,
    up_bias,
    down_bias,
    attn_gain,
    attn_shift,
    ffn_gain,
    ffn_shift,
):
    core = lax.axis_index("sp")
    other = 1 - core
    chips = lax.axis_size("dp")
    plane = chips // LINE
    chip = lax.axis_index("dp")
    spot = chip % GROUP
    level = chip // plane
    rows = hidden.shape[1]
    width = hidden.shape[2]
    length = 2 * rows
    half = width // 2
    inner = up_weight.shape[1]
    inner_half = inner // 2
    across, first_hop, middle_hop, last_hop = (Lane() for _ in range(4))

    def swap(value):
        return lax.ppermute(value, "sp", [(0, 1), (1, 0)])

    def in_plane(distance):
        return [(i, i // plane * plane + ((i % plane) ^ distance)) for i in range(chips)]

    def along(*moves):
        return [(a * plane + i, b * plane + i) for a, b in moves for i in range(plane)]

    inward, middle_moves, outward = (
        along((0, 1), (3, 2)),
        along((1, 2), (2, 1)),
        along((1, 0), (2, 3)),
    )

    def split(value, axis, size):
        return (
            lax.dynamic_slice_in_dim(value, core * size, size, axis),
            lax.dynamic_slice_in_dim(value, other * size, size, axis),
        )

    def exchange(blocks):
        return blocks[:1] + across.send([(blocks[d], in_plane(d)) for d in range(1, GROUP)])

    def gather_group(value):
        return exchange([value] * GROUP)

    def blocks_of(value, axis, size):
        return [
            lax.dynamic_slice_in_dim(value, (spot ^ d) * size, size, axis) for d in range(GROUP)
        ]

    def scatter_group(value, axis, size):
        return exchange(blocks_of(value, axis, size))

    end = (level == 0) | (level == LINE - 1)

    def line_start(value, after=()):
        return value + hold(first_hop.send([(value, inward)])[0], after)

    def line_middle(value):
        return value + middle_hop.send([(value, middle_moves)])[0]

    def line_end(value):
        return jnp.where(end, last_hop.send([(value, outward)])[0], value)

    def blocks_sum(value):
        distance = GROUP
        while distance < plane:
            value = value + lax.ppermute(value, "dp", in_plane(distance))
            distance *= 2
        return value

    def spread(value, after, more=()):
        size = value.shape[0] // 2
        first, second = across.send([(value, in_plane(1)), (value, in_plane(2))], after[0])
        upper, lower, *more = across.send(
            [(first[:size], in_plane(2)), (second[size:], in_plane(1)), *more], after[1]
        )
        return [value, first, second, upper, lower], more

    def table(size, start, count=None):
        return jnp.arange(size if count is None else count, dtype=jnp.int32) + start

    active = active_rows(exit_layers[0], core * rows, rows, length)
    core_number = core.astype(jnp.int32)[None]
    first_row = (core * rows).astype(jnp.int32)[None]
    full, part, line = (rows, width), (rows, half), (1, width)

    always = exit_layers[0, 1] > 0

    def segment(steps, *operands):
        def skip(*_):
            return [blank(shape.shape, shape.dtype) for shape in jax.eval_shape(steps, *operands)]

        return lax.cond(always, lambda *o: list(steps(*o)), skip, *operands)

    mine, theirs, down_grad, down_sums = by_rows(
        norm_one_kernel,
        core_number,
        [(part, LOW), (part, LOW), (full, LOW), (line, F32)],
        hidden[0],
        attn_gain[None],
        attn_shift[None],
        cotangent[0],
        active,
    )
    down_mine = gather_group(down_grad)
    qkv_block = min(1024, half)
    qkv_count = half // qkv_block
    bias = jnp.stack([query_bias, jnp.zeros_like(query_bias), value_bias])
    bias = lax.dynamic_slice_in_dim(bias, core * half, half, 1).reshape(1, -1)

    def qkv_table(c):
        return jnp.concatenate(
            [table(qkv_count, (2 * p + c) * qkv_count) for p in range(3)]
        )

    def to_attended(mine, theirs, down_grad, qkv_weight, bias, my_table, their_table, first_row):
        normed = jnp.concatenate([mine, swap(theirs)])
        theirs = times_columns(normed, qkv_weight, their_table, qkv_block, LOW)
        theirs = swap(theirs)
        mine = times_columns(normed, qkv_weight, my_table, qkv_block, F32)
        results = attend_forward(first_row, mine, theirs, bias)
        both = jnp.concatenate([normed, results[3]], 1)
        return [*results, swap(down_grad), both]

    queries, keys, values, attended, down_grad_theirs, early = segment(
        to_attended, mine, theirs, down_grad, qkv_weight, bias,
        qkv_table(core), qkv_table(other), first_row,
    )
    attended, down_mine = lax.optimization_barrier((attended, down_mine))
    early = gather_group(early)
    block = min(1024, inner_half)
    count = inner_half // block

    def to_inner(
        hidden, active, attended, out_weight, lines, up_weight, tables, core_number,
        grads, down_weight,
    ):
        out_part = dot(attended, out_weight, 1, 0)
        middle, mine, theirs = by_rows(
            norm_two_kernel,
            core_number,
            [(full, F32), (part, LOW), (part, LOW)],
            hidden,
            active,
            out_part,
            swap(out_part[rows:]),
            *lines[:3],
        )
        normed = jnp.concatenate([mine, swap(theirs)])
        theirs = times_columns(normed, up_weight, tables[1], block, LOW)
        theirs = swap(theirs)
        mine = times_columns(normed, up_weight, tables[0], block, F32)
        results = inner_layer(
            grads, down_weight, mine, theirs, lines[3], min(512, inner_half)
        )
        return [middle, normed, *results]

    bias = lax.dynamic_slice_in_dim(up_bias, core * inner_half, inner_half).reshape(1, -1)
    middle, normed_two_half, inner_low, up_grad, up_sums = segment(
        to_inner, hidden[0], active, attended, out_weight,
        (out_bias[None], ffn_gain[None], ffn_shift[None], bias), up_weight,
        (table(count, core * count), table(count, other * count)), core_number,
        jnp.concatenate([down_grad, down_grad_theirs]), down_weight,
    )
    (inner_low, up_grad), early = lax.optimization_barrier(((inner_low, up_grad), early))

    down_left = scatter_group(inner_low, 1, inner_half // GROUP)

    def to_middle(
        up_grad, up_weight, middle, gain, cotangent, active, core_number, down_mine, tables
    ):
        theirs = swap(up_grad)
        grads = times_back(up_grad, up_weight, tables[0], inner_half, 256)
        grads = times_back(theirs, up_weight, tables[1], inner_half, 256, grads, True)
        results = by_rows(
            norm_two_back_kernel,
            core_number,
            [(full, F32), (full, LOW), (line, F32), (line, F32), (line, F32)],
            middle,
            gain,
            grads,
            swap(grads[rows:]),
            cotangent,
            active,
        )
        down_theirs = swap(jnp.concatenate(down_mine[1:]))
        return [*results, down_theirs, *blocks_of(up_grad, 1, inner_half // GROUP)]

    (
        middle_grad, attn_grad, attn_sums, gain_two_grad, shift_two_grad, down_theirs, *up_right
    ) = segment(
        to_middle, up_grad, up_weight, middle, ffn_gain[None], cotangent[0], active,
        core_number, down_mine, (table(1, core), table(1, other)),
    )
    down_theirs = [(down_grad_theirs, 0)] + [(down_theirs, d) for d in range(GROUP - 1)]

    def down_product(first, steps):
        rights = []
        for own, (value, row) in zip(down_mine, down_theirs):
            rights.append(columns_from(own, rows, 0, first, quarter))
            rights.append(columns_from(value, rows, row, first, quarter))
        lefts = [(left, 0) for left in down_left]
        return rows_product(lefts, rights, inner_half // GROUP, quarter, steps)

    quarter = width // 4
    down_left, attn_grad = lax.optimization_barrier((down_left, attn_grad))
    up_right = exchange(up_right)
    sums = [down_product(0, 1)]
    (come,) = first_hop.send([(sums[0], inward)])
    attn_grad, sums[0] = lax.optimization_barrier((attn_grad, sums[0]))

    def to_qkv(attn_grad, out_weight, first_row, *operands):
        grads = jnp.concatenate([attn_grad, swap(attn_grad)])
        grads = dot(grads, out_weight, 1, 1).astype(LOW)
        qkv_grad = attend_backward(first_row, *operands, grads)
        flat = jnp.concatenate([qkv_grad[0], qkv_grad[1], qkv_grad[2]], 1)
        blocks = []
        for wide, block in zip(
            blocks_of(attn_grad, 1, width // GROUP), blocks_of(qkv_grad, 2, half // GROUP)
        ):
            narrow = wide.shape[1] // 2
            wide = jnp.concatenate([wide[:, :narrow], wide[:, narrow:]])
            blocks.append(jnp.concatenate([block, wide[None]]))
        return [qkv_grad, flat, swap(flat), *blocks]

    qkv_grad, flat, flat_theirs, *late = segment(to_qkv, attn_grad, out_weight, first_row, queries, keys, values)
    sums.append(down_product(1, 1))
    qkv_grad, up_right, come, sums = lax.optimization_barrier((qkv_grad, up_right, come, sums))
    sums[0] += come
    (passed,) = middle_hop.send([(sums[0], middle_moves)])
    (come,) = first_hop.send([(sums[1], inward)])
    up_theirs = swap(jnp.concatenate(up_right))
    normed_two_half, up_theirs = lax.optimization_barrier((normed_two_half, up_theirs))
    up_left = gather_group(normed_two_half)

    def to_input(flat, theirs, qkv_weight, tables):
        grads = times_back(flat, qkv_weight, tables[0], qkv_block, 512)
        return [times_back(theirs, qkv_weight, tables[1], qkv_block, 512, grads, True)]

    (grads,) = segment(
        to_input, hold(flat, qkv_grad), flat_theirs, qkv_weight,
        (qkv_table(core), qkv_table(other)),
    )
    grads, up_left, passed, come = lax.optimization_barrier((grads, up_left, passed, come))
    sums[0] += passed
    sums[1] += come
    late = exchange(late)
    value = hold(down_product(2, 1), grads)
    come = first_hop.send([(value, inward)])
    passed, come, late = lax.optimization_barrier(
        (last_hop.send([(sums[0], outward)]), come, late)
    )
    late_theirs = swap(jnp.concatenate(late))
    passed, late_theirs = lax.optimization_barrier((passed, late_theirs))
    sums[0] = jnp.where(end, passed[0], sums[0])
    sums.append(value + come[0])
    sums.append(line_start(hold(down_product(3, 1), late)))

    def to_ends(grads, hidden, gain, middle_grad, core_number, inner_low, down_weight):
        results = by_rows(
            norm_one_back_kernel,
            core_number,
            [(full, LOW), (line, F32), (line, F32)],
            hidden,
            gain,
            grads,
            swap(grads[rows:]),
            middle_grad,
        )
        down_part = dot(inner_low, down_weight, 1, 0)
        return [*results, down_part[:rows], swap(down_part[rows:])]

    input_grad, gain_one_grad, shift_one_grad, mine, theirs = to_ends(
        hold(grads, sums[0]), hidden[0], attn_gain[None], middle_grad, core_number,
        inner_low, down_weight,
    )
    output = middle + active * (mine + theirs + down_bias)

    def widen(value):
        none = jnp.zeros_like(value)
        return jnp.where(
            core == 0, jnp.concatenate([value, none]), jnp.concatenate([none, value])
        )

    qkv_sums = jnp.sum(qkv_grad.astype(F32), axis=1)
    small = jnp.concatenate(
        [
            widen(qkv_sums[0]),
            widen(qkv_sums[2]),
            attn_sums[0],
            widen(up_sums[0]),
            down_sums[0],
            gain_one_grad[0],
            shift_one_grad[0],
            gain_two_grad[0],
            shift_two_grad[0],
        ]
    ).reshape(-1, 128)
    small = small + swap(small)

    small_sends = [(small, in_plane(d)) for d in range(1, GROUP)]

    def pair_sums(values):
        while len(values) > 1:
            values = [a + b for a, b in zip(values[::2], values[1::2])]
        return values[0]

    def line_moves(distance):
        return [(i, (i // plane ^ distance) * plane + i % plane) for i in range(chips)]

    chunks = [("down", value, index) for index, value in enumerate(sums)]
    chunks += [("up", None, 2 * GROUP * core), ("up", None, 2 * GROUP * core + 1)]
    chunks += [("up", None, 2 * GROUP * other), ("up", None, 2 * GROUP * other + 1)]
    chunks.append(("qkv", None, ((0, core), (1, core))))
    chunks.append(("qkv", None, ((2, core), (0, other))))
    chunks.append(("qkv", None, ((1, other), (2, other))))
    chunks.append(("out", None, 0))
    up_width = inner_half // GROUP
    up_block = min(512, up_width)

    def up_products(rights, turned):
        lefts = [(left, 0) for left in up_left]
        return [
            rows_product(lefts, [right(first) for right in rights], half, up_block, 1, turned)
            for first in range(up_width // up_block)
        ]

    def up_own():
        def place(right):
            return lambda first: columns_from(right, length, 0, first, up_block)

        return up_products([place(right) for right in hold(up_right, late)], False)

    def up_other(theirs):
        def place(d):
            return lambda first: columns_from(theirs, length, d, first, up_block)

        return up_products([place(d) for d in range(GROUP)], True)

    rest_block = half // GROUP

    def rest_product(rights, first, steps, turned):
        lefts = [(left, 0) for left in early]
        shape = (1, length, rest_block)
        rights = [
            (value, shape, functools.partial(lambda b, j: (b + j, 0, 0), 4 * d + first))
            for value, d in rights
        ]
        return rows_product(lefts, rights, half, rest_block, steps, turned)

    def rest_own(mine):
        rights = [(right, 0) for right in mine]
        return [rest_product(rights, 0, 2, False), rest_product(rights, 2, 1, False)]

    def rest_other(mine, theirs):
        def out_part(value, d):
            return value, (1, rows, rest_block), lambda j: (4 * d + 3, j, 0)

        rights = [(theirs, d) for d in range(GROUP)]
        results = [rest_product(rights, 0, 1, True), rest_product(rights, 1, 2, True)]
        lefts = [(left, 1) for left in early]
        rights = []
        for d, right in enumerate(mine):
            rights += [out_part(right, 0), out_part(theirs, d)]
        return [*results, rows_product(lefts, rights, half, rest_block, 2)]

    wholes = {
        "down": blank((inner_half, width)),
        "up": blank((half, inner)),
        "out": blank((half, width)),
        "qkv": blank((half, 3 * width)),
    }
    size = inner_half // GROUP
    begun, raw = sums, []
    middle, ended = [None, line_middle(begun[1])], [begun[0]]
    done = [(), ()]
    for index, (name, _, where) in enumerate(chunks):
        more, held = (), [done[-1]]
        if index == 0:
            held.append(begun[3])
        fresh = []
        if index == 0:
            fresh = up_own()
        if index == 1:
            fresh = up_other(hold(up_theirs, done[-1]))
        if index == 3:
            first_part, cut = rest_own(hold(late, done[-1]))
            fresh = [first_part]
        if index == 4:
            other_cut, *fresh = rest_other(*hold((late, late_theirs), done[-1]))
            fresh = [jnp.concatenate([cut, other_cut], 1), *fresh]
        raw += fresh
        held.append(fresh)
        if index + 1 < len(chunks):
            ended.append(line_end(middle[index + 1]))
        if index + 2 < len(chunks):
            middle.append(line_middle(begun[index + 2]))
        if index > 0:
            if index + 3 < len(chunks):
                begun.append(line_start(raw.pop(0)))
            held += [ended[index + 1 :], middle[index + 2 :], begun[index + 3 :]]
        else:
            held.append(begun[3])
        if index == len(chunks) - 2:
            more = small_sends
        if index == len(chunks) - 1:
            small = pair_sums([small, *more_results])
            distance = GROUP
            while distance < plane:
                small = small + lax.ppermute(small, "dp", in_plane(distance))
                distance *= 2
            lines = [lax.ppermute(small, "dp", line_moves(d)) for d in range(1, LINE)]
            held += [done[-1], lines]
        after = (), held
        value = ended[index]
        pieces, more_results = spread(blocks_sum(value), after, more)
        value = pieces[0]
        tall, wide = value.shape
        high = min(256, tall)
        broad = wide // 2 if name == "qkv" else wide
        places = []
        for d in range(GROUP):
            owner = spot ^ d
            for i in range(tall // high):
                row = jnp.int32(i)
                if name == "down":
                    row, columns = owner * (tall // high) + i, [jnp.int32(where)]
                elif name == "up":
                    columns = [where + owner * (size // wide)]
                elif name == "out":
                    columns = [owner]
                else:
                    columns = [(2 * p + c) * GROUP + owner for p, c in where]
                for column in columns:
                    places += [row, column]
        wholes[name] = place(pieces, wholes[name], places, high, broad)
        done.append(wholes[name])

    small = pair_sums([small, *lines]).reshape(-1)
    small_grads = []
    first = 0
    for size in (width, width, width, inner, width, width, width, width, width):
        small_grads.append(small[first : first + size])
        first += size

    return (
        output.astype(LOW)[None],
        input_grad[None],
        wholes["qkv"],
        wholes["out"],
        wholes["up"],
        wholes["down"],
        *small_grads,
    )


def solution(mesh):
    return jax.shard_map(
        per_device,
        mesh=mesh,
        in_specs=(
            P("dp", "sp", None),
            P("dp", "sp", None),
            P("dp", None),
            P("sp", None),
            P("sp", None),
            P("sp", None),
            P("sp", None),
            P(),
            P(),
            P(),
            P(),
            P(),
            P(),
            P(),
            P(),
            P(),
        ),
        out_specs=(
            P("dp", "sp", None),
            P("dp", "sp", None),
            P("sp", None),
            P("sp", None),
            P("sp", None),
            P("sp", None),
            P(),
            P(),
            P(),
            P(),
            P(),
            P(),
            P(),
            P(),
            P(),
        ),
        check_vma=False,
    )
```

```python
import functools

import jax
import jax.numpy as jnp
from jax import lax
from jax.experimental import pallas as pl
from jax.experimental.pallas import tpu as pltpu
from jax.sharding import PartitionSpec as P

HEAD_DIM = 64
TILE = 128
LAYER = 12
LINE = 4
STREAMS = 1
GROUP = 4
F32 = jnp.float32
LOW = jnp.bfloat16


def layer_norm(values, gain, shift):
    center = jnp.mean(values, axis=-1, keepdims=True)
    centered = values - center
    variance = jnp.mean(centered * centered, axis=-1, keepdims=True)
    return centered * lax.rsqrt(variance + 1e-05) * gain + shift


def active_rows(bounds, first_row, row_count, sequence_length):
    position = first_row + jnp.arange(row_count, dtype=jnp.int32)
    tile_start = position // TILE * TILE
    exit_layer = bounds[1] - (bounds[1] - bounds[0]) * tile_start // sequence_length
    return (exit_layer > LAYER).astype(F32)[:, None]


def gelu_and_slope(values):
    scale = (2.0 / jnp.pi) ** 0.5
    square = values * values
    bend = jnp.tanh(scale * values * (1.0 + 0.044715 * square))
    rise = 0.5 * (1.0 + bend)
    slope = rise + 0.5 * values * (1.0 - bend * bend) * scale * (1.0 + 0.134145 * square)
    return values * rise, slope


def dot(left, right, left_dim, right_dim):
    return lax.dot_general(
        left, right, (((left_dim,), (right_dim,)), ((), ())), preferred_element_type=F32
    )


def roll_rows(value):
    rows = value.shape[0] // 2
    return jnp.concatenate([value[rows:], value[:rows]])


def estimate(flops, size):
    return pl.CostEstimate(flops=flops // 4, bytes_accessed=size // 4, transcendentals=0)


def far(value):
    return pltpu.with_memory_space_constraint(value, pltpu.HBM)


def limit(mebibytes):
    return pltpu.CompilerParams(vmem_limit_bytes=mebibytes << 20)


def halves(core_ref, values, mine_ref, theirs_ref):
    width = mine_ref.shape[1]
    first = core_ref[0] == 0
    low, high = values[:, :width], values[:, width:]
    mine_ref[...] = jnp.where(first, low, high).astype(LOW)
    theirs_ref[...] = jnp.where(first, high, low).astype(LOW)


def norm_one_kernel(
    core_ref, x_ref, gain_ref, shift_ref, grad_ref, active_ref,
    mine_ref, theirs_ref, masked_ref, sum_ref,
):
    normed = layer_norm(x_ref[...].astype(F32), gain_ref[...], shift_ref[...])
    halves(core_ref, normed, mine_ref, theirs_ref)
    masked = active_ref[...] * grad_ref[...].astype(F32)
    masked_ref[...] = masked.astype(LOW)
    sum_ref[...] = jnp.sum(masked, axis=0, keepdims=True)


def norm_two_kernel(
    core_ref, x_ref, active_ref, part_ref, theirs_part_ref, bias_ref, gain_ref, shift_ref,
    middle_ref, mine_ref, theirs_ref,
):
    rows = x_ref.shape[0]
    attn = part_ref[:rows] + theirs_part_ref[...] + bias_ref[...]
    middle = x_ref[...].astype(F32) + active_ref[...] * attn
    middle_ref[...] = middle
    halves(core_ref, layer_norm(middle, gain_ref[...], shift_ref[...]), mine_ref, theirs_ref)


def norm_back(core_ref, value_ref, gain_ref, mine_ref, theirs_ref, gain_out_ref, shift_out_ref):
    values = value_ref[...].astype(F32)
    mine, theirs = mine_ref[: values.shape[0]], theirs_ref[...]
    grads = jnp.where(
        core_ref[0] == 0,
        jnp.concatenate([mine, theirs], 1),
        jnp.concatenate([theirs, mine], 1),
    )
    centered = values - jnp.mean(values, axis=-1, keepdims=True)
    scale = lax.rsqrt(jnp.mean(centered * centered, axis=-1, keepdims=True) + 1e-05)
    unit = centered * scale
    gain_out_ref[...] = jnp.sum(grads * unit, axis=0, keepdims=True)
    shift_out_ref[...] = jnp.sum(grads, axis=0, keepdims=True)
    grads = grads * gain_ref[...]
    inner = jnp.mean(grads * unit, axis=-1, keepdims=True)
    return scale * (grads - jnp.mean(grads, axis=-1, keepdims=True) - unit * inner)


def norm_two_back_kernel(
    core_ref, value_ref, gain_ref, mine_ref, theirs_ref, grad_ref, active_ref,
    total_ref, masked_ref, sum_ref, gain_out_ref, shift_out_ref,
):
    part = norm_back(
        core_ref, value_ref, gain_ref, mine_ref, theirs_ref, gain_out_ref, shift_out_ref
    )
    total = grad_ref[...].astype(F32) + part
    total_ref[...] = total
    masked = (active_ref[...] * total).astype(LOW)
    masked_ref[...] = masked
    sum_ref[...] = jnp.sum(masked.astype(F32), axis=0, keepdims=True)


def norm_one_back_kernel(
    core_ref, value_ref, gain_ref, mine_ref, theirs_ref, grad_ref,
    total_ref, gain_out_ref, shift_out_ref,
):
    part = norm_back(
        core_ref, value_ref, gain_ref, mine_ref, theirs_ref, gain_out_ref, shift_out_ref
    )
    total_ref[...] = (grad_ref[...].astype(F32) + part).astype(LOW)


def by_rows(kernel, core, outs, *operands):
    vmem = pl.BlockSpec(memory_space=pltpu.VMEM)
    return pl.pallas_call(
        kernel,
        in_specs=[pl.BlockSpec(memory_space=pltpu.SMEM)] + [vmem] * len(operands),
        out_specs=[vmem] * len(outs),
        out_shape=[jax.ShapeDtypeStruct(shape, dtype) for shape, dtype in outs],
        compiler_params=limit(24),
        cost_estimate=estimate(
            20 * operands[0].size, sum(o.size * o.dtype.itemsize for o in operands)
        ),
    )(core, *operands)


def product_kernel(count, turned, *refs):
    lefts, out_ref, left_turned, right = refs[:count], refs[-3], refs[-2], refs[-1]
    rights = refs[count:-3]
    length = lefts[0].shape[0]

    @pl.when(pl.program_id(0) == 0)
    def _():
        for d, left in enumerate(lefts):
            left_turned[:, d * length : (d + 1) * length] = left[...].T

    row = 0
    for piece in rights:
        value = piece[0] if len(piece.shape) == 3 else piece[...]
        if turned:
            value = roll_rows(value)
        right[row : row + value.shape[0]] = value
        row += value.shape[0]
    out_ref[...] = dot(left_turned[...], right[...], 1, 0).astype(LOW)


def rows_product(lefts, rights, tall, block, steps, turned=False):
    length = lefts[0][0].shape[0]
    left_specs = [
        pl.BlockSpec((length, tall), functools.partial(lambda c, j: (0, c), c)) for _, c in lefts
    ]
    right_specs = [pl.BlockSpec(shape, place) for _, shape, place in rights]
    total = length * len(lefts)
    return pl.pallas_call(
        functools.partial(product_kernel, len(lefts), turned),
        grid=(steps,),
        in_specs=left_specs + right_specs,
        out_specs=pl.BlockSpec((tall, block), lambda j: (0, j)),
        out_shape=jax.ShapeDtypeStruct((tall, steps * block), LOW),
        scratch_shapes=[pltpu.VMEM((tall, total), LOW), pltpu.VMEM((total, block), LOW)],
        compiler_params=limit(32),
        cost_estimate=estimate(
            2 * tall * total * steps * block, 2 * total * (tall + steps * block)
        ),
    )(*[left[0] for left in lefts], *[right[0] for right in rights])


def columns_from(value, rows, row, first, block):
    return value, (rows, block), lambda j: (row, first + j)


def hold(values, after):
    return lax.optimization_barrier((values, after))[0]


def columns_kernel(table_ref, left_ref, *refs):
    total, first = 0.0, 0
    for weight_ref in refs[:-1]:
        depth = weight_ref.shape[0]
        total += dot(left_ref[:, first : first + depth], weight_ref[...], 1, 0)
        first += depth
    refs[-1][...] = total.astype(refs[-1].dtype)


def times_columns(left, weight, table, block, dtype):
    rows, depth = left.shape
    steps = table.shape[0]
    return pl.pallas_call(
        columns_kernel,
        grid_spec=pltpu.PrefetchScalarGridSpec(
            num_scalar_prefetch=1,
            grid=(steps,),
            in_specs=[
                pl.BlockSpec((rows, depth), lambda i, t: (0, 0)),
                *[
                    pl.BlockSpec(
                        (depth // STREAMS, block),
                        functools.partial(lambda r, i, t: (r, t[i]), r),
                    )
                    for r in range(STREAMS)
                ],
            ],
            out_specs=pl.BlockSpec((rows, block), lambda i, t: (0, i)),
        ),
        out_shape=jax.ShapeDtypeStruct((rows, steps * block), dtype),
        compiler_params=limit(24),
        cost_estimate=estimate(2 * rows * depth * steps * block, 2 * depth * (rows + steps * block) + 4 * rows * steps * block),
    )(table, left, *[far(weight)] * STREAMS)


def back_kernel(turned, table_ref, left_ref, *refs):
    weights, out_ref = refs[:STREAMS], refs[-1]
    starts = refs[STREAMS:-1]
    left = left_ref[...]
    if turned:
        left = roll_rows(left)
    first = 0
    for weight_ref in weights:
        deep = weight_ref.shape[0]
        part = dot(left, weight_ref[...], 1, 1)
        columns = slice(first, first + deep)
        first += deep

        @pl.when(pl.program_id(1) == 0)
        def _(part=part, columns=columns):
            out_ref[:, columns] = part + starts[0][:, columns] if starts else part

        @pl.when(pl.program_id(1) > 0)
        def _(part=part, columns=columns):
            out_ref[:, columns] += part


def times_back(left, weight, table, block, deep, start=None, turned=False):
    rows = left.shape[0]
    depth = weight.shape[0]
    steps = table.shape[0]
    out_spec = pl.BlockSpec((rows, deep), lambda k, i, t: (0, k))
    in_specs = [
        pl.BlockSpec((rows, block), lambda k, i, t: (0, i)),
        *[
            pl.BlockSpec(
                (deep // STREAMS, block),
                functools.partial(lambda r, k, i, t: (k * STREAMS + r, t[i]), r),
            )
            for r in range(STREAMS)
        ],
    ]
    operands = [table, left, *[far(weight)] * STREAMS]
    if start is not None:
        in_specs.append(out_spec)
        operands.append(start)
    return pl.pallas_call(
        functools.partial(back_kernel, turned),
        grid_spec=pltpu.PrefetchScalarGridSpec(
            num_scalar_prefetch=1,
            grid=(depth // deep, steps),
            in_specs=in_specs,
            out_specs=out_spec,
        ),
        out_shape=jax.ShapeDtypeStruct((rows, depth), F32),
        compiler_params=limit(32),
        cost_estimate=estimate(2 * rows * depth * steps * block, 2 * steps * block * (rows + depth) + 8 * rows * depth),
    )(*operands)


def inner_kernel(grad_ref, *refs):
    weights = refs[:STREAMS]
    mine_ref, theirs_ref, bias_ref, act_ref, out_ref, sum_ref = refs[STREAMS:]
    first = 0
    for weight_ref in weights:
        columns = slice(first, first + weight_ref.shape[0])
        first += weight_ref.shape[0]
        theirs = roll_rows(theirs_ref[:, columns])
        act, slope = gelu_and_slope(mine_ref[:, columns] + theirs + bias_ref[:, columns])
        act_ref[:, columns] = act.astype(LOW)
        grad = (dot(grad_ref[...], weight_ref[...], 1, 1) * slope).astype(LOW)
        out_ref[:, columns] = grad
        sum_ref[:, columns] = jnp.sum(grad.astype(F32), axis=0, keepdims=True)


def inner_layer(grads, weight, mine, theirs, bias, block):
    rows, width = grads.shape
    hidden = weight.shape[0]
    part = pl.BlockSpec((rows, block), lambda i: (0, i))
    line = pl.BlockSpec((1, block), lambda i: (0, i))
    return pl.pallas_call(
        inner_kernel,
        grid=(hidden // block,),
        in_specs=[
            pl.BlockSpec((rows, width), lambda i: (0, 0)),
            *[
                pl.BlockSpec(
                    (block // STREAMS, width),
                    functools.partial(lambda r, i: (i * STREAMS + r, 0), r),
                )
                for r in range(STREAMS)
            ],
            part,
            part,
            line,
        ],
        out_specs=[part, part, line],
        out_shape=[
            jax.ShapeDtypeStruct((rows, hidden), LOW),
            jax.ShapeDtypeStruct((rows, hidden), LOW),
            jax.ShapeDtypeStruct((1, hidden), F32),
        ],
        compiler_params=limit(32),
        cost_estimate=estimate(2 * rows * width * hidden, 2 * width * (rows + hidden) + 12 * rows * hidden),
    )(grads, *[far(weight)] * STREAMS, mine, theirs, bias)


def head_chances(queries, keys, lanes_of_head, allowed):
    keys_of_head = jnp.where(lanes_of_head, keys, jnp.zeros_like(keys))
    scores = dot(queries, keys_of_head, 1, 1) * (HEAD_DIM**-0.5)
    scores = jnp.where(allowed, scores, -1e30)
    raised = jnp.exp(scores - jnp.max(scores, axis=-1, keepdims=True))
    return raised / jnp.sum(raised, axis=-1, keepdims=True)


def attend_masks(first, length, lanes):
    lane = lax.broadcasted_iota(jnp.int32, (length, lanes), 1)
    row = lax.broadcasted_iota(jnp.int32, (length, length), 0) + first
    column = lax.broadcasted_iota(jnp.int32, (length, length), 1) + first
    row = jnp.where(row >= length, row - length, row)
    column = jnp.where(column >= length, column - length, column)
    return lane, column <= row


def attend_forward_kernel(first_ref, *refs):
    mine, theirs, biases, lows, o_ref = refs[:3], refs[3:6], refs[6:9], refs[9:12], refs[12]
    sums = [
        (m[...] + roll_rows(t[...]) + b[...]).astype(LOW)
        for m, t, b in zip(mine, theirs, biases)
    ]
    for low, value in zip(lows, sums):
        low[...] = value
    queries, keys, values = sums
    lane, allowed = attend_masks(first_ref[0], *queries.shape)
    total = jnp.zeros(queries.shape, F32)
    for head in range(queries.shape[1] // HEAD_DIM):
        own = lane // HEAD_DIM == head
        chances = head_chances(queries, keys, own, allowed).astype(LOW)
        total += dot(chances, jnp.where(own, values, jnp.zeros_like(values)), 1, 0)
    o_ref[...] = total.astype(LOW)


def attend_forward(first, mine, theirs, bias):
    length, width = mine.shape
    width //= 3
    steps = width // 128
    parts = [
        pl.BlockSpec((length, 128), functools.partial(lambda p, i, t: (0, p * steps + i), p))
        for p in range(3)
    ]
    lines = [
        pl.BlockSpec((1, 128), functools.partial(lambda p, i, t: (0, p * steps + i), p))
        for p in range(3)
    ]
    return pl.pallas_call(
        attend_forward_kernel,
        grid_spec=pltpu.PrefetchScalarGridSpec(
            num_scalar_prefetch=1,
            grid=(steps,),
            in_specs=parts + parts + lines,
            out_specs=[parts[0]] * 4,
        ),
        out_shape=[jax.ShapeDtypeStruct((length, width), LOW)] * 4,
        compiler_params=limit(16),
        cost_estimate=estimate(4 * length * length * width, 32 * length * width),
    )(first, mine, mine, mine, theirs, theirs, theirs, bias, bias, bias)


def attend_backward_kernel(first_ref, q_ref, k_ref, v_ref, g_ref, out_ref):
    queries, keys, values, grads = q_ref[...], k_ref[...], v_ref[...], g_ref[...]
    lane, allowed = attend_masks(first_ref[0], *queries.shape)
    dq = jnp.zeros(queries.shape, F32)
    dk = jnp.zeros(queries.shape, F32)
    dv = jnp.zeros(queries.shape, F32)
    for head in range(queries.shape[1] // HEAD_DIM):
        own = lane // HEAD_DIM == head
        chances = head_chances(queries, keys, own, allowed)
        head_grads = jnp.where(own, grads, jnp.zeros_like(grads))
        dv += dot(chances.astype(LOW), head_grads, 0, 0)
        chance_grads = dot(head_grads, values, 1, 1)
        inner = jnp.sum(chances * chance_grads, axis=-1, keepdims=True)
        score_grads = (chances * (chance_grads - inner)).astype(LOW)
        dq += dot(score_grads, jnp.where(own, keys, jnp.zeros_like(keys)), 1, 0)
        dk += dot(score_grads, jnp.where(own, queries, jnp.zeros_like(queries)), 0, 0)
    scale = HEAD_DIM**-0.5
    out_ref[0] = (dq * scale).astype(LOW)
    out_ref[1] = (dk * scale).astype(LOW)
    out_ref[2] = dv.astype(LOW)


def attend_backward(first, *operands):
    length, width = operands[0].shape
    block = pl.BlockSpec((length, 128), lambda i, t: (0, i))
    return pl.pallas_call(
        attend_backward_kernel,
        grid_spec=pltpu.PrefetchScalarGridSpec(
            num_scalar_prefetch=1,
            grid=(width // 128,),
            in_specs=[block] * 4,
            out_specs=pl.BlockSpec((3, length, 128), lambda i, t: (0, 0, i)),
        ),
        out_shape=jax.ShapeDtypeStruct((3, length, width), LOW),
        compiler_params=limit(16),
        cost_estimate=estimate(10 * length * length * width, 14 * length * width),
    )(first, *operands)


def place_kernel(high, table_ref, *refs):
    count = len(refs) - 4
    pieces, out_ref, held, sems = refs[:count], refs[-3], refs[-2], refs[-1]
    slots, broad = held.shape[0], held.shape[2]

    def copy(step):
        row = pl.multiple_of(table_ref[2 * step] * high, high)
        column = pl.multiple_of(table_ref[2 * step + 1] * broad, broad)
        return pltpu.make_async_copy(
            held.at[step % slots],
            out_ref.at[pl.ds(row, high), pl.ds(column, broad)],
            sems.at[step % slots],
        )

    step = 0
    for piece in pieces:
        for i in range(piece.shape[0] // high):
            for j in range(piece.shape[1] // broad):
                if step >= slots:
                    copy(step - slots).wait()
                part = piece[i * high : (i + 1) * high, j * broad : (j + 1) * broad]
                held[step % slots] = part.astype(F32)
                copy(step).start()
                step += 1
    for waited in range(max(step - slots, 0), step):
        copy(waited).wait()


def place(pieces, whole, places, high, broad):
    slots = 4
    vmem = pl.BlockSpec(memory_space=pltpu.VMEM)
    return pl.pallas_call(
        functools.partial(place_kernel, high),
        in_specs=[pl.BlockSpec(memory_space=pltpu.SMEM)]
        + [vmem] * len(pieces)
        + [pl.BlockSpec(memory_space=pl.ANY)],
        out_specs=pl.BlockSpec(memory_space=pl.ANY),
        out_shape=jax.ShapeDtypeStruct(whole.shape, F32),
        scratch_shapes=[
            pltpu.VMEM((slots, high, broad), F32),
            pltpu.SemaphoreType.DMA((slots,)),
        ],
        input_output_aliases={len(pieces) + 1: 0},
        compiler_params=limit(32),
        cost_estimate=estimate(0, sum(6 * p.size for p in pieces)),
    )(jnp.stack(places).astype(jnp.int32), *pieces, whole)


def blank_kernel(out_ref):
    pass


def blank(shape, dtype=F32):
    return pl.pallas_call(
        blank_kernel,
        out_specs=pl.BlockSpec(memory_space=pl.ANY),
        out_shape=jax.ShapeDtypeStruct(shape, dtype),
    )()


class Lane:
    def __init__(self):
        self.last = ()

    def send(self, sends, after=()):
        values = hold([v for v, _ in sends], (self.last, after))
        self.last = [lax.ppermute(v, "dp", m) for v, (_, m) in zip(values, sends)]
        return self.last


def per_device(
    hidden,
    cotangent,
    exit_layers,
    qkv_weight,
    out_weight,
    up_weight,
    down_weight,
    query_bias,
    value_bias,
    out_bias,
    up_bias,
    down_bias,
    attn_gain,
    attn_shift,
    ffn_gain,
    ffn_shift,
):
    core = lax.axis_index("sp")
    other = 1 - core
    chips = lax.axis_size("dp")
    plane = chips // LINE
    chip = lax.axis_index("dp")
    spot = chip % GROUP
    level = chip // plane
    rows = hidden.shape[1]
    width = hidden.shape[2]
    length = 2 * rows
    half = width // 2
    inner = up_weight.shape[1]
    inner_half = inner // 2
    across, first_hop, middle_hop, last_hop = (Lane() for _ in range(4))

    def swap(value):
        return lax.ppermute(value, "sp", [(0, 1), (1, 0)])

    def in_plane(distance):
        return [(i, i // plane * plane + ((i % plane) ^ distance)) for i in range(chips)]

    def along(*moves):
        return [(a * plane + i, b * plane + i) for a, b in moves for i in range(plane)]

    inward, middle_moves, outward = (
        along((0, 1), (3, 2)),
        along((1, 2), (2, 1)),
        along((1, 0), (2, 3)),
    )

    def split(value, axis, size):
        return (
            lax.dynamic_slice_in_dim(value, core * size, size, axis),
            lax.dynamic_slice_in_dim(value, other * size, size, axis),
        )

    def exchange(blocks):
        return blocks[:1] + across.send([(blocks[d], in_plane(d)) for d in range(1, GROUP)])

    def gather_group(value):
        return exchange([value] * GROUP)

    def blocks_of(value, axis, size):
        return [
            lax.dynamic_slice_in_dim(value, (spot ^ d) * size, size, axis) for d in range(GROUP)
        ]

    def scatter_group(value, axis, size):
        return exchange(blocks_of(value, axis, size))

    end = (level == 0) | (level == LINE - 1)

    def line_start(value, after=()):
        return value + hold(first_hop.send([(value, inward)])[0], after)

    def line_middle(value):
        return value + middle_hop.send([(value, middle_moves)])[0]

    def line_end(value):
        return jnp.where(end, last_hop.send([(value, outward)])[0], value)

    def blocks_sum(value):
        distance = GROUP
        while distance < plane:
            value = value + lax.ppermute(value, "dp", in_plane(distance))
            distance *= 2
        return value

    def spread(value, after, more=()):
        size = value.shape[0] // 2
        first, second = across.send([(value, in_plane(1)), (value, in_plane(2))], after[0])
        upper, lower, *more = across.send(
            [(first[:size], in_plane(2)), (second[size:], in_plane(1)), *more], after[1]
        )
        return [value, first, second, upper, lower], more

    def table(size, start, count=None):
        return jnp.arange(size if count is None else count, dtype=jnp.int32) + start

    active = active_rows(exit_layers[0], core * rows, rows, length)
    core_number = core.astype(jnp.int32)[None]
    first_row = (core * rows).astype(jnp.int32)[None]
    full, part, line = (rows, width), (rows, half), (1, width)

    always = exit_layers[0, 1] > 0

    def segment(steps, *operands):
        def skip(*_):
            return [blank(shape.shape, shape.dtype) for shape in jax.eval_shape(steps, *operands)]

        return lax.cond(always, lambda *o: list(steps(*o)), skip, *operands)

    mine, theirs, down_grad, down_sums = by_rows(
        norm_one_kernel,
        core_number,
        [(part, LOW), (part, LOW), (full, LOW), (line, F32)],
        hidden[0],
        attn_gain[None],
        attn_shift[None],
        cotangent[0],
        active,
    )
    down_mine = gather_group(down_grad)
    qkv_block = min(1024, half)
    qkv_count = half // qkv_block
    bias = jnp.stack([query_bias, jnp.zeros_like(query_bias), value_bias])
    bias = lax.dynamic_slice_in_dim(bias, core * half, half, 1).reshape(1, -1)

    def qkv_table(c):
        return jnp.concatenate(
            [table(qkv_count, (2 * p + c) * qkv_count) for p in range(3)]
        )

    def to_attended(mine, theirs, down_grad, qkv_weight, bias, my_table, their_table, first_row):
        normed = jnp.concatenate([mine, swap(theirs)])
        theirs = times_columns(normed, qkv_weight, their_table, qkv_block, LOW)
        theirs = swap(theirs)
        mine = times_columns(normed, qkv_weight, my_table, qkv_block, F32)
        results = attend_forward(first_row, mine, theirs, bias)
        both = jnp.concatenate([normed, results[3]], 1)
        return [*results, swap(down_grad), both]

    queries, keys, values, attended, down_grad_theirs, early = segment(
        to_attended, mine, theirs, down_grad, qkv_weight, bias,
        qkv_table(core), qkv_table(other), first_row,
    )
    attended, down_mine = lax.optimization_barrier((attended, down_mine))
    early = gather_group(early)
    block = min(1024, inner_half)
    count = inner_half // block

    def to_inner(
        hidden, active, attended, out_weight, lines, up_weight, tables, core_number,
        grads, down_weight,
    ):
        out_part = dot(attended, out_weight, 1, 0)
        middle, mine, theirs = by_rows(
            norm_two_kernel,
            core_number,
            [(full, F32), (part, LOW), (part, LOW)],
            hidden,
            active,
            out_part,
            swap(out_part[rows:]),
            *lines[:3],
        )
        normed = jnp.concatenate([mine, swap(theirs)])
        theirs = times_columns(normed, up_weight, tables[1], block, LOW)
        theirs = swap(theirs)
        mine = times_columns(normed, up_weight, tables[0], block, F32)
        results = inner_layer(
            grads, down_weight, mine, theirs, lines[3], min(512, inner_half)
        )
        return [middle, normed, *results]

    bias = lax.dynamic_slice_in_dim(up_bias, core * inner_half, inner_half).reshape(1, -1)
    middle, normed_two_half, inner_low, up_grad, up_sums = segment(
        to_inner, hidden[0], active, attended, out_weight,
        (out_bias[None], ffn_gain[None], ffn_shift[None], bias), up_weight,
        (table(count, core * count), table(count, other * count)), core_number,
        jnp.concatenate([down_grad, down_grad_theirs]), down_weight,
    )
    (inner_low, up_grad), early = lax.optimization_barrier(((inner_low, up_grad), early))

    down_left = scatter_group(inner_low, 1, inner_half // GROUP)

    def to_middle(
        up_grad, up_weight, middle, gain, cotangent, active, core_number, down_mine, tables
    ):
        theirs = swap(up_grad)
        grads = times_back(up_grad, up_weight, tables[0], inner_half, 256)
        grads = times_back(theirs, up_weight, tables[1], inner_half, 256, grads, True)
        results = by_rows(
            norm_two_back_kernel,
            core_number,
            [(full, F32), (full, LOW), (line, F32), (line, F32), (line, F32)],
            middle,
            gain,
            grads,
            swap(grads[rows:]),
            cotangent,
            active,
        )
        down_theirs = swap(jnp.concatenate(down_mine[1:]))
        return [*results, down_theirs, *blocks_of(up_grad, 1, inner_half // GROUP)]

    (
        middle_grad, attn_grad, attn_sums, gain_two_grad, shift_two_grad, down_theirs, *up_right
    ) = segment(
        to_middle, up_grad, up_weight, middle, ffn_gain[None], cotangent[0], active,
        core_number, down_mine, (table(1, core), table(1, other)),
    )
    down_theirs = [(down_grad_theirs, 0)] + [(down_theirs, d) for d in range(GROUP - 1)]

    def down_product(first, steps):
        rights = []
        for own, (value, row) in zip(down_mine, down_theirs):
            rights.append(columns_from(own, rows, 0, first, quarter))
            rights.append(columns_from(value, rows, row, first, quarter))
        lefts = [(left, 0) for left in down_left]
        return rows_product(lefts, rights, inner_half // GROUP, quarter, steps)

    quarter = width // 4
    down_left, attn_grad = lax.optimization_barrier((down_left, attn_grad))
    up_right = exchange(up_right)
    sums = [down_product(0, 1)]
    (come,) = first_hop.send([(sums[0], inward)])
    attn_grad, sums[0] = lax.optimization_barrier((attn_grad, sums[0]))

    def to_qkv(attn_grad, out_weight, first_row, *operands):
        grads = jnp.concatenate([attn_grad, swap(attn_grad)])
        grads = dot(grads, out_weight, 1, 1).astype(LOW)
        qkv_grad = attend_backward(first_row, *operands, grads)
        flat = jnp.concatenate([qkv_grad[0], qkv_grad[1], qkv_grad[2]], 1)
        blocks = []
        for wide, block in zip(
            blocks_of(attn_grad, 1, width // GROUP), blocks_of(qkv_grad, 2, half // GROUP)
        ):
            narrow = wide.shape[1] // 2
            wide = jnp.concatenate([wide[:, :narrow], wide[:, narrow:]])
            blocks.append(jnp.concatenate([block, wide[None]]))
        return [qkv_grad, flat, swap(flat), *blocks]

    qkv_grad, flat, flat_theirs, *late = segment(to_qkv, attn_grad, out_weight, first_row, queries, keys, values)
    sums.append(down_product(1, 1))
    qkv_grad, up_right, come, sums = lax.optimization_barrier((qkv_grad, up_right, come, sums))
    sums[0] += come
    (passed,) = middle_hop.send([(sums[0], middle_moves)])
    (come,) = first_hop.send([(sums[1], inward)])
    up_left = gather_group(normed_two_half)

    def to_input(flat, theirs, qkv_weight, tables):
        grads = times_back(flat, qkv_weight, tables[0], qkv_block, 512)
        return [times_back(theirs, qkv_weight, tables[1], qkv_block, 512, grads, True)]

    (grads,) = segment(
        to_input, hold(flat, qkv_grad), flat_theirs, qkv_weight,
        (qkv_table(core), qkv_table(other)),
    )
    grads, up_left, passed, come = lax.optimization_barrier((grads, up_left, passed, come))
    sums[0] += passed
    sums[1] += come
    late = exchange(late)
    value = hold(down_product(2, 1), grads)
    come = first_hop.send([(value, inward)])
    passed, come, late = lax.optimization_barrier(
        (last_hop.send([(sums[0], outward)]), come, late)
    )
    sums[0] = jnp.where(end, passed[0], sums[0])
    sums.append(value + come[0])
    sums.append(line_start(hold(down_product(3, 1), late)))

    def to_ends(grads, hidden, gain, middle_grad, core_number, inner_low, down_weight):
        results = by_rows(
            norm_one_back_kernel,
            core_number,
            [(full, LOW), (line, F32), (line, F32)],
            hidden,
            gain,
            grads,
            swap(grads[rows:]),
            middle_grad,
        )
        down_part = dot(inner_low, down_weight, 1, 0)
        return [*results, down_part[:rows], swap(down_part[rows:])]

    input_grad, gain_one_grad, shift_one_grad, mine, theirs = to_ends(
        hold(grads, sums[0]), hidden[0], attn_gain[None], middle_grad, core_number,
        inner_low, down_weight,
    )
    output = middle + active * (mine + theirs + down_bias)

    def widen(value):
        none = jnp.zeros_like(value)
        return jnp.where(
            core == 0, jnp.concatenate([value, none]), jnp.concatenate([none, value])
        )

    qkv_sums = jnp.sum(qkv_grad.astype(F32), axis=1)
    small = jnp.concatenate(
        [
            widen(qkv_sums[0]),
            widen(qkv_sums[2]),
            attn_sums[0],
            widen(up_sums[0]),
            down_sums[0],
            gain_one_grad[0],
            shift_one_grad[0],
            gain_two_grad[0],
            shift_two_grad[0],
        ]
    ).reshape(-1, 128)
    small = small + swap(small)

    small_sends = [(small, in_plane(d)) for d in range(1, GROUP)]

    def pair_sums(values):
        while len(values) > 1:
            values = [a + b for a, b in zip(values[::2], values[1::2])]
        return values[0]

    def line_moves(distance):
        return [(i, (i // plane ^ distance) * plane + i % plane) for i in range(chips)]

    chunks = [("down", value, index) for index, value in enumerate(sums)]
    chunks += [("up", None, 2 * GROUP * core), ("up", None, 2 * GROUP * core + 1)]
    chunks += [("up", None, 2 * GROUP * other), ("up", None, 2 * GROUP * other + 1)]
    chunks += [("qkv", None, core), ("qkv", None, other), ("out", None, 0)]
    up_width = inner_half // GROUP
    up_block = min(512, up_width)

    def to_up(*operands):
        lefts = [(left, 0) for left in operands[:GROUP]]
        mine = operands[GROUP:]
        theirs = swap(jnp.concatenate(mine))
        results = []
        for first in range(inner_half // GROUP // up_block):
            rights = [columns_from(right, length, 0, first, up_block) for right in mine]
            results.append(rows_product(lefts, rights, half, up_block, 1))
        for first in range(inner_half // GROUP // up_block):
            rights = [columns_from(theirs, length, d, first, up_block) for d in range(GROUP)]
            results.append(rows_product(lefts, rights, half, up_block, 1, True))
        return results

    rest_block = half // GROUP

    def to_rest(*operands):
        early, mine = operands[:GROUP], operands[GROUP:]
        theirs = swap(jnp.concatenate(mine))

        def part(value, d):
            return value, (1, length, rest_block), lambda j: (4 * d + j, 0, 0)

        def out_part(value, d):
            return value, (1, rows, rest_block), lambda j: (4 * d + 3, j, 0)

        lefts = [(left, 0) for left in early]
        rights = [part(right, 0) for right in mine]
        own = rows_product(lefts, rights, half, rest_block, 3)
        rights = [part(theirs, d) for d in range(GROUP)]
        other_half = rows_product(lefts, rights, half, rest_block, 3, True)
        lefts = [(left, 1) for left in early]
        rights = []
        for d, right in enumerate(mine):
            rights += [out_part(right, 0), out_part(theirs, d)]
        return [own, other_half, rows_product(lefts, rights, half, rest_block, 2)]

    wholes = {
        "down": blank((inner_half, width)),
        "up": blank((half, inner)),
        "out": blank((half, width)),
        "qkv": blank((half, 3 * width)),
    }
    size = inner_half // GROUP
    begun, raw = sums, []
    done = [(), ()]
    for index, (name, value, where) in enumerate(chunks):
        value = begun[index]
        more, held = (), [done[-1]]
        if index == 0:
            held.append(begun[3])
        if index == 1:
            raw += segment(to_up, *hold(up_left, late), *up_right)
            held.append(raw)
        if index == 4:
            rest = segment(to_rest, *early, *late)
            raw += rest
            held.append(rest)
        if index == len(chunks) - 2:
            more = small_sends
        if index == len(chunks) - 1:
            small = pair_sums([small, *more_results])
            distance = GROUP
            while distance < plane:
                small = small + lax.ppermute(small, "dp", in_plane(distance))
                distance *= 2
            lines = [lax.ppermute(small, "dp", line_moves(d)) for d in range(1, LINE)]
            held += [done[-1], lines]
        after = (), held
        if 0 < index < len(chunks) - 1:
            value = line_end(line_middle(value))
        if index == len(chunks) - 2:
            last = line_middle(begun[-1])
            held.append(last)
            begun[-1] = line_end(last)
        pieces, more_results = spread(blocks_sum(value), after, more)
        value = pieces[0]
        tall, wide = value.shape
        high = min(256, tall)
        broad = wide // 3 if name == "qkv" else wide
        places = []
        for d in range(GROUP):
            owner = spot ^ d
            for i in range(tall // high):
                row = jnp.int32(i)
                if name == "down":
                    row, columns = owner * (tall // high) + i, [jnp.int32(where)]
                elif name == "up":
                    columns = [where + owner * (size // wide)]
                elif name == "out":
                    columns = [owner]
                else:
                    columns = [(2 * p + where) * GROUP + owner for p in range(3)]
                for column in columns:
                    places += [row, column]
        wholes[name] = place(pieces, wholes[name], places, high, broad)
        done.append(wholes[name])
        while len(begun) < len(chunks) and raw:
            number = len(begun)
            placed = number - (4 if number < 8 else 5)
            if placed > index:
                break
            begun.append(line_start(hold(raw.pop(0), done[placed + 2])))

    small = pair_sums([small, *lines]).reshape(-1)
    small_grads = []
    first = 0
    for size in (width, width, width, inner, width, width, width, width, width):
        small_grads.append(small[first : first + size])
        first += size

    return (
        output.astype(LOW)[None],
        input_grad[None],
        wholes["qkv"],
        wholes["out"],
        wholes["up"],
        wholes["down"],
        *small_grads,
    )


def solution(mesh):
    return jax.shard_map(
        per_device,
        mesh=mesh,
        in_specs=(
            P("dp", "sp", None),
            P("dp", "sp", None),
            P("dp", None),
            P("sp", None),
            P("sp", None),
            P("sp", None),
            P("sp", None),
            P(),
            P(),
            P(),
            P(),
            P(),
            P(),
            P(),
            P(),
            P(),
        ),
        out_specs=(
            P("dp", "sp", None),
            P("dp", "sp", None),
            P("sp", None),
            P("sp", None),
            P("sp", None),
            P("sp", None),
            P(),
            P(),
            P(),
            P(),
            P(),
            P(),
            P(),
            P(),
            P(),
        ),
        check_vma=False,
    )
```

```python
import functools

import jax
import jax.numpy as jnp
from jax import lax
from jax.experimental import pallas as pl
from jax.experimental.pallas import tpu as pltpu
from jax.sharding import PartitionSpec as P

HEAD_DIM = 64
TILE = 128
LAYER = 12
LINE = 4
STREAMS = 1
GROUP = 4
F32 = jnp.float32
LOW = jnp.bfloat16


def layer_norm(values, gain, shift):
    center = jnp.mean(values, axis=-1, keepdims=True)
    centered = values - center
    variance = jnp.mean(centered * centered, axis=-1, keepdims=True)
    return centered * lax.rsqrt(variance + 1e-05) * gain + shift


def active_rows(bounds, first_row, row_count, sequence_length):
    position = first_row + jnp.arange(row_count, dtype=jnp.int32)
    tile_start = position // TILE * TILE
    exit_layer = bounds[1] - (bounds[1] - bounds[0]) * tile_start // sequence_length
    return (exit_layer > LAYER).astype(F32)[:, None]


def gelu_and_slope(values):
    scale = (2.0 / jnp.pi) ** 0.5
    square = values * values
    bend = jnp.tanh(scale * values * (1.0 + 0.044715 * square))
    rise = 0.5 * (1.0 + bend)
    slope = rise + 0.5 * values * (1.0 - bend * bend) * scale * (1.0 + 0.134145 * square)
    return values * rise, slope


def dot(left, right, left_dim, right_dim):
    return lax.dot_general(
        left, right, (((left_dim,), (right_dim,)), ((), ())), preferred_element_type=F32
    )


def roll_rows(value):
    rows = value.shape[0] // 2
    return jnp.concatenate([value[rows:], value[:rows]])


def estimate(flops, size):
    return pl.CostEstimate(flops=flops // 4, bytes_accessed=size // 4, transcendentals=0)


def far(value):
    return pltpu.with_memory_space_constraint(value, pltpu.HBM)


def limit(mebibytes):
    return pltpu.CompilerParams(vmem_limit_bytes=mebibytes << 20)


def halves(core_ref, values, mine_ref, theirs_ref):
    width = mine_ref.shape[1]
    first = core_ref[0] == 0
    low, high = values[:, :width], values[:, width:]
    mine_ref[...] = jnp.where(first, low, high).astype(LOW)
    theirs_ref[...] = jnp.where(first, high, low).astype(LOW)


def norm_one_kernel(
    core_ref, x_ref, gain_ref, shift_ref, grad_ref, active_ref,
    mine_ref, theirs_ref, masked_ref, sum_ref,
):
    normed = layer_norm(x_ref[...].astype(F32), gain_ref[...], shift_ref[...])
    halves(core_ref, normed, mine_ref, theirs_ref)
    masked = active_ref[...] * grad_ref[...].astype(F32)
    masked_ref[...] = masked.astype(LOW)
    sum_ref[...] = jnp.sum(masked, axis=0, keepdims=True)


def norm_two_kernel(
    core_ref, x_ref, active_ref, part_ref, theirs_part_ref, bias_ref, gain_ref, shift_ref,
    middle_ref, mine_ref, theirs_ref,
):
    rows = x_ref.shape[0]
    attn = part_ref[:rows] + theirs_part_ref[...] + bias_ref[...]
    middle = x_ref[...].astype(F32) + active_ref[...] * attn
    middle_ref[...] = middle
    halves(core_ref, layer_norm(middle, gain_ref[...], shift_ref[...]), mine_ref, theirs_ref)


def norm_back(core_ref, value_ref, gain_ref, mine_ref, theirs_ref, gain_out_ref, shift_out_ref):
    values = value_ref[...].astype(F32)
    mine, theirs = mine_ref[: values.shape[0]], theirs_ref[...]
    grads = jnp.where(
        core_ref[0] == 0,
        jnp.concatenate([mine, theirs], 1),
        jnp.concatenate([theirs, mine], 1),
    )
    centered = values - jnp.mean(values, axis=-1, keepdims=True)
    scale = lax.rsqrt(jnp.mean(centered * centered, axis=-1, keepdims=True) + 1e-05)
    unit = centered * scale
    gain_out_ref[...] = jnp.sum(grads * unit, axis=0, keepdims=True)
    shift_out_ref[...] = jnp.sum(grads, axis=0, keepdims=True)
    grads = grads * gain_ref[...]
    inner = jnp.mean(grads * unit, axis=-1, keepdims=True)
    return scale * (grads - jnp.mean(grads, axis=-1, keepdims=True) - unit * inner)


def norm_two_back_kernel(
    core_ref, value_ref, gain_ref, mine_ref, theirs_ref, grad_ref, active_ref,
    total_ref, masked_ref, sum_ref, gain_out_ref, shift_out_ref,
):
    part = norm_back(
        core_ref, value_ref, gain_ref, mine_ref, theirs_ref, gain_out_ref, shift_out_ref
    )
    total = grad_ref[...].astype(F32) + part
    total_ref[...] = total
    masked = (active_ref[...] * total).astype(LOW)
    masked_ref[...] = masked
    sum_ref[...] = jnp.sum(masked.astype(F32), axis=0, keepdims=True)


def norm_one_back_kernel(
    core_ref, value_ref, gain_ref, mine_ref, theirs_ref, grad_ref,
    total_ref, gain_out_ref, shift_out_ref,
):
    part = norm_back(
        core_ref, value_ref, gain_ref, mine_ref, theirs_ref, gain_out_ref, shift_out_ref
    )
    total_ref[...] = (grad_ref[...].astype(F32) + part).astype(LOW)


def by_rows(kernel, core, outs, *operands):
    vmem = pl.BlockSpec(memory_space=pltpu.VMEM)
    return pl.pallas_call(
        kernel,
        in_specs=[pl.BlockSpec(memory_space=pltpu.SMEM)] + [vmem] * len(operands),
        out_specs=[vmem] * len(outs),
        out_shape=[jax.ShapeDtypeStruct(shape, dtype) for shape, dtype in outs],
        compiler_params=limit(24),
        cost_estimate=estimate(
            20 * operands[0].size, sum(o.size * o.dtype.itemsize for o in operands)
        ),
    )(core, *operands)


def product_kernel(count, turned, *refs):
    lefts, out_ref, left_turned, right = refs[:count], refs[-3], refs[-2], refs[-1]
    rights = refs[count:-3]
    length = lefts[0].shape[0]

    @pl.when(pl.program_id(0) == 0)
    def _():
        for d, left in enumerate(lefts):
            left_turned[:, d * length : (d + 1) * length] = left[...].T

    row = 0
    for piece in rights:
        value = piece[0] if len(piece.shape) == 3 else piece[...]
        if turned:
            value = roll_rows(value)
        right[row : row + value.shape[0]] = value
        row += value.shape[0]
    out_ref[...] = dot(left_turned[...], right[...], 1, 0).astype(LOW)


def rows_product(lefts, rights, tall, block, steps, turned=False):
    length = lefts[0][0].shape[0]
    left_specs = [
        pl.BlockSpec((length, tall), functools.partial(lambda c, j: (0, c), c)) for _, c in lefts
    ]
    right_specs = [pl.BlockSpec(shape, place) for _, shape, place in rights]
    total = length * len(lefts)
    return pl.pallas_call(
        functools.partial(product_kernel, len(lefts), turned),
        grid=(steps,),
        in_specs=left_specs + right_specs,
        out_specs=pl.BlockSpec((tall, block), lambda j: (0, j)),
        out_shape=jax.ShapeDtypeStruct((tall, steps * block), LOW),
        scratch_shapes=[pltpu.VMEM((tall, total), LOW), pltpu.VMEM((total, block), LOW)],
        compiler_params=limit(32),
        cost_estimate=estimate(
            2 * tall * total * steps * block, 2 * total * (tall + steps * block)
        ),
    )(*[left[0] for left in lefts], *[right[0] for right in rights])


def columns_from(value, rows, row, first, block):
    return value, (rows, block), lambda j: (row, first + j)


def hold(values, after):
    return lax.optimization_barrier((values, after))[0]


def columns_kernel(table_ref, left_ref, *refs):
    total, first = 0.0, 0
    for weight_ref in refs[:-1]:
        depth = weight_ref.shape[0]
        total += dot(left_ref[:, first : first + depth], weight_ref[...], 1, 0)
        first += depth
    refs[-1][...] = total.astype(refs[-1].dtype)


def times_columns(left, weight, table, block, dtype):
    rows, depth = left.shape
    steps = table.shape[0]
    return pl.pallas_call(
        columns_kernel,
        grid_spec=pltpu.PrefetchScalarGridSpec(
            num_scalar_prefetch=1,
            grid=(steps,),
            in_specs=[
                pl.BlockSpec((rows, depth), lambda i, t: (0, 0)),
                *[
                    pl.BlockSpec(
                        (depth // STREAMS, block),
                        functools.partial(lambda r, i, t: (r, t[i]), r),
                    )
                    for r in range(STREAMS)
                ],
            ],
            out_specs=pl.BlockSpec((rows, block), lambda i, t: (0, i)),
        ),
        out_shape=jax.ShapeDtypeStruct((rows, steps * block), dtype),
        compiler_params=limit(24),
        cost_estimate=estimate(2 * rows * depth * steps * block, 2 * depth * (rows + steps * block) + 4 * rows * steps * block),
    )(table, left, *[far(weight)] * STREAMS)


def back_kernel(turned, table_ref, left_ref, *refs):
    weights, out_ref = refs[:STREAMS], refs[-1]
    starts = refs[STREAMS:-1]
    left = left_ref[...]
    if turned:
        left = roll_rows(left)
    first = 0
    for weight_ref in weights:
        deep = weight_ref.shape[0]
        part = dot(left, weight_ref[...], 1, 1)
        columns = slice(first, first + deep)
        first += deep

        @pl.when(pl.program_id(1) == 0)
        def _(part=part, columns=columns):
            out_ref[:, columns] = part + starts[0][:, columns] if starts else part

        @pl.when(pl.program_id(1) > 0)
        def _(part=part, columns=columns):
            out_ref[:, columns] += part


def times_back(left, weight, table, block, deep, start=None, turned=False):
    rows = left.shape[0]
    depth = weight.shape[0]
    steps = table.shape[0]
    out_spec = pl.BlockSpec((rows, deep), lambda k, i, t: (0, k))
    in_specs = [
        pl.BlockSpec((rows, block), lambda k, i, t: (0, i)),
        *[
            pl.BlockSpec(
                (deep // STREAMS, block),
                functools.partial(lambda r, k, i, t: (k * STREAMS + r, t[i]), r),
            )
            for r in range(STREAMS)
        ],
    ]
    operands = [table, left, *[far(weight)] * STREAMS]
    if start is not None:
        in_specs.append(out_spec)
        operands.append(start)
    return pl.pallas_call(
        functools.partial(back_kernel, turned),
        grid_spec=pltpu.PrefetchScalarGridSpec(
            num_scalar_prefetch=1,
            grid=(depth // deep, steps),
            in_specs=in_specs,
            out_specs=out_spec,
        ),
        out_shape=jax.ShapeDtypeStruct((rows, depth), F32),
        compiler_params=limit(32),
        cost_estimate=estimate(2 * rows * depth * steps * block, 2 * steps * block * (rows + depth) + 8 * rows * depth),
    )(*operands)


def inner_kernel(grad_ref, *refs):
    weights = refs[:STREAMS]
    mine_ref, theirs_ref, bias_ref, act_ref, out_ref, sum_ref = refs[STREAMS:]
    first = 0
    for weight_ref in weights:
        columns = slice(first, first + weight_ref.shape[0])
        first += weight_ref.shape[0]
        theirs = roll_rows(theirs_ref[:, columns])
        act, slope = gelu_and_slope(mine_ref[:, columns] + theirs + bias_ref[:, columns])
        act_ref[:, columns] = act.astype(LOW)
        grad = (dot(grad_ref[...], weight_ref[...], 1, 1) * slope).astype(LOW)
        out_ref[:, columns] = grad
        sum_ref[:, columns] = jnp.sum(grad.astype(F32), axis=0, keepdims=True)


def inner_layer(grads, weight, mine, theirs, bias, block):
    rows, width = grads.shape
    hidden = weight.shape[0]
    part = pl.BlockSpec((rows, block), lambda i: (0, i))
    line = pl.BlockSpec((1, block), lambda i: (0, i))
    return pl.pallas_call(
        inner_kernel,
        grid=(hidden // block,),
        in_specs=[
            pl.BlockSpec((rows, width), lambda i: (0, 0)),
            *[
                pl.BlockSpec(
                    (block // STREAMS, width),
                    functools.partial(lambda r, i: (i * STREAMS + r, 0), r),
                )
                for r in range(STREAMS)
            ],
            part,
            part,
            line,
        ],
        out_specs=[part, part, line],
        out_shape=[
            jax.ShapeDtypeStruct((rows, hidden), LOW),
            jax.ShapeDtypeStruct((rows, hidden), LOW),
            jax.ShapeDtypeStruct((1, hidden), F32),
        ],
        compiler_params=limit(32),
        cost_estimate=estimate(2 * rows * width * hidden, 2 * width * (rows + hidden) + 12 * rows * hidden),
    )(grads, *[far(weight)] * STREAMS, mine, theirs, bias)


def head_chances(queries, keys, lanes_of_head, allowed):
    keys_of_head = jnp.where(lanes_of_head, keys, jnp.zeros_like(keys))
    scores = dot(queries, keys_of_head, 1, 1) * (HEAD_DIM**-0.5)
    scores = jnp.where(allowed, scores, -1e30)
    raised = jnp.exp(scores - jnp.max(scores, axis=-1, keepdims=True))
    return raised / jnp.sum(raised, axis=-1, keepdims=True)


def attend_masks(first, length, lanes):
    lane = lax.broadcasted_iota(jnp.int32, (length, lanes), 1)
    row = lax.broadcasted_iota(jnp.int32, (length, length), 0) + first
    column = lax.broadcasted_iota(jnp.int32, (length, length), 1) + first
    row = jnp.where(row >= length, row - length, row)
    column = jnp.where(column >= length, column - length, column)
    return lane, column <= row


def attend_forward_kernel(first_ref, *refs):
    mine, theirs, biases, lows, o_ref = refs[:3], refs[3:6], refs[6:9], refs[9:12], refs[12]
    sums = [
        (m[...] + roll_rows(t[...]) + b[...]).astype(LOW)
        for m, t, b in zip(mine, theirs, biases)
    ]
    for low, value in zip(lows, sums):
        low[...] = value
    queries, keys, values = sums
    lane, allowed = attend_masks(first_ref[0], *queries.shape)
    total = jnp.zeros(queries.shape, F32)
    for head in range(queries.shape[1] // HEAD_DIM):
        own = lane // HEAD_DIM == head
        chances = head_chances(queries, keys, own, allowed).astype(LOW)
        total += dot(chances, jnp.where(own, values, jnp.zeros_like(values)), 1, 0)
    o_ref[...] = total.astype(LOW)


def attend_forward(first, mine, theirs, bias):
    length, width = mine.shape
    width //= 3
    steps = width // 128
    parts = [
        pl.BlockSpec((length, 128), functools.partial(lambda p, i, t: (0, p * steps + i), p))
        for p in range(3)
    ]
    lines = [
        pl.BlockSpec((1, 128), functools.partial(lambda p, i, t: (0, p * steps + i), p))
        for p in range(3)
    ]
    return pl.pallas_call(
        attend_forward_kernel,
        grid_spec=pltpu.PrefetchScalarGridSpec(
            num_scalar_prefetch=1,
            grid=(steps,),
            in_specs=parts + parts + lines,
            out_specs=[parts[0]] * 4,
        ),
        out_shape=[jax.ShapeDtypeStruct((length, width), LOW)] * 4,
        compiler_params=limit(16),
        cost_estimate=estimate(4 * length * length * width, 32 * length * width),
    )(first, mine, mine, mine, theirs, theirs, theirs, bias, bias, bias)


def attend_backward_kernel(first_ref, q_ref, k_ref, v_ref, g_ref, out_ref):
    queries, keys, values, grads = q_ref[...], k_ref[...], v_ref[...], g_ref[...]
    lane, allowed = attend_masks(first_ref[0], *queries.shape)
    dq = jnp.zeros(queries.shape, F32)
    dk = jnp.zeros(queries.shape, F32)
    dv = jnp.zeros(queries.shape, F32)
    for head in range(queries.shape[1] // HEAD_DIM):
        own = lane // HEAD_DIM == head
        chances = head_chances(queries, keys, own, allowed)
        head_grads = jnp.where(own, grads, jnp.zeros_like(grads))
        dv += dot(chances.astype(LOW), head_grads, 0, 0)
        chance_grads = dot(head_grads, values, 1, 1)
        inner = jnp.sum(chances * chance_grads, axis=-1, keepdims=True)
        score_grads = (chances * (chance_grads - inner)).astype(LOW)
        dq += dot(score_grads, jnp.where(own, keys, jnp.zeros_like(keys)), 1, 0)
        dk += dot(score_grads, jnp.where(own, queries, jnp.zeros_like(queries)), 0, 0)
    scale = HEAD_DIM**-0.5
    out_ref[0] = (dq * scale).astype(LOW)
    out_ref[1] = (dk * scale).astype(LOW)
    out_ref[2] = dv.astype(LOW)


def attend_backward(first, *operands):
    length, width = operands[0].shape
    block = pl.BlockSpec((length, 128), lambda i, t: (0, i))
    return pl.pallas_call(
        attend_backward_kernel,
        grid_spec=pltpu.PrefetchScalarGridSpec(
            num_scalar_prefetch=1,
            grid=(width // 128,),
            in_specs=[block] * 4,
            out_specs=pl.BlockSpec((3, length, 128), lambda i, t: (0, 0, i)),
        ),
        out_shape=jax.ShapeDtypeStruct((3, length, width), LOW),
        compiler_params=limit(16),
        cost_estimate=estimate(10 * length * length * width, 14 * length * width),
    )(first, *operands)


def place_kernel(high, table_ref, *refs):
    count = len(refs) - 4
    pieces, out_ref, held, sems = refs[:count], refs[-3], refs[-2], refs[-1]
    slots, broad = held.shape[0], held.shape[2]

    def copy(step):
        row = pl.multiple_of(table_ref[2 * step] * high, high)
        column = pl.multiple_of(table_ref[2 * step + 1] * broad, broad)
        return pltpu.make_async_copy(
            held.at[step % slots],
            out_ref.at[pl.ds(row, high), pl.ds(column, broad)],
            sems.at[step % slots],
        )

    step = 0
    for piece in pieces:
        for i in range(piece.shape[0] // high):
            for j in range(piece.shape[1] // broad):
                if step >= slots:
                    copy(step - slots).wait()
                part = piece[i * high : (i + 1) * high, j * broad : (j + 1) * broad]
                held[step % slots] = part.astype(F32)
                copy(step).start()
                step += 1
    for waited in range(max(step - slots, 0), step):
        copy(waited).wait()


def place(pieces, whole, places, high, broad):
    slots = 4
    vmem = pl.BlockSpec(memory_space=pltpu.VMEM)
    return pl.pallas_call(
        functools.partial(place_kernel, high),
        in_specs=[pl.BlockSpec(memory_space=pltpu.SMEM)]
        + [vmem] * len(pieces)
        + [pl.BlockSpec(memory_space=pl.ANY)],
        out_specs=pl.BlockSpec(memory_space=pl.ANY),
        out_shape=jax.ShapeDtypeStruct(whole.shape, F32),
        scratch_shapes=[
            pltpu.VMEM((slots, high, broad), F32),
            pltpu.SemaphoreType.DMA((slots,)),
        ],
        input_output_aliases={len(pieces) + 1: 0},
        compiler_params=limit(32),
        cost_estimate=estimate(0, sum(6 * p.size for p in pieces)),
    )(jnp.stack(places).astype(jnp.int32), *pieces, whole)


def blank_kernel(out_ref):
    pass


def blank(shape, dtype=F32):
    return pl.pallas_call(
        blank_kernel,
        out_specs=pl.BlockSpec(memory_space=pl.ANY),
        out_shape=jax.ShapeDtypeStruct(shape, dtype),
    )()


class Lane:
    def __init__(self):
        self.last = ()

    def send(self, sends, after=()):
        values = hold([v for v, _ in sends], (self.last, after))
        self.last = [lax.ppermute(v, "dp", m) for v, (_, m) in zip(values, sends)]
        return self.last


def per_device(
    hidden,
    cotangent,
    exit_layers,
    qkv_weight,
    out_weight,
    up_weight,
    down_weight,
    query_bias,
    value_bias,
    out_bias,
    up_bias,
    down_bias,
    attn_gain,
    attn_shift,
    ffn_gain,
    ffn_shift,
):
    core = lax.axis_index("sp")
    other = 1 - core
    chips = lax.axis_size("dp")
    plane = chips // LINE
    chip = lax.axis_index("dp")
    spot = chip % GROUP
    level = chip // plane
    rows = hidden.shape[1]
    width = hidden.shape[2]
    length = 2 * rows
    half = width // 2
    inner = up_weight.shape[1]
    inner_half = inner // 2
    across, first_hop, middle_hop, last_hop = (Lane() for _ in range(4))

    def swap(value):
        return lax.ppermute(value, "sp", [(0, 1), (1, 0)])

    def in_plane(distance):
        return [(i, i // plane * plane + ((i % plane) ^ distance)) for i in range(chips)]

    def along(*moves):
        return [(a * plane + i, b * plane + i) for a, b in moves for i in range(plane)]

    inward, middle_moves, outward = (
        along((0, 1), (3, 2)),
        along((1, 2), (2, 1)),
        along((1, 0), (2, 3)),
    )

    def split(value, axis, size):
        return (
            lax.dynamic_slice_in_dim(value, core * size, size, axis),
            lax.dynamic_slice_in_dim(value, other * size, size, axis),
        )

    def exchange(blocks):
        return blocks[:1] + across.send([(blocks[d], in_plane(d)) for d in range(1, GROUP)])

    def gather_group(value):
        return exchange([value] * GROUP)

    def blocks_of(value, axis, size):
        return [
            lax.dynamic_slice_in_dim(value, (spot ^ d) * size, size, axis) for d in range(GROUP)
        ]

    def scatter_group(value, axis, size):
        return exchange(blocks_of(value, axis, size))

    end = (level == 0) | (level == LINE - 1)

    def line_start(value, after=()):
        return value + hold(first_hop.send([(value, inward)])[0], after)

    def line_middle(value):
        return value + middle_hop.send([(value, middle_moves)])[0]

    def line_end(value):
        return jnp.where(end, last_hop.send([(value, outward)])[0], value)

    def blocks_sum(value):
        distance = GROUP
        while distance < plane:
            value = value + lax.ppermute(value, "dp", in_plane(distance))
            distance *= 2
        return value

    def spread(value, after, more=()):
        size = value.shape[0] // 2
        first, second = across.send([(value, in_plane(1)), (value, in_plane(2))], after[0])
        upper, lower, *more = across.send(
            [(first[:size], in_plane(2)), (second[size:], in_plane(1)), *more], after[1]
        )
        return [value, first, second, upper, lower], more

    def table(size, start, count=None):
        return jnp.arange(size if count is None else count, dtype=jnp.int32) + start

    active = active_rows(exit_layers[0], core * rows, rows, length)
    core_number = core.astype(jnp.int32)[None]
    first_row = (core * rows).astype(jnp.int32)[None]
    full, part, line = (rows, width), (rows, half), (1, width)

    always = exit_layers[0, 1] > 0

    def segment(steps, *operands):
        def skip(*_):
            return [blank(shape.shape, shape.dtype) for shape in jax.eval_shape(steps, *operands)]

        return lax.cond(always, lambda *o: list(steps(*o)), skip, *operands)

    mine, theirs, down_grad, down_sums = by_rows(
        norm_one_kernel,
        core_number,
        [(part, LOW), (part, LOW), (full, LOW), (line, F32)],
        hidden[0],
        attn_gain[None],
        attn_shift[None],
        cotangent[0],
        active,
    )
    down_mine = gather_group(down_grad)
    qkv_block = min(1024, half)
    qkv_count = half // qkv_block
    bias = jnp.stack([query_bias, jnp.zeros_like(query_bias), value_bias])
    bias = lax.dynamic_slice_in_dim(bias, core * half, half, 1).reshape(1, -1)

    def qkv_table(c):
        return jnp.concatenate(
            [table(qkv_count, (2 * p + c) * qkv_count) for p in range(3)]
        )

    def to_attended(mine, theirs, down_grad, qkv_weight, bias, my_table, their_table, first_row):
        normed = jnp.concatenate([mine, swap(theirs)])
        theirs = times_columns(normed, qkv_weight, their_table, qkv_block, LOW)
        theirs = swap(theirs)
        mine = times_columns(normed, qkv_weight, my_table, qkv_block, F32)
        results = attend_forward(first_row, mine, theirs, bias)
        both = jnp.concatenate([normed, results[3]], 1)
        return [*results, swap(down_grad), both]

    queries, keys, values, attended, down_grad_theirs, early = segment(
        to_attended, mine, theirs, down_grad, qkv_weight, bias,
        qkv_table(core), qkv_table(other), first_row,
    )
    attended, down_mine = lax.optimization_barrier((attended, down_mine))
    early = gather_group(early)
    block = min(1024, inner_half)
    count = inner_half // block

    def to_inner(
        hidden, active, attended, out_weight, lines, up_weight, tables, core_number,
        grads, down_weight,
    ):
        out_part = dot(attended, out_weight, 1, 0)
        middle, mine, theirs = by_rows(
            norm_two_kernel,
            core_number,
            [(full, F32), (part, LOW), (part, LOW)],
            hidden,
            active,
            out_part,
            swap(out_part[rows:]),
            *lines[:3],
        )
        normed = jnp.concatenate([mine, swap(theirs)])
        theirs = times_columns(normed, up_weight, tables[1], block, LOW)
        theirs = swap(theirs)
        mine = times_columns(normed, up_weight, tables[0], block, F32)
        results = inner_layer(
            grads, down_weight, mine, theirs, lines[3], min(512, inner_half)
        )
        return [middle, normed, *results]

    bias = lax.dynamic_slice_in_dim(up_bias, core * inner_half, inner_half).reshape(1, -1)
    middle, normed_two_half, inner_low, up_grad, up_sums = segment(
        to_inner, hidden[0], active, attended, out_weight,
        (out_bias[None], ffn_gain[None], ffn_shift[None], bias), up_weight,
        (table(count, core * count), table(count, other * count)), core_number,
        jnp.concatenate([down_grad, down_grad_theirs]), down_weight,
    )
    (inner_low, up_grad), early = lax.optimization_barrier(((inner_low, up_grad), early))

    down_left = scatter_group(inner_low, 1, inner_half // GROUP)

    def to_middle(
        up_grad, up_weight, middle, gain, cotangent, active, core_number, down_mine, tables
    ):
        theirs = swap(up_grad)
        grads = times_back(up_grad, up_weight, tables[0], inner_half, 256)
        grads = times_back(theirs, up_weight, tables[1], inner_half, 256, grads, True)
        results = by_rows(
            norm_two_back_kernel,
            core_number,
            [(full, F32), (full, LOW), (line, F32), (line, F32), (line, F32)],
            middle,
            gain,
            grads,
            swap(grads[rows:]),
            cotangent,
            active,
        )
        down_theirs = swap(jnp.concatenate(down_mine[1:]))
        return [*results, down_theirs, *blocks_of(up_grad, 1, inner_half // GROUP)]

    (
        middle_grad, attn_grad, attn_sums, gain_two_grad, shift_two_grad, down_theirs, *up_right
    ) = segment(
        to_middle, up_grad, up_weight, middle, ffn_gain[None], cotangent[0], active,
        core_number, down_mine, (table(1, core), table(1, other)),
    )
    down_theirs = [(down_grad_theirs, 0)] + [(down_theirs, d) for d in range(GROUP - 1)]

    def down_product(first, steps):
        rights = []
        for own, (value, row) in zip(down_mine, down_theirs):
            rights.append(columns_from(own, rows, 0, first, quarter))
            rights.append(columns_from(value, rows, row, first, quarter))
        lefts = [(left, 0) for left in down_left]
        return rows_product(lefts, rights, inner_half // GROUP, quarter, steps)

    quarter = width // 4
    down_left, attn_grad = lax.optimization_barrier((down_left, attn_grad))
    up_right = exchange(up_right)
    sums = [down_product(0, 1)]
    (come,) = first_hop.send([(sums[0], inward)])
    attn_grad, sums[0] = lax.optimization_barrier((attn_grad, sums[0]))

    def to_qkv(attn_grad, out_weight, first_row, *operands):
        grads = jnp.concatenate([attn_grad, swap(attn_grad)])
        grads = dot(grads, out_weight, 1, 1).astype(LOW)
        qkv_grad = attend_backward(first_row, *operands, grads)
        flat = jnp.concatenate([qkv_grad[0], qkv_grad[1], qkv_grad[2]], 1)
        blocks = []
        for wide, block in zip(
            blocks_of(attn_grad, 1, width // GROUP), blocks_of(qkv_grad, 2, half // GROUP)
        ):
            narrow = wide.shape[1] // 2
            wide = jnp.concatenate([wide[:, :narrow], wide[:, narrow:]])
            blocks.append(jnp.concatenate([block, wide[None]]))
        return [qkv_grad, flat, swap(flat), *blocks]

    qkv_grad, flat, flat_theirs, *late = segment(to_qkv, attn_grad, out_weight, first_row, queries, keys, values)
    sums.append(down_product(1, 1))
    qkv_grad, up_right, come, sums = lax.optimization_barrier((qkv_grad, up_right, come, sums))
    sums[0] += come
    (passed,) = middle_hop.send([(sums[0], middle_moves)])
    (come,) = first_hop.send([(sums[1], inward)])
    up_left = gather_group(normed_two_half)

    def to_input(flat, theirs, qkv_weight, tables):
        grads = times_back(flat, qkv_weight, tables[0], qkv_block, 512)
        return [times_back(theirs, qkv_weight, tables[1], qkv_block, 512, grads, True)]

    (grads,) = segment(
        to_input, hold(flat, qkv_grad), flat_theirs, qkv_weight,
        (qkv_table(core), qkv_table(other)),
    )
    grads, up_left, passed, come = lax.optimization_barrier((grads, up_left, passed, come))
    sums[0] += passed
    sums[1] += come
    late = exchange(late)
    value = hold(down_product(2, 1), grads)
    come = first_hop.send([(value, inward)])
    passed, come, late = lax.optimization_barrier(
        (last_hop.send([(sums[0], outward)]), come, late)
    )
    sums[0] = jnp.where(end, passed[0], sums[0])
    sums.append(value + come[0])
    sums.append(line_start(hold(down_product(3, 1), late)))

    def to_ends(grads, hidden, gain, middle_grad, core_number, inner_low, down_weight):
        results = by_rows(
            norm_one_back_kernel,
            core_number,
            [(full, LOW), (line, F32), (line, F32)],
            hidden,
            gain,
            grads,
            swap(grads[rows:]),
            middle_grad,
        )
        down_part = dot(inner_low, down_weight, 1, 0)
        return [*results, down_part[:rows], swap(down_part[rows:])]

    input_grad, gain_one_grad, shift_one_grad, mine, theirs = to_ends(
        hold(grads, sums[0]), hidden[0], attn_gain[None], middle_grad, core_number,
        inner_low, down_weight,
    )
    output = middle + active * (mine + theirs + down_bias)

    def widen(value):
        none = jnp.zeros_like(value)
        return jnp.where(
            core == 0, jnp.concatenate([value, none]), jnp.concatenate([none, value])
        )

    qkv_sums = jnp.sum(qkv_grad.astype(F32), axis=1)
    small = jnp.concatenate(
        [
            widen(qkv_sums[0]),
            widen(qkv_sums[2]),
            attn_sums[0],
            widen(up_sums[0]),
            down_sums[0],
            gain_one_grad[0],
            shift_one_grad[0],
            gain_two_grad[0],
            shift_two_grad[0],
        ]
    ).reshape(-1, 128)
    small = small + swap(small)

    small_sends = [(small, in_plane(d)) for d in range(1, GROUP)]

    def pair_sums(values):
        while len(values) > 1:
            values = [a + b for a, b in zip(values[::2], values[1::2])]
        return values[0]

    def line_moves(distance):
        return [(i, (i // plane ^ distance) * plane + i % plane) for i in range(chips)]

    chunks = [("down", value, index) for index, value in enumerate(sums)]
    chunks += [("up", None, 2 * GROUP * core), ("up", None, 2 * GROUP * core + 1)]
    chunks += [("up", None, 2 * GROUP * other), ("up", None, 2 * GROUP * other + 1)]
    chunks += [("qkv", None, core), ("qkv", None, other), ("out", None, 0)]
    up_width = inner_half // GROUP
    up_block = min(512, up_width)

    def up_products(rights, turned):
        lefts = [(left, 0) for left in up_left]
        return [
            rows_product(lefts, [right(first) for right in rights], half, up_block, 1, turned)
            for first in range(up_width // up_block)
        ]

    def up_own():
        def place(right):
            return lambda first: columns_from(right, length, 0, first, up_block)

        return up_products([place(right) for right in hold(up_right, late)], False)

    def up_other(*mine):
        theirs = swap(jnp.concatenate(mine))

        def place(d):
            return lambda first: columns_from(theirs, length, d, first, up_block)

        return up_products([place(d) for d in range(GROUP)], True)

    rest_block = half // GROUP

    def rest_part(value, d):
        return value, (1, length, rest_block), lambda j: (4 * d + j, 0, 0)

    def rest_own(mine):
        lefts = [(left, 0) for left in early]
        rights = [rest_part(right, 0) for right in mine]
        return [rows_product(lefts, rights, half, rest_block, 3)]

    def rest_other(*mine):
        theirs = swap(jnp.concatenate(mine))

        def out_part(value, d):
            return value, (1, rows, rest_block), lambda j: (4 * d + 3, j, 0)

        lefts = [(left, 0) for left in early]
        rights = [rest_part(theirs, d) for d in range(GROUP)]
        other_half = rows_product(lefts, rights, half, rest_block, 3, True)
        lefts = [(left, 1) for left in early]
        rights = []
        for d, right in enumerate(mine):
            rights += [out_part(right, 0), out_part(theirs, d)]
        return [other_half, rows_product(lefts, rights, half, rest_block, 2)]

    wholes = {
        "down": blank((inner_half, width)),
        "up": blank((half, inner)),
        "out": blank((half, width)),
        "qkv": blank((half, 3 * width)),
    }
    size = inner_half // GROUP
    begun, raw = sums, []
    done = [(), ()]
    for index, (name, value, where) in enumerate(chunks):
        value = begun[index]
        more, held = (), [done[-1]]
        if index == 0:
            held.append(begun[3])
        fresh = []
        if index == 0:
            fresh = up_own()
        if index == 1:
            fresh = segment(up_other, *hold(up_right, done[-1]))
        if index == 3:
            fresh = rest_own(hold(late, done[-1]))
        if index == 4:
            fresh = segment(rest_other, *hold(late, done[-1]))
        raw += fresh
        held.append(fresh)
        if index == len(chunks) - 2:
            more = small_sends
        if index == len(chunks) - 1:
            small = pair_sums([small, *more_results])
            distance = GROUP
            while distance < plane:
                small = small + lax.ppermute(small, "dp", in_plane(distance))
                distance *= 2
            lines = [lax.ppermute(small, "dp", line_moves(d)) for d in range(1, LINE)]
            held += [done[-1], lines]
        after = (), held
        if 0 < index < len(chunks) - 1:
            value = line_end(line_middle(value))
        if index == len(chunks) - 2:
            last = line_middle(begun[-1])
            held.append(last)
            begun[-1] = line_end(last)
        pieces, more_results = spread(blocks_sum(value), after, more)
        value = pieces[0]
        tall, wide = value.shape
        high = min(256, tall)
        broad = wide // 3 if name == "qkv" else wide
        places = []
        for d in range(GROUP):
            owner = spot ^ d
            for i in range(tall // high):
                row = jnp.int32(i)
                if name == "down":
                    row, columns = owner * (tall // high) + i, [jnp.int32(where)]
                elif name == "up":
                    columns = [where + owner * (size // wide)]
                elif name == "out":
                    columns = [owner]
                else:
                    columns = [(2 * p + where) * GROUP + owner for p in range(3)]
                for column in columns:
                    places += [row, column]
        wholes[name] = place(pieces, wholes[name], places, high, broad)
        done.append(wholes[name])
        while len(begun) < len(chunks) and raw:
            number = len(begun)
            placed = number - (4 if number < 8 else 5)
            if placed > index:
                break
            begun.append(line_start(hold(raw.pop(0), done[placed + 2])))

    small = pair_sums([small, *lines]).reshape(-1)
    small_grads = []
    first = 0
    for size in (width, width, width, inner, width, width, width, width, width):
        small_grads.append(small[first : first + size])
        first += size

    return (
        output.astype(LOW)[None],
        input_grad[None],
        wholes["qkv"],
        wholes["out"],
        wholes["up"],
        wholes["down"],
        *small_grads,
    )


def solution(mesh):
    return jax.shard_map(
        per_device,
        mesh=mesh,
        in_specs=(
            P("dp", "sp", None),
            P("dp", "sp", None),
            P("dp", None),
            P("sp", None),
            P("sp", None),
            P("sp", None),
            P("sp", None),
            P(),
            P(),
            P(),
            P(),
            P(),
            P(),
            P(),
            P(),
            P(),
        ),
        out_specs=(
            P("dp", "sp", None),
            P("dp", "sp", None),
            P("sp", None),
            P("sp", None),
            P("sp", None),
            P("sp", None),
            P(),
            P(),
            P(),
            P(),
            P(),
            P(),
            P(),
            P(),
            P(),
        ),
        check_vma=False,
    )
```

```python
import functools

import jax
import jax.numpy as jnp
from jax import lax
from jax.experimental import pallas as pl
from jax.experimental.pallas import tpu as pltpu
from jax.sharding import PartitionSpec as P

HEAD_DIM = 64
TILE = 128
LAYER = 12
LINE = 4
STREAMS = 1
GROUP = 4
F32 = jnp.float32
LOW = jnp.bfloat16


def layer_norm(values, gain, shift):
    center = jnp.mean(values, axis=-1, keepdims=True)
    centered = values - center
    variance = jnp.mean(centered * centered, axis=-1, keepdims=True)
    return centered * lax.rsqrt(variance + 1e-05) * gain + shift


def active_rows(bounds, first_row, row_count, sequence_length):
    position = first_row + jnp.arange(row_count, dtype=jnp.int32)
    tile_start = position // TILE * TILE
    exit_layer = bounds[1] - (bounds[1] - bounds[0]) * tile_start // sequence_length
    return (exit_layer > LAYER).astype(F32)[:, None]


def gelu_and_slope(values):
    scale = (2.0 / jnp.pi) ** 0.5
    square = values * values
    bend = jnp.tanh(scale * values * (1.0 + 0.044715 * square))
    rise = 0.5 * (1.0 + bend)
    slope = rise + 0.5 * values * (1.0 - bend * bend) * scale * (1.0 + 0.134145 * square)
    return values * rise, slope


def dot(left, right, left_dim, right_dim):
    return lax.dot_general(
        left, right, (((left_dim,), (right_dim,)), ((), ())), preferred_element_type=F32
    )


def roll_rows(value):
    rows = value.shape[0] // 2
    return jnp.concatenate([value[rows:], value[:rows]])


def estimate(flops, size):
    return pl.CostEstimate(flops=flops // 4, bytes_accessed=size // 4, transcendentals=0)


def far(value):
    return pltpu.with_memory_space_constraint(value, pltpu.HBM)


def limit(mebibytes):
    return pltpu.CompilerParams(vmem_limit_bytes=mebibytes << 20)


def halves(core_ref, values, mine_ref, theirs_ref):
    width = mine_ref.shape[1]
    first = core_ref[0] == 0
    low, high = values[:, :width], values[:, width:]
    mine_ref[...] = jnp.where(first, low, high).astype(LOW)
    theirs_ref[...] = jnp.where(first, high, low).astype(LOW)


def norm_one_kernel(
    core_ref, x_ref, gain_ref, shift_ref, grad_ref, active_ref,
    mine_ref, theirs_ref, masked_ref, sum_ref,
):
    normed = layer_norm(x_ref[...].astype(F32), gain_ref[...], shift_ref[...])
    halves(core_ref, normed, mine_ref, theirs_ref)
    masked = active_ref[...] * grad_ref[...].astype(F32)
    masked_ref[...] = masked.astype(LOW)
    sum_ref[...] = jnp.sum(masked, axis=0, keepdims=True)


def norm_two_kernel(
    core_ref, x_ref, active_ref, part_ref, theirs_part_ref, bias_ref, gain_ref, shift_ref,
    middle_ref, mine_ref, theirs_ref,
):
    rows = x_ref.shape[0]
    attn = part_ref[:rows] + theirs_part_ref[...] + bias_ref[...]
    middle = x_ref[...].astype(F32) + active_ref[...] * attn
    middle_ref[...] = middle
    halves(core_ref, layer_norm(middle, gain_ref[...], shift_ref[...]), mine_ref, theirs_ref)


def norm_back(core_ref, value_ref, gain_ref, mine_ref, theirs_ref, gain_out_ref, shift_out_ref):
    values = value_ref[...].astype(F32)
    mine, theirs = mine_ref[: values.shape[0]], theirs_ref[...]
    grads = jnp.where(
        core_ref[0] == 0,
        jnp.concatenate([mine, theirs], 1),
        jnp.concatenate([theirs, mine], 1),
    )
    centered = values - jnp.mean(values, axis=-1, keepdims=True)
    scale = lax.rsqrt(jnp.mean(centered * centered, axis=-1, keepdims=True) + 1e-05)
    unit = centered * scale
    gain_out_ref[...] = jnp.sum(grads * unit, axis=0, keepdims=True)
    shift_out_ref[...] = jnp.sum(grads, axis=0, keepdims=True)
    grads = grads * gain_ref[...]
    inner = jnp.mean(grads * unit, axis=-1, keepdims=True)
    return scale * (grads - jnp.mean(grads, axis=-1, keepdims=True) - unit * inner)


def norm_two_back_kernel(
    core_ref, value_ref, gain_ref, mine_ref, theirs_ref, grad_ref, active_ref,
    total_ref, masked_ref, sum_ref, gain_out_ref, shift_out_ref,
):
    part = norm_back(
        core_ref, value_ref, gain_ref, mine_ref, theirs_ref, gain_out_ref, shift_out_ref
    )
    total = grad_ref[...].astype(F32) + part
    total_ref[...] = total
    masked = (active_ref[...] * total).astype(LOW)
    masked_ref[...] = masked
    sum_ref[...] = jnp.sum(masked.astype(F32), axis=0, keepdims=True)


def norm_one_back_kernel(
    core_ref, value_ref, gain_ref, mine_ref, theirs_ref, grad_ref,
    total_ref, gain_out_ref, shift_out_ref,
):
    part = norm_back(
        core_ref, value_ref, gain_ref, mine_ref, theirs_ref, gain_out_ref, shift_out_ref
    )
    total_ref[...] = (grad_ref[...].astype(F32) + part).astype(LOW)


def by_rows(kernel, core, outs, *operands):
    vmem = pl.BlockSpec(memory_space=pltpu.VMEM)
    return pl.pallas_call(
        kernel,
        in_specs=[pl.BlockSpec(memory_space=pltpu.SMEM)] + [vmem] * len(operands),
        out_specs=[vmem] * len(outs),
        out_shape=[jax.ShapeDtypeStruct(shape, dtype) for shape, dtype in outs],
        compiler_params=limit(24),
        cost_estimate=estimate(
            20 * operands[0].size, sum(o.size * o.dtype.itemsize for o in operands)
        ),
    )(core, *operands)


def product_kernel(count, turned, *refs):
    lefts, out_ref, left_turned, right = refs[:count], refs[-3], refs[-2], refs[-1]
    rights = refs[count:-3]
    length = lefts[0].shape[0]

    @pl.when(pl.program_id(0) == 0)
    def _():
        for d, left in enumerate(lefts):
            left_turned[:, d * length : (d + 1) * length] = left[...].T

    row = 0
    for piece in rights:
        value = piece[0] if len(piece.shape) == 3 else piece[...]
        if turned:
            value = roll_rows(value)
        right[row : row + value.shape[0]] = value
        row += value.shape[0]
    out_ref[...] = dot(left_turned[...], right[...], 1, 0).astype(LOW)


def rows_product(lefts, rights, tall, block, steps, turned=False):
    length = lefts[0][0].shape[0]
    left_specs = [
        pl.BlockSpec((length, tall), functools.partial(lambda c, j: (0, c), c)) for _, c in lefts
    ]
    right_specs = [pl.BlockSpec(shape, place) for _, shape, place in rights]
    total = length * len(lefts)
    return pl.pallas_call(
        functools.partial(product_kernel, len(lefts), turned),
        grid=(steps,),
        in_specs=left_specs + right_specs,
        out_specs=pl.BlockSpec((tall, block), lambda j: (0, j)),
        out_shape=jax.ShapeDtypeStruct((tall, steps * block), LOW),
        scratch_shapes=[pltpu.VMEM((tall, total), LOW), pltpu.VMEM((total, block), LOW)],
        compiler_params=limit(32),
        cost_estimate=estimate(
            2 * tall * total * steps * block, 2 * total * (tall + steps * block)
        ),
    )(*[left[0] for left in lefts], *[right[0] for right in rights])


def columns_from(value, rows, row, first, block):
    return value, (rows, block), lambda j: (row, first + j)


def hold(values, after):
    return lax.optimization_barrier((values, after))[0]


def columns_kernel(table_ref, left_ref, *refs):
    total, first = 0.0, 0
    for weight_ref in refs[:-1]:
        depth = weight_ref.shape[0]
        total += dot(left_ref[:, first : first + depth], weight_ref[...], 1, 0)
        first += depth
    refs[-1][...] = total.astype(refs[-1].dtype)


def times_columns(left, weight, table, block, dtype):
    rows, depth = left.shape
    steps = table.shape[0]
    return pl.pallas_call(
        columns_kernel,
        grid_spec=pltpu.PrefetchScalarGridSpec(
            num_scalar_prefetch=1,
            grid=(steps,),
            in_specs=[
                pl.BlockSpec((rows, depth), lambda i, t: (0, 0)),
                *[
                    pl.BlockSpec(
                        (depth // STREAMS, block),
                        functools.partial(lambda r, i, t: (r, t[i]), r),
                    )
                    for r in range(STREAMS)
                ],
            ],
            out_specs=pl.BlockSpec((rows, block), lambda i, t: (0, i)),
        ),
        out_shape=jax.ShapeDtypeStruct((rows, steps * block), dtype),
        compiler_params=limit(24),
        cost_estimate=estimate(2 * rows * depth * steps * block, 2 * depth * (rows + steps * block) + 4 * rows * steps * block),
    )(table, left, *[far(weight)] * STREAMS)


def back_kernel(turned, table_ref, left_ref, *refs):
    weights, out_ref = refs[:STREAMS], refs[-1]
    starts = refs[STREAMS:-1]
    left = left_ref[...]
    if turned:
        left = roll_rows(left)
    first = 0
    for weight_ref in weights:
        deep = weight_ref.shape[0]
        part = dot(left, weight_ref[...], 1, 1)
        columns = slice(first, first + deep)
        first += deep

        @pl.when(pl.program_id(1) == 0)
        def _(part=part, columns=columns):
            out_ref[:, columns] = part + starts[0][:, columns] if starts else part

        @pl.when(pl.program_id(1) > 0)
        def _(part=part, columns=columns):
            out_ref[:, columns] += part


def times_back(left, weight, table, block, deep, start=None, turned=False):
    rows = left.shape[0]
    depth = weight.shape[0]
    steps = table.shape[0]
    out_spec = pl.BlockSpec((rows, deep), lambda k, i, t: (0, k))
    in_specs = [
        pl.BlockSpec((rows, block), lambda k, i, t: (0, i)),
        *[
            pl.BlockSpec(
                (deep // STREAMS, block),
                functools.partial(lambda r, k, i, t: (k * STREAMS + r, t[i]), r),
            )
            for r in range(STREAMS)
        ],
    ]
    operands = [table, left, *[far(weight)] * STREAMS]
    if start is not None:
        in_specs.append(out_spec)
        operands.append(start)
    return pl.pallas_call(
        functools.partial(back_kernel, turned),
        grid_spec=pltpu.PrefetchScalarGridSpec(
            num_scalar_prefetch=1,
            grid=(depth // deep, steps),
            in_specs=in_specs,
            out_specs=out_spec,
        ),
        out_shape=jax.ShapeDtypeStruct((rows, depth), F32),
        compiler_params=limit(32),
        cost_estimate=estimate(2 * rows * depth * steps * block, 2 * steps * block * (rows + depth) + 8 * rows * depth),
    )(*operands)


def inner_kernel(grad_ref, *refs):
    weights = refs[:STREAMS]
    mine_ref, theirs_ref, bias_ref, act_ref, out_ref, sum_ref = refs[STREAMS:]
    first = 0
    for weight_ref in weights:
        columns = slice(first, first + weight_ref.shape[0])
        first += weight_ref.shape[0]
        theirs = roll_rows(theirs_ref[:, columns])
        act, slope = gelu_and_slope(mine_ref[:, columns] + theirs + bias_ref[:, columns])
        act_ref[:, columns] = act.astype(LOW)
        grad = (dot(grad_ref[...], weight_ref[...], 1, 1) * slope).astype(LOW)
        out_ref[:, columns] = grad
        sum_ref[:, columns] = jnp.sum(grad.astype(F32), axis=0, keepdims=True)


def inner_layer(grads, weight, mine, theirs, bias, block):
    rows, width = grads.shape
    hidden = weight.shape[0]
    part = pl.BlockSpec((rows, block), lambda i: (0, i))
    line = pl.BlockSpec((1, block), lambda i: (0, i))
    return pl.pallas_call(
        inner_kernel,
        grid=(hidden // block,),
        in_specs=[
            pl.BlockSpec((rows, width), lambda i: (0, 0)),
            *[
                pl.BlockSpec(
                    (block // STREAMS, width),
                    functools.partial(lambda r, i: (i * STREAMS + r, 0), r),
                )
                for r in range(STREAMS)
            ],
            part,
            part,
            line,
        ],
        out_specs=[part, part, line],
        out_shape=[
            jax.ShapeDtypeStruct((rows, hidden), LOW),
            jax.ShapeDtypeStruct((rows, hidden), LOW),
            jax.ShapeDtypeStruct((1, hidden), F32),
        ],
        compiler_params=limit(32),
        cost_estimate=estimate(2 * rows * width * hidden, 2 * width * (rows + hidden) + 12 * rows * hidden),
    )(grads, *[far(weight)] * STREAMS, mine, theirs, bias)


def head_chances(queries, keys, lanes_of_head, allowed):
    keys_of_head = jnp.where(lanes_of_head, keys, jnp.zeros_like(keys))
    scores = dot(queries, keys_of_head, 1, 1) * (HEAD_DIM**-0.5)
    scores = jnp.where(allowed, scores, -1e30)
    raised = jnp.exp(scores - jnp.max(scores, axis=-1, keepdims=True))
    return raised / jnp.sum(raised, axis=-1, keepdims=True)


def attend_masks(first, length, lanes):
    lane = lax.broadcasted_iota(jnp.int32, (length, lanes), 1)
    row = lax.broadcasted_iota(jnp.int32, (length, length), 0) + first
    column = lax.broadcasted_iota(jnp.int32, (length, length), 1) + first
    row = jnp.where(row >= length, row - length, row)
    column = jnp.where(column >= length, column - length, column)
    return lane, column <= row


def attend_forward_kernel(first_ref, *refs):
    mine, theirs, biases, lows, o_ref = refs[:3], refs[3:6], refs[6:9], refs[9:12], refs[12]
    sums = [
        (m[...] + roll_rows(t[...]) + b[...]).astype(LOW)
        for m, t, b in zip(mine, theirs, biases)
    ]
    for low, value in zip(lows, sums):
        low[...] = value
    queries, keys, values = sums
    lane, allowed = attend_masks(first_ref[0], *queries.shape)
    total = jnp.zeros(queries.shape, F32)
    for head in range(queries.shape[1] // HEAD_DIM):
        own = lane // HEAD_DIM == head
        chances = head_chances(queries, keys, own, allowed).astype(LOW)
        total += dot(chances, jnp.where(own, values, jnp.zeros_like(values)), 1, 0)
    o_ref[...] = total.astype(LOW)


def attend_forward(first, mine, theirs, bias):
    length, width = mine.shape
    width //= 3
    steps = width // 128
    parts = [
        pl.BlockSpec((length, 128), functools.partial(lambda p, i, t: (0, p * steps + i), p))
        for p in range(3)
    ]
    lines = [
        pl.BlockSpec((1, 128), functools.partial(lambda p, i, t: (0, p * steps + i), p))
        for p in range(3)
    ]
    return pl.pallas_call(
        attend_forward_kernel,
        grid_spec=pltpu.PrefetchScalarGridSpec(
            num_scalar_prefetch=1,
            grid=(steps,),
            in_specs=parts + parts + lines,
            out_specs=[parts[0]] * 4,
        ),
        out_shape=[jax.ShapeDtypeStruct((length, width), LOW)] * 4,
        compiler_params=limit(16),
        cost_estimate=estimate(4 * length * length * width, 32 * length * width),
    )(first, mine, mine, mine, theirs, theirs, theirs, bias, bias, bias)


def attend_backward_kernel(first_ref, q_ref, k_ref, v_ref, g_ref, out_ref):
    queries, keys, values, grads = q_ref[...], k_ref[...], v_ref[...], g_ref[...]
    lane, allowed = attend_masks(first_ref[0], *queries.shape)
    dq = jnp.zeros(queries.shape, F32)
    dk = jnp.zeros(queries.shape, F32)
    dv = jnp.zeros(queries.shape, F32)
    for head in range(queries.shape[1] // HEAD_DIM):
        own = lane // HEAD_DIM == head
        chances = head_chances(queries, keys, own, allowed)
        head_grads = jnp.where(own, grads, jnp.zeros_like(grads))
        dv += dot(chances.astype(LOW), head_grads, 0, 0)
        chance_grads = dot(head_grads, values, 1, 1)
        inner = jnp.sum(chances * chance_grads, axis=-1, keepdims=True)
        score_grads = (chances * (chance_grads - inner)).astype(LOW)
        dq += dot(score_grads, jnp.where(own, keys, jnp.zeros_like(keys)), 1, 0)
        dk += dot(score_grads, jnp.where(own, queries, jnp.zeros_like(queries)), 0, 0)
    scale = HEAD_DIM**-0.5
    out_ref[0] = (dq * scale).astype(LOW)
    out_ref[1] = (dk * scale).astype(LOW)
    out_ref[2] = dv.astype(LOW)


def attend_backward(first, *operands):
    length, width = operands[0].shape
    block = pl.BlockSpec((length, 128), lambda i, t: (0, i))
    return pl.pallas_call(
        attend_backward_kernel,
        grid_spec=pltpu.PrefetchScalarGridSpec(
            num_scalar_prefetch=1,
            grid=(width // 128,),
            in_specs=[block] * 4,
            out_specs=pl.BlockSpec((3, length, 128), lambda i, t: (0, 0, i)),
        ),
        out_shape=jax.ShapeDtypeStruct((3, length, width), LOW),
        compiler_params=limit(16),
        cost_estimate=estimate(10 * length * length * width, 14 * length * width),
    )(first, *operands)


def place_kernel(high, table_ref, *refs):
    count = len(refs) - 4
    pieces, out_ref, held, sems = refs[:count], refs[-3], refs[-2], refs[-1]
    slots, broad = held.shape[0], held.shape[2]

    def copy(step):
        row = pl.multiple_of(table_ref[2 * step] * high, high)
        column = pl.multiple_of(table_ref[2 * step + 1] * broad, broad)
        return pltpu.make_async_copy(
            held.at[step % slots],
            out_ref.at[pl.ds(row, high), pl.ds(column, broad)],
            sems.at[step % slots],
        )

    step = 0
    for piece in pieces:
        for i in range(piece.shape[0] // high):
            for j in range(piece.shape[1] // broad):
                if step >= slots:
                    copy(step - slots).wait()
                part = piece[i * high : (i + 1) * high, j * broad : (j + 1) * broad]
                held[step % slots] = part.astype(F32)
                copy(step).start()
                step += 1
    for waited in range(max(step - slots, 0), step):
        copy(waited).wait()


def place(pieces, whole, places, high, broad):
    slots = 4
    vmem = pl.BlockSpec(memory_space=pltpu.VMEM)
    return pl.pallas_call(
        functools.partial(place_kernel, high),
        in_specs=[pl.BlockSpec(memory_space=pltpu.SMEM)]
        + [vmem] * len(pieces)
        + [pl.BlockSpec(memory_space=pl.ANY)],
        out_specs=pl.BlockSpec(memory_space=pl.ANY),
        out_shape=jax.ShapeDtypeStruct(whole.shape, F32),
        scratch_shapes=[
            pltpu.VMEM((slots, high, broad), F32),
            pltpu.SemaphoreType.DMA((slots,)),
        ],
        input_output_aliases={len(pieces) + 1: 0},
        compiler_params=limit(32),
        cost_estimate=estimate(0, sum(6 * p.size for p in pieces)),
    )(jnp.stack(places).astype(jnp.int32), *pieces, whole)


def blank_kernel(out_ref):
    pass


def blank(shape, dtype=F32):
    return pl.pallas_call(
        blank_kernel,
        out_specs=pl.BlockSpec(memory_space=pl.ANY),
        out_shape=jax.ShapeDtypeStruct(shape, dtype),
    )()


class Lane:
    def __init__(self):
        self.last = ()

    def send(self, sends, after=()):
        values = hold([v for v, _ in sends], (self.last, after))
        self.last = [lax.ppermute(v, "dp", m) for v, (_, m) in zip(values, sends)]
        return self.last


def per_device(
    hidden,
    cotangent,
    exit_layers,
    qkv_weight,
    out_weight,
    up_weight,
    down_weight,
    query_bias,
    value_bias,
    out_bias,
    up_bias,
    down_bias,
    attn_gain,
    attn_shift,
    ffn_gain,
    ffn_shift,
):
    core = lax.axis_index("sp")
    other = 1 - core
    chips = lax.axis_size("dp")
    plane = chips // LINE
    chip = lax.axis_index("dp")
    spot = chip % GROUP
    level = chip // plane
    rows = hidden.shape[1]
    width = hidden.shape[2]
    length = 2 * rows
    half = width // 2
    inner = up_weight.shape[1]
    inner_half = inner // 2
    across, first_hop, middle_hop, last_hop = (Lane() for _ in range(4))

    def swap(value):
        return lax.ppermute(value, "sp", [(0, 1), (1, 0)])

    def in_plane(distance):
        return [(i, i // plane * plane + ((i % plane) ^ distance)) for i in range(chips)]

    def along(*moves):
        return [(a * plane + i, b * plane + i) for a, b in moves for i in range(plane)]

    inward, middle_moves, outward = (
        along((0, 1), (3, 2)),
        along((1, 2), (2, 1)),
        along((1, 0), (2, 3)),
    )

    def split(value, axis, size):
        return (
            lax.dynamic_slice_in_dim(value, core * size, size, axis),
            lax.dynamic_slice_in_dim(value, other * size, size, axis),
        )

    def exchange(blocks):
        return blocks[:1] + across.send([(blocks[d], in_plane(d)) for d in range(1, GROUP)])

    def gather_group(value):
        return exchange([value] * GROUP)

    def blocks_of(value, axis, size):
        return [
            lax.dynamic_slice_in_dim(value, (spot ^ d) * size, size, axis) for d in range(GROUP)
        ]

    def scatter_group(value, axis, size):
        return exchange(blocks_of(value, axis, size))

    end = (level == 0) | (level == LINE - 1)

    def line_start(value, after=()):
        return value + hold(first_hop.send([(value, inward)])[0], after)

    def line_middle(value):
        return value + middle_hop.send([(value, middle_moves)])[0]

    def line_end(value):
        return jnp.where(end, last_hop.send([(value, outward)])[0], value)

    def blocks_sum(value):
        distance = GROUP
        while distance < plane:
            value = value + lax.ppermute(value, "dp", in_plane(distance))
            distance *= 2
        return value

    def spread(value, after, more=()):
        size = value.shape[0] // 2
        first, second = across.send([(value, in_plane(1)), (value, in_plane(2))], after[0])
        upper, lower, *more = across.send(
            [(first[:size], in_plane(2)), (second[size:], in_plane(1)), *more], after[1]
        )
        return [value, first, second, upper, lower], more

    def table(size, start, count=None):
        return jnp.arange(size if count is None else count, dtype=jnp.int32) + start

    active = active_rows(exit_layers[0], core * rows, rows, length)
    core_number = core.astype(jnp.int32)[None]
    first_row = (core * rows).astype(jnp.int32)[None]
    full, part, line = (rows, width), (rows, half), (1, width)

    always = exit_layers[0, 1] > 0

    def segment(steps, *operands):
        def skip(*_):
            return [blank(shape.shape, shape.dtype) for shape in jax.eval_shape(steps, *operands)]

        return lax.cond(always, lambda *o: list(steps(*o)), skip, *operands)

    mine, theirs, down_grad, down_sums = by_rows(
        norm_one_kernel,
        core_number,
        [(part, LOW), (part, LOW), (full, LOW), (line, F32)],
        hidden[0],
        attn_gain[None],
        attn_shift[None],
        cotangent[0],
        active,
    )
    down_mine = gather_group(down_grad)
    qkv_block = min(1024, half)
    qkv_count = half // qkv_block
    bias = jnp.stack([query_bias, jnp.zeros_like(query_bias), value_bias])
    bias = lax.dynamic_slice_in_dim(bias, core * half, half, 1).reshape(1, -1)

    def qkv_table(c):
        return jnp.concatenate(
            [table(qkv_count, (2 * p + c) * qkv_count) for p in range(3)]
        )

    def to_attended(mine, theirs, down_grad, qkv_weight, bias, my_table, their_table, first_row):
        normed = jnp.concatenate([mine, swap(theirs)])
        theirs = times_columns(normed, qkv_weight, their_table, qkv_block, LOW)
        theirs = swap(theirs)
        mine = times_columns(normed, qkv_weight, my_table, qkv_block, F32)
        results = attend_forward(first_row, mine, theirs, bias)
        both = jnp.concatenate([normed, results[3]], 1)
        return [*results, swap(down_grad), both]

    queries, keys, values, attended, down_grad_theirs, early = segment(
        to_attended, mine, theirs, down_grad, qkv_weight, bias,
        qkv_table(core), qkv_table(other), first_row,
    )
    attended, down_mine = lax.optimization_barrier((attended, down_mine))
    early = gather_group(early)
    block = min(1024, inner_half)
    count = inner_half // block

    def to_inner(
        hidden, active, attended, out_weight, lines, up_weight, tables, core_number,
        grads, down_weight,
    ):
        out_part = dot(attended, out_weight, 1, 0)
        middle, mine, theirs = by_rows(
            norm_two_kernel,
            core_number,
            [(full, F32), (part, LOW), (part, LOW)],
            hidden,
            active,
            out_part,
            swap(out_part[rows:]),
            *lines[:3],
        )
        normed = jnp.concatenate([mine, swap(theirs)])
        theirs = times_columns(normed, up_weight, tables[1], block, LOW)
        theirs = swap(theirs)
        mine = times_columns(normed, up_weight, tables[0], block, F32)
        results = inner_layer(
            grads, down_weight, mine, theirs, lines[3], min(512, inner_half)
        )
        return [middle, normed, *results]

    bias = lax.dynamic_slice_in_dim(up_bias, core * inner_half, inner_half).reshape(1, -1)
    middle, normed_two_half, inner_low, up_grad, up_sums = segment(
        to_inner, hidden[0], active, attended, out_weight,
        (out_bias[None], ffn_gain[None], ffn_shift[None], bias), up_weight,
        (table(count, core * count), table(count, other * count)), core_number,
        jnp.concatenate([down_grad, down_grad_theirs]), down_weight,
    )
    (inner_low, up_grad), early = lax.optimization_barrier(((inner_low, up_grad), early))

    down_left = scatter_group(inner_low, 1, inner_half // GROUP)

    def to_middle(
        up_grad, up_weight, middle, gain, cotangent, active, core_number, down_mine, tables
    ):
        theirs = swap(up_grad)
        grads = times_back(up_grad, up_weight, tables[0], inner_half, 256)
        grads = times_back(theirs, up_weight, tables[1], inner_half, 256, grads, True)
        results = by_rows(
            norm_two_back_kernel,
            core_number,
            [(full, F32), (full, LOW), (line, F32), (line, F32), (line, F32)],
            middle,
            gain,
            grads,
            swap(grads[rows:]),
            cotangent,
            active,
        )
        down_theirs = swap(jnp.concatenate(down_mine[1:]))
        return [*results, down_theirs, *blocks_of(up_grad, 1, inner_half // GROUP)]

    (
        middle_grad, attn_grad, attn_sums, gain_two_grad, shift_two_grad, down_theirs, *up_right
    ) = segment(
        to_middle, up_grad, up_weight, middle, ffn_gain[None], cotangent[0], active,
        core_number, down_mine, (table(1, core), table(1, other)),
    )
    down_theirs = [(down_grad_theirs, 0)] + [(down_theirs, d) for d in range(GROUP - 1)]

    def down_product(first, steps):
        rights = []
        for own, (value, row) in zip(down_mine, down_theirs):
            rights.append(columns_from(own, rows, 0, first, quarter))
            rights.append(columns_from(value, rows, row, first, quarter))
        lefts = [(left, 0) for left in down_left]
        return rows_product(lefts, rights, inner_half // GROUP, quarter, steps)

    quarter = width // 4
    down_left, attn_grad = lax.optimization_barrier((down_left, attn_grad))
    up_right = exchange(up_right)
    sums = [down_product(0, 1)]
    (come,) = first_hop.send([(sums[0], inward)])
    attn_grad, sums[0] = lax.optimization_barrier((attn_grad, sums[0]))

    def to_qkv(attn_grad, out_weight, first_row, *operands):
        grads = jnp.concatenate([attn_grad, swap(attn_grad)])
        grads = dot(grads, out_weight, 1, 1).astype(LOW)
        qkv_grad = attend_backward(first_row, *operands, grads)
        flat = jnp.concatenate([qkv_grad[0], qkv_grad[1], qkv_grad[2]], 1)
        blocks = []
        for wide, block in zip(
            blocks_of(attn_grad, 1, width // GROUP), blocks_of(qkv_grad, 2, half // GROUP)
        ):
            narrow = wide.shape[1] // 2
            wide = jnp.concatenate([wide[:, :narrow], wide[:, narrow:]])
            blocks.append(jnp.concatenate([block, wide[None]]))
        return [qkv_grad, flat, swap(flat), *blocks]

    qkv_grad, flat, flat_theirs, *late = segment(to_qkv, attn_grad, out_weight, first_row, queries, keys, values)
    sums.append(down_product(1, 1))
    qkv_grad, up_right, come, sums = lax.optimization_barrier((qkv_grad, up_right, come, sums))
    sums[0] += come
    (passed,) = middle_hop.send([(sums[0], middle_moves)])
    (come,) = first_hop.send([(sums[1], inward)])
    up_left = gather_group(normed_two_half)

    def to_input(flat, theirs, qkv_weight, tables):
        grads = times_back(flat, qkv_weight, tables[0], qkv_block, 512)
        return [times_back(theirs, qkv_weight, tables[1], qkv_block, 512, grads, True)]

    (grads,) = segment(
        to_input, hold(flat, qkv_grad), flat_theirs, qkv_weight,
        (qkv_table(core), qkv_table(other)),
    )
    grads, up_left, passed, come = lax.optimization_barrier((grads, up_left, passed, come))
    sums[0] += passed
    sums[1] += come
    late = exchange(late)
    value = hold(down_product(2, 1), grads)
    come = first_hop.send([(value, inward)])
    passed, come, late = lax.optimization_barrier(
        (last_hop.send([(sums[0], outward)]), come, late)
    )
    sums[0] = jnp.where(end, passed[0], sums[0])
    sums.append(value + come[0])
    sums.append(line_start(hold(down_product(3, 1), late)))

    def to_ends(grads, hidden, gain, middle_grad, core_number, inner_low, down_weight):
        results = by_rows(
            norm_one_back_kernel,
            core_number,
            [(full, LOW), (line, F32), (line, F32)],
            hidden,
            gain,
            grads,
            swap(grads[rows:]),
            middle_grad,
        )
        down_part = dot(inner_low, down_weight, 1, 0)
        return [*results, down_part[:rows], swap(down_part[rows:])]

    input_grad, gain_one_grad, shift_one_grad, mine, theirs = to_ends(
        hold(grads, sums[0]), hidden[0], attn_gain[None], middle_grad, core_number,
        inner_low, down_weight,
    )
    output = middle + active * (mine + theirs + down_bias)

    def widen(value):
        none = jnp.zeros_like(value)
        return jnp.where(
            core == 0, jnp.concatenate([value, none]), jnp.concatenate([none, value])
        )

    qkv_sums = jnp.sum(qkv_grad.astype(F32), axis=1)
    small = jnp.concatenate(
        [
            widen(qkv_sums[0]),
            widen(qkv_sums[2]),
            attn_sums[0],
            widen(up_sums[0]),
            down_sums[0],
            gain_one_grad[0],
            shift_one_grad[0],
            gain_two_grad[0],
            shift_two_grad[0],
        ]
    ).reshape(-1, 128)
    small = small + swap(small)

    small_sends = [(small, in_plane(d)) for d in range(1, GROUP)]

    def pair_sums(values):
        while len(values) > 1:
            values = [a + b for a, b in zip(values[::2], values[1::2])]
        return values[0]

    def line_moves(distance):
        return [(i, (i // plane ^ distance) * plane + i % plane) for i in range(chips)]

    chunks = [("down", value, index) for index, value in enumerate(sums)]
    chunks += [("up", None, 2 * GROUP * core), ("up", None, 2 * GROUP * core + 1)]
    chunks += [("up", None, 2 * GROUP * other), ("up", None, 2 * GROUP * other + 1)]
    chunks += [("qkv", None, core), ("qkv", None, other), ("out", None, 0)]
    up_width = inner_half // GROUP
    up_block = min(512, up_width)

    def up_products(rights, turned):
        lefts = [(left, 0) for left in up_left]
        return [
            rows_product(lefts, [right(first) for right in rights], half, up_block, 1, turned)
            for first in range(up_width // up_block)
        ]

    def up_own():
        def place(right):
            return lambda first: columns_from(right, length, 0, first, up_block)

        return up_products([place(right) for right in hold(up_right, late)], False)

    def up_other(*mine):
        theirs = swap(jnp.concatenate(mine))

        def place(d):
            return lambda first: columns_from(theirs, length, d, first, up_block)

        return up_products([place(d) for d in range(GROUP)], True)

    rest_block = half // GROUP

    def rest_part(value, d):
        return value, (1, length, rest_block), lambda j: (4 * d + j, 0, 0)

    def rest_own(mine):
        lefts = [(left, 0) for left in early]
        rights = [rest_part(right, 0) for right in mine]
        return [rows_product(lefts, rights, half, rest_block, 3)]

    def rest_other(*mine):
        theirs = swap(jnp.concatenate(mine))

        def out_part(value, d):
            return value, (1, rows, rest_block), lambda j: (4 * d + 3, j, 0)

        lefts = [(left, 0) for left in early]
        rights = [rest_part(theirs, d) for d in range(GROUP)]
        other_half = rows_product(lefts, rights, half, rest_block, 3, True)
        lefts = [(left, 1) for left in early]
        rights = []
        for d, right in enumerate(mine):
            rights += [out_part(right, 0), out_part(theirs, d)]
        return [other_half, rows_product(lefts, rights, half, rest_block, 2)]

    wholes = {
        "down": blank((inner_half, width)),
        "up": blank((half, inner)),
        "out": blank((half, width)),
        "qkv": blank((half, 3 * width)),
    }
    size = inner_half // GROUP
    begun, raw = sums, []
    done = [(), ()]
    for index, (name, value, where) in enumerate(chunks):
        value = begun[index]
        more, held = (), [done[-1]]
        if index == 0:
            held.append(begun[3])
        fresh = []
        if index == 0:
            fresh = up_own()
        if index == 1:
            fresh = segment(up_other, *hold(up_right, done[-1]))
        if index == 3:
            fresh = rest_own(hold(late, done[-1]))
        if index == 5:
            fresh = segment(rest_other, *hold(late, done[-1]))
        raw += fresh
        held.append(fresh)
        if index == len(chunks) - 2:
            more = small_sends
        if index == len(chunks) - 1:
            small = pair_sums([small, *more_results])
            distance = GROUP
            while distance < plane:
                small = small + lax.ppermute(small, "dp", in_plane(distance))
                distance *= 2
            lines = [lax.ppermute(small, "dp", line_moves(d)) for d in range(1, LINE)]
            held += [done[-1], lines]
        after = (), held
        if 0 < index < len(chunks) - 1:
            value = line_end(line_middle(value))
        if index == len(chunks) - 2:
            last = line_middle(begun[-1])
            held.append(last)
            begun[-1] = line_end(last)
        pieces, more_results = spread(blocks_sum(value), after, more)
        value = pieces[0]
        tall, wide = value.shape
        high = min(256, tall)
        broad = wide // 3 if name == "qkv" else wide
        places = []
        for d in range(GROUP):
            owner = spot ^ d
            for i in range(tall // high):
                row = jnp.int32(i)
                if name == "down":
                    row, columns = owner * (tall // high) + i, [jnp.int32(where)]
                elif name == "up":
                    columns = [where + owner * (size // wide)]
                elif name == "out":
                    columns = [owner]
                else:
                    columns = [(2 * p + where) * GROUP + owner for p in range(3)]
                for column in columns:
                    places += [row, column]
        wholes[name] = place(pieces, wholes[name], places, high, broad)
        done.append(wholes[name])
        while len(begun) < len(chunks) and raw:
            number = len(begun)
            placed = number - (4 if number < 8 else 5)
            if placed > index:
                break
            begun.append(line_start(hold(raw.pop(0), done[placed + 2])))

    small = pair_sums([small, *lines]).reshape(-1)
    small_grads = []
    first = 0
    for size in (width, width, width, inner, width, width, width, width, width):
        small_grads.append(small[first : first + size])
        first += size

    return (
        output.astype(LOW)[None],
        input_grad[None],
        wholes["qkv"],
        wholes["out"],
        wholes["up"],
        wholes["down"],
        *small_grads,
    )


def solution(mesh):
    return jax.shard_map(
        per_device,
        mesh=mesh,
        in_specs=(
            P("dp", "sp", None),
            P("dp", "sp", None),
            P("dp", None),
            P("sp", None),
            P("sp", None),
            P("sp", None),
            P("sp", None),
            P(),
            P(),
            P(),
            P(),
            P(),
            P(),
            P(),
            P(),
            P(),
        ),
        out_specs=(
            P("dp", "sp", None),
            P("dp", "sp", None),
            P("sp", None),
            P("sp", None),
            P("sp", None),
            P("sp", None),
            P(),
            P(),
            P(),
            P(),
            P(),
            P(),
            P(),
            P(),
            P(),
        ),
        check_vma=False,
    )
```
